32 devices in a mesh: groups: 2 (over x), feat: 8 (over z, y), rep: 2 (over core).
Axes of the slice: x: 2, y: 2, z: 4, core: 2. Of those that a mesh axis runs over, the one named last changes fastest.
Arguments:
- src_feats: bfloat16 [768, 24576], P('feat', 'groups'), parts along dimension 1, may hold values from -6 to 6
- nbr_one: int32 [16, 2, 10, 192], P('groups', 'rep'), parts along dimension 0, may hold values from 0 to 12287
- counts: int32 [16, 2], P(('groups', 'feat'), 'rep'), parts along dimension 0, may hold values from 1 to 192, as said below
- seed_rows: int32 [2048], P(('groups', 'feat', 'rep')), parts along dimension 0, may hold values from 0 to 3071, as said below
- nbr_two: int32 [2048, 15], P(('groups', 'feat', 'rep')), parts along dimension 0, may hold values from 0 to 3071, as said below
- w1_self: bfloat16 [768, 512], P('feat'), may hold values from -0.15625 to 0.15625
- w1_nbr: bfloat16 [768, 512], P('feat'), may hold values from -0.15625 to 0.15625
- bias_one: float32 [512], replicated, may hold values from -3 to 3
- w2_self: bfloat16 [512, 512], replicated, may hold values from -0.25 to 0.25
- w2_nbr: bfloat16 [512, 512], replicated, may hold values from -0.25 to 0.25
- bias_two: float32 [512], replicated, may hold values from -3 to 3
Outputs:
- hidden_one: bfloat16 [16, 2, 192, 512], P(('groups', 'feat'), 'rep'), parts along dimension 0
- seed_out: bfloat16 [2048, 512], P(('groups', 'feat', 'rep')), parts along dimension 0
The draws below stay inside these ranges and needn't reach their ends.
There are 2 independent parts, one for each index of `groups`. The reference program is written for one: setup_inputs(seed, part) draws one part's arguments, and reference() takes and returns one part's arrays. A program takes and returns all parts, laid end to end along the dimension named above; an argument that names none is the same for every part. Nothing has to cross between parts.
Inputs may be any that keep to these rules, and one draw needn't show every extreme that they name: `counts`: in every draw one partition has exactly 192 live rows. `seed_rows`: every entry is a live layer-one row p * 192 + j with j < the live rows of partition p. `nbr_two`: every entry is a live layer-one row p * 192 + j with j < the live rows of partition p.
All inputs are finite; a program needn't handle non-finite values.
Results may differ from the reference program's by a relative error of at most 0.013.
Values may be sent and summed in bfloat16 or wider, within the bound.
No kernel may reach another device: no remote copies, remote signals or barrier semaphores. Data moves between devices by JAX's collectives and lax.ppermute only.
A program may use at most 128 MiB of HBM per device.

```python
import jax
import jax.numpy as jnp

F = 768
H = 512
K1 = 10
K2 = 15
PCAP = 192
PARTS_SIZE = 16
N2 = 12288
SEEDS = 1024
N_FEAT = 8
N_REP = 2


def live_counts(key):
    key = jax.random.fold_in(key, 11)
    first, second = jax.random.split(key)
    lowest = max(PCAP // 8, 1)
    raw = jax.random.randint(first, (PARTS_SIZE,), lowest, PCAP + 1)
    full = jax.random.randint(second, (), 0, PARTS_SIZE)
    return jnp.where(jnp.arange(PARTS_SIZE) == full, PCAP, raw).astype(jnp.int32)


def pick_rows(key, live, shape):
    first, second = jax.random.split(key)
    partition = jax.random.randint(first, shape, 0, PARTS_SIZE)
    offset = jax.random.randint(second, shape, 0, 1 << 20) % live[partition]
    return (partition * PCAP + offset).astype(jnp.int32)


def draw_counts(key, part):
    live = live_counts(key)
    return live.reshape(N_FEAT, N_REP)


def draw_seed_rows(key, part):
    live = live_counts(key)
    key = jax.random.fold_in(key, 3)
    return pick_rows(key, live, (SEEDS,))


def draw_nbr_two(key, part):
    live = live_counts(key)
    key = jax.random.fold_in(key, 7)
    return pick_rows(key, live, (SEEDS, K2))


def plant(entries, own_key, least, top_value):
    longest = entries.shape.index(max(entries.shape))
    spots = []
    for shift in (0, 1):
        where = [jax.random.randint(jax.random.fold_in(own_key, axis), (), 0, length) for axis, length in enumerate(entries.shape)]
        where[longest] = (where[longest] + shift) % entries.shape[longest]
        spots.append(tuple(where))
    return entries.at[spots[0]].set(least).at[spots[1]].set(top_value)


def steps_of(stream_key, extent, cuts, least, largest):
    loudness, own = 1.0, jax.random.fold_in(stream_key, 6)
    for dim, blocks in cuts:
        steps = jnp.exp(jax.random.uniform(jax.random.fold_in(own, dim), (blocks,), jnp.float32, least / len(cuts), largest / len(cuts)))
        loudness = loudness * jnp.repeat(steps, extent[dim] // blocks).reshape([-1 if axis == dim else 1 for axis in range(len(extent))])
    return loudness


def gaussian(key, dims, spread, limit, cuts=(), kind=jnp.bfloat16):
    values = jax.random.normal(key, dims, jnp.float32) * spread
    if len(cuts) > 0:
        values = steps_of(key, dims, cuts, -0.22, 0.18) * values
    return jnp.clip(values, min=-limit, max=limit).astype(kind)


def setup_inputs(seed: int = 0, part: int = 0) -> dict:
    splits = jax.random.split(jax.random.key(seed), 12)
    own_keys = jax.random.split(jax.random.fold_in(splits[11], part), 12)
    src_feats = gaussian(own_keys[0], (F, N2), 1.0, 6.0, ((0, 8),))
    nbr_one = plant(jax.random.randint(own_keys[1], (N_FEAT, N_REP, K1, PCAP), 0, N2), jax.random.fold_in(own_keys[1], 1), 0, N2 - 1).astype(jnp.int32)
    counts = draw_counts(jax.random.fold_in(jax.random.fold_in(splits[11], part), 71), part)
    seed_rows = draw_seed_rows(jax.random.fold_in(jax.random.fold_in(splits[11], part), 71), part)
    nbr_two = draw_nbr_two(jax.random.fold_in(jax.random.fold_in(splits[11], part), 71), part)
    w1_self = gaussian(splits[5], (F, H), (2 * F) ** -0.5, 0.15625, ((0, 8),))
    w1_nbr = gaussian(splits[6], (F, H), (2 * F) ** -0.5, 0.15625, ((0, 8),))
    bias_one = gaussian(splits[7], (H,), 0.5, 3.0, (), jnp.float32)
    w2_self = gaussian(splits[8], (H, H), H ** -0.5, 0.25)
    w2_nbr = gaussian(splits[9], (H, H), H ** -0.5, 0.25)
    bias_two = gaussian(splits[10], (H,), 0.5, 3.0, (), jnp.float32)
    return dict(src_feats=src_feats, nbr_one=nbr_one, counts=counts, seed_rows=seed_rows, nbr_two=nbr_two, w1_self=w1_self, w1_nbr=w1_nbr, bias_one=bias_one, w2_self=w2_self, w2_nbr=w2_nbr, bias_two=bias_two)


def reference(src_feats, nbr_one, counts, seed_rows, nbr_two, w1_self, w1_nbr, bias_one, w2_self, w2_nbr, bias_two):
    parts = N_FEAT * N_REP
    rows_one = parts * PCAP
    self_rows = src_feats[:, :rows_one].T
    neighbor = jnp.transpose(nbr_one, (0, 1, 3, 2)).reshape(rows_one, K1)
    picked = jnp.take(src_feats, neighbor.reshape(-1), axis=1).astype(jnp.float32).reshape(F, rows_one, K1)
    agg_one = (jnp.sum(picked, axis=2) / K1).astype(jnp.bfloat16)
    pre_one = jnp.dot(self_rows, w1_self, preferred_element_type=jnp.float32) + jnp.dot(agg_one.T, w1_nbr, preferred_element_type=jnp.float32) + bias_one
    position = jnp.arange(rows_one, dtype=jnp.int32)
    live = (position % PCAP) < counts.reshape(parts)[position // PCAP]
    table = jnp.where(live[:, None], jnp.maximum(pre_one, 0.0), 0.0).astype(jnp.bfloat16)
    hidden_one = table.reshape(N_FEAT, N_REP, PCAP, H)
    self_two = jnp.take(table, seed_rows, axis=0)
    near = jnp.take(table, nbr_two.reshape(-1), axis=0).astype(jnp.float32).reshape(SEEDS, K2, H)
    agg_two = (jnp.sum(near, axis=1) / K2).astype(jnp.bfloat16)
    pre_two = jnp.dot(self_two, w2_self, preferred_element_type=jnp.float32) + jnp.dot(agg_two, w2_nbr, preferred_element_type=jnp.float32) + bias_two
    seed_out = jnp.maximum(pre_two, 0.0).astype(jnp.bfloat16)
    return hidden_one, seed_out
```

```python
import functools

import jax
import jax.numpy as jnp
from jax import lax
from jax.experimental import pallas as pl
from jax.experimental.pallas import tpu as pltpu
from jax.sharding import PartitionSpec as P

LANES = 128
VMEM_LIMIT = 50 * 1024 * 1024


def folds(fslice, pcap):
    return 4 * fslice == 3 * LANES and pcap % 64 == 0


def lookup_kernel(n_feat, n_rep, fanout, pcap, nbr_ref, src_ref, out_ref, table, total):
    fslice, nodes = src_ref.shape
    rep_pos = lax.axis_index("rep")
    width = 512

    def turn(step, carry):
        at = pl.multiple_of(step * width, width)
        block = src_ref[:, pl.ds(at, width)].astype(jnp.float32)
        table[pl.ds(at, width), :fslice] = block.T
        return carry

    lax.fori_loop(0, nodes // width, turn, 0)

    def partition(p, carry):
        first = p * (fanout * pcap)

        def group(g, inner):
            at = pl.multiple_of(g * 8, 8)
            for u in range(8):
                rows = [
                    table[pl.ds(nbr_ref[first + k * pcap + at + u], 1), :] for k in range(fanout)
                ]
                while len(rows) > 1:
                    rows = [a + b for a, b in zip(rows[::2], rows[1::2])] + (
                        [rows[-1]] if len(rows) % 2 else []
                    )
                total[pl.ds(at + u, 1), :] = rows[0]
            return inner

        lax.fori_loop(0, pcap // 8, group, 0)
        own_at = pl.multiple_of((p * n_rep + rep_pos) * pcap, 64)
        own = table[pl.ds(own_at, pcap), :]
        mean = total[...] / fanout
        if folds(fslice, pcap):
            lane = lax.broadcasted_iota(jnp.int32, (pcap, LANES), 1)
            turned = pltpu.roll(mean, fslice, 1)
            left = jnp.where(lane < fslice, own, turned)
            cut = pcap // 4 * 3
            part = pcap // 4
            tail_left = left[cut:]
            tail_right = turned[cut:]
            extra = jnp.concatenate(
                [pltpu.roll(tail_left, 64, 1), tail_left, pltpu.roll(tail_right, 64, 1)], axis=0
            )
            right = jnp.where(lane[:cut] < 64, turned[:cut], extra)
            out_ref[p, :, :LANES] = left[:cut].astype(jnp.bfloat16)
            out_ref[p, :, LANES:] = right.astype(jnp.bfloat16)
        else:
            out_ref[p, :, :fslice] = own[:, :fslice].astype(jnp.bfloat16)
            out_ref[p, :, fslice:] = mean[:, :fslice].astype(jnp.bfloat16)
        return carry

    lax.fori_loop(0, n_feat, partition, 0)


def count_kernel(pcap, idx_ref, out_ref):
    base = (lax.axis_index("feat") * lax.axis_size("rep") + lax.axis_index("rep")) * pcap
    seeds, columns = idx_ref.shape
    block = 256

    def rows(step, carry):
        at = pl.multiple_of(step * block, block)
        idx = idx_ref[pl.ds(at, block), :] - base
        slot = lax.broadcasted_iota(jnp.int32, (block, pcap), 1)
        own = jnp.where(slot == idx[:, :1], 1.0, 0.0)
        near = jnp.zeros((block, pcap), jnp.float32)
        for k in range(1, columns):
            near = near + jnp.where(slot == idx[:, k : k + 1], 1.0, 0.0)
        out_ref[0, pl.ds(at, block), :] = own.astype(jnp.bfloat16)
        out_ref[1, pl.ds(at, block), :] = near.astype(jnp.bfloat16)
        return carry

    lax.fori_loop(0, seeds // block, rows, 0)


def layer_kernel(
    pcap, fanout_two, count_ref, got_ref, w_ref, bias_ref, ws_ref, wn_ref, times_ref, hidden_ref, part_ref
):
    n_feat, _, _ = got_ref.shape
    width = w_ref.shape[2]
    pre = jnp.zeros((pcap, width), jnp.float32)
    for f in range(n_feat):
        block = got_ref[f]
        weight = w_ref[f]
        if block.shape[0] != pcap:
            cut = block.shape[0]
            part = cut // 3
            tail = block[:, LANES:].astype(jnp.float32)
            lane = lax.broadcasted_iota(jnp.int32, (part, LANES), 1)
            turned = pltpu.roll(tail, 64, 1)
            low_left = jnp.where(lane < 64, turned[:part], tail[part : 2 * part])
            left = jnp.concatenate([block[:, :LANES], low_left.astype(jnp.bfloat16)], axis=0)
            right = jnp.concatenate([tail, turned[2 * part :]], axis=0).astype(jnp.bfloat16)
            pre = pre + jnp.dot(left, weight[:LANES], preferred_element_type=jnp.float32)
            pre = pre + jnp.dot(right[:, :64], weight[LANES:], preferred_element_type=jnp.float32)
        else:
            pre = pre + jnp.dot(block, weight, preferred_element_type=jnp.float32)
    live = lax.broadcasted_iota(jnp.int32, (pcap, width), 0) < count_ref[0, 0]
    hidden = jnp.where(live, jnp.maximum(pre + bias_ref[...], 0.0), 0.0).astype(jnp.bfloat16)
    hidden_ref[...] = hidden
    own = jnp.dot(hidden, ws_ref[...], preferred_element_type=jnp.float32).astype(jnp.bfloat16)
    near = (
        jnp.dot(hidden, wn_ref[...], preferred_element_type=jnp.float32) / fanout_two
    ).astype(jnp.bfloat16)
    block = 256

    def rows(step, carry):
        at = pl.multiple_of(step * block, block)
        value = jnp.dot(
            times_ref[0, pl.ds(at, block), :], own, preferred_element_type=jnp.float32
        ) + jnp.dot(times_ref[1, pl.ds(at, block), :], near, preferred_element_type=jnp.float32)
        part_ref[pl.ds(at, block), :] = value.astype(jnp.bfloat16)
        return carry

    lax.fori_loop(0, part_ref.shape[0] // block, rows, 0)


def body(
    src_feats,
    nbr_one,
    counts,
    seed_rows,
    nbr_two,
    w1_self,
    w1_nbr,
    bias_one,
    w2_self,
    w2_nbr,
    bias_two,
):
    n_feat = lax.axis_size("feat")
    n_rep = lax.axis_size("rep")
    fslice, nodes = src_feats.shape
    fanout_one, pcap = nbr_one.shape[2:]
    width = w1_self.shape[1]
    seed_count, fanout_two = nbr_two.shape
    seeds = seed_count * n_feat * n_rep
    params = pltpu.CompilerParams(vmem_limit_bytes=VMEM_LIMIT)
    vmem = pl.BlockSpec(memory_space=pltpu.VMEM)
    smem = pl.BlockSpec(memory_space=pltpu.SMEM)

    weights = lax.all_gather(jnp.concatenate([w1_self, w1_nbr], axis=0), "feat", axis=0)
    wanted = jnp.concatenate([seed_rows[:, None], nbr_two], axis=1)
    wanted = lax.all_gather(wanted, ("feat", "rep"), axis=0, tiled=True)

    sent_shape = (pcap // 4 * 3, 2 * LANES) if folds(fslice, pcap) else (pcap, 2 * fslice)
    sent = pl.pallas_call(
        functools.partial(lookup_kernel, n_feat, n_rep, fanout_one, pcap),
        out_shape=jax.ShapeDtypeStruct((n_feat, *sent_shape), jnp.bfloat16),
        in_specs=[smem, vmem],
        out_specs=vmem,
        scratch_shapes=[
            pltpu.VMEM((nodes, LANES), jnp.float32),
            pltpu.VMEM((pcap, LANES), jnp.float32),
        ],
        compiler_params=params,
        name="lookup",
    )(nbr_one.reshape(-1), src_feats)
    got = lax.all_to_all(sent, "feat", 0, 0, tiled=True)

    times = pl.pallas_call(
        functools.partial(count_kernel, pcap),
        out_shape=jax.ShapeDtypeStruct((2, seeds, pcap), jnp.bfloat16),
        in_specs=[vmem],
        out_specs=vmem,
        compiler_params=params,
        name="times",
    )(wanted)

    hidden, partial_seed = pl.pallas_call(
        functools.partial(layer_kernel, pcap, fanout_two),
        out_shape=(
            jax.ShapeDtypeStruct((pcap, width), jnp.bfloat16),
            jax.ShapeDtypeStruct((seeds, width), jnp.bfloat16),
        ),
        in_specs=[smem] + [vmem] * 6,
        out_specs=(vmem, vmem),
        compiler_params=params,
        name="layers",
    )(counts, got, weights, bias_one[None], w2_self, w2_nbr, times)

    parts = lax.all_to_all(
        partial_seed.reshape(n_feat * n_rep, seed_count, width), ("feat", "rep"), 0, 0, tiled=True
    )
    pre_two = jnp.sum(parts.astype(jnp.float32), axis=0) + bias_two
    seed_out = jnp.maximum(pre_two, 0.0).astype(jnp.bfloat16)
    return (hidden[None, None], seed_out)


def solution(mesh):
    placed = (
        P("feat", "groups"),
        P("groups", "rep", None, None),
        P(("groups", "feat"), "rep"),
        P(("groups", "feat", "rep")),
        P(("groups", "feat", "rep"), None),
        P("feat", None),
        P("feat", None),
        P(),
        P(),
        P(),
        P(),
    )
    return jax.shard_map(
        body,
        mesh=mesh,
        in_specs=placed,
        out_specs=(P(("groups", "feat"), "rep", None, None), P(("groups", "feat", "rep"), None)),
        check_vma=False,
    )
```

```python
import functools

import jax
import jax.numpy as jnp
from jax import lax
from jax.experimental import pallas as pl
from jax.experimental.pallas import tpu as pltpu
from jax.sharding import PartitionSpec as P

LANES = 128
MIB = 1024 * 1024


def folds(fslice, pcap):
    return 4 * fslice == 3 * LANES and pcap % 64 == 0


def turn_kernel(src_ref, table_ref):
    fslice, nodes = src_ref.shape
    width = 512

    def turn(step, carry):
        at = pl.multiple_of(step * width, width)
        table_ref[pl.ds(at, width), :fslice] = src_ref[:, pl.ds(at, width)].astype(jnp.float32).T
        return carry

    lax.fori_loop(0, nodes // width, turn, 0)


def mean_kernel(steps, n_rep, fanout, pcap, fslice, nbr_ref, table_ref, *refs):
    out_refs, total = refs[:-1], refs[-1]
    feat_pos = lax.axis_index("feat")
    rep_pos = lax.axis_index("rep")
    for step, out_ref in zip(steps, out_refs):
        p = jnp.bitwise_xor(feat_pos, step)
        first = p * (fanout * pcap)

        def group(g, carry):
            at = pl.multiple_of(g * 8, 8)
            for u in range(8):
                rows = [
                    table_ref[pl.ds(nbr_ref[first + k * pcap + at + u], 1), :]
                    for k in range(fanout)
                ]
                while len(rows) > 1:
                    rows = [a + b for a, b in zip(rows[::2], rows[1::2])] + (
                        [rows[-1]] if len(rows) % 2 else []
                    )
                total[pl.ds(at + u, 1), :] = rows[0]
            return carry

        lax.fori_loop(0, pcap // 8, group, 0)
        own_at = pl.multiple_of((p * n_rep + rep_pos) * pcap, 64)
        own = table_ref[pl.ds(own_at, pcap), :]
        mean = total[...] / fanout
        if folds(fslice, pcap):
            lane = lax.broadcasted_iota(jnp.int32, (pcap, LANES), 1)
            turned = pltpu.roll(mean, fslice, 1)
            left = jnp.where(lane < fslice, own, turned)
            cut = pcap // 4 * 3
            tail_left = left[cut:]
            tail_right = turned[cut:]
            extra = jnp.concatenate(
                [pltpu.roll(tail_left, 64, 1), tail_left, pltpu.roll(tail_right, 64, 1)], axis=0
            )
            right = jnp.where(lane[:cut] < 64, turned[:cut], extra)
            out_ref[:, :LANES] = left[:cut].astype(jnp.bfloat16)
            out_ref[:, LANES:] = right.astype(jnp.bfloat16)
        else:
            out_ref[:, :fslice] = own[:, :fslice].astype(jnp.bfloat16)
            out_ref[:, fslice:] = mean[:, :fslice].astype(jnp.bfloat16)


def prepare_kernel(fslice, pcap, seed_count, n_idx, mine_ref, other_ref, w_ref, own_ref, near_ref):
    n_feat = mine_ref.shape[0]
    rep_pos = lax.axis_index("rep")
    base = (lax.axis_index("feat") * lax.axis_size("rep") + rep_pos) * pcap
    base = base.astype(jnp.float32)
    pair = 2 * seed_count
    slot = lax.broadcasted_iota(jnp.int32, (pcap, pair), 0).astype(jnp.float32)
    low = lax.broadcasted_iota(jnp.int32, (n_idx, pair), 1) < seed_count
    for half, ref in enumerate((mine_ref, other_ref)):
        for s in range(n_feat):
            w_ref[s, rep_pos if half == 0 else 1 - rep_pos] = ref[s, :fslice]
        for s in range(0, n_feat, 2):
            first = ref[s, fslice : fslice + n_idx, :pair].astype(jnp.float32)
            second = ref[s + 1, fslice : fslice + n_idx, :pair].astype(jnp.float32)
            high_part = jnp.where(low, first, pltpu.roll(second, seed_count, 1))
            low_part = jnp.where(low, pltpu.roll(first, seed_count, 1), second)
            row = high_part * 128.0 + low_part - base
            own = jnp.where(slot == row[:1], 1.0, 0.0)
            near = jnp.zeros((pcap, pair), jnp.float32)
            for k in range(1, n_idx):
                near = near + jnp.where(slot == row[k : k + 1], 1.0, 0.0)
            place = pl.ds(s * seed_count, pair)
            own_ref[half, place, :] = own.T.astype(jnp.bfloat16)
            near_ref[half, place, :] = near.T.astype(jnp.bfloat16)


def layer_kernel(fanout_two, n_feat, *refs):
    count_ref = refs[0]
    got_refs = refs[1 : 1 + n_feat]
    w_ref, bias_ref, ws_ref, wn_ref, own_ref, near_ref = refs[1 + n_feat : 7 + n_feat]
    hidden_ref, value_ref, part_ref = refs[7 + n_feat :]
    pcap, width = hidden_ref.shape
    fslice = w_ref.shape[2]
    pre = jnp.zeros((pcap, width), jnp.float32)
    for f, got_ref in enumerate(got_refs):
        block = got_ref[...]
        weight = w_ref[f].reshape(2 * fslice, width)
        if block.shape[0] != pcap:
            part = block.shape[0] // 3
            tail = block[:, LANES:].astype(jnp.float32)
            lane = lax.broadcasted_iota(jnp.int32, (part, LANES), 1)
            turned = pltpu.roll(tail, 64, 1)
            low_left = jnp.where(lane < 64, turned[:part], tail[part : 2 * part])
            left = jnp.concatenate([block[:, :LANES], low_left.astype(jnp.bfloat16)], axis=0)
            right = jnp.concatenate([tail, turned[2 * part :]], axis=0).astype(jnp.bfloat16)
            pre = pre + jnp.dot(left, weight[:LANES], preferred_element_type=jnp.float32)
            pre = pre + jnp.dot(right[:, :64], weight[LANES:], preferred_element_type=jnp.float32)
        else:
            pre = pre + jnp.dot(block, weight, preferred_element_type=jnp.float32)
    live = lax.broadcasted_iota(jnp.int32, (pcap, width), 0) < count_ref[0, 0]
    hidden = jnp.where(live, jnp.maximum(pre + bias_ref[...], 0.0), 0.0).astype(jnp.bfloat16)
    hidden_ref[...] = hidden
    value_ref[0] = jnp.dot(hidden, ws_ref[...], preferred_element_type=jnp.float32).astype(
        jnp.bfloat16
    )
    value_ref[1] = (
        jnp.dot(hidden, wn_ref[...], preferred_element_type=jnp.float32) / fanout_two
    ).astype(jnp.bfloat16)
    part_ref[...] = (
        jnp.dot(own_ref[1], value_ref[0], preferred_element_type=jnp.float32)
        + jnp.dot(near_ref[1], value_ref[1], preferred_element_type=jnp.float32)
    ).astype(jnp.bfloat16)


def share_kernel(own_ref, near_ref, value_ref, got_ref, *out_refs):
    rows = out_refs[0].shape[0]
    for s, out_ref in enumerate(out_refs):
        place = pl.ds(s * rows, rows)
        out_ref[...] = (
            jnp.dot(own_ref[0, place, :], value_ref[0], preferred_element_type=jnp.float32)
            + jnp.dot(near_ref[0, place, :], value_ref[1], preferred_element_type=jnp.float32)
            + got_ref[place, :].astype(jnp.float32)
        ).astype(jnp.bfloat16)


def swap(value, axis, step):
    size = lax.axis_size(axis)
    return lax.ppermute(value, axis, [(i, i ^ step) for i in range(size)])


def body(
    src_feats,
    nbr_one,
    counts,
    seed_rows,
    nbr_two,
    w1_self,
    w1_nbr,
    bias_one,
    w2_self,
    w2_nbr,
    bias_two,
):
    n_feat = lax.axis_size("feat")
    n_rep = lax.axis_size("rep")
    fslice, nodes = src_feats.shape
    fanout_one, pcap = nbr_one.shape[2:]
    width = w1_self.shape[1]
    seed_count, fanout_two = nbr_two.shape
    n_idx = fanout_two + 1
    bf16 = jnp.bfloat16
    vmem = pl.BlockSpec(memory_space=pltpu.VMEM)
    smem = pl.BlockSpec(memory_space=pltpu.SMEM)
    table_bytes = nodes * LANES * 4

    def call(kernel, name, shapes, ins, args, scratch=(), limit=16 * MIB):
        return pl.pallas_call(
            kernel,
            out_shape=tuple(jax.ShapeDtypeStruct(shape, dtype) for shape, dtype in shapes),
            in_specs=ins,
            out_specs=(vmem,) * len(shapes),
            scratch_shapes=scratch,
            compiler_params=pltpu.CompilerParams(vmem_limit_bytes=limit),
            name=name,
        )(*args)

    rows = jnp.concatenate([seed_rows[None], nbr_two.T], axis=0)
    digits = jnp.concatenate([rows // 128, rows % 128], axis=1).astype(bf16)
    digits = jnp.pad(digits, ((0, 0), (0, width - 2 * seed_count)))
    half = jnp.where(lax.axis_index("rep") == 0, w1_self, w1_nbr)
    parcel = jnp.concatenate([half, digits], axis=0)
    parcels = [parcel] + [swap(parcel, "feat", s) for s in range(1, n_feat)]

    (table,) = call(
        turn_kernel,
        "turn",
        [((nodes, LANES), jnp.float32)],
        [vmem],
        (src_feats,),
        limit=table_bytes + 12 * MIB,
    )
    neighbors = nbr_one.reshape(-1)
    sent_shape = (pcap // 4 * 3, 2 * LANES) if folds(fslice, pcap) else (pcap, 2 * fslice)
    far = list(range(n_feat // 2, n_feat))
    close = list(range(1, n_feat // 2)) + [0]
    got = [None] * n_feat
    for steps in (far, close):
        sent = call(
            functools.partial(mean_kernel, steps, n_rep, fanout_one, pcap, fslice),
            "mean",
            [(sent_shape, bf16)] * len(steps),
            [smem, vmem],
            (neighbors, table),
            scratch=[pltpu.VMEM((pcap, LANES), jnp.float32)],
            limit=table_bytes + 8 * MIB,
        )
        for step, chunk in zip(steps, sent):
            got[step] = swap(chunk, "feat", step) if step else chunk

    mine = jnp.stack(parcels)
    other = swap(mine, "rep", 1)
    weights, own_times, near_times = call(
        functools.partial(prepare_kernel, fslice, pcap, seed_count, n_idx),
        "prepare",
        [
            ((n_feat, n_rep, fslice, width), bf16),
            ((2, n_feat * seed_count, pcap), bf16),
            ((2, n_feat * seed_count, pcap), bf16),
        ],
        [vmem] * 2,
        (mine, other),
    )
    hidden, value, for_other = call(
        functools.partial(layer_kernel, fanout_two, n_feat),
        "layers",
        [
            ((pcap, width), bf16),
            ((2, pcap, width), bf16),
            ((n_feat * seed_count, width), bf16),
        ],
        [smem] + [vmem] * (n_feat + 6),
        (counts, *got, weights, bias_one[None], w2_self, w2_nbr, own_times, near_times),
    )
    from_other = swap(for_other, "rep", 1)
    shares = call(
        share_kernel,
        "share",
        [((seed_count, width), bf16)] * n_feat,
        [vmem] * 4,
        (own_times, near_times, value, from_other),
    )
    pre_two = bias_two
    for s, share in enumerate(shares):
        pre_two = pre_two + (swap(share, "feat", s) if s else share).astype(jnp.float32)
    seed_out = jnp.maximum(pre_two, 0.0).astype(bf16)
    return (hidden[None, None], seed_out)


def solution(mesh):
    placed = (
        P("feat", "groups"),
        P("groups", "rep", None, None),
        P(("groups", "feat"), "rep"),
        P(("groups", "feat", "rep")),
        P(("groups", "feat", "rep"), None),
        P("feat", None),
        P("feat", None),
        P(),
        P(),
        P(),
        P(),
    )
    return jax.shard_map(
        body,
        mesh=mesh,
        in_specs=placed,
        out_specs=(P(("groups", "feat"), "rep", None, None), P(("groups", "feat", "rep"), None)),
        check_vma=False,
    )
```

```python
import functools

import jax
import jax.numpy as jnp
from jax import lax
from jax.experimental import pallas as pl
from jax.experimental.pallas import tpu as pltpu
from jax.sharding import PartitionSpec as P

LANES = 128
MIB = 1024 * 1024


def folds(fslice, pcap):
    return 4 * fslice == 3 * LANES and pcap % 64 == 0


def split_rows(fslice):
    return -(-fslice // 32) * 16


def turn_kernel(pcap, src_ref, seed_ref, nbr_ref, w_self_ref, w_nbr_ref, table_ref, parcel_ref):
    fslice, nodes = src_ref.shape
    n_feat = parcel_ref.shape[0]
    first_core = lax.axis_index("rep") == 0
    width = 512

    def turn(step, carry):
        at = pl.multiple_of(step * width, width)
        table_ref[pl.ds(at, width), :fslice] = src_ref[:, pl.ds(at, width)].astype(jnp.float32).T
        return carry

    lax.fori_loop(0, nodes // width, turn, 0)

    part = split_rows(fslice)
    idx = jnp.concatenate([seed_ref[...], nbr_ref[...]], axis=0)
    high = lax.shift_right_logical(idx, 7)
    digits = jnp.concatenate([high, idx - high * 128], axis=1).astype(jnp.float32)
    digits = digits.astype(jnp.bfloat16)
    half = jnp.where(first_core, w_self_ref[...], w_nbr_ref[...])
    for p in range(n_feat):
        block = src_ref[:, 2 * p * pcap : 2 * (p + 1) * pcap].astype(jnp.float32)
        own = jnp.where(first_core, block[:, :pcap], block[:, pcap:])
        rest = own[part:]
        if rest.shape[0] < part:
            rest = jnp.concatenate([rest, own[: part - rest.shape[0]]], axis=0)
        parcel_ref[p, :fslice, :] = half
        parcel_ref[p, fslice:, : 2 * pcap] = jnp.concatenate([own[:part], rest], axis=1).astype(
            jnp.bfloat16
        )
        parcel_ref[p, fslice : fslice + idx.shape[0], 2 * pcap :] = digits


def mean_kernel(fanout, pcap, fslice, nbr_ref, table_ref, out_ref, total):
    def partition(p, carry):
        first = p * (fanout * pcap)

        def group(g, inner):
            at = pl.multiple_of(g * 8, 8)
            for u in range(8):
                rows = [
                    table_ref[pl.ds(nbr_ref[first + k * pcap + at + u], 1), :]
                    for k in range(fanout)
                ]
                while len(rows) > 1:
                    rows = [a + b for a, b in zip(rows[::2], rows[1::2])] + (
                        [rows[-1]] if len(rows) % 2 else []
                    )
                total[pl.ds(at + u, 1), :] = rows[0]
            return inner

        lax.fori_loop(0, pcap // 8, group, 0)
        mean = total[...] / fanout
        if folds(fslice, pcap):
            lane = lax.broadcasted_iota(jnp.int32, (pcap // 4, LANES), 1)
            cut = pcap // 4 * 3
            part = pcap // 4
            tail = mean[cut:]
            for b in range(3):
                shift = (fslice - 32 * b) % LANES
                moved = pltpu.roll(tail, shift, 1) if shift else tail
                rows = pl.ds(b * part, part)
                out_ref[p, rows, :] = jnp.where(
                    lane < fslice, mean[b * part : (b + 1) * part], moved
                ).astype(jnp.bfloat16)
        else:
            out_ref[p] = mean[:, :fslice].astype(jnp.bfloat16)
        return carry

    lax.fori_loop(0, out_ref.shape[0], partition, 0)


def unfold(block, fslice, pcap):
    if block.shape[0] == pcap:
        return block
    part = block.shape[0] // 3
    wide = block.astype(jnp.float32)
    lane = lax.broadcasted_iota(jnp.int32, (part, LANES), 1)
    tail = pltpu.roll(wide[:part], LANES - fslice, 1)
    for b in (1, 2):
        shift = (32 * b - fslice) % LANES
        moved = wide[b * part : (b + 1) * part]
        moved = pltpu.roll(moved, shift, 1) if shift else moved
        tail = jnp.where(lane // 32 == b, moved, tail)
    return jnp.concatenate([wide, tail], axis=0)[:, :fslice].astype(jnp.bfloat16)


def prepare_kernel(
    fslice, seed_count, n_idx, mine_ref, other_ref, bias_ref, pre_ref, w_ref, own_ref, near_ref
):
    n_feat = mine_ref.shape[0]
    pcap = pre_ref.shape[0]
    part = split_rows(fslice)
    rep_pos = lax.axis_index("rep")
    first_core = rep_pos == 0
    base = (lax.axis_index("feat") * lax.axis_size("rep") + rep_pos) * pcap
    base = base.astype(jnp.float32)
    pair = 2 * seed_count
    slot = lax.broadcasted_iota(jnp.int32, (pcap, pair), 0).astype(jnp.float32)
    low = lax.broadcasted_iota(jnp.int32, (n_idx, pair), 1) < seed_count
    pre = jnp.zeros(pre_ref.shape, jnp.float32)
    for f in range(n_feat):
        mine, other = mine_ref[f, :fslice], other_ref[f, :fslice]
        w_ref[f] = jnp.where(first_core, other, mine)
        both = mine_ref[f, fslice:, : 2 * pcap].astype(jnp.float32)
        own = jnp.concatenate([both[:, :pcap], both[: fslice - part, pcap:]], axis=0)
        pre = pre + jnp.dot(
            own.T.astype(jnp.bfloat16),
            jnp.where(first_core, mine, other),
            preferred_element_type=jnp.float32,
        )
    pre_ref[...] = pre + bias_ref[...]
    for half, ref in enumerate((mine_ref, other_ref)):
        for s in range(0, n_feat, 2):
            first = ref[s, fslice : fslice + n_idx, 2 * pcap :].astype(jnp.float32)
            second = ref[s + 1, fslice : fslice + n_idx, 2 * pcap :].astype(jnp.float32)
            high_part = jnp.where(low, first, pltpu.roll(second, seed_count, 1))
            low_part = jnp.where(low, pltpu.roll(first, seed_count, 1), second)
            row = high_part * 128.0 + low_part - base
            own = jnp.where(slot == row[:1], 1.0, 0.0)
            near = jnp.zeros((pcap, pair), jnp.float32)
            for k in range(1, n_idx):
                near = near + jnp.where(slot == row[k : k + 1], 1.0, 0.0)
            place = pl.ds(s * seed_count, pair)
            own_ref[half, place, :] = own.T.astype(jnp.bfloat16)
            near_ref[half, place, :] = near.T.astype(jnp.bfloat16)


def layer_kernel(
    fanout_two,
    count_ref,
    got_ref,
    pre_ref,
    w_ref,
    ws_ref,
    wn_ref,
    own_ref,
    near_ref,
    hidden_ref,
    value_ref,
    part_ref,
):
    pcap, width = hidden_ref.shape
    fslice = w_ref.shape[1]
    pre = pre_ref[...]
    for f in range(got_ref.shape[0]):
        pre = pre + jnp.dot(
            unfold(got_ref[f], fslice, pcap), w_ref[f], preferred_element_type=jnp.float32
        )
    live = lax.broadcasted_iota(jnp.int32, (pcap, width), 0) < count_ref[0, 0]
    hidden = jnp.where(live, jnp.maximum(pre, 0.0), 0.0).astype(jnp.bfloat16)
    hidden_ref[...] = hidden
    value_ref[0] = jnp.dot(hidden, ws_ref[...], preferred_element_type=jnp.float32).astype(
        jnp.bfloat16
    )
    value_ref[1] = (
        jnp.dot(hidden, wn_ref[...], preferred_element_type=jnp.float32) / fanout_two
    ).astype(jnp.bfloat16)
    part_ref[...] = (
        jnp.dot(own_ref[1], value_ref[0], preferred_element_type=jnp.float32)
        + jnp.dot(near_ref[1], value_ref[1], preferred_element_type=jnp.float32)
    ).astype(jnp.bfloat16)


def share_kernel(own_ref, near_ref, value_ref, got_ref, out_ref):
    out_ref[...] = (
        jnp.dot(own_ref[0], value_ref[0], preferred_element_type=jnp.float32)
        + jnp.dot(near_ref[0], value_ref[1], preferred_element_type=jnp.float32)
        + got_ref[...].astype(jnp.float32)
    ).astype(jnp.bfloat16)


def swap(value, axis, step):
    size = lax.axis_size(axis)
    return lax.ppermute(value, axis, [(i, i ^ step) for i in range(size)])


def body(
    src_feats,
    nbr_one,
    counts,
    seed_rows,
    nbr_two,
    w1_self,
    w1_nbr,
    bias_one,
    w2_self,
    w2_nbr,
    bias_two,
):
    n_feat = lax.axis_size("feat")
    fslice, nodes = src_feats.shape
    fanout_one, pcap = nbr_one.shape[2:]
    width = w1_self.shape[1]
    seed_count, fanout_two = nbr_two.shape
    n_idx = fanout_two + 1
    bf16 = jnp.bfloat16
    vmem = pl.BlockSpec(memory_space=pltpu.VMEM)
    smem = pl.BlockSpec(memory_space=pltpu.SMEM)
    table_bytes = nodes * LANES * 4

    def call(kernel, name, shapes, ins, args, scratch=(), limit=16 * MIB, cost_us=1):
        return pl.pallas_call(
            kernel,
            out_shape=tuple(jax.ShapeDtypeStruct(shape, dtype) for shape, dtype in shapes),
            in_specs=ins,
            out_specs=(vmem,) * len(shapes),
            scratch_shapes=scratch,
            compiler_params=pltpu.CompilerParams(vmem_limit_bytes=limit),
            cost_estimate=pl.CostEstimate(
                flops=0, bytes_accessed=int(cost_us * 3_600_000), transcendentals=0
            ),
            name=name,
        )(*args)

    table, parcel = call(
        functools.partial(turn_kernel, pcap),
        "turn",
        [
            ((nodes, LANES), jnp.float32),
            ((n_feat, fslice + split_rows(fslice), width), bf16),
        ],
        [vmem] * 5,
        (src_feats, seed_rows[None], nbr_two.T, w1_self, w1_nbr),
        limit=table_bytes + 12 * MIB,
        cost_us=3,
    )
    mine = lax.all_to_all(parcel, "feat", 0, 0, tiled=True)

    sent_shape = (pcap // 4 * 3, LANES) if folds(fslice, pcap) else (pcap, fslice)
    (sent,) = call(
        functools.partial(mean_kernel, fanout_one, pcap, fslice),
        "mean",
        [((n_feat, *sent_shape), bf16)],
        [smem, vmem],
        (nbr_one.reshape(-1), table),
        scratch=[pltpu.VMEM((pcap, LANES), jnp.float32)],
        limit=table_bytes + 8 * MIB,
        cost_us=20,
    )
    got = lax.all_to_all(sent, "feat", 0, 0, tiled=True)

    other = swap(mine, "rep", 1)
    pre, w_nbr, own_times, near_times = call(
        functools.partial(prepare_kernel, fslice, seed_count, n_idx),
        "prepare",
        [
            ((pcap, width), jnp.float32),
            ((n_feat, fslice, width), bf16),
            ((2, n_feat * seed_count, pcap), bf16),
            ((2, n_feat * seed_count, pcap), bf16),
        ],
        [vmem] * 3,
        (mine, other, bias_one[None]),
        cost_us=3,
    )
    hidden, value, for_other = call(
        functools.partial(layer_kernel, fanout_two),
        "layers",
        [
            ((pcap, width), bf16),
            ((2, pcap, width), bf16),
            ((n_feat * seed_count, width), bf16),
        ],
        [smem] + [vmem] * 7,
        (counts, got, pre, w_nbr, w2_self, w2_nbr, own_times, near_times),
    )
    from_other = swap(for_other, "rep", 1)
    (shares,) = call(
        share_kernel,
        "share",
        [((n_feat * seed_count, width), bf16)],
        [vmem] * 4,
        (own_times, near_times, value, from_other),
    )
    parts = lax.all_to_all(shares.reshape(n_feat, seed_count, width), "feat", 0, 0, tiled=True)
    pre_two = jnp.sum(parts.astype(jnp.float32), axis=0) + bias_two
    seed_out = jnp.maximum(pre_two, 0.0).astype(bf16)
    return (hidden[None, None], seed_out)


def solution(mesh):
    placed = (
        P("feat", "groups"),
        P("groups", "rep", None, None),
        P(("groups", "feat"), "rep"),
        P(("groups", "feat", "rep")),
        P(("groups", "feat", "rep"), None),
        P("feat", None),
        P("feat", None),
        P(),
        P(),
        P(),
        P(),
    )
    return jax.shard_map(
        body,
        mesh=mesh,
        in_specs=placed,
        out_specs=(P(("groups", "feat"), "rep", None, None), P(("groups", "feat", "rep"), None)),
        check_vma=False,
    )
```

```python
import functools

import jax
import jax.numpy as jnp
from jax import lax
from jax.experimental import pallas as pl
from jax.experimental.pallas import tpu as pltpu
from jax.sharding import PartitionSpec as P

LANES = 128
MIB = 1024 * 1024


def folds(fslice, pcap):
    return 4 * fslice == 3 * LANES and pcap % 64 == 0


def pack_kernel(
    n_feat,
    pcap,
    src_hbm,
    seed_hbm,
    nbr_hbm,
    w_self_hbm,
    w_nbr_hbm,
    *refs,
):
    half = n_feat // 2
    parcel_refs = refs[:half]
    src_ref, seed_ref, nbr_ref, w_self_ref, w_nbr_ref, sems = refs[half:]
    fslice = w_self_ref.shape[0]
    copies = [
        pltpu.make_async_copy(a, b, sems.at[i])
        for i, (a, b) in enumerate(
            (
                (src_hbm.at[:, pl.ds(0, src_ref.shape[1])], src_ref),
                (seed_hbm, seed_ref),
                (nbr_hbm, nbr_ref),
                (w_self_hbm, w_self_ref),
                (w_nbr_hbm, w_nbr_ref),
            )
        )
    ]
    for copy in copies:
        copy.start()
    for copy in copies:
        copy.wait()
    feat_pos = lax.axis_index("feat")
    first_core = lax.axis_index("rep") == 0
    idx = jnp.concatenate([seed_ref[...], nbr_ref[...]], axis=0)
    high = lax.shift_right_logical(idx, 7)
    digits = jnp.concatenate([high, idx - high * 128], axis=1).astype(jnp.float32)
    digits = digits.astype(jnp.bfloat16)
    weight = jnp.where(first_core, w_self_ref[...], w_nbr_ref[...])
    for s, parcel_ref in enumerate(parcel_refs):
        parcel_ref[:fslice, :] = weight
        for place, step in enumerate((s, s ^ half)):
            at = pl.multiple_of(jnp.bitwise_xor(feat_pos, step) * (2 * pcap), LANES)
            block = src_ref[:, pl.ds(at, 2 * pcap)].astype(jnp.float32)
            own = jnp.where(first_core, block[:, :pcap], block[:, pcap:])
            if place == 0:
                near_side = own
        both = jnp.concatenate([near_side, own], axis=1)
        parcel_ref[fslice:, : 2 * pcap] = both.astype(jnp.bfloat16)
        parcel_ref[fslice : fslice + idx.shape[0], 2 * pcap :] = digits


def turn_kernel(src_hbm, table_ref, src_ref, sems):
    fslice, nodes = src_hbm.shape
    pieces = sems.shape[0]
    piece = nodes // pieces
    width = 512
    copies = [
        pltpu.make_async_copy(
            src_hbm.at[:, pl.ds(i * piece, piece)], src_ref.at[:, pl.ds(i * piece, piece)], sems.at[i]
        )
        for i in range(pieces)
    ]
    for copy in copies:
        copy.start()
    for i, copy in enumerate(copies):
        copy.wait()

        def turn(step, carry):
            at = pl.multiple_of(i * piece + step * width, width)
            block = src_ref[:, pl.ds(at, width)].astype(jnp.float32)
            table_ref[pl.ds(at, width), :fslice] = block.T
            return carry

        lax.fori_loop(0, piece // width, turn, 0)


def mean_kernel(steps, fanout, pcap, fslice, nbr_hbm, table_ref, *refs):
    out_refs, (total, nbr_ref, sems) = refs[: len(steps)], refs[len(steps) :]
    feat_pos = lax.axis_index("feat")
    copies = [
        pltpu.make_async_copy(nbr_hbm.at[jnp.bitwise_xor(feat_pos, step)], nbr_ref.at[i], sems.at[i])
        for i, step in enumerate(steps)
    ]
    for copy in copies:
        copy.start()
    for i, out_ref in enumerate(out_refs):
        copies[i].wait()

        def group(g, carry):
            at = pl.multiple_of(g * 8, 8)
            for u in range(8):
                rows = [table_ref[nbr_ref[i, 0, at + (k * pcap + u)]] for k in range(fanout)]
                while len(rows) > 1:
                    rows = [a + b for a, b in zip(rows[::2], rows[1::2])] + (
                        [rows[-1]] if len(rows) % 2 else []
                    )
                total[pl.ds(at + u, 1), :] = rows[0]
            return carry

        lax.fori_loop(0, pcap // 8, group, 0)
        mean = total[...] / fanout
        if folds(fslice, pcap):
            part = pcap // 4
            lane = lax.broadcasted_iota(jnp.int32, (part, LANES), 1)
            tail = mean[3 * part :]
            for b in range(3):
                shift = (fslice - 32 * b) % LANES
                moved = pltpu.roll(tail, shift, 1) if shift else tail
                out_ref[pl.ds(b * part, part), :] = jnp.where(
                    lane < fslice, mean[b * part : (b + 1) * part], moved
                ).astype(jnp.bfloat16)
        else:
            out_ref[...] = mean[:, :fslice].astype(jnp.bfloat16)


def unfold(block, fslice, pcap):
    if block.shape[0] == pcap:
        return block
    part = block.shape[0] // 3
    wide = block.astype(jnp.float32)
    lane = lax.broadcasted_iota(jnp.int32, (part, LANES), 1)
    tail = pltpu.roll(wide[:part], LANES - fslice, 1)
    for b in (1, 2):
        shift = (32 * b - fslice) % LANES
        moved = wide[b * part : (b + 1) * part]
        moved = pltpu.roll(moved, shift, 1) if shift else moved
        tail = jnp.where(lane // 32 == b, moved, tail)
    return jnp.concatenate([wide, tail], axis=0)[:, :fslice].astype(jnp.bfloat16)


def halves_kernel(*refs):
    out_ref = refs[-1]
    for s, ref in enumerate(refs[:-1]):
        out_ref[s] = ref[: out_ref.shape[1], :]


def prepare_kernel(half, n_idx, *refs):
    parcel_refs, mean_refs = refs[:half], refs[half : 2 * half]
    other_ref, bias_ref, w_ref, pre_ref, cross_ref = refs[2 * half :]
    fslice = w_ref.shape[1]
    pcap, width = pre_ref.shape
    first_core = lax.axis_index("rep") == 0
    both = jnp.zeros((2 * pcap, width), jnp.float32)
    far = jnp.zeros((pcap, width), jnp.float32)
    for s in range(half):
        mine, other = parcel_refs[s][:fslice, :], other_ref[s]
        w_nbr = jnp.where(first_core, other, mine)
        w_ref[s] = w_nbr
        feats = parcel_refs[s][fslice:, : 2 * pcap].astype(jnp.float32).T.astype(jnp.bfloat16)
        both = both + jnp.dot(
            feats, jnp.where(first_core, mine, other), preferred_element_type=jnp.float32
        )
        far = far + jnp.dot(
            unfold(mean_refs[s][...], fslice, pcap), w_nbr, preferred_element_type=jnp.float32
        )
        rows = pl.ds(pcap + s // 4 * n_idx, n_idx)
        cross_ref[rows, s % 4 * LANES : (s % 4 + 1) * LANES] = parcel_refs[s][
            fslice : fslice + n_idx, 2 * pcap :
        ]
    pre_ref[...] = both[:pcap] + bias_ref[...]
    cross_ref[:pcap, :] = (both[pcap:] + far).astype(jnp.bfloat16)


def store_times(pcap, blocks, out_ref):
    n_idx, pair = blocks[0].shape
    seed_count = pair // 2
    core_rows = lax.axis_index("feat") * (2 * pcap)
    rep_pos = lax.axis_index("rep")
    row = lax.broadcasted_iota(jnp.int32, (2 * pcap, pair), 0)
    slot = jnp.where(
        row < pcap, row + core_rows + rep_pos * pcap, row + core_rows - rep_pos * pcap
    ).astype(jnp.float32)
    low = lax.broadcasted_iota(jnp.int32, (n_idx, pair), 1) < seed_count
    for s in range(0, len(blocks), 2):
        first, second = blocks[s].astype(jnp.float32), blocks[s + 1].astype(jnp.float32)
        high_part = jnp.where(low, first, pltpu.roll(second, seed_count, 1))
        low_part = jnp.where(low, pltpu.roll(first, seed_count, 1), second)
        name = high_part * 128.0 + low_part
        own = jnp.where(slot == name[:1], 1.0, 0.0)
        near = jnp.zeros((2 * pcap, pair), jnp.float32)
        for k in range(1, n_idx):
            near = near + jnp.where(slot == name[k : k + 1], 1.0, 0.0)
        place = pl.ds(s * seed_count, pair)
        out_ref[place, : 2 * pcap] = own.T.astype(jnp.bfloat16)
        out_ref[place, 2 * pcap :] = near.T.astype(jnp.bfloat16)


def near_times_kernel(half, fslice, pcap, n_idx, *refs):
    blocks = [ref[fslice : fslice + n_idx, 2 * pcap :] for ref in refs[:half]]
    store_times(pcap, blocks, refs[half])


def far_times_kernel(
    half, n_idx, fanout_two, cross_ref, hidden_ref, ws_ref, wn_ref, out_ref, value_ref
):
    pcap = hidden_ref.shape[0]
    blocks = [
        cross_ref[
            pl.ds(pcap + s // 4 * n_idx, n_idx), s % 4 * LANES : (s % 4 + 1) * LANES
        ]
        for s in range(half)
    ]
    store_times(pcap, blocks, out_ref)
    store_values(hidden_ref[...], ws_ref, wn_ref, fanout_two, value_ref)


def store_values(hidden, ws_ref, wn_ref, fanout_two, value_ref):
    value_ref[0] = jnp.dot(hidden, ws_ref[...], preferred_element_type=jnp.float32).astype(
        jnp.bfloat16
    )
    value_ref[1] = (
        jnp.dot(hidden, wn_ref[...], preferred_element_type=jnp.float32) / fanout_two
    ).astype(jnp.bfloat16)


def layer_kernel(half, count_ref, *refs):
    mean_refs = refs[:half]
    pre_ref, w_ref, cross_ref, hidden_ref = refs[half:]
    pcap, width = hidden_ref.shape
    fslice = w_ref.shape[1]
    pre = pre_ref[...] + cross_ref[:pcap, :].astype(jnp.float32)
    for s in range(half):
        pre = pre + jnp.dot(
            unfold(mean_refs[s][...], fslice, pcap), w_ref[s], preferred_element_type=jnp.float32
        )
    live = lax.broadcasted_iota(jnp.int32, (pcap, width), 0) < count_ref[0, 0]
    hidden_ref[...] = jnp.where(live, jnp.maximum(pre, 0.0), 0.0).astype(jnp.bfloat16)


def share_kernel(
    half, fanout_two, near_ref, far_ref, value_ref, hidden_ref, ws_ref, wn_ref, *refs
):
    out_refs, other_ref = refs[:half], refs[half]
    store_values(hidden_ref[...], ws_ref, wn_ref, fanout_two, other_ref)
    values = jnp.concatenate(
        [value_ref[0], other_ref[0], value_ref[1], other_ref[1]], axis=0
    )
    near = jnp.dot(near_ref[...], values, preferred_element_type=jnp.float32)
    far = jnp.dot(far_ref[...], values, preferred_element_type=jnp.float32)
    rows = out_refs[0].shape[0] // 2
    for s, out_ref in enumerate(out_refs):
        out_ref[:rows, :] = near[s * rows : (s + 1) * rows].astype(jnp.bfloat16)
        out_ref[rows:, :] = far[s * rows : (s + 1) * rows].astype(jnp.bfloat16)


def side_sum_kernel(*refs):
    near_ref, far_ref = refs[-2:]
    rows = near_ref.shape[0]
    total = refs[0][...].astype(jnp.float32)
    for ref in refs[1:-2]:
        total = total + ref[...].astype(jnp.float32)
    near_ref[...] = total[:rows]
    far_ref[...] = total[rows:].astype(jnp.bfloat16)


def swap(value, axis, step):
    size = lax.axis_size(axis)
    return lax.ppermute(value, axis, [(i, i ^ step) for i in range(size)])


def body(
    src_feats,
    nbr_one,
    counts,
    seed_rows,
    nbr_two,
    w1_self,
    w1_nbr,
    bias_one,
    w2_self,
    w2_nbr,
    bias_two,
):
    n_feat = lax.axis_size("feat")
    half = n_feat // 2
    fslice, nodes = src_feats.shape
    fanout_one, pcap = nbr_one.shape[2:]
    width = w1_self.shape[1]
    seed_count, fanout_two = nbr_two.shape
    n_idx = fanout_two + 1
    bf16 = jnp.bfloat16
    vmem = pl.BlockSpec(memory_space=pltpu.VMEM)
    smem = pl.BlockSpec(memory_space=pltpu.SMEM)
    hbm = pl.BlockSpec(memory_space=pltpu.HBM)
    anywhere = pl.BlockSpec(memory_space=pl.ANY)
    table_bytes = nodes * LANES * 4

    def call(kernel, name, shapes, ins, args, after=(), scratch=(), limit=16 * MIB, cost_us=1):
        def wrapped(*refs):
            kernel(*refs[: len(args)], *refs[len(args) + len(after) :])

        return pl.pallas_call(
            wrapped,
            out_shape=tuple(jax.ShapeDtypeStruct(shape, dtype) for shape, dtype in shapes),
            in_specs=[*ins, *([anywhere] * len(after))],
            out_specs=(vmem,) * len(shapes),
            scratch_shapes=scratch,
            compiler_params=pltpu.CompilerParams(vmem_limit_bytes=limit),
            cost_estimate=pl.CostEstimate(
                flops=int(cost_us * 1_100_000_000), bytes_accessed=0, transcendentals=0
            ),
            name=name,
        )(*args, *after)

    def send(chunks):
        return [chunk if s == 0 else swap(chunk, "feat", s) for s, chunk in enumerate(chunks)]

    parcels = call(
        functools.partial(pack_kernel, n_feat, pcap),
        "pack",
        [((2 * fslice, width), bf16)] * half,
        [hbm] * 5,
        (src_feats, seed_rows[None], nbr_two.T, w1_self, w1_nbr),
        scratch=[
            pltpu.VMEM((fslice, n_feat * 2 * pcap), bf16),
            pltpu.VMEM((1, seed_count), jnp.int32),
            pltpu.VMEM((fanout_two, seed_count), jnp.int32),
            pltpu.VMEM((fslice, width), bf16),
            pltpu.VMEM((fslice, width), bf16),
            pltpu.SemaphoreType.DMA((5,)),
        ],
        cost_us=2,
    )
    arrived = send(parcels)
    (table,) = call(
        turn_kernel,
        "turn",
        [((nodes, LANES), jnp.float32)],
        [hbm],
        (src_feats,),
        after=(parcels[0],),
        scratch=[pltpu.VMEM((fslice, nodes), bf16), pltpu.SemaphoreType.DMA((6,))],
        limit=table_bytes + 12 * MIB,
        cost_us=3,
    )
    table = table.reshape(nodes, 1, LANES)
    neighbors = nbr_one.reshape(n_feat, 1, fanout_one * pcap)
    chunk_shape = (pcap // 4 * 3, LANES) if folds(fslice, pcap) else (pcap, fslice)

    def means(steps, after):
        return call(
            functools.partial(mean_kernel, steps, fanout_one, pcap, fslice),
            "mean",
            [(chunk_shape, bf16)] * len(steps),
            [anywhere, vmem],
            (neighbors, table),
            after=after,
            scratch=[
                pltpu.VMEM((pcap, LANES), jnp.float32),
                pltpu.SMEM((len(steps), 1, fanout_one * pcap), jnp.int32),
                pltpu.SemaphoreType.DMA((len(steps),)),
            ],
            limit=table_bytes + 8 * MIB,
            cost_us=2.3 * len(steps),
        )

    far_means = means([s + half for s in range(half)], ())
    far_arrived = send(far_means)
    (halves,) = call(
        halves_kernel,
        "halves",
        [((half, fslice, width), bf16)],
        [vmem] * half,
        arrived,
        after=far_means[:1],
    )
    other_halves = swap(halves, "rep", 1)
    (last_mean,) = means([half - 1], far_means[:1])
    w_nbr, pre, cross = call(
        functools.partial(prepare_kernel, half, n_idx),
        "prepare",
        [
            ((half, fslice, width), bf16),
            ((pcap, width), jnp.float32),
            ((pcap + -(-half // 4) * n_idx, width), bf16),
        ],
        [vmem] * (2 * half + 2),
        (*arrived, *far_arrived, other_halves, bias_one[None]),
        after=(last_mean,),
        cost_us=2,
    )
    cross_arrived = swap(cross, "feat", half)
    near_means = means(list(range(half - 1)), (cross,))
    near_arrived = send([*near_means, last_mean])
    (near_times,) = call(
        functools.partial(near_times_kernel, half, fslice, pcap, n_idx),
        "near_times",
        [((half * seed_count, 4 * pcap), bf16)],
        [vmem] * half,
        arrived,
        after=near_means[:1],
    )
    (hidden,) = call(
        functools.partial(layer_kernel, half),
        "hidden",
        [((pcap, width), bf16)],
        [smem] + [vmem] * (half + 3),
        (counts, *near_arrived, pre, w_nbr, cross_arrived),
    )
    other_hidden = swap(hidden, "rep", 1)
    far_times, value = call(
        functools.partial(far_times_kernel, half, n_idx, fanout_two),
        "far_times",
        [((half * seed_count, 4 * pcap), bf16), ((2, pcap, width), bf16)],
        [vmem] * 4,
        (cross_arrived, hidden, w2_self, w2_nbr),
    )
    shares = call(
        functools.partial(share_kernel, half, fanout_two),
        "share",
        [((2 * seed_count, width), bf16)] * half,
        [vmem] * 6,
        (near_times, far_times, value, other_hidden, w2_self, w2_nbr),
        scratch=[pltpu.VMEM((2, pcap, width), bf16)],
        limit=32 * MIB,
    )
    near_sum, far_sum = call(
        side_sum_kernel,
        "side_sum",
        [((seed_count, width), jnp.float32), ((seed_count, width), bf16)],
        [vmem] * half,
        send(shares),
    )
    pre_two = near_sum + swap(far_sum, "feat", half).astype(jnp.float32) + bias_two
    seed_out = jnp.maximum(pre_two, 0.0).astype(bf16)
    return (hidden[None, None], seed_out)


def solution(mesh):
    placed = (
        P("feat", "groups"),
        P("groups", "rep", None, None),
        P(("groups", "feat"), "rep"),
        P(("groups", "feat", "rep")),
        P(("groups", "feat", "rep"), None),
        P("feat", None),
        P("feat", None),
        P(),
        P(),
        P(),
        P(),
    )
    return jax.shard_map(
        body,
        mesh=mesh,
        in_specs=placed,
        out_specs=(P(("groups", "feat"), "rep", None, None), P(("groups", "feat", "rep"), None)),
        check_vma=False,
    )
```

```python
import functools

import jax
import jax.numpy as jnp
from jax import lax
from jax.experimental import pallas as pl
from jax.experimental.pallas import tpu as pltpu
from jax.sharding import PartitionSpec as P

LANES = 128
MIB = 1024 * 1024


def folds(fslice, pcap):
    return 4 * fslice == 3 * LANES and pcap % 64 == 0


def pack_kernel(
    n_feat,
    pcap,
    src_hbm,
    seed_hbm,
    nbr_hbm,
    w_self_hbm,
    w_nbr_hbm,
    *refs,
):
    half = n_feat // 2
    parcel_refs = refs[:half]
    src_ref, seed_ref, nbr_ref, w_self_ref, w_nbr_ref, sems = refs[half:]
    fslice = w_self_ref.shape[0]
    copies = [
        pltpu.make_async_copy(a, b, sems.at[i])
        for i, (a, b) in enumerate(
            (
                (src_hbm.at[:, pl.ds(0, src_ref.shape[1])], src_ref),
                (seed_hbm, seed_ref),
                (nbr_hbm, nbr_ref),
                (w_self_hbm, w_self_ref),
                (w_nbr_hbm, w_nbr_ref),
            )
        )
    ]
    for copy in copies:
        copy.start()
    for copy in copies:
        copy.wait()
    feat_pos = lax.axis_index("feat")
    first_core = lax.axis_index("rep") == 0
    idx = jnp.concatenate([seed_ref[...], nbr_ref[...]], axis=0)
    high = lax.shift_right_logical(idx, 7)
    digits = jnp.concatenate([high, idx - high * 128], axis=1).astype(jnp.float32)
    digits = digits.astype(jnp.bfloat16)
    weight = jnp.where(first_core, w_self_ref[...], w_nbr_ref[...])
    for s, parcel_ref in enumerate(parcel_refs):
        parcel_ref[:fslice, :] = weight
        for place, step in enumerate((s, s ^ half)):
            at = pl.multiple_of(jnp.bitwise_xor(feat_pos, step) * (2 * pcap), LANES)
            block = src_ref[:, pl.ds(at, 2 * pcap)].astype(jnp.float32)
            own = jnp.where(first_core, block[:, :pcap], block[:, pcap:])
            if place == 0:
                near_side = own
        both = jnp.concatenate([near_side, own], axis=1)
        parcel_ref[fslice:, : 2 * pcap] = both.astype(jnp.bfloat16)
        parcel_ref[fslice : fslice + idx.shape[0], 2 * pcap :] = digits


def turn_kernel(src_hbm, table_ref, src_ref, sems):
    fslice, nodes = src_hbm.shape
    pieces = sems.shape[0]
    piece = nodes // pieces
    width = 512
    copies = [
        pltpu.make_async_copy(
            src_hbm.at[:, pl.ds(i * piece, piece)], src_ref.at[:, pl.ds(i * piece, piece)], sems.at[i]
        )
        for i in range(pieces)
    ]
    for copy in copies:
        copy.start()
    for i, copy in enumerate(copies):
        copy.wait()

        def turn(step, carry):
            at = pl.multiple_of(i * piece + step * width, width)
            block = src_ref[:, pl.ds(at, width)].astype(jnp.float32)
            table_ref[pl.ds(at, width), :fslice] = block.T
            return carry

        lax.fori_loop(0, piece // width, turn, 0)


def mean_kernel(base, fanout, pcap, fslice, nbr_ref, table_ref, out_ref, total):
    feat_pos = lax.axis_index("feat")

    def partition(i, carry):
        first = jnp.bitwise_xor(feat_pos, base + i) * (fanout * pcap)

        def group(g, inner):
            at = pl.multiple_of(g * 8, 8)
            for u in range(8):
                rows = [table_ref[nbr_ref[first + k * pcap + at + u]] for k in range(fanout)]
                while len(rows) > 1:
                    rows = [a + b for a, b in zip(rows[::2], rows[1::2])] + (
                        [rows[-1]] if len(rows) % 2 else []
                    )
                total[pl.ds(at + u, 1), :] = rows[0]
            return inner

        lax.fori_loop(0, pcap // 8, group, 0)
        mean = total[...] / fanout
        if folds(fslice, pcap):
            part = pcap // 4
            lane = lax.broadcasted_iota(jnp.int32, (part, LANES), 1)
            tail = mean[3 * part :]
            for b in range(3):
                shift = (fslice - 32 * b) % LANES
                moved = pltpu.roll(tail, shift, 1) if shift else tail
                out_ref[i, pl.ds(b * part, part), :] = jnp.where(
                    lane < fslice, mean[b * part : (b + 1) * part], moved
                ).astype(jnp.bfloat16)
        else:
            out_ref[i] = mean[:, :fslice].astype(jnp.bfloat16)
        return carry

    lax.fori_loop(0, out_ref.shape[0], partition, 0)


def unfold(block, fslice, pcap):
    if block.shape[0] == pcap:
        return block
    part = block.shape[0] // 3
    wide = block.astype(jnp.float32)
    lane = lax.broadcasted_iota(jnp.int32, (part, LANES), 1)
    tail = pltpu.roll(wide[:part], LANES - fslice, 1)
    for b in (1, 2):
        shift = (32 * b - fslice) % LANES
        moved = wide[b * part : (b + 1) * part]
        moved = pltpu.roll(moved, shift, 1) if shift else moved
        tail = jnp.where(lane // 32 == b, moved, tail)
    return jnp.concatenate([wide, tail], axis=0)[:, :fslice].astype(jnp.bfloat16)


def halves_kernel(*refs):
    out_ref = refs[-1]
    for s, ref in enumerate(refs[:-1]):
        out_ref[s] = ref[: out_ref.shape[1], :]


def prepare_kernel(half, n_idx, *refs):
    parcel_refs, mean_refs = refs[:half], refs[half : 2 * half]
    other_ref, bias_ref, w_ref, pre_ref, cross_ref = refs[2 * half :]
    fslice = w_ref.shape[1]
    pcap, width = pre_ref.shape
    first_core = lax.axis_index("rep") == 0
    both = jnp.zeros((2 * pcap, width), jnp.float32)
    far = jnp.zeros((pcap, width), jnp.float32)
    for s in range(half):
        mine, other = parcel_refs[s][:fslice, :], other_ref[s]
        w_nbr = jnp.where(first_core, other, mine)
        w_ref[s] = w_nbr
        feats = parcel_refs[s][fslice:, : 2 * pcap].astype(jnp.float32).T.astype(jnp.bfloat16)
        both = both + jnp.dot(
            feats, jnp.where(first_core, mine, other), preferred_element_type=jnp.float32
        )
        far = far + jnp.dot(
            unfold(mean_refs[s][...], fslice, pcap), w_nbr, preferred_element_type=jnp.float32
        )
        rows = pl.ds(pcap + s // 4 * n_idx, n_idx)
        cross_ref[rows, s % 4 * LANES : (s % 4 + 1) * LANES] = parcel_refs[s][
            fslice : fslice + n_idx, 2 * pcap :
        ]
    pre_ref[...] = both[:pcap] + bias_ref[...]
    cross_ref[:pcap, :] = (both[pcap:] + far).astype(jnp.bfloat16)


def store_times(pcap, blocks, out_ref):
    n_idx, pair = blocks[0].shape
    seed_count = pair // 2
    core_rows = lax.axis_index("feat") * (2 * pcap)
    rep_pos = lax.axis_index("rep")
    row = lax.broadcasted_iota(jnp.int32, (2 * pcap, pair), 0)
    slot = jnp.where(
        row < pcap, row + core_rows + rep_pos * pcap, row + core_rows - rep_pos * pcap
    ).astype(jnp.float32)
    low = lax.broadcasted_iota(jnp.int32, (n_idx, pair), 1) < seed_count
    for s in range(0, len(blocks), 2):
        first, second = blocks[s].astype(jnp.float32), blocks[s + 1].astype(jnp.float32)
        high_part = jnp.where(low, first, pltpu.roll(second, seed_count, 1))
        low_part = jnp.where(low, pltpu.roll(first, seed_count, 1), second)
        name = high_part * 128.0 + low_part
        own = jnp.where(slot == name[:1], 1.0, 0.0)
        near = jnp.zeros((2 * pcap, pair), jnp.float32)
        for k in range(1, n_idx):
            near = near + jnp.where(slot == name[k : k + 1], 1.0, 0.0)
        place = pl.ds(s * seed_count, pair)
        out_ref[place, : 2 * pcap] = own.T.astype(jnp.bfloat16)
        out_ref[place, 2 * pcap :] = near.T.astype(jnp.bfloat16)


def near_times_kernel(half, fslice, pcap, n_idx, *refs):
    blocks = [ref[fslice : fslice + n_idx, 2 * pcap :] for ref in refs[:half]]
    store_times(pcap, blocks, refs[half])


def far_times_kernel(
    half, n_idx, fanout_two, cross_ref, hidden_ref, ws_ref, wn_ref, out_ref, value_ref
):
    pcap = hidden_ref.shape[0]
    blocks = [
        cross_ref[
            pl.ds(pcap + s // 4 * n_idx, n_idx), s % 4 * LANES : (s % 4 + 1) * LANES
        ]
        for s in range(half)
    ]
    store_times(pcap, blocks, out_ref)
    store_values(hidden_ref[...], ws_ref, wn_ref, fanout_two, value_ref)


def store_values(hidden, ws_ref, wn_ref, fanout_two, value_ref):
    value_ref[0] = jnp.dot(hidden, ws_ref[...], preferred_element_type=jnp.float32).astype(
        jnp.bfloat16
    )
    value_ref[1] = (
        jnp.dot(hidden, wn_ref[...], preferred_element_type=jnp.float32) / fanout_two
    ).astype(jnp.bfloat16)


def layer_kernel(half, count_ref, *refs):
    mean_refs = refs[:half]
    pre_ref, w_ref, cross_ref, hidden_ref, result_ref = refs[half:]
    pcap, width = hidden_ref.shape
    fslice = w_ref.shape[1]
    pre = pre_ref[...] + cross_ref[:pcap, :].astype(jnp.float32)
    for s in range(half):
        pre = pre + jnp.dot(
            unfold(mean_refs[s][...], fslice, pcap), w_ref[s], preferred_element_type=jnp.float32
        )
    live = lax.broadcasted_iota(jnp.int32, (pcap, width), 0) < count_ref[0, 0]
    hidden = jnp.where(live, jnp.maximum(pre, 0.0), 0.0).astype(jnp.bfloat16)
    hidden_ref[...] = hidden
    result_ref[...] = hidden


def share_kernel(
    half, fanout_two, near_ref, far_ref, value_ref, hidden_ref, ws_ref, wn_ref, *refs
):
    out_refs, other_ref = refs[:half], refs[half]
    store_values(hidden_ref[...], ws_ref, wn_ref, fanout_two, other_ref)
    values = jnp.concatenate(
        [value_ref[0], other_ref[0], value_ref[1], other_ref[1]], axis=0
    )
    near = jnp.dot(near_ref[...], values, preferred_element_type=jnp.float32)
    far = jnp.dot(far_ref[...], values, preferred_element_type=jnp.float32)
    rows = out_refs[0].shape[0] // 2
    for s, out_ref in enumerate(out_refs):
        out_ref[:rows, :] = near[s * rows : (s + 1) * rows].astype(jnp.bfloat16)
        out_ref[rows:, :] = far[s * rows : (s + 1) * rows].astype(jnp.bfloat16)


def side_sum_kernel(*refs):
    near_ref, far_ref = refs[-2:]
    rows = near_ref.shape[0]
    total = refs[0][...].astype(jnp.float32)
    for ref in refs[1:-2]:
        total = total + ref[...].astype(jnp.float32)
    near_ref[...] = total[:rows]
    far_ref[...] = total[rows:].astype(jnp.bfloat16)


def swap(value, axis, step):
    size = lax.axis_size(axis)
    return lax.ppermute(value, axis, [(i, i ^ step) for i in range(size)])


def body(
    src_feats,
    nbr_one,
    counts,
    seed_rows,
    nbr_two,
    w1_self,
    w1_nbr,
    bias_one,
    w2_self,
    w2_nbr,
    bias_two,
):
    n_feat = lax.axis_size("feat")
    half = n_feat // 2
    fslice, nodes = src_feats.shape
    fanout_one, pcap = nbr_one.shape[2:]
    width = w1_self.shape[1]
    seed_count, fanout_two = nbr_two.shape
    n_idx = fanout_two + 1
    bf16 = jnp.bfloat16
    vmem = pl.BlockSpec(memory_space=pltpu.VMEM)
    smem = pl.BlockSpec(memory_space=pltpu.SMEM)
    hbm = pl.BlockSpec(memory_space=pltpu.HBM)
    anywhere = pl.BlockSpec(memory_space=pl.ANY)
    table_bytes = nodes * LANES * 4

    def call(kernel, name, shapes, ins, args, after=(), scratch=(), limit=16 * MIB):
        def wrapped(*refs):
            kernel(*refs[: len(args)], *refs[len(args) + len(after) :])

        return pl.pallas_call(
            wrapped,
            out_shape=tuple(jax.ShapeDtypeStruct(shape, dtype) for shape, dtype in shapes),
            in_specs=[*ins, *([anywhere] * len(after))],
            out_specs=(vmem,) * len(shapes),
            scratch_shapes=scratch,
            compiler_params=pltpu.CompilerParams(vmem_limit_bytes=limit),
            name=name,
        )(*args, *after)

    def pinned(value):
        return pltpu.with_memory_space_constraint(value, pltpu.HBM)

    def send(chunks):
        return [chunk if s == 0 else swap(chunk, "feat", s) for s, chunk in enumerate(chunks)]

    parcels = call(
        functools.partial(pack_kernel, n_feat, pcap),
        "pack",
        [((2 * fslice, width), bf16)] * half,
        [hbm] * 5,
        [pinned(x) for x in (src_feats, seed_rows[None], nbr_two.T, w1_self, w1_nbr)],
        scratch=[
            pltpu.VMEM((fslice, n_feat * 2 * pcap), bf16),
            pltpu.VMEM((1, seed_count), jnp.int32),
            pltpu.VMEM((fanout_two, seed_count), jnp.int32),
            pltpu.VMEM((fslice, width), bf16),
            pltpu.VMEM((fslice, width), bf16),
            pltpu.SemaphoreType.DMA((5,)),
        ],
    )
    arrived = send(parcels)
    (table,) = call(
        turn_kernel,
        "turn",
        [((nodes, LANES), jnp.float32)],
        [hbm],
        (pinned(src_feats),),
        after=(parcels[0],),
        scratch=[pltpu.VMEM((fslice, nodes), bf16), pltpu.SemaphoreType.DMA((6,))],
        limit=table_bytes + 12 * MIB,
    )
    table = table.reshape(nodes, 1, LANES)
    neighbors = nbr_one.reshape(-1)
    chunk_shape = (pcap // 4 * 3, LANES) if folds(fslice, pcap) else (pcap, fslice)

    def means(base, count, after):
        (chunks,) = call(
            functools.partial(mean_kernel, base, fanout_one, pcap, fslice),
            "mean",
            [((count, *chunk_shape), bf16)],
            [smem, vmem],
            (neighbors, table),
            after=after,
            scratch=[pltpu.VMEM((pcap, LANES), jnp.float32)],
            limit=table_bytes + 8 * MIB,
        )
        return [chunks[i] for i in range(count)]

    far_means = means(half, half, ())
    far_arrived = send(far_means)
    (halves,) = call(
        halves_kernel,
        "halves",
        [((half, fslice, width), bf16)],
        [vmem] * half,
        arrived,
        after=far_means[:1],
    )
    other_halves = swap(halves, "rep", 1)
    (last_mean,) = means(half - 1, 1, far_means[:1])
    w_nbr, pre, cross = call(
        functools.partial(prepare_kernel, half, n_idx),
        "prepare",
        [
            ((half, fslice, width), bf16),
            ((pcap, width), jnp.float32),
            ((pcap + -(-half // 4) * n_idx, width), bf16),
        ],
        [vmem] * (2 * half + 2),
        (*arrived, *far_arrived, other_halves, bias_one[None]),
        after=(last_mean,),
    )
    cross_arrived = swap(cross, "feat", half)
    near_means = means(0, half - 1, (cross,))
    near_arrived = send([*near_means, last_mean])
    (near_times,) = call(
        functools.partial(near_times_kernel, half, fslice, pcap, n_idx),
        "near_times",
        [((half * seed_count, 4 * pcap), bf16)],
        [vmem] * half,
        arrived,
        after=near_means[:1],
    )
    hidden, result = call(
        functools.partial(layer_kernel, half),
        "hidden",
        [((pcap, width), bf16)] * 2,
        [smem] + [vmem] * (half + 3),
        (counts, *near_arrived, pre, w_nbr, cross_arrived),
    )
    other_hidden = swap(hidden, "rep", 1)
    far_times, value = call(
        functools.partial(far_times_kernel, half, n_idx, fanout_two),
        "far_times",
        [((half * seed_count, 4 * pcap), bf16), ((2, pcap, width), bf16)],
        [vmem] * 4,
        (cross_arrived, hidden, w2_self, w2_nbr),
    )
    shares = call(
        functools.partial(share_kernel, half, fanout_two),
        "share",
        [((2 * seed_count, width), bf16)] * half,
        [vmem] * 6,
        (near_times, far_times, value, other_hidden, w2_self, w2_nbr),
        scratch=[pltpu.VMEM((2, pcap, width), bf16)],
        limit=32 * MIB,
    )
    near_sum, far_sum = call(
        side_sum_kernel,
        "side_sum",
        [((seed_count, width), jnp.float32), ((seed_count, width), bf16)],
        [vmem] * half,
        send(shares),
    )
    pre_two = near_sum + swap(far_sum, "feat", half).astype(jnp.float32) + bias_two
    seed_out = jnp.maximum(pre_two, 0.0).astype(bf16)
    return (result[None, None], seed_out)


def solution(mesh):
    placed = (
        P("feat", "groups"),
        P("groups", "rep", None, None),
        P(("groups", "feat"), "rep"),
        P(("groups", "feat", "rep")),
        P(("groups", "feat", "rep"), None),
        P("feat", None),
        P("feat", None),
        P(),
        P(),
        P(),
        P(),
    )
    return jax.shard_map(
        body,
        mesh=mesh,
        in_specs=placed,
        out_specs=(P(("groups", "feat"), "rep", None, None), P(("groups", "feat", "rep"), None)),
        check_vma=False,
    )
```

```python
import functools

import jax
import jax.numpy as jnp
from jax import lax
from jax.experimental import pallas as pl
from jax.experimental.pallas import tpu as pltpu
from jax.sharding import PartitionSpec as P

LANES = 128
MIB = 1024 * 1024


def folds(fslice, pcap):
    return 4 * fslice == 3 * LANES and pcap % 64 == 0


def pack_kernel(
    n_feat,
    pcap,
    src_hbm,
    seed_hbm,
    nbr_hbm,
    w_self_hbm,
    w_nbr_hbm,
    *refs,
):
    half = n_feat // 2
    parcel_refs = refs[:half]
    src_ref, seed_ref, nbr_ref, w_self_ref, w_nbr_ref, sems = refs[half:]
    fslice = w_self_ref.shape[0]
    copies = [
        pltpu.make_async_copy(a, b, sems.at[i])
        for i, (a, b) in enumerate(
            (
                (src_hbm.at[:, pl.ds(0, src_ref.shape[1])], src_ref),
                (seed_hbm, seed_ref),
                (nbr_hbm, nbr_ref),
                (w_self_hbm, w_self_ref),
                (w_nbr_hbm, w_nbr_ref),
            )
        )
    ]
    for copy in copies:
        copy.start()
    for copy in copies:
        copy.wait()
    feat_pos = lax.axis_index("feat")
    first_core = lax.axis_index("rep") == 0
    idx = jnp.concatenate([seed_ref[...], nbr_ref[...]], axis=0)
    high = lax.shift_right_logical(idx, 7)
    digits = jnp.concatenate([high, idx - high * 128], axis=1).astype(jnp.float32)
    digits = digits.astype(jnp.bfloat16)
    weight = jnp.where(first_core, w_self_ref[...], w_nbr_ref[...])
    for s, parcel_ref in enumerate(parcel_refs):
        parcel_ref[:fslice, :] = weight
        for place, step in enumerate((s, s ^ half)):
            at = pl.multiple_of(jnp.bitwise_xor(feat_pos, step) * (2 * pcap), LANES)
            block = src_ref[:, pl.ds(at, 2 * pcap)].astype(jnp.float32)
            own = jnp.where(first_core, block[:, :pcap], block[:, pcap:])
            if place == 0:
                near_side = own
        both = jnp.concatenate([near_side, own], axis=1)
        parcel_ref[fslice:, : 2 * pcap] = both.astype(jnp.bfloat16)
        parcel_ref[fslice : fslice + idx.shape[0], 2 * pcap :] = digits


def turn_kernel(src_hbm, table_ref, src_ref, sems):
    fslice, nodes = src_hbm.shape
    pieces = sems.shape[0]
    piece = nodes // pieces
    width = 512
    copies = [
        pltpu.make_async_copy(
            src_hbm.at[:, pl.ds(i * piece, piece)], src_ref.at[:, pl.ds(i * piece, piece)], sems.at[i]
        )
        for i in range(pieces)
    ]
    for copy in copies:
        copy.start()
    for i, copy in enumerate(copies):
        copy.wait()

        def turn(step, carry):
            at = pl.multiple_of(i * piece + step * width, width)
            block = src_ref[:, pl.ds(at, width)].astype(jnp.float32)
            table_ref[pl.ds(at, width), :fslice] = block.T
            return carry

        lax.fori_loop(0, piece // width, turn, 0)


def mean_kernel(
    base, count, fanout, pcap, fslice, nbr_hbm, table_ref, out_ref, total, nbr_ref, sems
):
    feat_pos = lax.axis_index("feat")
    stride = nbr_ref.shape[0] // count
    copies = [
        pltpu.make_async_copy(
            nbr_hbm.at[pl.ds(pl.multiple_of((feat_pos ^ (base + i)) * stride, stride), stride)],
            nbr_ref.at[pl.ds(i * stride, stride)],
            sems.at[i],
        )
        for i in range(count)
    ]
    for copy in copies:
        copy.start()
    for copy in copies:
        copy.wait()

    def partition(i, carry):
        first = i * stride

        def group(g, inner):
            at = pl.multiple_of(g * 8, 8)
            for u in range(8):
                rows = [table_ref[nbr_ref[first + k * pcap + at + u]] for k in range(fanout)]
                while len(rows) > 1:
                    rows = [a + b for a, b in zip(rows[::2], rows[1::2])] + (
                        [rows[-1]] if len(rows) % 2 else []
                    )
                total[pl.ds(at + u, 1), :] = rows[0]
            return inner

        lax.fori_loop(0, pcap // 8, group, 0)
        mean = total[...] / fanout
        if folds(fslice, pcap):
            part = pcap // 4
            lane = lax.broadcasted_iota(jnp.int32, (part, LANES), 1)
            tail = mean[3 * part :]
            for b in range(3):
                shift = (fslice - 32 * b) % LANES
                moved = pltpu.roll(tail, shift, 1) if shift else tail
                out_ref[i, pl.ds(b * part, part), :] = jnp.where(
                    lane < fslice, mean[b * part : (b + 1) * part], moved
                ).astype(jnp.bfloat16)
        else:
            out_ref[i] = mean[:, :fslice].astype(jnp.bfloat16)
        return carry

    lax.fori_loop(0, count, partition, 0)


def unfold(block, fslice, pcap):
    if block.shape[0] == pcap:
        return block
    part = block.shape[0] // 3
    wide = block.astype(jnp.float32)
    lane = lax.broadcasted_iota(jnp.int32, (part, LANES), 1)
    tail = pltpu.roll(wide[:part], LANES - fslice, 1)
    for b in (1, 2):
        shift = (32 * b - fslice) % LANES
        moved = wide[b * part : (b + 1) * part]
        moved = pltpu.roll(moved, shift, 1) if shift else moved
        tail = jnp.where(lane // 32 == b, moved, tail)
    return jnp.concatenate([wide, tail], axis=0)[:, :fslice].astype(jnp.bfloat16)


def halves_kernel(*refs):
    out_ref = refs[-1]
    for s, ref in enumerate(refs[:-1]):
        out_ref[s] = ref[: out_ref.shape[1], :]


def prepare_kernel(half, n_idx, *refs):
    parcel_refs, mean_refs = refs[:half], refs[half : 2 * half]
    other_ref, bias_ref, last_ref, w_ref, pre_ref, cross_ref, moved_ref = refs[2 * half :]
    moved_ref[...] = last_ref[0]
    fslice = w_ref.shape[1]
    pcap, width = pre_ref.shape
    first_core = lax.axis_index("rep") == 0
    both = jnp.zeros((2 * pcap, width), jnp.float32)
    far = jnp.zeros((pcap, width), jnp.float32)
    for s in range(half):
        mine, other = parcel_refs[s][:fslice, :], other_ref[s]
        w_nbr = jnp.where(first_core, other, mine)
        w_ref[s] = w_nbr
        feats = parcel_refs[s][fslice:, : 2 * pcap].astype(jnp.float32).T.astype(jnp.bfloat16)
        both = both + jnp.dot(
            feats, jnp.where(first_core, mine, other), preferred_element_type=jnp.float32
        )
        far = far + jnp.dot(
            unfold(mean_refs[s][...], fslice, pcap), w_nbr, preferred_element_type=jnp.float32
        )
        rows = pl.ds(pcap + s // 4 * n_idx, n_idx)
        cross_ref[rows, s % 4 * LANES : (s % 4 + 1) * LANES] = parcel_refs[s][
            fslice : fslice + n_idx, 2 * pcap :
        ]
    pre_ref[...] = both[:pcap] + bias_ref[...]
    cross_ref[:pcap, :] = (both[pcap:] + far).astype(jnp.bfloat16)


def store_times(pcap, blocks, out_ref):
    n_idx, pair = blocks[0].shape
    seed_count = pair // 2
    core_rows = lax.axis_index("feat") * (2 * pcap)
    rep_pos = lax.axis_index("rep")
    row = lax.broadcasted_iota(jnp.int32, (2 * pcap, pair), 0)
    slot = jnp.where(
        row < pcap, row + core_rows + rep_pos * pcap, row + core_rows - rep_pos * pcap
    ).astype(jnp.float32)
    low = lax.broadcasted_iota(jnp.int32, (n_idx, pair), 1) < seed_count
    for s in range(0, len(blocks), 2):
        first, second = blocks[s].astype(jnp.float32), blocks[s + 1].astype(jnp.float32)
        high_part = jnp.where(low, first, pltpu.roll(second, seed_count, 1))
        low_part = jnp.where(low, pltpu.roll(first, seed_count, 1), second)
        name = high_part * 128.0 + low_part
        own = jnp.where(slot == name[:1], 1.0, 0.0)
        near = jnp.zeros((2 * pcap, pair), jnp.float32)
        for k in range(1, n_idx):
            near = near + jnp.where(slot == name[k : k + 1], 1.0, 0.0)
        place = pl.ds(s * seed_count, pair)
        out_ref[place, : 2 * pcap] = own.T.astype(jnp.bfloat16)
        out_ref[place, 2 * pcap :] = near.T.astype(jnp.bfloat16)


def near_times_kernel(half, fslice, pcap, n_idx, *refs):
    blocks = [ref[fslice : fslice + n_idx, 2 * pcap :] for ref in refs[:half]]
    store_times(pcap, blocks, refs[half])


def far_times_kernel(
    half, n_idx, fanout_two, cross_ref, hidden_ref, ws_ref, wn_ref, out_ref, value_ref
):
    pcap = hidden_ref.shape[0]
    blocks = [
        cross_ref[
            pl.ds(pcap + s // 4 * n_idx, n_idx), s % 4 * LANES : (s % 4 + 1) * LANES
        ]
        for s in range(half)
    ]
    store_times(pcap, blocks, out_ref)
    store_values(hidden_ref[...], ws_ref, wn_ref, fanout_two, value_ref)


def store_values(hidden, ws_ref, wn_ref, fanout_two, value_ref):
    value_ref[0] = jnp.dot(hidden, ws_ref[...], preferred_element_type=jnp.float32).astype(
        jnp.bfloat16
    )
    value_ref[1] = (
        jnp.dot(hidden, wn_ref[...], preferred_element_type=jnp.float32) / fanout_two
    ).astype(jnp.bfloat16)


def layer_kernel(half, count_ref, *refs):
    mean_refs = refs[:half]
    pre_ref, w_ref, cross_ref, hidden_ref, result_ref = refs[half:]
    pcap, width = hidden_ref.shape
    fslice = w_ref.shape[1]
    pre = pre_ref[...] + cross_ref[:pcap, :].astype(jnp.float32)
    for s in range(half):
        pre = pre + jnp.dot(
            unfold(mean_refs[s][...], fslice, pcap), w_ref[s], preferred_element_type=jnp.float32
        )
    live = lax.broadcasted_iota(jnp.int32, (pcap, width), 0) < count_ref[0, 0]
    hidden = jnp.where(live, jnp.maximum(pre, 0.0), 0.0).astype(jnp.bfloat16)
    hidden_ref[...] = hidden
    result_ref[...] = hidden


def share_kernel(
    half, fanout_two, near_ref, far_ref, value_ref, hidden_ref, ws_ref, wn_ref, *refs
):
    near_refs, far_refs, other_ref = refs[:half], refs[half : 2 * half], refs[2 * half]
    store_values(hidden_ref[...], ws_ref, wn_ref, fanout_two, other_ref)
    values = jnp.concatenate(
        [value_ref[0], other_ref[0], value_ref[1], other_ref[1]], axis=0
    )
    for times_ref, out_refs in ((far_ref, far_refs), (near_ref, near_refs)):
        part = jnp.dot(times_ref[...], values, preferred_element_type=jnp.float32)
        rows = out_refs[0].shape[0]
        for s, out_ref in enumerate(out_refs):
            out_ref[...] = part[s * rows : (s + 1) * rows].astype(jnp.bfloat16)


def side_sum_kernel(*refs):
    total = refs[0][...].astype(jnp.float32)
    for ref in refs[1:-1]:
        total = total + ref[...].astype(jnp.float32)
    refs[-1][...] = total.astype(jnp.bfloat16)


def last_kernel(bias_ref, *refs):
    total = bias_ref[...] + refs[0][...].astype(jnp.float32)
    for ref in refs[1:-1]:
        total = total + ref[...].astype(jnp.float32)
    refs[-1][...] = jnp.maximum(total, 0.0).astype(jnp.bfloat16)


def swap(value, axis, step):
    size = lax.axis_size(axis)
    return lax.ppermute(value, axis, [(i, i ^ step) for i in range(size)])


def body(
    src_feats,
    nbr_one,
    counts,
    seed_rows,
    nbr_two,
    w1_self,
    w1_nbr,
    bias_one,
    w2_self,
    w2_nbr,
    bias_two,
):
    n_feat = lax.axis_size("feat")
    half = n_feat // 2
    fslice, nodes = src_feats.shape
    fanout_one, pcap = nbr_one.shape[2:]
    width = w1_self.shape[1]
    seed_count, fanout_two = nbr_two.shape
    n_idx = fanout_two + 1
    bf16 = jnp.bfloat16
    vmem = pl.BlockSpec(memory_space=pltpu.VMEM)
    smem = pl.BlockSpec(memory_space=pltpu.SMEM)
    hbm = pl.BlockSpec(memory_space=pltpu.HBM)
    anywhere = pl.BlockSpec(memory_space=pl.ANY)
    table_bytes = nodes * LANES * 4

    def spaced(shape):
        return shape if len(shape) == 3 else (*shape, jax.ShapeDtypeStruct)

    def call(kernel, name, shapes, ins, args, after=(), scratch=(), limit=16 * MIB, cost_us=1):
        def wrapped(*refs):
            kernel(*refs[: len(args)], *refs[len(args) + len(after) :])

        return pl.pallas_call(
            wrapped,
            out_shape=tuple(
                space(shape, dtype) for shape, dtype, space in map(spaced, shapes)
            ),
            in_specs=[*ins, *([anywhere] * len(after))],
            out_specs=(vmem,) * len(shapes),
            scratch_shapes=scratch,
            compiler_params=pltpu.CompilerParams(vmem_limit_bytes=limit),
            cost_estimate=pl.CostEstimate(
                flops=int(cost_us * 1_100_000_000), bytes_accessed=0, transcendentals=0
            ),
            name=name,
        )(*args, *after)

    def pinned(value, space=pltpu.HBM):
        return pltpu.with_memory_space_constraint(value, space)

    def send(chunks):
        return [chunk if s == 0 else swap(chunk, "feat", s) for s, chunk in enumerate(chunks)]

    parcels = call(
        functools.partial(pack_kernel, n_feat, pcap),
        "pack",
        [((2 * fslice, width), bf16)] * half,
        [hbm] * 5,
        [pinned(x) for x in (src_feats, seed_rows[None], nbr_two.T, w1_self, w1_nbr)],
        scratch=[
            pltpu.VMEM((fslice, n_feat * 2 * pcap), bf16),
            pltpu.VMEM((1, seed_count), jnp.int32),
            pltpu.VMEM((fanout_two, seed_count), jnp.int32),
            pltpu.VMEM((fslice, width), bf16),
            pltpu.VMEM((fslice, width), bf16),
            pltpu.SemaphoreType.DMA((5,)),
        ],
    )
    arrived = send(parcels)
    (table,) = call(
        turn_kernel,
        "turn",
        [((nodes, LANES), jnp.float32, pltpu.VMEM)],
        [hbm],
        (pinned(src_feats),),
        after=(parcels[0],),
        scratch=[pltpu.VMEM((fslice, nodes), bf16), pltpu.SemaphoreType.DMA((6,))],
        limit=table_bytes + 12 * MIB,
        cost_us=3,
    )
    table = table.reshape(nodes, 1, LANES)
    stride = -(-fanout_one * pcap // 1024) * 1024
    neighbors = jnp.pad(
        nbr_one.reshape(n_feat, fanout_one * pcap), ((0, 0), (0, stride - fanout_one * pcap))
    ).reshape(-1)
    chunk_shape = (pcap // 4 * 3, LANES) if folds(fslice, pcap) else (pcap, fslice)

    def means(base, count, after):
        (chunks,) = call(
            functools.partial(mean_kernel, base, count, fanout_one, pcap, fslice),
            "mean",
            [((count, *chunk_shape), bf16)],
            [anywhere, vmem],
            (neighbors, pinned(table, pltpu.VMEM)),
            after=after,
            scratch=[
                pltpu.VMEM((pcap, LANES), jnp.float32),
                pltpu.SMEM((count * stride,), jnp.int32),
                pltpu.SemaphoreType.DMA((count,)),
            ],
            limit=table_bytes + 8 * MIB,
            cost_us=2 * count,
        )
        return chunks

    def split(chunks):
        return [chunks[i] for i in range(chunks.shape[0])]

    far_means = means(half, half, ())
    far_arrived = send(split(far_means))
    (halves,) = call(
        halves_kernel,
        "halves",
        [((half, fslice, width), bf16)],
        [vmem] * half,
        arrived,
        after=(far_means,),
    )
    other_halves = swap(halves, "rep", 1)
    last_mean = means(half - 1, 1, (far_means,))
    w_nbr, pre, cross, moved = call(
        functools.partial(prepare_kernel, half, n_idx),
        "prepare",
        [
            ((half, fslice, width), bf16),
            ((pcap, width), jnp.float32),
            ((pcap + -(-half // 4) * n_idx, width), bf16),
            (chunk_shape, bf16),
        ],
        [vmem] * (2 * half + 3),
        (*arrived, *far_arrived, other_halves, bias_one[None], last_mean),
    )
    cross_arrived = swap(cross, "feat", half)
    (near_times,) = call(
        functools.partial(near_times_kernel, half, fslice, pcap, n_idx),
        "near_times",
        [((half * seed_count, 4 * pcap), bf16)],
        [vmem] * half,
        arrived,
        after=(far_means,),
    )
    near_means = means(0, half - 1, (cross, near_times))
    near_arrived = send([*split(near_means), moved])
    hidden, result = call(
        functools.partial(layer_kernel, half),
        "hidden",
        [((pcap, width), bf16)] * 2,
        [smem] + [vmem] * (half + 3),
        (counts, *near_arrived, pre, w_nbr, cross_arrived),
    )
    other_hidden = swap(hidden, "rep", 1)
    far_times, value = call(
        functools.partial(far_times_kernel, half, n_idx, fanout_two),
        "far_times",
        [((half * seed_count, 4 * pcap), bf16), ((2, pcap, width), bf16)],
        [vmem] * 4,
        (cross_arrived, hidden, w2_self, w2_nbr),
    )
    shares = call(
        functools.partial(share_kernel, half, fanout_two),
        "share",
        [((seed_count, width), bf16)] * (2 * half),
        [vmem] * 6,
        (near_times, far_times, value, other_hidden, w2_self, w2_nbr),
        scratch=[pltpu.VMEM((2, pcap, width), bf16)],
        limit=32 * MIB,
    )
    far_shares = send(shares[half:])
    near_shares = send(shares[:half])
    (far_sum,) = call(
        side_sum_kernel, "side_sum", [((seed_count, width), bf16)], [vmem] * half, far_shares
    )
    (seed_out,) = call(
        last_kernel,
        "seeds",
        [((seed_count, width), bf16)],
        [vmem] * (half + 2),
        (bias_two[None], *near_shares, swap(far_sum, "feat", half)),
    )
    return (result[None, None], seed_out)


def solution(mesh):
    placed = (
        P("feat", "groups"),
        P("groups", "rep", None, None),
        P(("groups", "feat"), "rep"),
        P(("groups", "feat", "rep")),
        P(("groups", "feat", "rep"), None),
        P("feat", None),
        P("feat", None),
        P(),
        P(),
        P(),
        P(),
    )
    return jax.shard_map(
        body,
        mesh=mesh,
        in_specs=placed,
        out_specs=(P(("groups", "feat"), "rep", None, None), P(("groups", "feat", "rep"), None)),
        check_vma=False,
    )
```

```python
import functools

import jax
import jax.numpy as jnp
from jax import lax
from jax.experimental import pallas as pl
from jax.experimental.pallas import tpu as pltpu
from jax.sharding import PartitionSpec as P

LANES = 128
MIB = 1024 * 1024


def folds(fslice, pcap):
    return 4 * fslice == 3 * LANES and pcap % 64 == 0


def pack_kernel(
    n_feat,
    pcap,
    src_hbm,
    seed_hbm,
    nbr_hbm,
    w_self_hbm,
    w_nbr_hbm,
    count_ref,
    *refs,
):
    half = n_feat // 2
    parcel_refs = refs[:half]
    src_ref, seed_ref, nbr_ref, w_self_ref, w_nbr_ref, sems = refs[half:]
    fslice = w_self_ref.shape[0]
    copies = [
        pltpu.make_async_copy(a, b, sems.at[i])
        for i, (a, b) in enumerate(
            (
                (src_hbm.at[:, pl.ds(0, src_ref.shape[1])], src_ref),
                (seed_hbm, seed_ref),
                (nbr_hbm, nbr_ref),
                (w_self_hbm, w_self_ref),
                (w_nbr_hbm, w_nbr_ref),
            )
        )
    ]
    for copy in copies:
        copy.start()
    for copy in copies:
        copy.wait()
    feat_pos = lax.axis_index("feat")
    first_core = lax.axis_index("rep") == 0
    idx = jnp.concatenate([seed_ref[...], nbr_ref[...]], axis=0)
    high = lax.shift_right_logical(idx, 7)
    digits = jnp.concatenate([high, idx - high * 128], axis=1).astype(jnp.float32)
    digits = digits.astype(jnp.bfloat16)
    weight = jnp.where(first_core, w_self_ref[...], w_nbr_ref[...])
    live = jnp.full((8, LANES), count_ref[0, 0].astype(jnp.float32)).astype(jnp.bfloat16)
    tags = jnp.concatenate([digits, live], axis=0)
    for s, parcel_ref in enumerate(parcel_refs):
        parcel_ref[:fslice, :] = weight
        for place, step in enumerate((s, s ^ half)):
            at = pl.multiple_of(jnp.bitwise_xor(feat_pos, step) * (2 * pcap), LANES)
            block = src_ref[:, pl.ds(at, 2 * pcap)].astype(jnp.float32)
            own = jnp.where(first_core, block[:, :pcap], block[:, pcap:])
            if place == 0:
                near_side = own
        both = jnp.concatenate([near_side, own], axis=1)
        parcel_ref[fslice:, : 2 * pcap] = both.astype(jnp.bfloat16)
        parcel_ref[fslice : fslice + tags.shape[0], 2 * pcap :] = tags


def turn_kernel(src_hbm, table_ref, src_ref, sems):
    fslice, nodes = src_hbm.shape
    pieces = sems.shape[0]
    piece = nodes // pieces
    width = 512
    copies = [
        pltpu.make_async_copy(
            src_hbm.at[:, pl.ds(i * piece, piece)], src_ref.at[:, pl.ds(i * piece, piece)], sems.at[i]
        )
        for i in range(pieces)
    ]
    for copy in copies:
        copy.start()
    for i, copy in enumerate(copies):
        copy.wait()

        def turn(step, carry):
            at = pl.multiple_of(i * piece + step * width, width)
            table_ref[pl.ds(at, width), :fslice] = src_ref[:, pl.ds(at, width)].T.astype(
                jnp.float32
            )
            return carry

        lax.fori_loop(0, piece // width, turn, 0)


def mean_kernel(base, count, fanout, pcap, fslice, n_idx, nbr_hbm, table_ref, *refs):
    parcel_refs, (out_ref, total, nbr_ref, live_ref, sems) = refs[:-5], refs[-5:]
    feat_pos = lax.axis_index("feat")
    stride = nbr_ref.shape[0] // count
    copies = [
        pltpu.make_async_copy(
            nbr_hbm.at[pl.ds(pl.multiple_of((feat_pos ^ (base + i)) * stride, stride), stride)],
            nbr_ref.at[pl.ds(i * stride, stride)],
            sems.at[i],
        )
        for i in range(count)
    ]
    for copy in copies:
        copy.start()
    for i in range(count):
        live_ref[i] = pcap
    for i, ref in enumerate(parcel_refs):
        tag = ref[fslice + n_idx : fslice + n_idx + 8, 2 * pcap :]
        live_ref[i] = jnp.max(tag.astype(jnp.float32)).astype(jnp.int32)
    for copy in copies:
        copy.wait()

    def partition(i, carry):
        first = i * stride

        def group(g, inner):
            at = pl.multiple_of(g * 16, 16)
            for u in range(16):
                rows = [table_ref[nbr_ref[first + k * pcap + at + u]] for k in range(fanout)]
                while len(rows) > 1:
                    rows = [a + b for a, b in zip(rows[::2], rows[1::2])] + (
                        [rows[-1]] if len(rows) % 2 else []
                    )
                total[pl.ds(at + u, 1), :] = rows[0]
            return inner

        lax.fori_loop(0, lax.div(live_ref[i] + 15, 16), group, 0)
        mean = total[...] / fanout
        if folds(fslice, pcap):
            part = pcap // 4
            lane = lax.broadcasted_iota(jnp.int32, (part, LANES), 1)
            tail = mean[3 * part :]
            for b in range(3):
                shift = (fslice - 32 * b) % LANES
                moved = pltpu.roll(tail, shift, 1) if shift else tail
                out_ref[i, pl.ds(b * part, part), :] = jnp.where(
                    lane < fslice, mean[b * part : (b + 1) * part], moved
                ).astype(jnp.bfloat16)
        else:
            out_ref[i] = mean[:, :fslice].astype(jnp.bfloat16)
        return carry

    lax.fori_loop(0, count, partition, 0)


def unfold(block, fslice, pcap):
    if block.shape[0] == pcap:
        return block
    part = block.shape[0] // 3
    wide = block.astype(jnp.float32)
    lane = lax.broadcasted_iota(jnp.int32, (part, LANES), 1)
    tail = pltpu.roll(wide[:part], LANES - fslice, 1)
    for b in (1, 2):
        shift = (32 * b - fslice) % LANES
        moved = wide[b * part : (b + 1) * part]
        moved = pltpu.roll(moved, shift, 1) if shift else moved
        tail = jnp.where(lane // 32 == b, moved, tail)
    return jnp.concatenate([wide, tail], axis=0)[:, :fslice].astype(jnp.bfloat16)


def halves_kernel(half, *refs):
    parcel_refs, chunks_ref, out_ref, chunk_refs = (
        refs[:half],
        refs[half],
        refs[half + 1],
        refs[half + 2 :],
    )
    for s in range(half):
        out_ref[s] = parcel_refs[s][: out_ref.shape[1], :]
        chunk_refs[s][...] = chunks_ref[s]


def prepare_kernel(half, n_idx, *refs):
    parcel_refs, mean_refs = refs[:half], refs[half : 2 * half]
    other_ref, bias_ref, last_ref, w_ref, pre_ref, cross_ref, moved_ref = refs[2 * half :]
    moved_ref[...] = last_ref[0]
    fslice = w_ref.shape[1]
    pcap, width = pre_ref.shape
    first_core = lax.axis_index("rep") == 0
    both = jnp.zeros((2 * pcap, width), jnp.float32)
    far = jnp.zeros((pcap, width), jnp.float32)
    for s in range(half):
        mine, other = parcel_refs[s][:fslice, :], other_ref[s]
        w_nbr = jnp.where(first_core, other, mine)
        w_ref[s] = w_nbr
        feats = parcel_refs[s][fslice:, : 2 * pcap].astype(jnp.float32).T.astype(jnp.bfloat16)
        both = both + jnp.dot(
            feats, jnp.where(first_core, mine, other), preferred_element_type=jnp.float32
        )
        far = far + jnp.dot(
            unfold(mean_refs[s][...], fslice, pcap), w_nbr, preferred_element_type=jnp.float32
        )
        rows = pl.ds(pcap + s // 4 * n_idx, n_idx)
        cross_ref[rows, s % 4 * LANES : (s % 4 + 1) * LANES] = parcel_refs[s][
            fslice : fslice + n_idx, 2 * pcap :
        ]
    pre_ref[...] = both[:pcap] + bias_ref[...]
    cross_ref[:pcap, :] = (both[pcap:] + far).astype(jnp.bfloat16)


def store_times(pcap, blocks, out_ref):
    n_idx, pair = blocks[0].shape
    seed_count = pair // 2
    core_rows = lax.axis_index("feat") * (2 * pcap)
    rep_pos = lax.axis_index("rep")
    row = lax.broadcasted_iota(jnp.int32, (2 * pcap, pair), 0)
    slot = jnp.where(
        row < pcap, row + core_rows + rep_pos * pcap, row + core_rows - rep_pos * pcap
    ).astype(jnp.float32)
    low = lax.broadcasted_iota(jnp.int32, (n_idx, pair), 1) < seed_count
    for s in range(0, len(blocks), 2):
        first, second = blocks[s].astype(jnp.float32), blocks[s + 1].astype(jnp.float32)
        high_part = jnp.where(low, first, pltpu.roll(second, seed_count, 1))
        low_part = jnp.where(low, pltpu.roll(first, seed_count, 1), second)
        name = high_part * 128.0 + low_part
        own = jnp.where(slot == name[:1], 1.0, 0.0)
        near = jnp.zeros((2 * pcap, pair), jnp.float32)
        for k in range(1, n_idx):
            near = near + jnp.where(slot == name[k : k + 1], 1.0, 0.0)
        place = pl.ds(s * seed_count, pair)
        out_ref[place, : 2 * pcap] = own.T.astype(jnp.bfloat16)
        out_ref[place, 2 * pcap :] = near.T.astype(jnp.bfloat16)


def near_times_kernel(half, fslice, pcap, n_idx, *refs):
    blocks = [ref[fslice : fslice + n_idx, 2 * pcap :] for ref in refs[:half]]
    store_times(pcap, blocks, refs[half])


def far_times_kernel(
    half, n_idx, fanout_two, cross_ref, hidden_ref, ws_ref, wn_ref, out_ref, value_ref
):
    pcap = hidden_ref.shape[0]
    blocks = [
        cross_ref[
            pl.ds(pcap + s // 4 * n_idx, n_idx), s % 4 * LANES : (s % 4 + 1) * LANES
        ]
        for s in range(half)
    ]
    store_times(pcap, blocks, out_ref)
    store_values(hidden_ref[...], ws_ref, wn_ref, fanout_two, value_ref)


def store_values(hidden, ws_ref, wn_ref, fanout_two, value_ref):
    value_ref[0] = jnp.dot(hidden, ws_ref[...], preferred_element_type=jnp.float32).astype(
        jnp.bfloat16
    )
    value_ref[1] = (
        jnp.dot(hidden, wn_ref[...], preferred_element_type=jnp.float32) / fanout_two
    ).astype(jnp.bfloat16)


def layer_kernel(half, count_ref, *refs):
    mean_refs = refs[:half]
    pre_ref, w_ref, cross_ref, hidden_ref, result_ref = refs[half:]
    pcap, width = hidden_ref.shape
    fslice = w_ref.shape[1]
    pre = pre_ref[...] + cross_ref[:pcap, :].astype(jnp.float32)
    for s in range(half):
        pre = pre + jnp.dot(
            unfold(mean_refs[s][...], fslice, pcap), w_ref[s], preferred_element_type=jnp.float32
        )
    live = lax.broadcasted_iota(jnp.int32, (pcap, width), 0) < count_ref[0, 0]
    hidden = jnp.where(live, jnp.maximum(pre, 0.0), 0.0).astype(jnp.bfloat16)
    hidden_ref[...] = hidden
    result_ref[...] = hidden


def far_share_kernel(
    half, fanout_two, far_ref, value_ref, hidden_ref, ws_ref, wn_ref, *refs
):
    out_refs, values_ref, other_ref = refs[:half], refs[half], refs[half + 1]
    pcap = hidden_ref.shape[0]
    store_values(hidden_ref[...], ws_ref, wn_ref, fanout_two, other_ref)
    for i in range(2):
        values_ref[pl.ds(2 * i * pcap, pcap), :] = value_ref[i]
        values_ref[pl.ds((2 * i + 1) * pcap, pcap), :] = other_ref[i]
    store_shares(far_ref, values_ref, out_refs)


def store_shares(times_ref, values_ref, out_refs):
    rows = out_refs[0].shape[0]
    part = jnp.dot(times_ref[...], values_ref[...], preferred_element_type=jnp.float32)
    for s, out_ref in enumerate(out_refs):
        out_ref[...] = part[s * rows : (s + 1) * rows].astype(jnp.bfloat16)


def near_share_kernel(near_ref, values_ref, *out_refs):
    store_shares(near_ref, values_ref, out_refs)


def side_sum_kernel(*refs):
    total = refs[0][...].astype(jnp.float32)
    for ref in refs[1:-1]:
        total = total + ref[...].astype(jnp.float32)
    refs[-1][: total.shape[0], :] = total.astype(jnp.bfloat16)


def last_kernel(bias_ref, *refs):
    total = bias_ref[...]
    for ref in refs[:-1]:
        total = total + ref[: refs[-1].shape[0], :].astype(jnp.float32)
    refs[-1][...] = jnp.maximum(total, 0.0).astype(jnp.bfloat16)


def swap(value, axis, step):
    size = lax.axis_size(axis)
    return lax.ppermute(value, axis, [(i, i ^ step) for i in range(size)])


def body(
    src_feats,
    nbr_one,
    counts,
    seed_rows,
    nbr_two,
    w1_self,
    w1_nbr,
    bias_one,
    w2_self,
    w2_nbr,
    bias_two,
):
    n_feat = lax.axis_size("feat")
    half = n_feat // 2
    fslice, nodes = src_feats.shape
    fanout_one, pcap = nbr_one.shape[2:]
    width = w1_self.shape[1]
    seed_count, fanout_two = nbr_two.shape
    n_idx = fanout_two + 1
    bf16 = jnp.bfloat16
    vmem = pl.BlockSpec(memory_space=pltpu.VMEM)
    smem = pl.BlockSpec(memory_space=pltpu.SMEM)
    hbm = pl.BlockSpec(memory_space=pltpu.HBM)
    anywhere = pl.BlockSpec(memory_space=pl.ANY)
    table_bytes = nodes * LANES * 4

    def call(kernel, name, shapes, ins, args, after=(), scratch=(), limit=16 * MIB, cost_us=1):
        def wrapped(*refs):
            kernel(*refs[: len(args)], *refs[len(args) + len(after) :])

        return pl.pallas_call(
            wrapped,
            out_shape=tuple(jax.ShapeDtypeStruct(shape, dtype) for shape, dtype in shapes),
            in_specs=[*ins, *([anywhere] * len(after))],
            out_specs=(vmem,) * len(shapes),
            scratch_shapes=scratch,
            compiler_params=pltpu.CompilerParams(vmem_limit_bytes=limit),
            cost_estimate=pl.CostEstimate(
                flops=int(cost_us * 1_100_000_000), bytes_accessed=0, transcendentals=0
            ),
            name=name,
        )(*args, *after)

    def pinned(value):
        return pltpu.with_memory_space_constraint(value, pltpu.HBM)

    def send(chunks):
        return [chunk if s == 0 else swap(chunk, "feat", s) for s, chunk in enumerate(chunks)]

    stride = -(-fanout_one * pcap // 1024) * 1024
    neighbors = jnp.pad(
        nbr_one.reshape(n_feat, fanout_one * pcap), ((0, 0), (0, stride - fanout_one * pcap))
    ).reshape(-1)
    parcels = call(
        functools.partial(pack_kernel, n_feat, pcap),
        "pack",
        [((2 * fslice, width), bf16)] * half,
        [hbm] * 5 + [smem],
        [pinned(x) for x in (src_feats, seed_rows[None], nbr_two.T, w1_self, w1_nbr)] + [counts],
        scratch=[
            pltpu.VMEM((fslice, n_feat * 2 * pcap), bf16),
            pltpu.VMEM((1, seed_count), jnp.int32),
            pltpu.VMEM((fanout_two, seed_count), jnp.int32),
            pltpu.VMEM((fslice, width), bf16),
            pltpu.VMEM((fslice, width), bf16),
            pltpu.SemaphoreType.DMA((5,)),
        ],
    )
    arrived = send(parcels)
    (table,) = call(
        turn_kernel,
        "turn",
        [((nodes, LANES), jnp.float32)],
        [hbm],
        (pinned(src_feats),),
        after=(parcels[0], neighbors),
        scratch=[pltpu.VMEM((fslice, nodes), bf16), pltpu.SemaphoreType.DMA((6,))],
        limit=table_bytes + 12 * MIB,
        cost_us=3,
    )
    table = table.reshape(nodes, 1, LANES)
    chunk_shape = (pcap // 4 * 3, LANES) if folds(fslice, pcap) else (pcap, fslice)

    def means(base, count, parcels=(), after=()):
        (chunks,) = call(
            functools.partial(mean_kernel, base, count, fanout_one, pcap, fslice, n_idx),
            "mean",
            [((count, *chunk_shape), bf16)],
            [anywhere] + [vmem] * (1 + len(parcels)),
            (neighbors, table, *parcels),
            after=after,
            scratch=[
                pltpu.VMEM((pcap, LANES), jnp.float32),
                pltpu.SMEM((count * stride,), jnp.int32),
                pltpu.SMEM((count,), jnp.int32),
                pltpu.SemaphoreType.DMA((count,)),
            ],
            limit=table_bytes + 8 * MIB,
            cost_us=2 * count,
        )
        return chunks

    far_means = means(half, half)
    halves, *far_chunks = call(
        functools.partial(halves_kernel, half),
        "halves",
        [((half, fslice, width), bf16)] + [(chunk_shape, bf16)] * half,
        [vmem] * (half + 1),
        (*arrived, far_means),
    )
    far_arrived = send(far_chunks)
    other_halves = swap(halves, "rep", 1)
    last_mean = means(half - 1, 1, arrived[half - 1 :], (far_chunks[0],))
    w_nbr, pre, cross, moved = call(
        functools.partial(prepare_kernel, half, n_idx),
        "prepare",
        [
            ((half, fslice, width), bf16),
            ((pcap, width), jnp.float32),
            ((pcap + -(-half // 4) * n_idx, width), bf16),
            (chunk_shape, bf16),
        ],
        [vmem] * (2 * half + 3),
        (*arrived, *far_arrived, other_halves, bias_one[None], last_mean),
    )
    cross_arrived = swap(cross, "feat", half)
    (near_times,) = call(
        functools.partial(near_times_kernel, half, fslice, pcap, n_idx),
        "near_times",
        [((half * seed_count, 4 * pcap), bf16)],
        [vmem] * half,
        arrived,
        after=(far_means,),
    )
    near_means = means(0, half - 1, arrived[: half - 1], (cross, near_times))
    near_arrived = send([*(near_means[i] for i in range(half - 1)), moved])
    hidden, result = call(
        functools.partial(layer_kernel, half),
        "hidden",
        [((pcap, width), bf16)] * 2,
        [smem] + [vmem] * (half + 3),
        (counts, *near_arrived, pre, w_nbr, cross_arrived),
    )
    other_hidden = swap(hidden, "rep", 1)
    far_times, value = call(
        functools.partial(far_times_kernel, half, n_idx, fanout_two),
        "far_times",
        [((half * seed_count, 4 * pcap), bf16), ((2, pcap, width), bf16)],
        [vmem] * 4,
        (cross_arrived, hidden, w2_self, w2_nbr),
    )
    *far_shares, values = call(
        functools.partial(far_share_kernel, half, fanout_two),
        "far_share",
        [((seed_count, width), bf16)] * half + [((4 * pcap, width), bf16)],
        [vmem] * 5,
        (far_times, value, other_hidden, w2_self, w2_nbr),
        scratch=[pltpu.VMEM((2, pcap, width), bf16)],
        limit=32 * MIB,
    )
    (far_sum,) = call(
        side_sum_kernel, "side_sum", [((seed_count + 8, width), bf16)], [vmem] * half, send(far_shares)
    )
    near_shares = send(
        call(
            near_share_kernel,
            "near_share",
            [((seed_count, width), bf16)] * half,
            [vmem] * 2,
            (near_times, values),
            after=(far_sum,),
            limit=32 * MIB,
        )
    )
    (seed_out,) = call(
        last_kernel,
        "seeds",
        [((seed_count, width), bf16)],
        [vmem] * (half + 2),
        (bias_two[None], swap(far_sum, "feat", half), *near_shares),
    )
    return (result[None, None], seed_out)


def solution(mesh):
    placed = (
        P("feat", "groups"),
        P("groups", "rep", None, None),
        P(("groups", "feat"), "rep"),
        P(("groups", "feat", "rep")),
        P(("groups", "feat", "rep"), None),
        P("feat", None),
        P("feat", None),
        P(),
        P(),
        P(),
        P(),
    )
    return jax.shard_map(
        body,
        mesh=mesh,
        in_specs=placed,
        out_specs=(P(("groups", "feat"), "rep", None, None), P(("groups", "feat", "rep"), None)),
        check_vma=False,
    )
```

```python
import functools

import jax
import jax.numpy as jnp
from jax import lax
from jax.experimental import pallas as pl
from jax.experimental.pallas import tpu as pltpu
from jax.sharding import PartitionSpec as P

LANES = 128
MIB = 1024 * 1024


def folds(fslice, pcap):
    return 4 * fslice == 3 * LANES and pcap % 64 == 0


def pack_kernel(
    n_feat,
    pcap,
    src_hbm,
    seed_hbm,
    nbr_hbm,
    w_self_hbm,
    w_nbr_hbm,
    pick_hbm,
    live_ref,
    *refs,
):
    half = n_feat // 2
    parcel_refs, pick_ref = refs[:half], refs[half]
    src_ref, seed_ref, nbr_ref, w_self_ref, w_nbr_ref, sems = refs[half + 1 :]
    fslice = w_self_ref.shape[0]
    copies = [
        pltpu.make_async_copy(a, b, sems.at[i])
        for i, (a, b) in enumerate(
            (
                (src_hbm.at[:, pl.ds(0, src_ref.shape[1])], src_ref),
                (seed_hbm, seed_ref),
                (nbr_hbm, nbr_ref),
                (w_self_hbm, w_self_ref),
                (w_nbr_hbm, w_nbr_ref),
                (pick_hbm, pick_ref),
            )
        )
    ]
    for copy in copies:
        copy.start()
    for copy in copies:
        copy.wait()
    feat_pos = lax.axis_index("feat")
    first_core = lax.axis_index("rep") == 0
    idx = jnp.concatenate([seed_ref[...], nbr_ref[...]], axis=0)
    high = lax.shift_right_logical(idx, 7)
    digits = jnp.concatenate([high, idx - high * 128], axis=1).astype(jnp.float32)
    digits = digits.astype(jnp.bfloat16)
    weight = jnp.where(first_core, w_self_ref[...], w_nbr_ref[...])
    live = jnp.full((8, LANES), live_ref[0, 0].astype(jnp.float32)).astype(jnp.bfloat16)
    tags = jnp.concatenate([digits, live], axis=0)
    for s, parcel_ref in enumerate(reversed(parcel_refs)):
        parcel_ref[:fslice, :] = weight
        for place, step in enumerate((s, s ^ half)):
            at = pl.multiple_of(jnp.bitwise_xor(feat_pos, step) * (2 * pcap), LANES)
            block = src_ref[:, pl.ds(at, 2 * pcap)].astype(jnp.float32)
            own = jnp.where(first_core, block[:, :pcap], block[:, pcap:])
            if place == 0:
                near_side = own
        both = jnp.concatenate([near_side, own], axis=1)
        parcel_ref[fslice:, : 2 * pcap] = both.astype(jnp.bfloat16)
        parcel_ref[fslice : fslice + tags.shape[0], 2 * pcap :] = tags


def turn_kernel(src_hbm, table_ref, src_ref, sems):
    fslice, nodes = src_hbm.shape
    pieces = sems.shape[0]
    piece = nodes // pieces
    width = 512
    copies = [
        pltpu.make_async_copy(
            src_hbm.at[:, pl.ds(i * piece, piece)], src_ref.at[:, pl.ds(i * piece, piece)], sems.at[i]
        )
        for i in range(pieces)
    ]
    for copy in copies:
        copy.start()
    for i, copy in enumerate(copies):
        copy.wait()

        def turn(step, carry):
            at = pl.multiple_of(i * piece + step * width, width)
            table_ref[pl.ds(at, width), :fslice] = src_ref[:, pl.ds(at, width)].T.astype(
                jnp.float32
            )
            return carry

        lax.fori_loop(0, piece // width, turn, 0)


def live_rows(parcel_ref, row, lane):
    return jnp.max(parcel_ref[row : row + 8, lane:].astype(jnp.float32)).astype(jnp.int32)


def mean_kernel(chosen, fanout, pcap, fslice, n_idx, nbr_hbm, table_ref, *refs):
    parcel_refs, (out_ref, total, nbr_ref, live_ref, sems) = refs[:-5], refs[-5:]
    feat_pos = lax.axis_index("feat")
    count = len(chosen)
    stride = nbr_ref.shape[0] // count
    copies = [
        pltpu.make_async_copy(
            nbr_hbm.at[pl.ds(pl.multiple_of((feat_pos ^ step) * stride, stride), stride)],
            nbr_ref.at[pl.ds(i * stride, stride)],
            sems.at[i],
        )
        for i, step in enumerate(chosen)
    ]
    for copy in copies:
        copy.start()
    for i in range(count):
        live_ref[i] = pcap
    for i, ref in enumerate(parcel_refs):
        live_ref[i] = live_rows(ref, fslice + n_idx, 2 * pcap)
    for copy in copies:
        copy.wait()

    def partition(i, carry):
        first = i * stride

        def group(g, inner):
            at = pl.multiple_of(g * 16, 16)
            for u in range(16):
                rows = [table_ref[nbr_ref[first + k * pcap + at + u]] for k in range(fanout)]
                while len(rows) > 1:
                    rows = [a + b for a, b in zip(rows[::2], rows[1::2])] + (
                        [rows[-1]] if len(rows) % 2 else []
                    )
                total[pl.ds(at + u, 1), :] = rows[0]
            return inner

        lax.fori_loop(0, lax.div(live_ref[i] + 15, 16), group, 0)
        mean = total[...] / fanout
        if folds(fslice, pcap):
            part = pcap // 4
            lane = lax.broadcasted_iota(jnp.int32, (part, LANES), 1)
            tail = mean[3 * part :]
            for b in range(3):
                shift = (fslice - 32 * b) % LANES
                moved = pltpu.roll(tail, shift, 1) if shift else tail
                out_ref[i, pl.ds(b * part, part), :] = jnp.where(
                    lane < fslice, mean[b * part : (b + 1) * part], moved
                ).astype(jnp.bfloat16)
        else:
            out_ref[i] = mean[:, :fslice].astype(jnp.bfloat16)
        return carry

    lax.fori_loop(0, count, partition, 0)


def unfold(block, fslice, pcap):
    if block.shape[0] == pcap:
        return block
    part = block.shape[0] // 3
    wide = block.astype(jnp.float32)
    lane = lax.broadcasted_iota(jnp.int32, (part, LANES), 1)
    tail = pltpu.roll(wide[:part], LANES - fslice, 1)
    for b in (1, 2):
        shift = (32 * b - fslice) % LANES
        moved = wide[b * part : (b + 1) * part]
        moved = pltpu.roll(moved, shift, 1) if shift else moved
        tail = jnp.where(lane // 32 == b, moved, tail)
    return jnp.concatenate([wide, tail], axis=0)[:, :fslice].astype(jnp.bfloat16)


def halves_kernel(half, *refs):
    parcel_refs, chunks_ref, out_ref, chunk_refs = (
        refs[:half],
        refs[half],
        refs[half + 1],
        refs[half + 2 :],
    )
    for s in range(half):
        out_ref[s] = parcel_refs[s][: out_ref.shape[1], :]
        chunk_refs[s][...] = chunks_ref[s]


def prepare_kernel(half, n_idx, *refs):
    parcel_refs, mean_refs = refs[:half], refs[half : 2 * half]
    other_ref, bias_ref, first_ref, w_ref, pre_ref, cross_ref, moved_ref = refs[2 * half :]
    moved_ref[...] = first_ref[0]
    fslice = w_ref.shape[1]
    pcap, width = pre_ref.shape
    first_core = lax.axis_index("rep") == 0
    both = jnp.zeros((2 * pcap, width), jnp.float32)
    far = jnp.zeros((pcap, width), jnp.float32)
    for s in range(half):
        mine, other = parcel_refs[s][:fslice, :], other_ref[s]
        w_nbr = jnp.where(first_core, other, mine)
        w_ref[s] = w_nbr
        feats = parcel_refs[s][fslice:, : 2 * pcap].astype(jnp.float32).T.astype(jnp.bfloat16)
        both = both + jnp.dot(
            feats, jnp.where(first_core, mine, other), preferred_element_type=jnp.float32
        )
        far = far + jnp.dot(
            unfold(mean_refs[s][...], fslice, pcap), w_nbr, preferred_element_type=jnp.float32
        )
        rows = pl.ds(pcap + s // 4 * n_idx, n_idx)
        cross_ref[rows, s % 4 * LANES : (s % 4 + 1) * LANES] = parcel_refs[s][
            fslice : fslice + n_idx, 2 * pcap :
        ]
    pre_ref[...] = both[:pcap] + bias_ref[...]
    cross_ref[:pcap, :] = (both[pcap:] + far).astype(jnp.bfloat16)


def store_times(pcap, blocks, out_ref):
    n_idx, pair = blocks[0].shape
    seed_count = pair // 2
    core_rows = lax.axis_index("feat") * (2 * pcap)
    rep_pos = lax.axis_index("rep")
    row = lax.broadcasted_iota(jnp.int32, (2 * pcap, pair), 0)
    slot = jnp.where(
        row < pcap, row + core_rows + rep_pos * pcap, row + core_rows - rep_pos * pcap
    ).astype(jnp.float32)
    low = lax.broadcasted_iota(jnp.int32, (n_idx, pair), 1) < seed_count
    for s in range(0, len(blocks), 2):
        first, second = blocks[s].astype(jnp.float32), blocks[s + 1].astype(jnp.float32)
        high_part = jnp.where(low, first, pltpu.roll(second, seed_count, 1))
        low_part = jnp.where(low, pltpu.roll(first, seed_count, 1), second)
        name = high_part * 128.0 + low_part
        own = jnp.where(slot == name[:1], 1.0, 0.0)
        near = jnp.zeros((2 * pcap, pair), jnp.float32)
        for k in range(1, n_idx):
            near = near + jnp.where(slot == name[k : k + 1], 1.0, 0.0)
        place = pl.ds(s * seed_count, pair)
        out_ref[place, : 2 * pcap] = own.T.astype(jnp.bfloat16)
        out_ref[place, 2 * pcap :] = near.T.astype(jnp.bfloat16)


def near_times_kernel(half, fslice, pcap, n_idx, *refs):
    blocks = [ref[fslice : fslice + n_idx, 2 * pcap :] for ref in refs[:half]]
    store_times(pcap, blocks, refs[half])


def far_times_kernel(
    half, n_idx, fanout_two, cross_ref, hidden_ref, ws_ref, wn_ref, out_ref, value_ref
):
    pcap = hidden_ref.shape[0]
    blocks = [
        cross_ref[
            pl.ds(pcap + s // 4 * n_idx, n_idx), s % 4 * LANES : (s % 4 + 1) * LANES
        ]
        for s in range(half)
    ]
    store_times(pcap, blocks, out_ref)
    store_values(hidden_ref[...], ws_ref, wn_ref, fanout_two, value_ref)


def store_values(hidden, ws_ref, wn_ref, fanout_two, value_ref):
    value_ref[0] = jnp.dot(hidden, ws_ref[...], preferred_element_type=jnp.float32).astype(
        jnp.bfloat16
    )
    value_ref[1] = (
        jnp.dot(hidden, wn_ref[...], preferred_element_type=jnp.float32) / fanout_two
    ).astype(jnp.bfloat16)


def layer_kernel(half, n_idx, parcel_ref, *refs):
    mean_refs = refs[:half]
    pre_ref, w_ref, cross_ref, hidden_ref, result_ref = refs[half:]
    pcap, width = hidden_ref.shape
    fslice = w_ref.shape[1]
    pre = pre_ref[...] + cross_ref[:pcap, :].astype(jnp.float32)
    for s in range(half):
        pre = pre + jnp.dot(
            unfold(mean_refs[s][...], fslice, pcap), w_ref[s], preferred_element_type=jnp.float32
        )
    count = live_rows(parcel_ref, fslice + n_idx, 2 * pcap)
    live = lax.broadcasted_iota(jnp.int32, (pcap, width), 0) < count
    hidden = jnp.where(live, jnp.maximum(pre, 0.0), 0.0).astype(jnp.bfloat16)
    hidden_ref[...] = hidden
    result_ref[...] = hidden


def share_kernel(
    half, fanout_two, near_ref, far_ref, value_ref, hidden_ref, ws_ref, wn_ref, *refs
):
    near_refs, far_refs, other_ref = refs[:half], refs[half : 2 * half], refs[2 * half]
    store_values(hidden_ref[...], ws_ref, wn_ref, fanout_two, other_ref)
    values = jnp.concatenate(
        [value_ref[0], other_ref[0], value_ref[1], other_ref[1]], axis=0
    )
    for times_ref, out_refs in ((far_ref, far_refs), (near_ref, near_refs)):
        part = jnp.dot(times_ref[...], values, preferred_element_type=jnp.float32)
        rows = out_refs[0].shape[0]
        for s, out_ref in enumerate(out_refs):
            out_ref[...] = part[s * rows : (s + 1) * rows].astype(jnp.bfloat16)


def side_sum_kernel(*refs):
    total = refs[0][...].astype(jnp.float32)
    for ref in refs[1:-1]:
        total = total + ref[...].astype(jnp.float32)
    refs[-1][...] = total.astype(jnp.bfloat16)


def last_kernel(bias_ref, *refs):
    total = bias_ref[...] + refs[0][...].astype(jnp.float32)
    for ref in refs[1:-1]:
        total = total + ref[...].astype(jnp.float32)
    refs[-1][...] = jnp.maximum(total, 0.0).astype(jnp.bfloat16)


def swap(value, axis, step):
    size = lax.axis_size(axis)
    return lax.ppermute(value, axis, [(i, i ^ step) for i in range(size)])


def body(
    src_feats,
    nbr_one,
    counts,
    seed_rows,
    nbr_two,
    w1_self,
    w1_nbr,
    bias_one,
    w2_self,
    w2_nbr,
    bias_two,
):
    n_feat = lax.axis_size("feat")
    half = n_feat // 2
    steps = range(half - 1, -1, -1)
    fslice, nodes = src_feats.shape
    fanout_one, pcap = nbr_one.shape[2:]
    width = w1_self.shape[1]
    seed_count, fanout_two = nbr_two.shape
    n_idx = fanout_two + 1
    bf16 = jnp.bfloat16
    vmem = pl.BlockSpec(memory_space=pltpu.VMEM)
    smem = pl.BlockSpec(memory_space=pltpu.SMEM)
    hbm = pl.BlockSpec(memory_space=pltpu.HBM)
    anywhere = pl.BlockSpec(memory_space=pl.ANY)
    table_bytes = nodes * LANES * 4

    def call(kernel, name, shapes, ins, args, after=(), scratch=(), limit=16 * MIB, cost_us=1):
        def wrapped(*refs):
            kernel(*refs[: len(args)], *refs[len(args) + len(after) :])

        return pl.pallas_call(
            wrapped,
            out_shape=tuple(jax.ShapeDtypeStruct(shape, dtype) for shape, dtype in shapes),
            in_specs=[*ins, *([anywhere] * len(after))],
            out_specs=(vmem,) * len(shapes),
            scratch_shapes=scratch,
            compiler_params=pltpu.CompilerParams(vmem_limit_bytes=limit),
            cost_estimate=pl.CostEstimate(
                flops=int(cost_us * 1_100_000_000), bytes_accessed=0, transcendentals=0
            ),
            name=name,
        )(*args, *after)

    def pinned(value):
        return pltpu.with_memory_space_constraint(value, pltpu.HBM)

    def send(chunks):
        return [swap(chunk, "feat", s) if s else chunk for s, chunk in zip(steps, chunks)]

    picks = jnp.transpose(nbr_one, (0, 2, 1, 3))
    *parcels, picks = call(
        functools.partial(pack_kernel, n_feat, pcap),
        "pack",
        [((2 * fslice, width), bf16)] * half + [(picks.shape, jnp.int32)],
        [hbm] * 6 + [smem],
        [
            *(pinned(x) for x in (src_feats, seed_rows[None], nbr_two.T, w1_self, w1_nbr, picks)),
            counts,
        ],
        scratch=[
            pltpu.VMEM((fslice, n_feat * 2 * pcap), bf16),
            pltpu.VMEM((1, seed_count), jnp.int32),
            pltpu.VMEM((fanout_two, seed_count), jnp.int32),
            pltpu.VMEM((fslice, width), bf16),
            pltpu.VMEM((fslice, width), bf16),
            pltpu.SemaphoreType.DMA((6,)),
        ],
    )
    stride = -(-fanout_one * pcap // 1024) * 1024
    neighbors = jnp.pad(
        picks.reshape(n_feat, fanout_one * pcap), ((0, 0), (0, stride - fanout_one * pcap))
    ).reshape(-1)
    arrived = send(parcels)
    (table,) = call(
        turn_kernel,
        "turn",
        [((nodes, LANES), jnp.float32)],
        [hbm],
        (pinned(src_feats),),
        after=(parcels[-1], neighbors),
        scratch=[pltpu.VMEM((fslice, nodes), bf16), pltpu.SemaphoreType.DMA((6,))],
        limit=table_bytes + 12 * MIB,
        cost_us=3,
    )
    table = table.reshape(nodes, 1, LANES)
    chunk_shape = (pcap // 4 * 3, LANES) if folds(fslice, pcap) else (pcap, fslice)

    def means(chosen, parcels=(), after=()):
        count = len(chosen)
        (chunks,) = call(
            functools.partial(mean_kernel, tuple(chosen), fanout_one, pcap, fslice, n_idx),
            "mean",
            [((count, *chunk_shape), bf16)],
            [anywhere] + [vmem] * (1 + len(parcels)),
            (neighbors, table, *parcels),
            after=after,
            scratch=[
                pltpu.VMEM((pcap, LANES), jnp.float32),
                pltpu.SMEM((count * stride,), jnp.int32),
                pltpu.SMEM((count,), jnp.int32),
                pltpu.SemaphoreType.DMA((count,)),
            ],
            limit=table_bytes + 8 * MIB,
            cost_us=2 * count,
        )
        return chunks

    far_means = means([s + half for s in steps])
    halves, *far_chunks = call(
        functools.partial(halves_kernel, half),
        "halves",
        [((half, fslice, width), bf16)] + [(chunk_shape, bf16)] * half,
        [vmem] * (half + 1),
        (*arrived, far_means),
    )
    far_arrived = send(far_chunks)
    other_halves = swap(halves, "rep", 1)
    first_mean = means([1], arrived[-2:-1], (far_chunks[-1],))
    w_nbr, pre, cross, moved = call(
        functools.partial(prepare_kernel, half, n_idx),
        "prepare",
        [
            ((half, fslice, width), bf16),
            ((pcap, width), jnp.float32),
            ((pcap + -(-half // 4) * n_idx, width), bf16),
            (chunk_shape, bf16),
        ],
        [vmem] * (2 * half + 3),
        (*arrived, *far_arrived, other_halves, bias_one[None], first_mean),
    )
    cross_arrived = swap(cross, "feat", half)
    (near_times,) = call(
        functools.partial(near_times_kernel, half, fslice, pcap, n_idx),
        "near_times",
        [((half * seed_count, 4 * pcap), bf16)],
        [vmem] * half,
        arrived,
        after=(far_means,),
    )
    near_means = means(
        [s for s in steps if s != 1], [*arrived[:-2], arrived[-1]], (cross, near_times)
    )
    near_means = [near_means[i] for i in range(half - 1)]
    near_arrived = send([*near_means[:-1], moved, near_means[-1]])
    hidden, result = call(
        functools.partial(layer_kernel, half, n_idx),
        "hidden",
        [((pcap, width), bf16)] * 2,
        [vmem] * (half + 4),
        (parcels[-1], *near_arrived, pre, w_nbr, cross_arrived),
    )
    other_hidden = swap(hidden, "rep", 1)
    far_times, value = call(
        functools.partial(far_times_kernel, half, n_idx, fanout_two),
        "far_times",
        [((half * seed_count, 4 * pcap), bf16), ((2, pcap, width), bf16)],
        [vmem] * 4,
        (cross_arrived, hidden, w2_self, w2_nbr),
    )
    shares = call(
        functools.partial(share_kernel, half, fanout_two),
        "share",
        [((seed_count, width), bf16)] * (2 * half),
        [vmem] * 6,
        (near_times, far_times, value, other_hidden, w2_self, w2_nbr),
        scratch=[pltpu.VMEM((2, pcap, width), bf16)],
        limit=32 * MIB,
    )
    far_shares = send(shares[half:])
    near_shares = send(shares[:half])
    (far_sum,) = call(
        side_sum_kernel, "side_sum", [((seed_count, width), bf16)], [vmem] * half, far_shares
    )
    (seed_out,) = call(
        last_kernel,
        "seeds",
        [((seed_count, width), bf16)],
        [vmem] * (half + 2),
        (bias_two[None], *near_shares, swap(far_sum, "feat", half)),
    )
    return (result[None, None], seed_out)


def solution(mesh):
    placed = (
        P("feat", "groups"),
        P("groups", "rep", None, None),
        P(("groups", "feat"), "rep"),
        P(("groups", "feat", "rep")),
        P(("groups", "feat", "rep"), None),
        P("feat", None),
        P("feat", None),
        P(),
        P(),
        P(),
        P(),
    )
    return jax.shard_map(
        body,
        mesh=mesh,
        in_specs=placed,
        out_specs=(P(("groups", "feat"), "rep", None, None), P(("groups", "feat", "rep"), None)),
        check_vma=False,
    )
```

```python
import functools

import jax
import jax.numpy as jnp
from jax import lax
from jax.experimental import pallas as pl
from jax.experimental.pallas import tpu as pltpu
from jax.sharding import PartitionSpec as P

LANES = 128
MIB = 1024 * 1024


def folds(fslice, pcap):
    return 4 * fslice == 3 * LANES and pcap % 64 == 0


def pack_kernel(
    n_feat,
    pcap,
    src_hbm,
    seed_hbm,
    nbr_hbm,
    w_self_hbm,
    w_nbr_hbm,
    pick_hbm,
    live_ref,
    *refs,
):
    half = n_feat // 2
    parcel_refs, pick_ref = refs[:half], refs[half]
    src_ref, seed_ref, nbr_ref, w_self_ref, w_nbr_ref, sems = refs[half + 1 :]
    fslice = w_self_ref.shape[0]
    copies = [
        pltpu.make_async_copy(a, b, sems.at[i])
        for i, (a, b) in enumerate(
            (
                (src_hbm.at[:, pl.ds(0, src_ref.shape[1])], src_ref),
                (seed_hbm, seed_ref),
                (nbr_hbm, nbr_ref),
                (w_self_hbm, w_self_ref),
                (w_nbr_hbm, w_nbr_ref),
                (pick_hbm, pick_ref),
            )
        )
    ]
    for copy in copies:
        copy.start()
    for copy in copies:
        copy.wait()
    feat_pos = lax.axis_index("feat")
    first_core = lax.axis_index("rep") == 0
    idx = jnp.concatenate([seed_ref[...], nbr_ref[...]], axis=0)
    high = lax.shift_right_logical(idx, 7)
    digits = jnp.concatenate([high, idx - high * 128], axis=1).astype(jnp.float32)
    digits = digits.astype(jnp.bfloat16)
    weight = jnp.where(first_core, w_self_ref[...], w_nbr_ref[...])
    live = jnp.full((8, LANES), live_ref[0, 0].astype(jnp.float32)).astype(jnp.bfloat16)
    tags = jnp.concatenate([digits, live], axis=0)
    for s, parcel_ref in enumerate(reversed(parcel_refs)):
        parcel_ref[:fslice, :] = weight
        for place, step in enumerate((s, s ^ half)):
            at = pl.multiple_of(jnp.bitwise_xor(feat_pos, step) * (2 * pcap), LANES)
            block = src_ref[:, pl.ds(at, 2 * pcap)].astype(jnp.float32)
            own = jnp.where(first_core, block[:, :pcap], block[:, pcap:])
            if place == 0:
                near_side = own
        both = jnp.concatenate([near_side, own], axis=1)
        parcel_ref[fslice:, : 2 * pcap] = both.astype(jnp.bfloat16)
        parcel_ref[fslice : fslice + tags.shape[0], 2 * pcap :] = tags


def turn_kernel(src_hbm, table_ref, src_ref, sems):
    fslice, nodes = src_hbm.shape
    pieces = sems.shape[0]
    piece = nodes // pieces
    width = 512
    copies = [
        pltpu.make_async_copy(
            src_hbm.at[:, pl.ds(i * piece, piece)], src_ref.at[:, pl.ds(i * piece, piece)], sems.at[i]
        )
        for i in range(pieces)
    ]
    for copy in copies:
        copy.start()
    for i, copy in enumerate(copies):
        copy.wait()

        def turn(step, carry):
            at = pl.multiple_of(i * piece + step * width, width)
            table_ref[pl.ds(at, width), :fslice] = src_ref[:, pl.ds(at, width)].T.astype(
                jnp.float32
            )
            return carry

        lax.fori_loop(0, piece // width, turn, 0)


def live_rows(parcel_ref, row, lane):
    return jnp.max(parcel_ref[row : row + 8, lane:].astype(jnp.float32)).astype(jnp.int32)


def mean_kernel(chosen, fanout, pcap, fslice, n_idx, nbr_hbm, table_ref, *refs):
    count = len(chosen)
    out_ref, total, nbr_ref, live_ref, sems = refs[-5:]
    chunk_refs, parcel_refs = refs[-5 - count : -5], refs[: -5 - count]
    feat_pos = lax.axis_index("feat")
    stride = nbr_ref.shape[0] // count
    copies = [
        pltpu.make_async_copy(
            nbr_hbm.at[pl.ds(pl.multiple_of((feat_pos ^ step) * stride, stride), stride)],
            nbr_ref.at[pl.ds(i * stride, stride)],
            sems.at[i],
        )
        for i, step in enumerate(chosen)
    ]
    for copy in copies:
        copy.start()
    for i in range(count):
        live_ref[i] = pcap
    for i, ref in enumerate(parcel_refs):
        live_ref[i] = live_rows(ref, fslice + n_idx, 2 * pcap)
    for copy in copies:
        copy.wait()

    def partition(i, carry):
        first = i * stride

        def group(g, inner):
            at = pl.multiple_of(g * 16, 16)
            sums = []
            for u in range(16):
                rows = [table_ref[nbr_ref[first + k * pcap + at + u]] for k in range(fanout)]
                while len(rows) > 1:
                    rows = [a + b for a, b in zip(rows[::2], rows[1::2])] + (
                        [rows[-1]] if len(rows) % 2 else []
                    )
                sums.append(rows[0])
            for u, row in enumerate(sums):
                total[pl.ds(at + u, 1), :] = row
            return inner

        lax.fori_loop(0, lax.div(live_ref[i] + 15, 16), group, 0)
        mean = total[...] / fanout
        if folds(fslice, pcap):
            part = pcap // 4
            lane = lax.broadcasted_iota(jnp.int32, (part, LANES), 1)
            tail = mean[3 * part :]
            for b in range(3):
                shift = (fslice - 32 * b) % LANES
                moved = pltpu.roll(tail, shift, 1) if shift else tail
                out_ref[i, pl.ds(b * part, part), :] = jnp.where(
                    lane < fslice, mean[b * part : (b + 1) * part], moved
                ).astype(jnp.bfloat16)
        else:
            out_ref[i] = mean[:, :fslice].astype(jnp.bfloat16)
        return carry

    lax.fori_loop(0, count, partition, 0)
    for i, ref in enumerate(chunk_refs):
        ref[...] = out_ref[i]


def unfold(block, fslice, pcap):
    if block.shape[0] == pcap:
        return block
    part = block.shape[0] // 3
    wide = block.astype(jnp.float32)
    lane = lax.broadcasted_iota(jnp.int32, (part, LANES), 1)
    tail = pltpu.roll(wide[:part], LANES - fslice, 1)
    for b in (1, 2):
        shift = (32 * b - fslice) % LANES
        moved = wide[b * part : (b + 1) * part]
        moved = pltpu.roll(moved, shift, 1) if shift else moved
        tail = jnp.where(lane // 32 == b, moved, tail)
    return jnp.concatenate([wide, tail], axis=0)[:, :fslice].astype(jnp.bfloat16)


def halves_kernel(half, *refs):
    for s in range(half):
        refs[half][s] = refs[s][: refs[half].shape[1], :]


def prepare_kernel(half, n_idx, *refs):
    parcel_refs, mean_refs = refs[:half], refs[half : 2 * half]
    other_ref, bias_ref, w_ref, pre_ref, cross_ref = refs[2 * half :]
    fslice = w_ref.shape[1]
    pcap, width = pre_ref.shape
    first_core = lax.axis_index("rep") == 0
    both = jnp.zeros((2 * pcap, width), jnp.float32)
    far = jnp.zeros((pcap, width), jnp.float32)
    for s in range(half):
        mine, other = parcel_refs[s][:fslice, :], other_ref[s]
        w_nbr = jnp.where(first_core, other, mine)
        w_ref[s] = w_nbr
        feats = parcel_refs[s][fslice:, : 2 * pcap].astype(jnp.float32).T.astype(jnp.bfloat16)
        both = both + jnp.dot(
            feats, jnp.where(first_core, mine, other), preferred_element_type=jnp.float32
        )
        far = far + jnp.dot(
            unfold(mean_refs[s][...], fslice, pcap), w_nbr, preferred_element_type=jnp.float32
        )
        rows = pl.ds(pcap + s // 4 * n_idx, n_idx)
        cross_ref[rows, s % 4 * LANES : (s % 4 + 1) * LANES] = parcel_refs[s][
            fslice : fslice + n_idx, 2 * pcap :
        ]
    pre_ref[...] = both[:pcap] + bias_ref[...]
    cross_ref[:pcap, :] = (both[pcap:] + far).astype(jnp.bfloat16)


def store_times(pcap, blocks, out_ref):
    n_idx, pair = blocks[0].shape
    seed_count = pair // 2
    core_rows = lax.axis_index("feat") * (2 * pcap)
    rep_pos = lax.axis_index("rep")
    row = lax.broadcasted_iota(jnp.int32, (2 * pcap, pair), 0)
    slot = jnp.where(
        row < pcap, row + core_rows + rep_pos * pcap, row + core_rows - rep_pos * pcap
    ).astype(jnp.float32)
    low = lax.broadcasted_iota(jnp.int32, (n_idx, pair), 1) < seed_count
    for s in range(0, len(blocks), 2):
        first, second = blocks[s].astype(jnp.float32), blocks[s + 1].astype(jnp.float32)
        high_part = jnp.where(low, first, pltpu.roll(second, seed_count, 1))
        low_part = jnp.where(low, pltpu.roll(first, seed_count, 1), second)
        name = high_part * 128.0 + low_part
        own = jnp.where(slot == name[:1], 1.0, 0.0)
        near = jnp.zeros((2 * pcap, pair), jnp.float32)
        for k in range(1, n_idx):
            near = near + jnp.where(slot == name[k : k + 1], 1.0, 0.0)
        place = pl.ds(s * seed_count, pair)
        out_ref[place, : 2 * pcap] = own.T.astype(jnp.bfloat16)
        out_ref[place, 2 * pcap :] = near.T.astype(jnp.bfloat16)


def near_times_kernel(half, fslice, pcap, n_idx, *refs):
    blocks = [ref[fslice : fslice + n_idx, 2 * pcap :] for ref in refs[:half]]
    store_times(pcap, blocks, refs[half])


def far_times_kernel(
    half, n_idx, fanout_two, cross_ref, hidden_ref, ws_ref, wn_ref, out_ref, value_ref
):
    pcap = hidden_ref.shape[0]
    blocks = [
        cross_ref[
            pl.ds(pcap + s // 4 * n_idx, n_idx), s % 4 * LANES : (s % 4 + 1) * LANES
        ]
        for s in range(half)
    ]
    store_times(pcap, blocks, out_ref)
    store_values(hidden_ref[...], ws_ref, wn_ref, fanout_two, value_ref)


def store_values(hidden, ws_ref, wn_ref, fanout_two, value_ref):
    value_ref[0] = jnp.dot(hidden, ws_ref[...], preferred_element_type=jnp.float32).astype(
        jnp.bfloat16
    )
    value_ref[1] = (
        jnp.dot(hidden, wn_ref[...], preferred_element_type=jnp.float32) / fanout_two
    ).astype(jnp.bfloat16)


def layer_kernel(half, n_idx, parcel_ref, *refs):
    mean_refs = refs[:half]
    pre_ref, w_ref, cross_ref, hidden_ref, result_ref = refs[half:]
    pcap, width = hidden_ref.shape
    fslice = w_ref.shape[1]
    pre = pre_ref[...] + cross_ref[:pcap, :].astype(jnp.float32)
    for s in range(half):
        pre = pre + jnp.dot(
            unfold(mean_refs[s][...], fslice, pcap), w_ref[s], preferred_element_type=jnp.float32
        )
    count = live_rows(parcel_ref, fslice + n_idx, 2 * pcap)
    live = lax.broadcasted_iota(jnp.int32, (pcap, width), 0) < count
    hidden = jnp.where(live, jnp.maximum(pre, 0.0), 0.0).astype(jnp.bfloat16)
    hidden_ref[...] = hidden
    result_ref[...] = hidden


def share_kernel(
    half, fanout_two, near_ref, far_ref, value_ref, hidden_ref, ws_ref, wn_ref, *refs
):
    near_refs, far_refs, other_ref = refs[:half], refs[half : 2 * half], refs[2 * half]
    store_values(hidden_ref[...], ws_ref, wn_ref, fanout_two, other_ref)
    values = jnp.concatenate(
        [value_ref[0], other_ref[0], value_ref[1], other_ref[1]], axis=0
    )
    for times_ref, out_refs in ((far_ref, far_refs), (near_ref, near_refs)):
        part = jnp.dot(times_ref[...], values, preferred_element_type=jnp.float32)
        rows = out_refs[0].shape[0]
        for s, out_ref in enumerate(out_refs):
            out_ref[...] = part[s * rows : (s + 1) * rows].astype(jnp.bfloat16)


def side_sum_kernel(*refs):
    total = refs[0][...].astype(jnp.float32)
    for ref in refs[1:-1]:
        total = total + ref[...].astype(jnp.float32)
    refs[-1][...] = total.astype(jnp.bfloat16)


def last_kernel(bias_ref, *refs):
    total = bias_ref[...] + refs[0][...].astype(jnp.float32)
    for ref in refs[1:-1]:
        total = total + ref[...].astype(jnp.float32)
    refs[-1][...] = jnp.maximum(total, 0.0).astype(jnp.bfloat16)


def swap(value, axis, step):
    size = lax.axis_size(axis)
    return lax.ppermute(value, axis, [(i, i ^ step) for i in range(size)])


def body(
    src_feats,
    nbr_one,
    counts,
    seed_rows,
    nbr_two,
    w1_self,
    w1_nbr,
    bias_one,
    w2_self,
    w2_nbr,
    bias_two,
):
    n_feat = lax.axis_size("feat")
    half = n_feat // 2
    steps = range(half - 1, -1, -1)
    fslice, nodes = src_feats.shape
    fanout_one, pcap = nbr_one.shape[2:]
    width = w1_self.shape[1]
    seed_count, fanout_two = nbr_two.shape
    n_idx = fanout_two + 1
    bf16 = jnp.bfloat16
    vmem = pl.BlockSpec(memory_space=pltpu.VMEM)
    smem = pl.BlockSpec(memory_space=pltpu.SMEM)
    hbm = pl.BlockSpec(memory_space=pltpu.HBM)
    anywhere = pl.BlockSpec(memory_space=pl.ANY)
    table_bytes = nodes * LANES * 4

    def call(kernel, name, shapes, ins, args, after=(), scratch=(), limit=16 * MIB, cost_us=1):
        def wrapped(*refs):
            kernel(*refs[: len(args)], *refs[len(args) + len(after) :])

        return pl.pallas_call(
            wrapped,
            out_shape=tuple(jax.ShapeDtypeStruct(shape, dtype) for shape, dtype in shapes),
            in_specs=[*ins, *([anywhere] * len(after))],
            out_specs=(vmem,) * len(shapes),
            scratch_shapes=scratch,
            compiler_params=pltpu.CompilerParams(vmem_limit_bytes=limit),
            cost_estimate=pl.CostEstimate(
                flops=int(cost_us * 1_100_000_000), bytes_accessed=0, transcendentals=0
            ),
            name=name,
        )(*args, *after)

    def pinned(value):
        return pltpu.with_memory_space_constraint(value, pltpu.HBM)

    def send(chunks):
        return [swap(chunk, "feat", s) if s else chunk for s, chunk in zip(steps, chunks)]

    picks = jnp.transpose(nbr_one, (0, 2, 1, 3))
    *parcels, picks = call(
        functools.partial(pack_kernel, n_feat, pcap),
        "pack",
        [((2 * fslice, width), bf16)] * half + [(picks.shape, jnp.int32)],
        [hbm] * 6 + [smem],
        [
            *(pinned(x) for x in (src_feats, seed_rows[None], nbr_two.T, w1_self, w1_nbr, picks)),
            counts,
        ],
        scratch=[
            pltpu.VMEM((fslice, n_feat * 2 * pcap), bf16),
            pltpu.VMEM((1, seed_count), jnp.int32),
            pltpu.VMEM((fanout_two, seed_count), jnp.int32),
            pltpu.VMEM((fslice, width), bf16),
            pltpu.VMEM((fslice, width), bf16),
            pltpu.SemaphoreType.DMA((6,)),
        ],
    )
    stride = -(-fanout_one * pcap // 1024) * 1024
    neighbors = jnp.pad(
        picks.reshape(n_feat, fanout_one * pcap), ((0, 0), (0, stride - fanout_one * pcap))
    ).reshape(-1)
    arrived = send(parcels)
    (table,) = call(
        turn_kernel,
        "turn",
        [((nodes, LANES), jnp.float32)],
        [hbm],
        (pinned(src_feats),),
        after=(parcels[-1], neighbors),
        scratch=[pltpu.VMEM((fslice, nodes), bf16), pltpu.SemaphoreType.DMA((6,))],
        limit=table_bytes + 12 * MIB,
        cost_us=3,
    )
    table = table.reshape(nodes, 1, LANES)
    chunk_shape = (pcap // 4 * 3, LANES) if folds(fslice, pcap) else (pcap, fslice)

    def means(chosen, parcels=(), after=()):
        count = len(chosen)
        return call(
            functools.partial(mean_kernel, tuple(chosen), fanout_one, pcap, fslice, n_idx),
            "mean",
            [(chunk_shape, bf16)] * count,
            [anywhere] + [vmem] * (1 + len(parcels)),
            (neighbors, table, *parcels),
            after=after,
            scratch=[
                pltpu.VMEM((count, *chunk_shape), bf16),
                pltpu.VMEM((pcap, LANES), jnp.float32),
                pltpu.SMEM((count * stride,), jnp.int32),
                pltpu.SMEM((count,), jnp.int32),
                pltpu.SemaphoreType.DMA((count,)),
            ],
            limit=table_bytes + 8 * MIB,
            cost_us=2 * count if count > 1 else 0.5,
        )

    far_means = means([s + half for s in steps if s])
    (halves,) = call(
        functools.partial(halves_kernel, half),
        "halves",
        [((half, fslice, width), bf16)],
        [vmem] * half,
        arrived,
        after=far_means[:1],
    )
    far_arrived = send(far_means)
    other_halves = swap(halves, "rep", 1)
    (far_own,) = means([half], after=(halves,))
    w_nbr, pre, cross = call(
        functools.partial(prepare_kernel, half, n_idx),
        "prepare",
        [
            ((half, fslice, width), bf16),
            ((pcap, width), jnp.float32),
            ((pcap + -(-half // 4) * n_idx, width), bf16),
        ],
        [vmem] * (2 * half + 2),
        (*arrived, *far_arrived, far_own, other_halves, bias_one[None]),
    )
    cross_arrived = swap(cross, "feat", half)
    (near_times,) = call(
        functools.partial(near_times_kernel, half, fslice, pcap, n_idx),
        "near_times",
        [((half * seed_count, 4 * pcap), bf16)],
        [vmem] * half,
        arrived,
        after=far_means[:1],
    )
    near_means = means([s for s in steps if s], arrived[:-1], (cross, near_times))
    near_arrived = send(near_means)
    (near_own,) = means([0], arrived[-1:], near_means[:1])
    hidden, result = call(
        functools.partial(layer_kernel, half, n_idx),
        "hidden",
        [((pcap, width), bf16)] * 2,
        [vmem] * (half + 4),
        (parcels[-1], *near_arrived, near_own, pre, w_nbr, cross_arrived),
    )
    other_hidden = swap(hidden, "rep", 1)
    far_times, value = call(
        functools.partial(far_times_kernel, half, n_idx, fanout_two),
        "far_times",
        [((half * seed_count, 4 * pcap), bf16), ((2, pcap, width), bf16)],
        [vmem] * 4,
        (cross_arrived, hidden, w2_self, w2_nbr),
    )
    shares = call(
        functools.partial(share_kernel, half, fanout_two),
        "share",
        [((seed_count, width), bf16)] * (2 * half),
        [vmem] * 6,
        (near_times, far_times, value, other_hidden, w2_self, w2_nbr),
        scratch=[pltpu.VMEM((2, pcap, width), bf16)],
        limit=32 * MIB,
    )
    far_shares = send(shares[half:])
    near_shares = send(shares[:half])
    (far_sum,) = call(
        side_sum_kernel, "side_sum", [((seed_count, width), bf16)], [vmem] * half, far_shares
    )
    (seed_out,) = call(
        last_kernel,
        "seeds",
        [((seed_count, width), bf16)],
        [vmem] * (half + 2),
        (bias_two[None], *near_shares, swap(far_sum, "feat", half)),
    )
    return (result[None, None], seed_out)


def solution(mesh):
    placed = (
        P("feat", "groups"),
        P("groups", "rep", None, None),
        P(("groups", "feat"), "rep"),
        P(("groups", "feat", "rep")),
        P(("groups", "feat", "rep"), None),
        P("feat", None),
        P("feat", None),
        P(),
        P(),
        P(),
        P(),
    )
    return jax.shard_map(
        body,
        mesh=mesh,
        in_specs=placed,
        out_specs=(P(("groups", "feat"), "rep", None, None), P(("groups", "feat", "rep"), None)),
        check_vma=False,
    )
```

```python
import functools

import jax
import jax.numpy as jnp
from jax import lax
from jax.experimental import pallas as pl
from jax.experimental.pallas import tpu as pltpu
from jax.sharding import PartitionSpec as P

LANES = 128
MIB = 1024 * 1024


def folds(fslice, pcap):
    return 4 * fslice == 3 * LANES and pcap % 64 == 0


def pack_kernel(
    n_feat,
    pcap,
    src_hbm,
    seed_hbm,
    nbr_hbm,
    w_self_hbm,
    w_nbr_hbm,
    pick_hbm,
    live_ref,
    *refs,
):
    half = n_feat // 2
    parcel_refs, pick_ref = refs[:half], refs[half]
    src_ref, seed_ref, nbr_ref, w_self_ref, w_nbr_ref, fetched_ref, sems = refs[half + 1 :]
    fslice = w_self_ref.shape[0]
    copies = [
        pltpu.make_async_copy(a, b, sems.at[i])
        for i, (a, b) in enumerate(
            (
                (src_hbm.at[:, pl.ds(0, src_ref.shape[1])], src_ref),
                (seed_hbm, seed_ref),
                (nbr_hbm, nbr_ref),
                (w_self_hbm, w_self_ref),
                (w_nbr_hbm, w_nbr_ref),
                (pick_hbm, fetched_ref),
            )
        )
    ]
    for copy in copies:
        copy.start()
    for copy in copies:
        copy.wait()
    words = pick_ref.shape[1]
    if fetched_ref.shape[1] == words:
        pick_ref[...] = fetched_ref[...]
    else:
        pick_ref[...] = fetched_ref[:, :words] | (fetched_ref[:, words:] << 16)
    feat_pos = lax.axis_index("feat")
    first_core = lax.axis_index("rep") == 0
    idx = jnp.concatenate([seed_ref[...], nbr_ref[...]], axis=0)
    high = lax.shift_right_logical(idx, 7)
    digits = jnp.concatenate([high, idx - high * 128], axis=1).astype(jnp.float32)
    digits = digits.astype(jnp.bfloat16)
    weight = jnp.where(first_core, w_self_ref[...], w_nbr_ref[...])
    live = jnp.full((8, LANES), live_ref[0, 0].astype(jnp.float32)).astype(jnp.bfloat16)
    tags = jnp.concatenate([digits, live], axis=0)
    for s, parcel_ref in enumerate(reversed(parcel_refs)):
        parcel_ref[:fslice, :] = weight
        for place, step in enumerate((s, s ^ half)):
            at = pl.multiple_of(jnp.bitwise_xor(feat_pos, step) * (2 * pcap), LANES)
            block = src_ref[:, pl.ds(at, 2 * pcap)].astype(jnp.float32)
            own = jnp.where(first_core, block[:, :pcap], block[:, pcap:])
            if place == 0:
                near_side = own
        both = jnp.concatenate([near_side, own], axis=1)
        parcel_ref[fslice:, : 2 * pcap] = both.astype(jnp.bfloat16)
        parcel_ref[fslice : fslice + tags.shape[0], 2 * pcap :] = tags


def turn_kernel(src_hbm, table_ref, src_ref, sems):
    fslice, nodes = src_hbm.shape
    pieces = sems.shape[0]
    piece = nodes // pieces
    width = piece if piece <= 2048 else 512
    copies = [
        pltpu.make_async_copy(
            src_hbm.at[:, pl.ds(i * piece, piece)], src_ref.at[:, pl.ds(i * piece, piece)], sems.at[i]
        )
        for i in range(pieces)
    ]
    for copy in copies:
        copy.start()
    for i, copy in enumerate(copies):
        copy.wait()

        def turn(step, carry):
            at = pl.multiple_of(i * piece + step * width, width)
            table_ref[pl.ds(at, width), :fslice] = src_ref[:, pl.ds(at, width)].T.astype(
                jnp.float32
            )
            return carry

        lax.fori_loop(0, piece // width, turn, 0)


def live_rows(parcel_ref, row, lane):
    return jnp.max(parcel_ref[row : row + 8, lane:].astype(jnp.float32)).astype(jnp.int32)


def mean_kernel(chosen, packed, fanout, pcap, fslice, n_idx, nbr_hbm, table_ref, *refs):
    count = len(chosen)
    out_ref, total, nbr_ref, live_ref, sems = refs[-5:]
    chunk_refs, parcel_refs = refs[-5 - count : -5], refs[: -5 - count]
    feat_pos = lax.axis_index("feat")
    stride = nbr_ref.shape[0] // count
    copies = [
        pltpu.make_async_copy(
            nbr_hbm.at[pl.ds(pl.multiple_of((feat_pos ^ step) * stride, stride), stride)],
            nbr_ref.at[pl.ds(i * stride, stride)],
            sems.at[i],
        )
        for i, step in enumerate(chosen)
    ]
    for copy in copies:
        copy.start()
    for i in range(count):
        live_ref[i] = pcap
    for i, ref in enumerate(parcel_refs):
        live_ref[i] = live_rows(ref, fslice + n_idx, 2 * pcap)
    for copy in copies:
        copy.wait()

    def partition(i, carry):
        first = i * stride

        def group(g, inner):
            at = pl.multiple_of(g * 16, 16)
            start = first + at
            sums = []
            for u in range(16):
                names = [nbr_ref[start + (k * pcap + u)] for k in range(fanout // packed)]
                if packed == 2:
                    names = [
                        part
                        for name in names
                        for part in (name & 0xFFFF, lax.shift_right_logical(name, 16))
                    ]
                rows = [table_ref[name] for name in names]
                while len(rows) > 1:
                    rows = [a + b for a, b in zip(rows[::2], rows[1::2])] + (
                        [rows[-1]] if len(rows) % 2 else []
                    )
                sums.append(rows[0])
            for u, row in enumerate(sums):
                total[pl.ds(at + u, 1), :] = row
            return inner

        lax.fori_loop(0, lax.div(live_ref[i] + 15, 16), group, 0)
        mean = total[...] / fanout
        if folds(fslice, pcap):
            part = pcap // 4
            lane = lax.broadcasted_iota(jnp.int32, (part, LANES), 1)
            tail = mean[3 * part :]
            for b in range(3):
                shift = (fslice - 32 * b) % LANES
                moved = pltpu.roll(tail, shift, 1) if shift else tail
                out_ref[i, pl.ds(b * part, part), :] = jnp.where(
                    lane < fslice, mean[b * part : (b + 1) * part], moved
                ).astype(jnp.bfloat16)
        else:
            out_ref[i] = mean[:, :fslice].astype(jnp.bfloat16)
        return carry

    lax.fori_loop(0, count, partition, 0)
    for i, ref in enumerate(chunk_refs):
        ref[...] = out_ref[i]


def unfold(block, fslice, pcap):
    if block.shape[0] == pcap:
        return block
    part = block.shape[0] // 3
    wide = block.astype(jnp.float32)
    lane = lax.broadcasted_iota(jnp.int32, (part, LANES), 1)
    tail = pltpu.roll(wide[:part], LANES - fslice, 1)
    for b in (1, 2):
        shift = (32 * b - fslice) % LANES
        moved = wide[b * part : (b + 1) * part]
        moved = pltpu.roll(moved, shift, 1) if shift else moved
        tail = jnp.where(lane // 32 == b, moved, tail)
    return jnp.concatenate([wide, tail], axis=0)[:, :fslice].astype(jnp.bfloat16)


def halves_kernel(half, *refs):
    for s in range(half):
        refs[half][s] = refs[s][: refs[half].shape[1], :]


def own_kernel(half, n_idx, *refs):
    parcel_refs = refs[:half]
    other_ref, bias_ref, w_ref, pre_ref, far_ref, idx_ref = refs[half:]
    fslice = w_ref.shape[1]
    pcap, width = pre_ref.shape
    first_core = lax.axis_index("rep") == 0
    both = jnp.zeros((2 * pcap, width), jnp.float32)
    for s in range(half):
        mine, other = parcel_refs[s][:fslice, :], other_ref[s]
        w_ref[s] = jnp.where(first_core, other, mine)
        feats = parcel_refs[s][fslice:, : 2 * pcap].astype(jnp.float32).T.astype(jnp.bfloat16)
        both = both + jnp.dot(
            feats, jnp.where(first_core, mine, other), preferred_element_type=jnp.float32
        )
        rows = pl.ds(s // 4 * n_idx, n_idx)
        idx_ref[rows, s % 4 * LANES : (s % 4 + 1) * LANES] = parcel_refs[s][
            fslice : fslice + n_idx, 2 * pcap :
        ]
    pre_ref[...] = both[:pcap] + bias_ref[...]
    far_ref[...] = both[pcap:]


def add_means(half, pre, mean_refs, w_ref):
    for s in range(half):
        pre = pre + jnp.dot(
            unfold(mean_refs[s][...], w_ref.shape[1], pre.shape[0]),
            w_ref[s],
            preferred_element_type=jnp.float32,
        )
    return pre


def far_kernel(half, *refs):
    far_ref, w_ref, idx_ref, cross_ref = refs[half:]
    pcap = far_ref.shape[0]
    cross_ref[:pcap, :] = add_means(half, far_ref[...], refs[:half], w_ref).astype(jnp.bfloat16)
    cross_ref[pcap:, :] = idx_ref[...]


def store_times(pcap, blocks, out_ref):
    n_idx, pair = blocks[0].shape
    seed_count = pair // 2
    core_rows = lax.axis_index("feat") * (2 * pcap)
    rep_pos = lax.axis_index("rep")
    row = lax.broadcasted_iota(jnp.int32, (2 * pcap, pair), 0)
    slot = jnp.where(
        row < pcap, row + core_rows + rep_pos * pcap, row + core_rows - rep_pos * pcap
    ).astype(jnp.float32)
    low = lax.broadcasted_iota(jnp.int32, (n_idx, pair), 1) < seed_count
    for s in range(0, len(blocks), 2):
        first, second = blocks[s].astype(jnp.float32), blocks[s + 1].astype(jnp.float32)
        high_part = jnp.where(low, first, pltpu.roll(second, seed_count, 1))
        low_part = jnp.where(low, pltpu.roll(first, seed_count, 1), second)
        name = high_part * 128.0 + low_part
        own = jnp.where(slot == name[:1], 1.0, 0.0)
        near = jnp.zeros((2 * pcap, pair), jnp.float32)
        for k in range(1, n_idx):
            near = near + jnp.where(slot == name[k : k + 1], 1.0, 0.0)
        place = pl.ds(s * seed_count, pair)
        out_ref[place, : 2 * pcap] = own.T.astype(jnp.bfloat16)
        out_ref[place, 2 * pcap :] = near.T.astype(jnp.bfloat16)


def near_times_kernel(half, fslice, pcap, n_idx, *refs):
    blocks = [ref[fslice : fslice + n_idx, 2 * pcap :] for ref in refs[:half]]
    store_times(pcap, blocks, refs[half])


def far_times_kernel(
    half, n_idx, fanout_two, cross_ref, hidden_ref, ws_ref, wn_ref, out_ref, value_ref
):
    pcap = hidden_ref.shape[0]
    blocks = [
        cross_ref[
            pl.ds(pcap + s // 4 * n_idx, n_idx), s % 4 * LANES : (s % 4 + 1) * LANES
        ]
        for s in range(half)
    ]
    store_times(pcap, blocks, out_ref)
    store_values(hidden_ref[...], ws_ref, wn_ref, fanout_two, value_ref)


def store_values(hidden, ws_ref, wn_ref, fanout_two, value_ref):
    value_ref[0] = jnp.dot(hidden, ws_ref[...], preferred_element_type=jnp.float32).astype(
        jnp.bfloat16
    )
    value_ref[1] = (
        jnp.dot(hidden, wn_ref[...], preferred_element_type=jnp.float32) / fanout_two
    ).astype(jnp.bfloat16)


def near_kernel(half, *refs):
    pre_ref, w_ref, out_ref = refs[half:]
    out_ref[...] = add_means(half, pre_ref[...], refs[:half], w_ref)


def hidden_kernel(fslice, n_idx, parcel_ref, pre_ref, cross_ref, hidden_ref, result_ref):
    pcap, width = hidden_ref.shape
    pre = pre_ref[...] + cross_ref[:pcap, :].astype(jnp.float32)
    count = live_rows(parcel_ref, fslice + n_idx, 2 * pcap)
    live = lax.broadcasted_iota(jnp.int32, (pcap, width), 0) < count
    hidden = jnp.where(live, jnp.maximum(pre, 0.0), 0.0).astype(jnp.bfloat16)
    hidden_ref[...] = hidden
    result_ref[...] = hidden


def share_kernel(
    half, fanout_two, near_ref, far_ref, value_ref, hidden_ref, ws_ref, wn_ref, *refs
):
    *out_refs, other_ref = refs
    store_values(hidden_ref[...], ws_ref, wn_ref, fanout_two, other_ref)
    values = jnp.concatenate(
        [value_ref[0], other_ref[0], value_ref[1], other_ref[1]], axis=0
    )
    rows = far_ref.shape[0] // half
    both_ref, far_refs, near_refs = out_refs[0], out_refs[1:half], out_refs[half:]
    for times_ref, refs, low in ((far_ref, far_refs, 0), (near_ref, near_refs, rows)):
        part = jnp.dot(times_ref[...], values, preferred_element_type=jnp.float32)
        part = part.astype(jnp.bfloat16)
        both_ref[low : low + rows, :] = part[(half - 2) * rows : (half - 1) * rows]
        for i, ref in enumerate(refs):
            place = i if i < half - 2 else half - 1
            ref[...] = part[place * rows : (place + 1) * rows]


def sum_rows(first, low, refs, rows):
    total = first
    for i, ref in enumerate(refs):
        at = low if i == 0 else 0
        total = total + ref[at : at + rows, :].astype(jnp.float32)
    return total


def side_sum_kernel(*refs):
    rows = refs[-1].shape[0]
    refs[-1][...] = sum_rows(0.0, 0, refs[:-1], rows).astype(jnp.bfloat16)


def last_kernel(bias_ref, *refs):
    rows = refs[-1].shape[0]
    total = sum_rows(bias_ref[...], rows, refs[:-1], rows)
    refs[-1][...] = jnp.maximum(total, 0.0).astype(jnp.bfloat16)


def swap(value, axis, step):
    size = lax.axis_size(axis)
    return lax.ppermute(value, axis, [(i, i ^ step) for i in range(size)])


def body(
    src_feats,
    nbr_one,
    counts,
    seed_rows,
    nbr_two,
    w1_self,
    w1_nbr,
    bias_one,
    w2_self,
    w2_nbr,
    bias_two,
):
    n_feat = lax.axis_size("feat")
    half = n_feat // 2
    steps = range(half - 1, -1, -1)
    fslice, nodes = src_feats.shape
    fanout_one, pcap = nbr_one.shape[2:]
    width = w1_self.shape[1]
    seed_count, fanout_two = nbr_two.shape
    n_idx = fanout_two + 1
    bf16 = jnp.bfloat16
    vmem = pl.BlockSpec(memory_space=pltpu.VMEM)
    smem = pl.BlockSpec(memory_space=pltpu.SMEM)
    hbm = pl.BlockSpec(memory_space=pltpu.HBM)
    anywhere = pl.BlockSpec(memory_space=pl.ANY)
    table_bytes = nodes * LANES * 4

    def call(kernel, name, shapes, ins, args, after=(), scratch=(), limit=16 * MIB, cost_us=1):
        def wrapped(*refs):
            kernel(*refs[: len(args)], *refs[len(args) + len(after) :])

        return pl.pallas_call(
            wrapped,
            out_shape=tuple(jax.ShapeDtypeStruct(shape, dtype) for shape, dtype in shapes),
            in_specs=[*ins, *([anywhere] * len(after))],
            out_specs=(vmem,) * len(shapes),
            scratch_shapes=scratch,
            compiler_params=pltpu.CompilerParams(vmem_limit_bytes=limit),
            cost_estimate=pl.CostEstimate(
                flops=int(cost_us * 1_100_000_000), bytes_accessed=0, transcendentals=0
            ),
            name=name,
        )(*args, *after)

    def pinned(value):
        return pltpu.with_memory_space_constraint(value, pltpu.HBM)

    def send(chunks, steps=steps):
        return [swap(chunk, "feat", s) if s else chunk for s, chunk in zip(steps, chunks)]

    picks = jnp.transpose(nbr_one, (0, 2, 1, 3))
    packed = 2 if fanout_one % 2 == 0 and nodes <= 1 << 16 else 1
    words = (n_feat, fanout_one // packed, 1, pcap)
    *parcels, picks = call(
        functools.partial(pack_kernel, n_feat, pcap),
        "pack",
        [((2 * fslice, width), bf16)] * half + [(words, jnp.int32)],
        [hbm] * 6 + [smem],
        [
            *(pinned(x) for x in (src_feats, seed_rows[None], nbr_two.T, w1_self, w1_nbr, picks)),
            counts,
        ],
        scratch=[
            pltpu.VMEM((fslice, n_feat * 2 * pcap), bf16),
            pltpu.VMEM((1, seed_count), jnp.int32),
            pltpu.VMEM((fanout_two, seed_count), jnp.int32),
            pltpu.VMEM((fslice, width), bf16),
            pltpu.VMEM((fslice, width), bf16),
            pltpu.VMEM((n_feat, fanout_one, 1, pcap), jnp.int32),
            pltpu.SemaphoreType.DMA((6,)),
        ],
    )
    picks = picks.reshape(n_feat, -1)
    stride = -(-picks.shape[1] // 1024) * 1024
    neighbors = jnp.pad(picks, ((0, 0), (0, stride - picks.shape[1]))).reshape(-1)
    arrived = send(parcels)
    (table,) = call(
        turn_kernel,
        "turn",
        [((nodes, LANES), jnp.float32)],
        [hbm],
        (pinned(src_feats),),
        after=(parcels[-1], neighbors),
        scratch=[pltpu.VMEM((fslice, nodes), bf16), pltpu.SemaphoreType.DMA((6,))],
        limit=table_bytes + 12 * MIB,
        cost_us=3,
    )
    table = table.reshape(nodes, 1, LANES)
    chunk_shape = (pcap // 4 * 3, LANES) if folds(fslice, pcap) else (pcap, fslice)

    def means(chosen, parcels=(), after=()):
        count = len(chosen)
        return call(
            functools.partial(mean_kernel, tuple(chosen), packed, fanout_one, pcap, fslice, n_idx),
            "mean",
            [(chunk_shape, bf16)] * count,
            [anywhere] + [vmem] * (1 + len(parcels)),
            (neighbors, table, *parcels),
            after=after,
            scratch=[
                pltpu.VMEM((count, *chunk_shape), bf16),
                pltpu.VMEM((pcap, LANES), jnp.float32),
                pltpu.SMEM((count * stride,), jnp.int32),
                pltpu.SMEM((count,), jnp.int32),
                pltpu.SemaphoreType.DMA((count,)),
            ],
            limit=table_bytes + 8 * MIB,
            cost_us=2 * count if count > 1 else 0,
        )

    far_means = means([s + half for s in steps if s])
    (halves,) = call(
        functools.partial(halves_kernel, half),
        "halves",
        [((half, fslice, width), bf16)],
        [vmem] * half,
        arrived,
        after=far_means[:1],
    )
    far_arrived = send(far_means)
    other_halves = swap(halves, "rep", 1)
    (far_own,) = means([half], after=(halves,))
    idx_rows = -(-half // 4) * n_idx
    w_nbr, pre, far_pre, idx_tags = call(
        functools.partial(own_kernel, half, n_idx),
        "own",
        [
            ((half, fslice, width), bf16),
            ((pcap, width), jnp.float32),
            ((pcap, width), jnp.float32),
            ((idx_rows, width), bf16),
        ],
        [vmem] * (half + 2),
        (*arrived, other_halves, bias_one[None]),
        after=(far_own,),
    )
    (cross,) = call(
        functools.partial(far_kernel, half),
        "far",
        [((pcap + idx_rows, width), bf16)],
        [vmem] * (half + 3),
        (*far_arrived, far_own, far_pre, w_nbr, idx_tags),
    )
    cross_arrived = swap(cross, "feat", half)
    near_means = means([s for s in steps if s], arrived[:-1], (cross,))
    near_arrived = send(near_means)
    (near_own,) = means([0], arrived[-1:], near_means[-1:])
    (near_times,) = call(
        functools.partial(near_times_kernel, half, fslice, pcap, n_idx),
        "near_times",
        [((half * seed_count, 4 * pcap), bf16)],
        [vmem] * half,
        arrived,
        after=(near_own,),
        cost_us=0,
    )
    (near_pre,) = call(
        functools.partial(near_kernel, half),
        "near",
        [((pcap, width), jnp.float32)],
        [vmem] * (half + 2),
        (*near_arrived, near_own, pre, w_nbr),
        after=(near_times,),
        cost_us=0,
    )
    hidden, result = call(
        functools.partial(hidden_kernel, fslice, n_idx),
        "hidden",
        [((pcap, width), bf16)] * 2,
        [vmem] * 3,
        (parcels[-1], near_pre, cross_arrived),
    )
    other_hidden = swap(hidden, "rep", 1)
    far_times, value = call(
        functools.partial(far_times_kernel, half, n_idx, fanout_two),
        "far_times",
        [((half * seed_count, 4 * pcap), bf16), ((2, pcap, width), bf16)],
        [vmem] * 4,
        (cross_arrived, hidden, w2_self, w2_nbr),
    )
    shares = call(
        functools.partial(share_kernel, half, fanout_two),
        "share",
        [((2 * seed_count, width), bf16)] + [((seed_count, width), bf16)] * (2 * half - 2),
        [vmem] * 6,
        (near_times, far_times, value, other_hidden, w2_self, w2_nbr),
        scratch=[pltpu.VMEM((2, pcap, width), bf16)],
        limit=32 * MIB,
    )
    both = swap(shares[0], "feat", 1)
    others = [*steps[: half - 2], 0]
    far_shares = send(shares[1:half], others)
    near_shares = send(shares[half:], others)
    (far_sum,) = call(
        side_sum_kernel,
        "side_sum",
        [((seed_count, width), bf16)],
        [vmem] * half,
        (both, *far_shares),
    )
    (seed_out,) = call(
        last_kernel,
        "seeds",
        [((seed_count, width), bf16)],
        [vmem] * (half + 2),
        (bias_two[None], both, *near_shares, swap(far_sum, "feat", half)),
    )
    return (result[None, None], seed_out)


def solution(mesh):
    placed = (
        P("feat", "groups"),
        P("groups", "rep", None, None),
        P(("groups", "feat"), "rep"),
        P(("groups", "feat", "rep")),
        P(("groups", "feat", "rep"), None),
        P("feat", None),
        P("feat", None),
        P(),
        P(),
        P(),
        P(),
    )
    return jax.shard_map(
        body,
        mesh=mesh,
        in_specs=placed,
        out_specs=(P(("groups", "feat"), "rep", None, None), P(("groups", "feat", "rep"), None)),
        check_vma=False,
    )
```

```python
import functools

import jax
import jax.numpy as jnp
from jax import lax
from jax.experimental import pallas as pl
from jax.experimental.pallas import tpu as pltpu
from jax.sharding import PartitionSpec as P

LANES = 128
MIB = 1024 * 1024


def folds(fslice, pcap):
    return 4 * fslice == 3 * LANES and pcap % 64 == 0


def is_dense(fslice, n_idx):
    return fslice % 32 == 0 and n_idx == 16


def parcel_rows(fslice, n_idx):
    return 2 * fslice - fslice // 4 + 8 if is_dense(fslice, n_idx) else 2 * fslice


def write_parcel(ref, weight, feats, digits, live):
    fslice, lanes = feats.shape
    ref[:fslice, :] = weight
    if is_dense(fslice, digits.shape[0]):
        cut = fslice // 4 * 3
        tail = jnp.concatenate([feats[cut:, i : i + LANES] for i in range(0, lanes, LANES)], axis=0)
        tags = jnp.concatenate([digits[:8], digits[8:], live, live], axis=1)
        body = jnp.concatenate([feats[:cut], tail], axis=1)
        ref[fslice:, :] = jnp.concatenate([body, tags], axis=0).astype(jnp.bfloat16)
    else:
        tags = jnp.concatenate([digits, live], axis=0).astype(jnp.bfloat16)
        ref[fslice:, :lanes] = feats.astype(jnp.bfloat16)
        ref[fslice : fslice + tags.shape[0], lanes:] = tags


def read_feats(ref, fslice, n_idx, lanes):
    if not is_dense(fslice, n_idx):
        return ref[fslice:, :lanes].astype(jnp.float32)
    cut, part = fslice // 4 * 3, fslice // 4
    tail = ref[fslice : fslice + cut, lanes:].astype(jnp.float32)
    tail = jnp.concatenate([tail[i : i + part] for i in range(0, cut, part)], axis=1)
    return jnp.concatenate([ref[fslice : fslice + cut, :lanes].astype(jnp.float32), tail], axis=0)


def read_digits(ref, fslice, n_idx, lanes):
    if not is_dense(fslice, n_idx):
        return ref[fslice : fslice + n_idx, lanes:].astype(jnp.float32)
    tags = ref[-8:, : 2 * LANES].astype(jnp.float32)
    return jnp.concatenate([tags[:, :LANES], tags[:, LANES:]], axis=0)


def live_rows(ref, fslice, n_idx, lanes):
    if is_dense(fslice, n_idx):
        tag = ref[-8:, 2 * LANES : 3 * LANES]
    else:
        tag = ref[fslice + n_idx : fslice + n_idx + 8, lanes:]
    return jnp.max(tag.astype(jnp.float32)).astype(jnp.int32)


def pack_kernel(
    n_feat,
    pcap,
    src_hbm,
    seed_hbm,
    nbr_hbm,
    w_self_hbm,
    w_nbr_hbm,
    pick_hbm,
    live_ref,
    *refs,
):
    half = n_feat // 2
    parcel_refs, pick_ref, src_ref = refs[:half], refs[half], refs[half + 1]
    seed_ref, nbr_ref, w_self_ref, w_nbr_ref, fetched_ref, sems = refs[half + 2 :]
    owned = n_feat * 2 * pcap
    first, rest = pl.ds(0, owned), pl.ds(owned, src_ref.shape[1] - owned)
    copies = [
        pltpu.make_async_copy(a, b, sems.at[i])
        for i, (a, b) in enumerate(
            (
                (src_hbm.at[:, first], src_ref.at[:, first]),
                (w_self_hbm, w_self_ref),
                (w_nbr_hbm, w_nbr_ref),
                (seed_hbm, seed_ref),
                (nbr_hbm, nbr_ref),
                (pick_hbm, fetched_ref),
                (src_hbm.at[:, rest], src_ref.at[:, rest]),
            )
        )
    ]
    for copy in copies:
        copy.start()
    for copy in copies[:-1]:
        copy.wait()
    words = pick_ref.shape[1]
    if fetched_ref.shape[1] == words:
        pick_ref[:, :, :, :pcap] = fetched_ref[...]
    else:
        pick_ref[:, :, :, :pcap] = fetched_ref[:, :words] | (fetched_ref[:, words:] << 16)
    feat_pos = lax.axis_index("feat")
    first_core = lax.axis_index("rep") == 0
    idx = jnp.concatenate([seed_ref[...], nbr_ref[...]], axis=0)
    high = lax.shift_right_logical(idx, 7)
    digits = jnp.concatenate([high, idx - high * 128], axis=1).astype(jnp.float32)
    weight = jnp.where(first_core, w_self_ref[...], w_nbr_ref[...])
    live = jnp.full((8, LANES), live_ref[0, 0].astype(jnp.float32))
    for s, parcel_ref in enumerate(reversed(parcel_refs)):
        sides = []
        for step in (s, s ^ half):
            at = pl.multiple_of(jnp.bitwise_xor(feat_pos, step) * (2 * pcap), LANES)
            block = src_ref[:, pl.ds(at, 2 * pcap)].astype(jnp.float32)
            sides.append(jnp.where(first_core, block[:, :pcap], block[:, pcap:]))
        write_parcel(parcel_ref, weight, jnp.concatenate(sides, axis=1), digits, live)
    copies[-1].wait()


def turn_kernel(src_ref, table_ref):
    fslice, nodes = src_ref.shape
    width = 2048 if nodes % 2048 == 0 else 512

    def turn(step, carry):
        at = pl.multiple_of(step * width, width)
        table_ref[pl.ds(at, width), :fslice] = src_ref[:, pl.ds(at, width)].T.astype(jnp.float32)
        return carry

    lax.fori_loop(0, nodes // width, turn, 0)


def mean_kernel(chosen, packed, fanout, pcap, fslice, n_idx, nbr_any, table_ref, *refs):
    count = len(chosen)
    out_ref, total, nbr_ref, live_ref, sems = refs[-5:]
    chunk_refs, parcel_refs = refs[-5 - count : -5], refs[: -5 - count]
    feat_pos = lax.axis_index("feat")
    words = fanout // packed
    stride = -(-pcap // LANES) * LANES
    copies = [
        pltpu.make_async_copy(
            nbr_any.at[feat_pos ^ step, k, 0],
            nbr_ref.at[pl.ds((i * words + k) * stride, stride)],
            sems.at[i * words + k],
        )
        for i, step in enumerate(chosen)
        for k in range(words)
    ]
    for copy in copies:
        copy.start()
    for i in range(count):
        live_ref[i] = pcap
    for i, ref in enumerate(parcel_refs):
        live_ref[i] = live_rows(ref, fslice, n_idx, 2 * pcap)
    for copy in copies:
        copy.wait()

    def partition(i, carry):
        first = i * (words * stride)

        def group(g, inner):
            at = pl.multiple_of(g * 16, 16)
            start = first + at
            sums = []
            for u in range(16):
                names = [nbr_ref[start + (k * stride + u)] for k in range(words)]
                if packed == 2:
                    names = [
                        part
                        for name in names
                        for part in (name & 0xFFFF, lax.shift_right_logical(name, 16))
                    ]
                rows = [table_ref[name] for name in names]
                while len(rows) > 1:
                    rows = [a + b for a, b in zip(rows[::2], rows[1::2])] + (
                        [rows[-1]] if len(rows) % 2 else []
                    )
                sums.append(rows[0])
            for u, row in enumerate(sums):
                total[pl.ds(at + u, 1), :] = row
            return inner

        lax.fori_loop(0, lax.div(live_ref[i] + 15, 16), group, 0)
        mean = total[...] / fanout
        if folds(fslice, pcap):
            part = pcap // 4
            lane = lax.broadcasted_iota(jnp.int32, (part, LANES), 1)
            tail = mean[3 * part :]
            for b in range(3):
                shift = (fslice - 32 * b) % LANES
                moved = pltpu.roll(tail, shift, 1) if shift else tail
                out_ref[i, pl.ds(b * part, part), :] = jnp.where(
                    lane < fslice, mean[b * part : (b + 1) * part], moved
                ).astype(jnp.bfloat16)
        else:
            out_ref[i] = mean[:, :fslice].astype(jnp.bfloat16)
        return carry

    lax.fori_loop(0, count, partition, 0)
    for i, ref in enumerate(chunk_refs):
        ref[...] = out_ref[i]


def unfold(block, fslice, pcap):
    if block.shape[0] == pcap:
        return block
    part = block.shape[0] // 3
    wide = block.astype(jnp.float32)
    lane = lax.broadcasted_iota(jnp.int32, (part, LANES), 1)
    tail = pltpu.roll(wide[:part], LANES - fslice, 1)
    for b in (1, 2):
        shift = (32 * b - fslice) % LANES
        moved = wide[b * part : (b + 1) * part]
        moved = pltpu.roll(moved, shift, 1) if shift else moved
        tail = jnp.where(lane // 32 == b, moved, tail)
    return jnp.concatenate([wide, tail], axis=0)[:, :fslice].astype(jnp.bfloat16)


def halves_kernel(half, *refs):
    for s in range(half):
        refs[half][s] = refs[s][: refs[half].shape[1], :]


def own_kernel(half, n_idx, *refs):
    parcel_refs = refs[:half]
    other_ref, bias_ref, w_ref, pre_ref, far_ref, idx_ref = refs[half:]
    fslice = w_ref.shape[1]
    pcap, width = pre_ref.shape
    first_core = lax.axis_index("rep") == 0
    both = jnp.zeros((2 * pcap, width), jnp.float32)
    for s in range(half):
        mine, other = parcel_refs[s][:fslice, :], other_ref[s]
        w_ref[s] = jnp.where(first_core, other, mine)
        feats = read_feats(parcel_refs[s], fslice, n_idx, 2 * pcap).T.astype(jnp.bfloat16)
        both = both + jnp.dot(
            feats, jnp.where(first_core, mine, other), preferred_element_type=jnp.float32
        )
        rows = pl.ds(s // 4 * n_idx, n_idx)
        digits = read_digits(parcel_refs[s], fslice, n_idx, 2 * pcap)
        idx_ref[rows, s % 4 * LANES : (s % 4 + 1) * LANES] = digits.astype(jnp.bfloat16)
    pre_ref[...] = both[:pcap] + bias_ref[...]
    far_ref[...] = both[pcap:]


def add_means(half, pre, mean_refs, w_ref):
    for s in range(half):
        pre = pre + jnp.dot(
            unfold(mean_refs[s][...], w_ref.shape[1], pre.shape[0]),
            w_ref[s],
            preferred_element_type=jnp.float32,
        )
    return pre


def far_kernel(half, *refs):
    far_ref, w_ref, idx_ref, cross_ref = refs[half:]
    pcap = far_ref.shape[0]
    cross_ref[:pcap, :] = add_means(half, far_ref[...], refs[:half], w_ref).astype(jnp.bfloat16)
    cross_ref[pcap:, :] = idx_ref[...]


def store_times(pcap, blocks, out_ref):
    n_idx, pair = blocks[0].shape
    seed_count = pair // 2
    core_rows = lax.axis_index("feat") * (2 * pcap)
    rep_pos = lax.axis_index("rep")
    row = lax.broadcasted_iota(jnp.int32, (2 * pcap, pair), 0)
    slot = jnp.where(
        row < pcap, row + core_rows + rep_pos * pcap, row + core_rows - rep_pos * pcap
    ).astype(jnp.float32)
    low = lax.broadcasted_iota(jnp.int32, (n_idx, pair), 1) < seed_count
    for s in range(0, len(blocks), 2):
        first, second = blocks[s].astype(jnp.float32), blocks[s + 1].astype(jnp.float32)
        high_part = jnp.where(low, first, pltpu.roll(second, seed_count, 1))
        low_part = jnp.where(low, pltpu.roll(first, seed_count, 1), second)
        name = high_part * 128.0 + low_part
        own = jnp.where(slot == name[:1], 1.0, 0.0)
        near = jnp.zeros((2 * pcap, pair), jnp.float32)
        for k in range(1, n_idx):
            near = near + jnp.where(slot == name[k : k + 1], 1.0, 0.0)
        place = pl.ds(s * seed_count, pair)
        out_ref[place, : 2 * pcap] = own.T.astype(jnp.bfloat16)
        out_ref[place, 2 * pcap :] = near.T.astype(jnp.bfloat16)


def near_times_kernel(half, fslice, pcap, n_idx, *refs):
    blocks = [read_digits(ref, fslice, n_idx, 2 * pcap) for ref in refs[:half]]
    store_times(pcap, blocks, refs[half])


def far_times_kernel(
    half,
    n_idx,
    fanout_two,
    cross_ref,
    hidden_ref,
    ws_ref,
    wn_ref,
    out_ref,
    value_ref,
    result_ref,
    sem,
):
    copy = pltpu.make_async_copy(hidden_ref, result_ref, sem)
    copy.start()
    pcap = hidden_ref.shape[0]
    blocks = [
        cross_ref[
            pl.ds(pcap + s // 4 * n_idx, n_idx), s % 4 * LANES : (s % 4 + 1) * LANES
        ]
        for s in range(half)
    ]
    store_times(pcap, blocks, out_ref)
    store_values(hidden_ref[...], ws_ref, wn_ref, fanout_two, value_ref)
    copy.wait()


def store_values(hidden, ws_ref, wn_ref, fanout_two, value_ref):
    value_ref[0] = jnp.dot(hidden, ws_ref[...], preferred_element_type=jnp.float32).astype(
        jnp.bfloat16
    )
    value_ref[1] = (
        jnp.dot(hidden, wn_ref[...], preferred_element_type=jnp.float32) / fanout_two
    ).astype(jnp.bfloat16)


def near_kernel(half, *refs):
    pre_ref, w_ref, out_ref = refs[half:]
    out_ref[...] = add_means(half, pre_ref[...], refs[:half], w_ref)


def hidden_kernel(fslice, n_idx, parcel_ref, pre_ref, cross_ref, hidden_ref):
    pcap, width = hidden_ref.shape
    pre = pre_ref[...] + cross_ref[:pcap, :].astype(jnp.float32)
    count = live_rows(parcel_ref, fslice, n_idx, 2 * pcap)
    live = lax.broadcasted_iota(jnp.int32, (pcap, width), 0) < count
    hidden_ref[...] = jnp.where(live, jnp.maximum(pre, 0.0), 0.0).astype(jnp.bfloat16)


def share_kernel(
    half, fanout_two, near_ref, far_ref, value_ref, hidden_ref, ws_ref, wn_ref, *refs
):
    *out_refs, other_ref = refs
    store_values(hidden_ref[...], ws_ref, wn_ref, fanout_two, other_ref)
    values = jnp.concatenate(
        [value_ref[0], other_ref[0], value_ref[1], other_ref[1]], axis=0
    )
    rows = far_ref.shape[0] // half
    both_ref, far_refs, near_refs = out_refs[0], out_refs[1:half], out_refs[half:]
    for times_ref, refs, low in ((far_ref, far_refs, 0), (near_ref, near_refs, rows)):
        part = jnp.dot(times_ref[...], values, preferred_element_type=jnp.float32)
        part = part.astype(jnp.bfloat16)
        both_ref[low : low + rows, :] = part[(half - 2) * rows : (half - 1) * rows]
        for i, ref in enumerate(refs):
            place = i if i < half - 2 else half - 1
            ref[...] = part[place * rows : (place + 1) * rows]


def sum_rows(first, low, refs, rows):
    total = first
    for i, ref in enumerate(refs):
        at = low if i == 0 else 0
        total = total + ref[at : at + rows, :].astype(jnp.float32)
    return total


def side_sum_kernel(*refs):
    rows = refs[-1].shape[0]
    refs[-1][...] = sum_rows(0.0, 0, refs[:-1], rows).astype(jnp.bfloat16)


def last_kernel(bias_ref, *refs):
    rows = refs[-1].shape[0]
    total = sum_rows(bias_ref[...], rows, refs[:-1], rows)
    refs[-1][...] = jnp.maximum(total, 0.0).astype(jnp.bfloat16)


def swap(value, axis, step):
    size = lax.axis_size(axis)
    return lax.ppermute(value, axis, [(i, i ^ step) for i in range(size)])


def body(
    src_feats,
    nbr_one,
    counts,
    seed_rows,
    nbr_two,
    w1_self,
    w1_nbr,
    bias_one,
    w2_self,
    w2_nbr,
    bias_two,
):
    n_feat = lax.axis_size("feat")
    half = n_feat // 2
    steps = range(half - 1, -1, -1)
    fslice, nodes = src_feats.shape
    fanout_one, pcap = nbr_one.shape[2:]
    width = w1_self.shape[1]
    seed_count, fanout_two = nbr_two.shape
    n_idx = fanout_two + 1
    bf16 = jnp.bfloat16
    vmem = pl.BlockSpec(memory_space=pltpu.VMEM)
    smem = pl.BlockSpec(memory_space=pltpu.SMEM)
    hbm = pl.BlockSpec(memory_space=pltpu.HBM)
    anywhere = pl.BlockSpec(memory_space=pl.ANY)
    table_bytes = nodes * LANES * 4

    def call(kernel, name, shapes, ins, args, after=(), scratch=(), limit=16 * MIB, cost_us=1, outs=None):
        def wrapped(*refs):
            kernel(*refs[: len(args)], *refs[len(args) + len(after) :])

        return pl.pallas_call(
            wrapped,
            out_shape=tuple(jax.ShapeDtypeStruct(shape, dtype) for shape, dtype in shapes),
            in_specs=[*ins, *([anywhere] * len(after))],
            out_specs=outs or (vmem,) * len(shapes),
            scratch_shapes=scratch,
            compiler_params=pltpu.CompilerParams(vmem_limit_bytes=limit),
            cost_estimate=pl.CostEstimate(
                flops=int(cost_us * 1_100_000_000), bytes_accessed=0, transcendentals=0
            ),
            name=name,
        )(*args, *after)

    def pinned(value):
        return pltpu.with_memory_space_constraint(value, pltpu.HBM)

    def send(chunks, steps=steps):
        return [swap(chunk, "feat", s) if s else chunk for s, chunk in zip(steps, chunks)]

    picks = jnp.transpose(nbr_one, (0, 2, 1, 3))
    packed = 2 if fanout_one % 2 == 0 and nodes <= 1 << 16 else 1
    words = (n_feat, fanout_one // packed, 1, -(-pcap // LANES) * LANES)
    *parcels, picks, feats = call(
        functools.partial(pack_kernel, n_feat, pcap),
        "pack",
        [((parcel_rows(fslice, n_idx), width), bf16)] * half
        + [(words, jnp.int32), ((fslice, nodes), bf16)],
        [hbm] * 6 + [smem],
        [
            *(pinned(x) for x in (src_feats, seed_rows[None], nbr_two.T, w1_self, w1_nbr, picks)),
            counts,
        ],
        scratch=[
            pltpu.VMEM((1, seed_count), jnp.int32),
            pltpu.VMEM((fanout_two, seed_count), jnp.int32),
            pltpu.VMEM((fslice, width), bf16),
            pltpu.VMEM((fslice, width), bf16),
            pltpu.VMEM((n_feat, fanout_one, 1, pcap), jnp.int32),
            pltpu.SemaphoreType.DMA((7,)),
        ],
        limit=32 * MIB,
    )
    arrived = send(parcels)
    (table,) = call(
        turn_kernel,
        "turn",
        [((nodes, LANES), jnp.float32)],
        [vmem],
        (feats,),
        limit=table_bytes + 12 * MIB,
        cost_us=3,
    )
    table = table.reshape(nodes, 1, LANES)
    chunk_shape = (pcap // 4 * 3, LANES) if folds(fslice, pcap) else (pcap, fslice)

    def means(chosen, parcels=(), after=()):
        count = len(chosen)
        return call(
            functools.partial(mean_kernel, tuple(chosen), packed, fanout_one, pcap, fslice, n_idx),
            "mean",
            [(chunk_shape, bf16)] * count,
            [anywhere] + [vmem] * (1 + len(parcels)),
            (picks, table, *parcels),
            after=after,
            scratch=[
                pltpu.VMEM((count, *chunk_shape), bf16),
                pltpu.VMEM((pcap, LANES), jnp.float32),
                pltpu.SMEM((count * words[1] * words[3],), jnp.int32),
                pltpu.SMEM((count,), jnp.int32),
                pltpu.SemaphoreType.DMA((count * words[1],)),
            ],
            limit=table_bytes + 8 * MIB,
            cost_us=2 * count if count > 1 else 0,
        )

    far_means = means([s + half for s in steps if s])
    (halves,) = call(
        functools.partial(halves_kernel, half),
        "halves",
        [((half, fslice, width), bf16)],
        [vmem] * half,
        arrived,
        after=far_means[:1],
    )
    far_arrived = send(far_means)
    other_halves = swap(halves, "rep", 1)
    (far_own,) = means([half], after=(halves,))
    idx_rows = -(-half // 4) * n_idx
    w_nbr, pre, far_pre, idx_tags = call(
        functools.partial(own_kernel, half, n_idx),
        "own",
        [
            ((half, fslice, width), bf16),
            ((pcap, width), jnp.float32),
            ((pcap, width), jnp.float32),
            ((idx_rows, width), bf16),
        ],
        [vmem] * (half + 2),
        (*arrived, other_halves, bias_one[None]),
        after=(far_own,),
    )
    (cross,) = call(
        functools.partial(far_kernel, half),
        "far",
        [((pcap + idx_rows, width), bf16)],
        [vmem] * (half + 3),
        (*far_arrived, far_own, far_pre, w_nbr, idx_tags),
    )
    cross_arrived = swap(cross, "feat", half)
    near_means = means([s for s in steps if s], arrived[:-1], (cross,))
    near_arrived = send(near_means)
    (near_own,) = means([0], arrived[-1:], near_means[-1:])
    (near_times,) = call(
        functools.partial(near_times_kernel, half, fslice, pcap, n_idx),
        "near_times",
        [((half * seed_count, 4 * pcap), bf16)],
        [vmem] * half,
        arrived,
        after=(near_own,),
        cost_us=0,
    )
    (near_pre,) = call(
        functools.partial(near_kernel, half),
        "near",
        [((pcap, width), jnp.float32)],
        [vmem] * (half + 2),
        (*near_arrived, near_own, pre, w_nbr),
        after=(near_times,),
        cost_us=0,
    )
    (hidden,) = call(
        functools.partial(hidden_kernel, fslice, n_idx),
        "hidden",
        [((pcap, width), bf16)],
        [vmem] * 3,
        (parcels[-1], near_pre, cross_arrived),
    )
    other_hidden = swap(hidden, "rep", 1)
    far_times, value, result = call(
        functools.partial(far_times_kernel, half, n_idx, fanout_two),
        "far_times",
        [
            ((half * seed_count, 4 * pcap), bf16),
            ((2, pcap, width), bf16),
            ((pcap, width), bf16),
        ],
        [vmem] * 4,
        (cross_arrived, hidden, w2_self, w2_nbr),
        scratch=[pltpu.SemaphoreType.DMA],
        outs=(vmem, vmem, anywhere),
    )
    shares = call(
        functools.partial(share_kernel, half, fanout_two),
        "share",
        [((2 * seed_count, width), bf16)] + [((seed_count, width), bf16)] * (2 * half - 2),
        [vmem] * 6,
        (near_times, far_times, value, other_hidden, w2_self, w2_nbr),
        scratch=[pltpu.VMEM((2, pcap, width), bf16)],
        limit=32 * MIB,
    )
    both = swap(shares[0], "feat", 1)
    others = [*steps[: half - 2], 0]
    far_shares = send(shares[1:half], others)
    near_shares = send(shares[half:], others)
    (far_sum,) = call(
        side_sum_kernel,
        "side_sum",
        [((seed_count, width), bf16)],
        [vmem] * half,
        (both, *far_shares),
    )
    (seed_out,) = call(
        last_kernel,
        "seeds",
        [((seed_count, width), bf16)],
        [vmem] * (half + 2),
        (bias_two[None], both, *near_shares, swap(far_sum, "feat", half)),
    )
    return (result[None, None], seed_out)


def solution(mesh):
    placed = (
        P("feat", "groups"),
        P("groups", "rep", None, None),
        P(("groups", "feat"), "rep"),
        P(("groups", "feat", "rep")),
        P(("groups", "feat", "rep"), None),
        P("feat", None),
        P("feat", None),
        P(),
        P(),
        P(),
        P(),
    )
    return jax.shard_map(
        body,
        mesh=mesh,
        in_specs=placed,
        out_specs=(P(("groups", "feat"), "rep", None, None), P(("groups", "feat", "rep"), None)),
        check_vma=False,
    )
```

```python
import functools

import jax
import jax.numpy as jnp
from jax import lax
from jax.experimental import pallas as pl
from jax.experimental.pallas import tpu as pltpu
from jax.sharding import PartitionSpec as P

LANES = 128
MIB = 1024 * 1024


def folds(fslice, pcap):
    return 4 * fslice == 3 * LANES and pcap % 64 == 0


def is_dense(fslice, n_idx):
    return fslice % 32 == 0 and n_idx == 16


def parcel_rows(fslice, n_idx):
    return 2 * fslice - fslice // 4 + 8 if is_dense(fslice, n_idx) else 2 * fslice


def write_parcel(ref, weight, feats, digits):
    fslice, lanes = feats.shape
    ref[:fslice, :] = weight
    if is_dense(fslice, digits.shape[0]):
        cut = fslice // 4 * 3
        tail = jnp.concatenate([feats[cut:, i : i + LANES] for i in range(0, lanes, LANES)], axis=0)
        tags = jnp.concatenate([digits[:8], digits[8:]] * 2, axis=1)
        body = jnp.concatenate([feats[:cut], tail], axis=1)
        ref[fslice:, :] = jnp.concatenate([body, tags], axis=0).astype(jnp.bfloat16)
    else:
        ref[fslice:, :lanes] = feats.astype(jnp.bfloat16)
        ref[fslice : fslice + digits.shape[0], lanes:] = digits.astype(jnp.bfloat16)


def read_feats(ref, fslice, n_idx, lanes):
    if not is_dense(fslice, n_idx):
        return ref[fslice:, :lanes].astype(jnp.float32)
    cut, part = fslice // 4 * 3, fslice // 4
    tail = ref[fslice : fslice + cut, lanes:].astype(jnp.float32)
    tail = jnp.concatenate([tail[i : i + part] for i in range(0, cut, part)], axis=1)
    return jnp.concatenate([ref[fslice : fslice + cut, :lanes].astype(jnp.float32), tail], axis=0)


def read_digits(ref, fslice, n_idx, lanes):
    if not is_dense(fslice, n_idx):
        return ref[fslice : fslice + n_idx, lanes:].astype(jnp.float32)
    tags = ref[-8:, : 2 * LANES].astype(jnp.float32)
    return jnp.concatenate([tags[:, :LANES], tags[:, LANES:]], axis=0)


TAG_ROWS = 16


def live_rows(ref):
    return jnp.max(ref[-TAG_ROWS:, :].astype(jnp.float32)).astype(jnp.int32)


def pack_kernel(
    n_feat,
    pcap,
    src_hbm,
    seed_hbm,
    nbr_hbm,
    w_self_hbm,
    w_nbr_hbm,
    pick_hbm,
    *refs,
):
    half = n_feat // 2
    parcel_refs, pick_ref, src_ref = refs[:half], refs[half], refs[half + 1]
    seed_ref, nbr_ref, w_self_ref, w_nbr_ref, fetched_ref, sems = refs[half + 2 :]
    owned = n_feat * 2 * pcap
    first, rest = pl.ds(0, owned), pl.ds(owned, src_ref.shape[1] - owned)
    copies = [
        pltpu.make_async_copy(a, b, sems.at[i])
        for i, (a, b) in enumerate(
            (
                (src_hbm.at[:, first], src_ref.at[:, first]),
                (w_self_hbm, w_self_ref),
                (w_nbr_hbm, w_nbr_ref),
                (seed_hbm, seed_ref),
                (nbr_hbm, nbr_ref),
                (pick_hbm, fetched_ref),
                (src_hbm.at[:, rest], src_ref.at[:, rest]),
            )
        )
    ]
    for copy in copies:
        copy.start()
    for copy in copies[:-1]:
        copy.wait()
    words = pick_ref.shape[1]
    if fetched_ref.shape[1] == words:
        pick_ref[:, :, :, :pcap] = fetched_ref[...]
    else:
        pick_ref[:, :, :, :pcap] = fetched_ref[:, :words] | (fetched_ref[:, words:] << 16)
    feat_pos = lax.axis_index("feat")
    first_core = lax.axis_index("rep") == 0
    idx = jnp.concatenate([seed_ref[...], nbr_ref[...]], axis=0)
    high = lax.shift_right_logical(idx, 7)
    digits = jnp.concatenate([high, idx - high * 128], axis=1).astype(jnp.float32)
    weight = jnp.where(first_core, w_self_ref[...], w_nbr_ref[...])
    for s, parcel_ref in enumerate(reversed(parcel_refs)):
        sides = []
        for step in (s, s ^ half):
            at = pl.multiple_of(jnp.bitwise_xor(feat_pos, step) * (2 * pcap), LANES)
            block = src_ref[:, pl.ds(at, 2 * pcap)].astype(jnp.float32)
            sides.append(jnp.where(first_core, block[:, :pcap], block[:, pcap:]))
        write_parcel(parcel_ref, weight, jnp.concatenate(sides, axis=1), digits)
    copies[-1].wait()


def turn_kernel(src_ref, table_ref):
    fslice, nodes = src_ref.shape
    width = 2048 if nodes % 2048 == 0 else 512

    def turn(step, carry):
        at = pl.multiple_of(step * width, width)
        table_ref[pl.ds(at, width), :fslice] = src_ref[:, pl.ds(at, width)].T.astype(jnp.float32)
        return carry

    lax.fori_loop(0, nodes // width, turn, 0)


def mean_kernel(chosen, packed, fanout, pcap, fslice, nbr_any, table_ref, *refs):
    count = len(chosen)
    token_ref, out_ref, total, nbr_ref, live_ref, sems = refs[-6:]
    chunk_refs, tagged_refs = refs[-6 - count : -6], refs[: -6 - count]
    token_ref[...] = jnp.zeros(token_ref.shape, jnp.float32)
    feat_pos = lax.axis_index("feat")
    words = fanout // packed
    stride = -(-pcap // LANES) * LANES
    copies = [
        pltpu.make_async_copy(
            nbr_any.at[feat_pos ^ step, k, 0],
            nbr_ref.at[pl.ds((i * words + k) * stride, stride)],
            sems.at[i * words + k],
        )
        for i, step in enumerate(chosen)
        for k in range(words)
    ]
    for copy in copies:
        copy.start()
    for i in range(count):
        live_ref[i] = pcap
    for i, ref in enumerate(tagged_refs):
        live_ref[i] = live_rows(ref)
    for copy in copies:
        copy.wait()

    def partition(i, carry):
        first = i * (words * stride)

        def group(g, inner):
            at = pl.multiple_of(g * 16, 16)
            start = first + at
            sums = []
            for u in range(16):
                names = [nbr_ref[start + (k * stride + u)] for k in range(words)]
                if packed == 2:
                    names = [
                        part
                        for name in names
                        for part in (name & 0xFFFF, lax.shift_right_logical(name, 16))
                    ]
                rows = [table_ref[name] for name in names]
                while len(rows) > 1:
                    rows = [a + b for a, b in zip(rows[::2], rows[1::2])] + (
                        [rows[-1]] if len(rows) % 2 else []
                    )
                sums.append(rows[0])
            for u, row in enumerate(sums):
                total[pl.ds(at + u, 1), :] = row
            return inner

        lax.fori_loop(0, lax.div(live_ref[i] + 15, 16), group, 0)
        mean = total[...] / fanout
        if folds(fslice, pcap):
            part = pcap // 4
            lane = lax.broadcasted_iota(jnp.int32, (part, LANES), 1)
            tail = mean[3 * part :]
            for b in range(3):
                shift = (fslice - 32 * b) % LANES
                moved = pltpu.roll(tail, shift, 1) if shift else tail
                out_ref[i, pl.ds(b * part, part), :] = jnp.where(
                    lane < fslice, mean[b * part : (b + 1) * part], moved
                ).astype(jnp.bfloat16)
        else:
            out_ref[i] = mean[:, :fslice].astype(jnp.bfloat16)
        return carry

    lax.fori_loop(0, count, partition, 0)
    for i, ref in enumerate(chunk_refs):
        ref[...] = out_ref[i]


def unfold(ref, fslice, pcap):
    if not folds(fslice, pcap):
        return ref[:pcap, :]
    part = pcap // 4
    wide = ref[: 3 * part, :].astype(jnp.float32)
    lane = lax.broadcasted_iota(jnp.int32, (part, LANES), 1)
    tail = pltpu.roll(wide[:part], LANES - fslice, 1)
    for b in (1, 2):
        shift = (32 * b - fslice) % LANES
        moved = wide[b * part : (b + 1) * part]
        moved = pltpu.roll(moved, shift, 1) if shift else moved
        tail = jnp.where(lane // 32 == b, moved, tail)
    return jnp.concatenate([wide, tail], axis=0)[:, :fslice].astype(jnp.bfloat16)


def halves_kernel(half, count_ref, *refs):
    parcel_refs, chunk_refs = refs[:half], refs[half : 2 * half - 1]
    out_ref, *tagged_refs, live_ref = refs[2 * half - 1 :]
    for s, ref in enumerate(parcel_refs):
        out_ref[s] = ref[: out_ref.shape[1], :]
    live = jnp.full(live_ref.shape, count_ref[0, 0].astype(jnp.float32)).astype(jnp.bfloat16)
    live_ref[...] = live
    for chunk_ref, ref in zip(chunk_refs, tagged_refs):
        ref[:-TAG_ROWS, :] = chunk_ref[...]
        ref[-TAG_ROWS:, :] = live


def own_kernel(half, n_idx, *refs):
    parcel_refs = refs[:half]
    other_ref, bias_ref, w_ref, pre_ref, far_ref, idx_ref = refs[half:]
    fslice = w_ref.shape[1]
    pcap, width = pre_ref.shape
    first_core = lax.axis_index("rep") == 0
    both = jnp.zeros((2 * pcap, width), jnp.float32)
    for s in range(half):
        mine, other = parcel_refs[s][:fslice, :], other_ref[s]
        w_ref[s] = jnp.where(first_core, other, mine)
        feats = read_feats(parcel_refs[s], fslice, n_idx, 2 * pcap).T.astype(jnp.bfloat16)
        both = both + jnp.dot(
            feats, jnp.where(first_core, mine, other), preferred_element_type=jnp.float32
        )
        rows = pl.ds(s // 4 * n_idx, n_idx)
        digits = read_digits(parcel_refs[s], fslice, n_idx, 2 * pcap)
        idx_ref[rows, s % 4 * LANES : (s % 4 + 1) * LANES] = digits.astype(jnp.bfloat16)
    pre_ref[...] = both[:pcap] + bias_ref[...]
    far_ref[...] = both[pcap:]


def add_means(half, pre, mean_refs, w_ref, turn=0):
    for s, ref in enumerate(mean_refs):
        pre = pre + jnp.dot(
            unfold(ref, w_ref.shape[1], pre.shape[0]),
            w_ref[(s + turn) % (half - 1) if s < half - 1 else s],
            preferred_element_type=jnp.float32,
        )
    return pre


def far_kernel(half, *refs):
    far_ref, w_ref, idx_ref, cross_ref = refs[half:]
    pcap = far_ref.shape[0]
    cross_ref[:pcap, :] = add_means(half, far_ref[...], refs[:half], w_ref).astype(jnp.bfloat16)
    cross_ref[pcap:, :] = idx_ref[...]


def store_times(pcap, blocks, out_ref):
    n_idx, pair = blocks[0].shape
    seed_count = pair // 2
    core_rows = lax.axis_index("feat") * (2 * pcap)
    rep_pos = lax.axis_index("rep")
    row = lax.broadcasted_iota(jnp.int32, (2 * pcap, pair), 0)
    slot = jnp.where(
        row < pcap, row + core_rows + rep_pos * pcap, row + core_rows - rep_pos * pcap
    ).astype(jnp.float32)
    low = lax.broadcasted_iota(jnp.int32, (n_idx, pair), 1) < seed_count
    for s in range(0, len(blocks), 2):
        first, second = blocks[s].astype(jnp.float32), blocks[s + 1].astype(jnp.float32)
        high_part = jnp.where(low, first, pltpu.roll(second, seed_count, 1))
        low_part = jnp.where(low, pltpu.roll(first, seed_count, 1), second)
        name = high_part * 128.0 + low_part
        own = jnp.where(slot == name[:1], 1.0, 0.0)
        near = jnp.zeros((2 * pcap, pair), jnp.float32)
        for k in range(1, n_idx):
            near = near + jnp.where(slot == name[k : k + 1], 1.0, 0.0)
        place = pl.ds(s * seed_count, pair)
        out_ref[place, : 2 * pcap] = own.T.astype(jnp.bfloat16)
        out_ref[place, 2 * pcap :] = near.T.astype(jnp.bfloat16)


def near_times_kernel(half, fslice, pcap, n_idx, _, __, *refs):
    blocks = [read_digits(ref, fslice, n_idx, 2 * pcap) for ref in refs[:half]]
    store_times(pcap, blocks, refs[half])


def far_times_kernel(
    half,
    n_idx,
    fanout_two,
    cross_ref,
    hidden_ref,
    ws_ref,
    wn_ref,
    out_ref,
    value_ref,
    result_ref,
    sem,
):
    copy = pltpu.make_async_copy(hidden_ref, result_ref, sem)
    copy.start()
    pcap = hidden_ref.shape[0]
    blocks = [
        cross_ref[
            pl.ds(pcap + s // 4 * n_idx, n_idx), s % 4 * LANES : (s % 4 + 1) * LANES
        ]
        for s in range(half)
    ]
    store_times(pcap, blocks, out_ref)
    store_values(hidden_ref[...], ws_ref, wn_ref, fanout_two, value_ref)
    copy.wait()


def store_values(hidden, ws_ref, wn_ref, fanout_two, value_ref):
    value_ref[0] = jnp.dot(hidden, ws_ref[...], preferred_element_type=jnp.float32).astype(
        jnp.bfloat16
    )
    value_ref[1] = (
        jnp.dot(hidden, wn_ref[...], preferred_element_type=jnp.float32) / fanout_two
    ).astype(jnp.bfloat16)


def near_kernel(half, *refs):
    pre_ref, w_ref, out_ref = refs[half:]
    out_ref[...] = add_means(half, pre_ref[...], refs[:half], w_ref, 1)


def hidden_kernel(live_ref, pre_ref, cross_ref, hidden_ref):
    pcap, width = hidden_ref.shape
    pre = pre_ref[...] + cross_ref[:pcap, :].astype(jnp.float32)
    live = lax.broadcasted_iota(jnp.int32, (pcap, width), 0) < live_rows(live_ref)
    hidden_ref[...] = jnp.where(live, jnp.maximum(pre, 0.0), 0.0).astype(jnp.bfloat16)


def share_kernel(
    half, fanout_two, near_ref, far_ref, value_ref, hidden_ref, ws_ref, wn_ref, *refs
):
    *out_refs, other_ref = refs
    store_values(hidden_ref[...], ws_ref, wn_ref, fanout_two, other_ref)
    values = jnp.concatenate(
        [value_ref[0], other_ref[0], value_ref[1], other_ref[1]], axis=0
    )
    rows = far_ref.shape[0] // half
    both_ref, far_refs, near_refs = out_refs[0], out_refs[1:half], out_refs[half:]
    for times_ref, refs, low in ((far_ref, far_refs, 0), (near_ref, near_refs, rows)):
        part = jnp.dot(times_ref[...], values, preferred_element_type=jnp.float32)
        part = part.astype(jnp.bfloat16)
        both_ref[low : low + rows, :] = part[(half - 2) * rows : (half - 1) * rows]
        for i, ref in enumerate(refs):
            place = i if i < half - 2 else half - 1
            ref[...] = part[place * rows : (place + 1) * rows]


def sum_rows(first, low, refs, rows):
    total = first
    for i, ref in enumerate(refs):
        at = low if i == 0 else 0
        total = total + ref[at : at + rows, :].astype(jnp.float32)
    return total


def side_sum_kernel(*refs):
    rows = refs[-1].shape[0]
    refs[-1][...] = sum_rows(0.0, 0, refs[:-1], rows).astype(jnp.bfloat16)


def last_kernel(bias_ref, *refs):
    rows = refs[-1].shape[0]
    total = sum_rows(bias_ref[...], rows, refs[:-1], rows)
    refs[-1][...] = jnp.maximum(total, 0.0).astype(jnp.bfloat16)


def swap(value, axis, step):
    size = lax.axis_size(axis)
    return lax.ppermute(value, axis, [(i, i ^ step) for i in range(size)])


def body(
    src_feats,
    nbr_one,
    counts,
    seed_rows,
    nbr_two,
    w1_self,
    w1_nbr,
    bias_one,
    w2_self,
    w2_nbr,
    bias_two,
):
    n_feat = lax.axis_size("feat")
    half = n_feat // 2
    steps = range(half - 1, -1, -1)
    fslice, nodes = src_feats.shape
    fanout_one, pcap = nbr_one.shape[2:]
    width = w1_self.shape[1]
    seed_count, fanout_two = nbr_two.shape
    n_idx = fanout_two + 1
    bf16 = jnp.bfloat16
    vmem = pl.BlockSpec(memory_space=pltpu.VMEM)
    smem = pl.BlockSpec(memory_space=pltpu.SMEM)
    hbm = pl.BlockSpec(memory_space=pltpu.HBM)
    anywhere = pl.BlockSpec(memory_space=pl.ANY)
    table_bytes = nodes * LANES * 4

    def call(kernel, name, shapes, ins, args, after=(), scratch=(), limit=16 * MIB, cost_us=1, outs=None):
        def wrapped(*refs):
            kernel(*refs[: len(args)], *refs[len(args) + len(after) :])

        return pl.pallas_call(
            wrapped,
            out_shape=tuple(jax.ShapeDtypeStruct(shape, dtype) for shape, dtype in shapes),
            in_specs=[*ins, *([anywhere] * len(after))],
            out_specs=outs or (vmem,) * len(shapes),
            scratch_shapes=scratch,
            compiler_params=pltpu.CompilerParams(vmem_limit_bytes=limit),
            cost_estimate=pl.CostEstimate(
                flops=int(cost_us * 1_100_000_000), bytes_accessed=0, transcendentals=0
            ),
            name=name,
        )(*args, *after)

    def pinned(value):
        return pltpu.with_memory_space_constraint(value, pltpu.HBM)

    def send(chunks, steps=steps):
        return [swap(chunk, "feat", s) if s else chunk for s, chunk in zip(steps, chunks)]

    picks = jnp.transpose(nbr_one, (0, 2, 1, 3))
    packed = 2 if fanout_one % 2 == 0 and nodes <= 1 << 16 else 1
    words = (n_feat, fanout_one // packed, 1, -(-pcap // LANES) * LANES)
    *parcels, picks, feats = call(
        functools.partial(pack_kernel, n_feat, pcap),
        "pack",
        [((parcel_rows(fslice, n_idx), width), bf16)] * half
        + [(words, jnp.int32), ((fslice, nodes), bf16)],
        [hbm] * 6,
        [pinned(x) for x in (src_feats, seed_rows[None], nbr_two.T, w1_self, w1_nbr, picks)],
        scratch=[
            pltpu.VMEM((1, seed_count), jnp.int32),
            pltpu.VMEM((fanout_two, seed_count), jnp.int32),
            pltpu.VMEM((fslice, width), bf16),
            pltpu.VMEM((fslice, width), bf16),
            pltpu.VMEM((n_feat, fanout_one, 1, pcap), jnp.int32),
            pltpu.SemaphoreType.DMA((7,)),
        ],
        limit=32 * MIB,
    )
    arrived = send(parcels)
    (table,) = call(
        turn_kernel,
        "turn",
        [((nodes, LANES), jnp.float32)],
        [vmem],
        (feats,),
        limit=table_bytes + 12 * MIB,
        cost_us=3,
    )
    table = table.reshape(nodes, 1, LANES)
    chunk_shape = (pcap // 4 * 3, LANES) if folds(fslice, pcap) else (pcap, fslice)

    def means(chosen, tagged=(), after=()):
        count = len(chosen)
        return call(
            functools.partial(mean_kernel, tuple(chosen), packed, fanout_one, pcap, fslice),
            "mean",
            [(chunk_shape, bf16)] * count + [((8, LANES), jnp.float32)],
            [anywhere] + [vmem] * (1 + len(tagged)),
            (picks, table, *tagged),
            after=after,
            scratch=[
                pltpu.VMEM((count, *chunk_shape), bf16),
                pltpu.VMEM((pcap, LANES), jnp.float32),
                pltpu.SMEM((count * words[1] * words[3],), jnp.int32),
                pltpu.SMEM((count,), jnp.int32),
                pltpu.SemaphoreType.DMA((count * words[1],)),
            ],
            limit=table_bytes + 8 * MIB,
            cost_us=2 * count if count > 1 else 0,
        )

    *far_means, _ = means([s + half for s in steps if s])
    tagged_shape = (chunk_shape[0] + TAG_ROWS, chunk_shape[1])
    halves, *tagged, live = call(
        functools.partial(halves_kernel, half),
        "halves",
        [
            ((half, fslice, width), bf16),
            *([(tagged_shape, bf16)] * (half - 1)),
            ((TAG_ROWS, chunk_shape[1]), bf16),
        ],
        [smem] + [vmem] * (2 * half - 1),
        (counts, *arrived, *far_means),
    )
    far_arrived = send(tagged)
    other_halves = swap(halves, "rep", 1)
    far_own, _ = means([half], after=(halves,))
    idx_rows = -(-half // 4) * n_idx
    w_nbr, pre, far_pre, idx_tags = call(
        functools.partial(own_kernel, half, n_idx),
        "own",
        [
            ((half, fslice, width), bf16),
            ((pcap, width), jnp.float32),
            ((pcap, width), jnp.float32),
            ((idx_rows, width), bf16),
        ],
        [vmem] * (half + 2),
        (*arrived, other_halves, bias_one[None]),
        after=(far_own,),
        cost_us=0,
    )
    (cross,) = call(
        functools.partial(far_kernel, half),
        "far",
        [((pcap + idx_rows, width), bf16)],
        [vmem] * (half + 3),
        (*far_arrived, far_own, far_pre, w_nbr, idx_tags),
    )
    cross_arrived = swap(cross, "feat", half)
    turned = [*steps[1:-1], steps[0]]
    *near_means, token = means(turned, [*far_arrived[1:], far_arrived[0]], (cross,))
    near_arrived = send(near_means, turned)
    near_own, _ = means([0], [live], (token,))
    (near_times,) = call(
        functools.partial(near_times_kernel, half, fslice, pcap, n_idx),
        "near_times",
        [((half * seed_count, 4 * pcap), bf16)],
        [vmem] * (half + 2),
        (w2_self, w2_nbr, *arrived),
        after=(near_own,),
        cost_us=0,
    )
    (near_pre,) = call(
        functools.partial(near_kernel, half),
        "near",
        [((pcap, width), jnp.float32)],
        [vmem] * (half + 2),
        (*near_arrived, near_own, pre, w_nbr),
        after=(near_times,),
        cost_us=0,
    )
    (hidden,) = call(
        hidden_kernel,
        "hidden",
        [((pcap, width), bf16)],
        [vmem] * 3,
        (live, near_pre, cross_arrived),
    )
    other_hidden = swap(hidden, "rep", 1)
    far_times, value, result = call(
        functools.partial(far_times_kernel, half, n_idx, fanout_two),
        "far_times",
        [
            ((half * seed_count, 4 * pcap), bf16),
            ((2, pcap, width), bf16),
            ((pcap, width), bf16),
        ],
        [vmem] * 4,
        (cross_arrived, hidden, w2_self, w2_nbr),
        scratch=[pltpu.SemaphoreType.DMA],
        outs=(vmem, vmem, anywhere),
    )
    shares = call(
        functools.partial(share_kernel, half, fanout_two),
        "share",
        [((2 * seed_count, width), bf16)] + [((seed_count, width), bf16)] * (2 * half - 2),
        [vmem] * 6,
        (near_times, far_times, value, other_hidden, w2_self, w2_nbr),
        scratch=[pltpu.VMEM((2, pcap, width), bf16)],
        limit=32 * MIB,
    )
    both = swap(shares[0], "feat", 1)
    others = [*steps[: half - 2], 0]
    far_shares = send(shares[1:half], others)
    near_shares = send(shares[half:], others)
    (far_sum,) = call(
        side_sum_kernel,
        "side_sum",
        [((seed_count, width), bf16)],
        [vmem] * half,
        (both, *far_shares),
    )
    (seed_out,) = call(
        last_kernel,
        "seeds",
        [((seed_count, width), bf16)],
        [vmem] * (half + 2),
        (bias_two[None], both, *near_shares, swap(far_sum, "feat", half)),
    )
    return (result[None, None], seed_out)


def solution(mesh):
    placed = (
        P("feat", "groups"),
        P("groups", "rep", None, None),
        P(("groups", "feat"), "rep"),
        P(("groups", "feat", "rep")),
        P(("groups", "feat", "rep"), None),
        P("feat", None),
        P("feat", None),
        P(),
        P(),
        P(),
        P(),
    )
    return jax.shard_map(
        body,
        mesh=mesh,
        in_specs=placed,
        out_specs=(P(("groups", "feat"), "rep", None, None), P(("groups", "feat", "rep"), None)),
        check_vma=False,
    )
```

```python
import functools

import jax
import jax.numpy as jnp
from jax import lax
from jax.experimental import pallas as pl
from jax.experimental.pallas import tpu as pltpu
from jax.sharding import PartitionSpec as P

LANES = 128
MIB = 1024 * 1024


def folds(fslice, pcap):
    return 4 * fslice == 3 * LANES and pcap % 64 == 0


def is_dense(fslice, n_idx):
    return fslice % 32 == 0 and n_idx == 16


def parcel_rows(fslice, n_idx):
    return 2 * fslice - fslice // 4 + 8 if is_dense(fslice, n_idx) else 2 * fslice


def write_parcel(ref, weight, feats, digits):
    fslice, lanes = feats.shape
    ref[:fslice, :] = weight
    if is_dense(fslice, digits.shape[0]):
        cut = fslice // 4 * 3
        tail = jnp.concatenate([feats[cut:, i : i + LANES] for i in range(0, lanes, LANES)], axis=0)
        tags = jnp.concatenate([digits[:8], digits[8:]] * 2, axis=1)
        body = jnp.concatenate([feats[:cut], tail], axis=1)
        ref[fslice:, :] = jnp.concatenate([body, tags], axis=0).astype(jnp.bfloat16)
    else:
        ref[fslice:, :lanes] = feats.astype(jnp.bfloat16)
        ref[fslice : fslice + digits.shape[0], lanes:] = digits.astype(jnp.bfloat16)


def read_feats(ref, fslice, n_idx, lanes):
    if not is_dense(fslice, n_idx):
        return ref[fslice:, :lanes].astype(jnp.float32)
    cut, part = fslice // 4 * 3, fslice // 4
    tail = ref[fslice : fslice + cut, lanes:].astype(jnp.float32)
    tail = jnp.concatenate([tail[i : i + part] for i in range(0, cut, part)], axis=1)
    return jnp.concatenate([ref[fslice : fslice + cut, :lanes].astype(jnp.float32), tail], axis=0)


def read_digits(ref, fslice, n_idx, lanes):
    if not is_dense(fslice, n_idx):
        return ref[fslice : fslice + n_idx, lanes:].astype(jnp.float32)
    tags = ref[-8:, : 2 * LANES].astype(jnp.float32)
    return jnp.concatenate([tags[:, :LANES], tags[:, LANES:]], axis=0)


TAG_ROWS = 16


def live_rows(ref):
    return jnp.max(ref[-TAG_ROWS:, :].astype(jnp.float32)).astype(jnp.int32)


def pack_kernel(
    n_feat,
    pcap,
    src_hbm,
    seed_hbm,
    nbr_hbm,
    w_self_hbm,
    w_nbr_hbm,
    pick_hbm,
    *refs,
):
    half = n_feat // 2
    parcel_refs, pick_ref, src_ref = refs[:half], refs[half], refs[half + 1]
    seed_ref, nbr_ref, w_self_ref, w_nbr_ref, fetched_ref, sems = refs[half + 2 :]
    owned = n_feat * 2 * pcap
    first, rest = pl.ds(0, owned), pl.ds(owned, src_ref.shape[1] - owned)
    copies = [
        pltpu.make_async_copy(a, b, sems.at[i])
        for i, (a, b) in enumerate(
            (
                (src_hbm.at[:, first], src_ref.at[:, first]),
                (w_self_hbm, w_self_ref),
                (w_nbr_hbm, w_nbr_ref),
                (seed_hbm, seed_ref),
                (nbr_hbm, nbr_ref),
                (pick_hbm, fetched_ref),
                (src_hbm.at[:, rest], src_ref.at[:, rest]),
            )
        )
    ]
    for copy in copies:
        copy.start()
    for copy in copies[1:-1]:
        copy.wait()
    stride = -(-pcap // LANES) * LANES
    words = pick_ref.shape[2] // stride
    for k in range(words):
        word = fetched_ref[:, k]
        if words < fetched_ref.shape[1]:
            word = word | (fetched_ref[:, words + k] << 16)
        pick_ref[:, :, k * stride : k * stride + pcap] = word
    feat_pos = lax.axis_index("feat")
    first_core = lax.axis_index("rep") == 0
    idx = jnp.concatenate([seed_ref[...], nbr_ref[...]], axis=0)
    high = lax.shift_right_logical(idx, 7)
    digits = jnp.concatenate([high, idx - high * 128], axis=1).astype(jnp.float32)
    weight = jnp.where(first_core, w_self_ref[...], w_nbr_ref[...])
    copies[0].wait()
    for s, parcel_ref in enumerate(reversed(parcel_refs)):
        sides = []
        for step in (s, s ^ half):
            at = pl.multiple_of(jnp.bitwise_xor(feat_pos, step) * (2 * pcap), LANES)
            block = src_ref[:, pl.ds(at, 2 * pcap)].astype(jnp.float32)
            sides.append(jnp.where(first_core, block[:, :pcap], block[:, pcap:]))
        write_parcel(parcel_ref, weight, jnp.concatenate(sides, axis=1), digits)
    copies[-1].wait()


def turn_kernel(src_ref, table_ref):
    fslice, nodes = src_ref.shape
    width = 2048 if nodes % 2048 == 0 else 512

    def turn(step, carry):
        at = pl.multiple_of(step * width, width)
        table_ref[pl.ds(at, width), :fslice] = src_ref[:, pl.ds(at, width)].T.astype(jnp.float32)
        return carry

    lax.fori_loop(0, nodes // width, turn, 0)


def mean_kernel(chosen, packed, fanout, pcap, fslice, before, n_before, *refs):
    count = len(chosen)
    before_in, refs = refs[: n_before[0]], refs[n_before[0] :]
    nbr_any, table_ref, *refs = refs
    out_ref, total, nbr_ref, live_ref, sems = refs[-5:]
    refs = refs[:-5]
    before_out = refs[len(refs) - n_before[1] :]
    refs = refs[: len(refs) - n_before[1]]
    chunk_refs, tagged_refs = refs[len(refs) - count :], refs[: len(refs) - count]
    feat_pos = lax.axis_index("feat")
    words = fanout // packed
    stride = -(-pcap // LANES) * LANES
    length = words * stride
    copies = [
        pltpu.make_async_copy(
            nbr_any.at[feat_pos ^ step, 0], nbr_ref.at[pl.ds(i * length, length)], sems.at[i]
        )
        for i, step in enumerate(chosen)
    ]
    for copy in copies:
        copy.start()
    for i in range(count):
        live_ref[i] = pcap
    for i, ref in enumerate(tagged_refs):
        live_ref[i] = live_rows(ref)
    if before is not None:
        before(*before_in, *before_out)
    for copy in copies:
        copy.wait()

    def partition(i, carry):
        first = i * length

        def group(g, inner):
            at = pl.multiple_of(g * 16, 16)
            start = first + at
            sums = []
            for u in range(16):
                names = [nbr_ref[start + (k * stride + u)] for k in range(words)]
                if packed == 2:
                    names = [
                        part
                        for name in names
                        for part in (name & 0xFFFF, lax.shift_right_logical(name, 16))
                    ]
                rows = [table_ref[name] for name in names]
                while len(rows) > 1:
                    rows = [a + b for a, b in zip(rows[::2], rows[1::2])] + (
                        [rows[-1]] if len(rows) % 2 else []
                    )
                sums.append(rows[0])
            for u, row in enumerate(sums):
                total[pl.ds(at + u, 1), :] = row
            return inner

        lax.fori_loop(0, lax.div(live_ref[i] + 15, 16), group, 0)
        mean = total[...] / fanout
        if folds(fslice, pcap):
            part = pcap // 4
            lane = lax.broadcasted_iota(jnp.int32, (part, LANES), 1)
            tail = mean[3 * part :]
            for b in range(3):
                shift = (fslice - 32 * b) % LANES
                moved = pltpu.roll(tail, shift, 1) if shift else tail
                out_ref[i, pl.ds(b * part, part), :] = jnp.where(
                    lane < fslice, mean[b * part : (b + 1) * part], moved
                ).astype(jnp.bfloat16)
        else:
            out_ref[i] = mean[:, :fslice].astype(jnp.bfloat16)
        return carry

    lax.fori_loop(0, count, partition, 0)
    for i, ref in enumerate(chunk_refs):
        ref[...] = out_ref[i]


def unfold(ref, fslice, pcap):
    if not folds(fslice, pcap):
        return ref[:pcap, :]
    part = pcap // 4
    wide = ref[: 3 * part, :].astype(jnp.float32)
    lane = lax.broadcasted_iota(jnp.int32, (part, LANES), 1)
    tail = pltpu.roll(wide[:part], LANES - fslice, 1)
    for b in (1, 2):
        shift = (32 * b - fslice) % LANES
        moved = wide[b * part : (b + 1) * part]
        moved = pltpu.roll(moved, shift, 1) if shift else moved
        tail = jnp.where(lane // 32 == b, moved, tail)
    return jnp.concatenate([wide, tail], axis=0)[:, :fslice].astype(jnp.bfloat16)


def halves_kernel(half, count_ref, *refs):
    parcel_refs, chunk_refs = refs[:half], refs[half : 2 * half - 1]
    out_ref, *tagged_refs, live_ref = refs[2 * half - 1 :]
    for s, ref in enumerate(parcel_refs):
        out_ref[s] = ref[: out_ref.shape[1], :]
    live = jnp.full(live_ref.shape, count_ref[0, 0].astype(jnp.float32)).astype(jnp.bfloat16)
    live_ref[...] = live
    for chunk_ref, ref in zip(chunk_refs, tagged_refs):
        ref[:-TAG_ROWS, :] = chunk_ref[...]
        ref[-TAG_ROWS:, :] = live


def own_kernel(half, n_idx, *refs):
    parcel_refs = refs[:half]
    other_ref, bias_ref, w_ref, pre_ref, far_ref, idx_ref = refs[half:]
    fslice = w_ref.shape[1]
    pcap, width = pre_ref.shape
    first_core = lax.axis_index("rep") == 0
    feats, weights = [], []
    for s in range(half):
        mine, other = parcel_refs[s][:fslice, :], other_ref[s]
        w_ref[s] = jnp.where(first_core, other, mine)
        weights.append(jnp.where(first_core, mine, other))
        feats.append(read_feats(parcel_refs[s], fslice, n_idx, 2 * pcap))
        rows = pl.ds(s // 4 * n_idx, n_idx)
        digits = read_digits(parcel_refs[s], fslice, n_idx, 2 * pcap)
        idx_ref[rows, s % 4 * LANES : (s % 4 + 1) * LANES] = digits.astype(jnp.bfloat16)
    both = jnp.dot(
        jnp.concatenate(feats, axis=0).T.astype(jnp.bfloat16),
        jnp.concatenate(weights, axis=0),
        preferred_element_type=jnp.float32,
    )
    pre_ref[...] = both[:pcap] + bias_ref[...]
    far_ref[...] = both[pcap:]


def add_means(half, pre, mean_refs, w_ref, turn=0):
    for s, ref in enumerate(mean_refs):
        pre = pre + jnp.dot(
            unfold(ref, w_ref.shape[1], pre.shape[0]),
            w_ref[(s + turn) % (half - 1) if s < half - 1 else s],
            preferred_element_type=jnp.float32,
        )
    return pre


def far_kernel(half, *refs):
    far_ref, w_ref, idx_ref, cross_ref = refs[half:]
    pcap = far_ref.shape[0]
    cross_ref[:pcap, :] = add_means(half, far_ref[...], refs[:half], w_ref).astype(jnp.bfloat16)
    cross_ref[pcap:, :] = idx_ref[...]


def store_times(pcap, blocks, out_ref):
    n_idx, pair = blocks[0].shape
    seed_count = pair // 2
    core_rows = lax.axis_index("feat") * (2 * pcap)
    rep_pos = lax.axis_index("rep")
    row = lax.broadcasted_iota(jnp.int32, (2 * pcap, pair), 0)
    slot = jnp.where(
        row < pcap, row + core_rows + rep_pos * pcap, row + core_rows - rep_pos * pcap
    ).astype(jnp.float32)
    low = lax.broadcasted_iota(jnp.int32, (n_idx, pair), 1) < seed_count
    for s in range(0, len(blocks), 2):
        first, second = blocks[s].astype(jnp.float32), blocks[s + 1].astype(jnp.float32)
        high_part = jnp.where(low, first, pltpu.roll(second, seed_count, 1))
        low_part = jnp.where(low, pltpu.roll(first, seed_count, 1), second)
        name = high_part * 128.0 + low_part
        own = jnp.where(slot == name[:1], 1.0, 0.0)
        near = jnp.zeros((2 * pcap, pair), jnp.float32)
        for k in range(1, n_idx):
            near = near + jnp.where(slot == name[k : k + 1], 1.0, 0.0)
        place = pl.ds(s * seed_count, pair)
        out_ref[place, : 2 * pcap] = own.T.astype(jnp.bfloat16)
        out_ref[place, 2 * pcap :] = near.T.astype(jnp.bfloat16)


def near_times_kernel(half, fslice, pcap, n_idx, _, __, *refs):
    blocks = [read_digits(ref, fslice, n_idx, 2 * pcap) for ref in refs[:half]]
    store_times(pcap, blocks, refs[half])


def far_times_kernel(
    half,
    n_idx,
    fanout_two,
    cross_ref,
    hidden_ref,
    ws_ref,
    wn_ref,
    out_ref,
    value_ref,
    result_ref,
    sem,
):
    copy = pltpu.make_async_copy(hidden_ref, result_ref, sem)
    copy.start()
    pcap = hidden_ref.shape[0]
    blocks = [
        cross_ref[
            pl.ds(pcap + s // 4 * n_idx, n_idx), s % 4 * LANES : (s % 4 + 1) * LANES
        ]
        for s in range(half)
    ]
    store_times(pcap, blocks, out_ref)
    store_values(hidden_ref[...], ws_ref, wn_ref, fanout_two, value_ref)
    copy.wait()


def store_values(hidden, ws_ref, wn_ref, fanout_two, value_ref):
    value_ref[0] = jnp.dot(hidden, ws_ref[...], preferred_element_type=jnp.float32).astype(
        jnp.bfloat16
    )
    value_ref[1] = (
        jnp.dot(hidden, wn_ref[...], preferred_element_type=jnp.float32) / fanout_two
    ).astype(jnp.bfloat16)


def near_kernel(half, *refs):
    pre_ref, w_ref, out_ref = refs[half:]
    out_ref[...] = add_means(half, pre_ref[...], refs[:half], w_ref, 1)


def hidden_kernel(live_ref, pre_ref, cross_ref, hidden_ref):
    pcap, width = hidden_ref.shape
    pre = pre_ref[...] + cross_ref[:pcap, :].astype(jnp.float32)
    live = lax.broadcasted_iota(jnp.int32, (pcap, width), 0) < live_rows(live_ref)
    hidden_ref[...] = jnp.where(live, jnp.maximum(pre, 0.0), 0.0).astype(jnp.bfloat16)


def share_kernel(
    half, fanout_two, near_ref, far_ref, value_ref, hidden_ref, ws_ref, wn_ref, *refs
):
    *out_refs, other_ref = refs
    store_values(hidden_ref[...], ws_ref, wn_ref, fanout_two, other_ref)
    values = jnp.concatenate(
        [value_ref[0], other_ref[0], value_ref[1], other_ref[1]], axis=0
    )
    rows = far_ref.shape[0] // half
    both_ref, far_refs, near_refs = out_refs[0], out_refs[1:half], out_refs[half:]
    for times_ref, refs, low in ((far_ref, far_refs, 0), (near_ref, near_refs, rows)):
        part = jnp.dot(times_ref[...], values, preferred_element_type=jnp.float32)
        part = part.astype(jnp.bfloat16)
        both_ref[low : low + rows, :] = part[(half - 2) * rows : (half - 1) * rows]
        for i, ref in enumerate(refs):
            place = i if i < half - 2 else half - 1
            ref[...] = part[place * rows : (place + 1) * rows]


def sum_rows(first, low, refs, rows):
    total = first
    for i, ref in enumerate(refs):
        at = low if i == 0 else 0
        total = total + ref[at : at + rows, :].astype(jnp.float32)
    return total


def side_sum_kernel(*refs):
    rows = refs[-1].shape[0]
    refs[-1][...] = sum_rows(0.0, 0, refs[:-1], rows).astype(jnp.bfloat16)


def last_kernel(bias_ref, *refs):
    rows = refs[-1].shape[0]
    total = sum_rows(bias_ref[...], rows, refs[:-1], rows)
    refs[-1][...] = jnp.maximum(total, 0.0).astype(jnp.bfloat16)


def swap(value, axis, step):
    size = lax.axis_size(axis)
    return lax.ppermute(value, axis, [(i, i ^ step) for i in range(size)])


def body(
    src_feats,
    nbr_one,
    counts,
    seed_rows,
    nbr_two,
    w1_self,
    w1_nbr,
    bias_one,
    w2_self,
    w2_nbr,
    bias_two,
):
    n_feat = lax.axis_size("feat")
    half = n_feat // 2
    steps = range(half - 1, -1, -1)
    fslice, nodes = src_feats.shape
    fanout_one, pcap = nbr_one.shape[2:]
    width = w1_self.shape[1]
    seed_count, fanout_two = nbr_two.shape
    n_idx = fanout_two + 1
    bf16 = jnp.bfloat16
    vmem = pl.BlockSpec(memory_space=pltpu.VMEM)
    smem = pl.BlockSpec(memory_space=pltpu.SMEM)
    hbm = pl.BlockSpec(memory_space=pltpu.HBM)
    anywhere = pl.BlockSpec(memory_space=pl.ANY)
    table_bytes = nodes * LANES * 4

    def call(kernel, name, shapes, ins, args, after=(), scratch=(), limit=16 * MIB, cost_us=1, outs=None):
        def wrapped(*refs):
            kernel(*refs[: len(args)], *refs[len(args) + len(after) :])

        return pl.pallas_call(
            wrapped,
            out_shape=tuple(jax.ShapeDtypeStruct(shape, dtype) for shape, dtype in shapes),
            in_specs=[*ins, *([anywhere] * len(after))],
            out_specs=outs or (vmem,) * len(shapes),
            scratch_shapes=scratch,
            compiler_params=pltpu.CompilerParams(vmem_limit_bytes=limit),
            cost_estimate=pl.CostEstimate(
                flops=int(cost_us * 1_100_000_000), bytes_accessed=0, transcendentals=0
            ),
            name=name,
        )(*args, *after)

    def pinned(value):
        return pltpu.with_memory_space_constraint(value, pltpu.HBM)

    def send(chunks, steps=steps):
        return [swap(chunk, "feat", s) if s else chunk for s, chunk in zip(steps, chunks)]

    picks = jnp.transpose(nbr_one, (0, 2, 1, 3))
    packed = 2 if fanout_one % 2 == 0 and nodes <= 1 << 16 else 1
    words = (n_feat, 1, fanout_one // packed * (-(-pcap // LANES) * LANES))
    *parcels, picks, feats = call(
        functools.partial(pack_kernel, n_feat, pcap),
        "pack",
        [((parcel_rows(fslice, n_idx), width), bf16)] * half
        + [(words, jnp.int32), ((fslice, nodes), bf16)],
        [hbm] * 6,
        [pinned(x) for x in (src_feats, seed_rows[None], nbr_two.T, w1_self, w1_nbr, picks)],
        scratch=[
            pltpu.VMEM((1, seed_count), jnp.int32),
            pltpu.VMEM((fanout_two, seed_count), jnp.int32),
            pltpu.VMEM((fslice, width), bf16),
            pltpu.VMEM((fslice, width), bf16),
            pltpu.VMEM((n_feat, fanout_one, 1, pcap), jnp.int32),
            pltpu.SemaphoreType.DMA((7,)),
        ],
        limit=32 * MIB,
    )
    arrived = send(parcels)
    (table,) = call(
        turn_kernel,
        "turn",
        [((nodes, LANES), jnp.float32)],
        [vmem],
        (feats,),
        limit=table_bytes + 12 * MIB,
        cost_us=3,
    )
    table = table.reshape(nodes, 1, LANES)
    chunk_shape = (pcap // 4 * 3, LANES) if folds(fslice, pcap) else (pcap, fslice)

    def means(chosen, tagged=(), after=(), before=None, ins=(), outs=()):
        count = len(chosen)
        return call(
            functools.partial(
                mean_kernel,
                tuple(chosen),
                packed,
                fanout_one,
                pcap,
                fslice,
                before,
                (len(ins), len(outs)),
            ),
            "mean",
            [(chunk_shape, bf16)] * count + list(outs),
            [vmem] * len(ins) + [anywhere] + [vmem] * (1 + len(tagged)),
            (*ins, picks, table, *tagged),
            after=after,
            scratch=[
                pltpu.VMEM((count, *chunk_shape), bf16),
                pltpu.VMEM((pcap, LANES), jnp.float32),
                pltpu.SMEM((count * words[2],), jnp.int32),
                pltpu.SMEM((count,), jnp.int32),
                pltpu.SemaphoreType.DMA((count,)),
            ],
            limit=table_bytes + 8 * MIB,
            cost_us=2 * count if count > 1 else 0,
        )

    far_means = means([s + half for s in steps if s])
    tagged_shape = (chunk_shape[0] + TAG_ROWS, chunk_shape[1])
    halves, *tagged, live = call(
        functools.partial(halves_kernel, half),
        "halves",
        [
            ((half, fslice, width), bf16),
            *([(tagged_shape, bf16)] * (half - 1)),
            ((TAG_ROWS, chunk_shape[1]), bf16),
        ],
        [smem] + [vmem] * (2 * half - 1),
        (counts, *arrived, *far_means),
    )
    far_arrived = send(tagged)
    other_halves = swap(halves, "rep", 1)
    idx_rows = -(-half // 4) * n_idx
    far_own, w_nbr, pre, far_pre, idx_tags = means(
        [half],
        before=functools.partial(own_kernel, half, n_idx),
        ins=(*arrived, other_halves, bias_one[None]),
        outs=[
            ((half, fslice, width), bf16),
            ((pcap, width), jnp.float32),
            ((pcap, width), jnp.float32),
            ((idx_rows, width), bf16),
        ],
    )
    (cross,) = call(
        functools.partial(far_kernel, half),
        "far",
        [((pcap + idx_rows, width), bf16)],
        [vmem] * (half + 3),
        (*far_arrived, far_own, far_pre, w_nbr, idx_tags),
    )
    cross_arrived = swap(cross, "feat", half)
    turned = [*steps[1:-1], steps[0]]
    near_means = means(turned, [*far_arrived[1:], far_arrived[0]], (cross,))
    near_arrived = send(near_means, turned)
    near_own, near_times = means(
        [0],
        [live],
        after=(cross,),
        before=functools.partial(near_times_kernel, half, fslice, pcap, n_idx),
        ins=(w2_self, w2_nbr, *arrived),
        outs=[((half * seed_count, 4 * pcap), bf16)],
    )
    (near_pre,) = call(
        functools.partial(near_kernel, half),
        "near",
        [((pcap, width), jnp.float32)],
        [vmem] * (half + 2),
        (*near_arrived, near_own, pre, w_nbr),
        cost_us=0,
    )
    (hidden,) = call(
        hidden_kernel,
        "hidden",
        [((pcap, width), bf16)],
        [vmem] * 3,
        (live, near_pre, cross_arrived),
    )
    other_hidden = swap(hidden, "rep", 1)
    far_times, value, result = call(
        functools.partial(far_times_kernel, half, n_idx, fanout_two),
        "far_times",
        [
            ((half * seed_count, 4 * pcap), bf16),
            ((2, pcap, width), bf16),
            ((pcap, width), bf16),
        ],
        [vmem] * 4,
        (cross_arrived, hidden, w2_self, w2_nbr),
        scratch=[pltpu.SemaphoreType.DMA],
        outs=(vmem, vmem, anywhere),
    )
    shares = call(
        functools.partial(share_kernel, half, fanout_two),
        "share",
        [((2 * seed_count, width), bf16)] + [((seed_count, width), bf16)] * (2 * half - 2),
        [vmem] * 6,
        (near_times, far_times, value, other_hidden, w2_self, w2_nbr),
        scratch=[pltpu.VMEM((2, pcap, width), bf16)],
        limit=32 * MIB,
    )
    both = swap(shares[0], "feat", 1)
    others = [*steps[: half - 2], 0]
    far_shares = send(shares[1:half], others)
    near_shares = send(shares[half:], others)
    (far_sum,) = call(
        side_sum_kernel,
        "side_sum",
        [((seed_count, width), bf16)],
        [vmem] * half,
        (both, *far_shares),
    )
    (seed_out,) = call(
        last_kernel,
        "seeds",
        [((seed_count, width), bf16)],
        [vmem] * (half + 2),
        (bias_two[None], both, *near_shares, swap(far_sum, "feat", half)),
    )
    return (result[None, None], seed_out)


def solution(mesh):
    placed = (
        P("feat", "groups"),
        P("groups", "rep", None, None),
        P(("groups", "feat"), "rep"),
        P(("groups", "feat", "rep")),
        P(("groups", "feat", "rep"), None),
        P("feat", None),
        P("feat", None),
        P(),
        P(),
        P(),
        P(),
    )
    return jax.shard_map(
        body,
        mesh=mesh,
        in_specs=placed,
        out_specs=(P(("groups", "feat"), "rep", None, None), P(("groups", "feat", "rep"), None)),
        check_vma=False,
    )
```

```python
import functools

import jax
import jax.numpy as jnp
from jax import lax
from jax.experimental import pallas as pl
from jax.experimental.pallas import tpu as pltpu
from jax.sharding import PartitionSpec as P

LANES = 128
MIB = 1024 * 1024


def folds(fslice, pcap):
    return 4 * fslice == 3 * LANES and pcap % 64 == 0


def is_dense(fslice, n_idx):
    return fslice % 32 == 0 and n_idx == 16


def parcel_rows(fslice, n_idx):
    return 2 * fslice - fslice // 4 + 8 if is_dense(fslice, n_idx) else 2 * fslice


def write_parcel(ref, weight, feats, digits):
    fslice, lanes = feats.shape
    ref[:fslice, :] = weight
    if is_dense(fslice, digits.shape[0]):
        cut = fslice // 4 * 3
        tail = jnp.concatenate([feats[cut:, i : i + LANES] for i in range(0, lanes, LANES)], axis=0)
        tags = jnp.concatenate([digits[:8], digits[8:]] * 2, axis=1)
        body = jnp.concatenate([feats[:cut], tail], axis=1)
        ref[fslice:, :] = jnp.concatenate([body, tags], axis=0).astype(jnp.bfloat16)
    else:
        ref[fslice:, :lanes] = feats.astype(jnp.bfloat16)
        ref[fslice : fslice + digits.shape[0], lanes:] = digits.astype(jnp.bfloat16)


def read_feats(ref, fslice, n_idx, lanes):
    if not is_dense(fslice, n_idx):
        return ref[fslice:, :lanes].astype(jnp.float32)
    cut, part = fslice // 4 * 3, fslice // 4
    tail = ref[fslice : fslice + cut, lanes:].astype(jnp.float32)
    tail = jnp.concatenate([tail[i : i + part] for i in range(0, cut, part)], axis=1)
    return jnp.concatenate([ref[fslice : fslice + cut, :lanes].astype(jnp.float32), tail], axis=0)


def read_digits(ref, fslice, n_idx, lanes):
    if not is_dense(fslice, n_idx):
        return ref[fslice : fslice + n_idx, lanes:].astype(jnp.float32)
    tags = ref[-8:, : 2 * LANES].astype(jnp.float32)
    return jnp.concatenate([tags[:, :LANES], tags[:, LANES:]], axis=0)


TAG_ROWS = 16


def live_rows(ref):
    return jnp.max(ref[-TAG_ROWS:, :].astype(jnp.float32)).astype(jnp.int32)


def pack_kernel(
    n_feat,
    pcap,
    src_hbm,
    seed_hbm,
    nbr_hbm,
    w_self_hbm,
    w_nbr_hbm,
    pick_hbm,
    *refs,
):
    half = n_feat // 2
    parcel_refs, pick_ref, src_ref = refs[:half], refs[half], refs[half + 1]
    seed_ref, nbr_ref, w_self_ref, w_nbr_ref, fetched_ref, sems = refs[half + 2 :]
    owned = n_feat * 2 * pcap
    first, rest = pl.ds(0, owned), pl.ds(owned, src_ref.shape[1] - owned)
    copies = [
        pltpu.make_async_copy(a, b, sems.at[i])
        for i, (a, b) in enumerate(
            (
                (src_hbm.at[:, first], src_ref.at[:, first]),
                (w_self_hbm, w_self_ref),
                (w_nbr_hbm, w_nbr_ref),
                (seed_hbm, seed_ref),
                (nbr_hbm, nbr_ref),
                (pick_hbm, fetched_ref),
                (src_hbm.at[:, rest], src_ref.at[:, rest]),
            )
        )
    ]
    for copy in copies:
        copy.start()
    for copy in copies[1:-1]:
        copy.wait()
    stride = -(-pcap // LANES) * LANES
    words = pick_ref.shape[2] // stride
    for k in range(words):
        word = fetched_ref[:, k]
        if words < fetched_ref.shape[1]:
            word = word | (fetched_ref[:, words + k] << 16)
        pick_ref[:, :, k * stride : k * stride + pcap] = word
    feat_pos = lax.axis_index("feat")
    first_core = lax.axis_index("rep") == 0
    idx = jnp.concatenate([seed_ref[...], nbr_ref[...]], axis=0)
    high = lax.shift_right_logical(idx, 7)
    digits = jnp.concatenate([high, idx - high * 128], axis=1).astype(jnp.float32)
    weight = jnp.where(first_core, w_self_ref[...], w_nbr_ref[...])
    copies[0].wait()
    for s, parcel_ref in enumerate(reversed(parcel_refs)):
        sides = []
        for step in (s, s ^ half):
            at = pl.multiple_of(jnp.bitwise_xor(feat_pos, step) * (2 * pcap), LANES)
            block = src_ref[:, pl.ds(at, 2 * pcap)].astype(jnp.float32)
            sides.append(jnp.where(first_core, block[:, :pcap], block[:, pcap:]))
        write_parcel(parcel_ref, weight, jnp.concatenate(sides, axis=1), digits)
    copies[-1].wait()


def turn_kernel(src_ref, table_ref):
    fslice, nodes = src_ref.shape
    width = 2048 if nodes % 2048 == 0 else 512

    def turn(step, carry):
        at = pl.multiple_of(step * width, width)
        table_ref[pl.ds(at, width), :fslice] = src_ref[:, pl.ds(at, width)].T.astype(jnp.float32)
        return carry

    lax.fori_loop(0, nodes // width, turn, 0)


def mean_kernel(chosen, packed, fanout, pcap, fslice, before, n_before, *refs):
    count = len(chosen)
    before_in, refs = refs[: n_before[0]], refs[n_before[0] :]
    nbr_any, table_ref, *refs = refs
    out_ref, total, nbr_ref, live_ref, sems = refs[-5:]
    refs = refs[:-5]
    before_out = refs[len(refs) - n_before[1] :]
    refs = refs[: len(refs) - n_before[1]]
    chunk_refs, tagged_refs = refs[len(refs) - count :], refs[: len(refs) - count]
    feat_pos = lax.axis_index("feat")
    words = fanout // packed
    stride = -(-pcap // LANES) * LANES
    length = words * stride
    copies = [
        pltpu.make_async_copy(
            nbr_any.at[feat_pos ^ step, 0], nbr_ref.at[pl.ds(i * length, length)], sems.at[i]
        )
        for i, step in enumerate(chosen)
    ]
    for copy in copies:
        copy.start()
    for i in range(count):
        live_ref[i] = pcap
    for i, ref in enumerate(tagged_refs):
        live_ref[i] = live_rows(ref)
    if before is not None:
        before(*before_in, *before_out)
    for copy in copies:
        copy.wait()

    def partition(i, carry):
        first = i * length

        def group(g, inner):
            at = pl.multiple_of(g * 16, 16)
            start = first + at
            sums = []
            for u in range(16):
                names = [nbr_ref[start + (k * stride + u)] for k in range(words)]
                if packed == 2:
                    names = [
                        part
                        for name in names
                        for part in (name & 0xFFFF, lax.shift_right_logical(name, 16))
                    ]
                rows = [table_ref[name] for name in names]
                while len(rows) > 1:
                    rows = [a + b for a, b in zip(rows[::2], rows[1::2])] + (
                        [rows[-1]] if len(rows) % 2 else []
                    )
                sums.append(rows[0])
            for u, row in enumerate(sums):
                total[pl.ds(at + u, 1), :] = row
            return inner

        lax.fori_loop(0, lax.div(live_ref[i] + 15, 16), group, 0)
        mean = total[...] / fanout
        if folds(fslice, pcap):
            part = pcap // 4
            lane = lax.broadcasted_iota(jnp.int32, (part, LANES), 1)
            tail = mean[3 * part :]
            for b in range(3):
                shift = (fslice - 32 * b) % LANES
                moved = pltpu.roll(tail, shift, 1) if shift else tail
                out_ref[i, pl.ds(b * part, part), :] = jnp.where(
                    lane < fslice, mean[b * part : (b + 1) * part], moved
                ).astype(jnp.bfloat16)
        else:
            out_ref[i] = mean[:, :fslice].astype(jnp.bfloat16)
        return carry

    lax.fori_loop(0, count, partition, 0)
    for i, ref in enumerate(chunk_refs):
        ref[...] = out_ref[i]


def unfold(ref, fslice, pcap):
    if not folds(fslice, pcap):
        return ref[:pcap, :]
    part = pcap // 4
    wide = ref[: 3 * part, :].astype(jnp.float32)
    lane = lax.broadcasted_iota(jnp.int32, (part, LANES), 1)
    tail = pltpu.roll(wide[:part], LANES - fslice, 1)
    for b in (1, 2):
        shift = (32 * b - fslice) % LANES
        moved = wide[b * part : (b + 1) * part]
        moved = pltpu.roll(moved, shift, 1) if shift else moved
        tail = jnp.where(lane // 32 == b, moved, tail)
    return jnp.concatenate([wide, tail], axis=0)[:, :fslice].astype(jnp.bfloat16)


def halves_kernel(half, count_ref, *refs):
    parcel_refs, chunk_refs = refs[:half], refs[half : 2 * half - 1]
    out_ref, *tagged_refs, live_ref = refs[2 * half - 1 :]
    for s, ref in enumerate(parcel_refs):
        out_ref[s] = ref[: out_ref.shape[1], :]
    live = jnp.full(live_ref.shape, count_ref[0, 0].astype(jnp.float32)).astype(jnp.bfloat16)
    live_ref[...] = live
    for chunk_ref, ref in zip(chunk_refs, tagged_refs):
        ref[:-TAG_ROWS, :] = chunk_ref[...]
        ref[-TAG_ROWS:, :] = live


def own_kernel(half, n_idx, *refs):
    parcel_refs = refs[:half]
    other_ref, bias_ref, w_ref, pre_ref, far_ref, idx_ref = refs[half:]
    fslice = w_ref.shape[1]
    pcap, width = pre_ref.shape
    first_core = lax.axis_index("rep") == 0
    feats, weights = [], []
    for s in range(half):
        mine, other = parcel_refs[s][:fslice, :], other_ref[s]
        w_ref[s] = jnp.where(first_core, other, mine)
        weights.append(jnp.where(first_core, mine, other))
        feats.append(read_feats(parcel_refs[s], fslice, n_idx, 2 * pcap))
        rows = pl.ds(s // 4 * n_idx, n_idx)
        digits = read_digits(parcel_refs[s], fslice, n_idx, 2 * pcap)
        idx_ref[rows, s % 4 * LANES : (s % 4 + 1) * LANES] = digits.astype(jnp.bfloat16)
    both = jnp.dot(
        jnp.concatenate(feats, axis=0).T.astype(jnp.bfloat16),
        jnp.concatenate(weights, axis=0),
        preferred_element_type=jnp.float32,
    )
    pre_ref[...] = both[:pcap] + bias_ref[...]
    far_ref[...] = both[pcap:]


def add_means(pre, mean_refs, w_ref):
    for s, ref in enumerate(mean_refs):
        pre = pre + jnp.dot(
            unfold(ref, w_ref.shape[1], pre.shape[0]),
            w_ref[s],
            preferred_element_type=jnp.float32,
        )
    return pre


def far_kernel(half, *refs):
    far_ref, w_ref, cross_ref = refs[half:]
    cross_ref[...] = add_means(far_ref[...], refs[:half], w_ref).astype(jnp.bfloat16)


def copy_kernel(in_ref, out_ref):
    out_ref[...] = in_ref[...]


def store_times(pcap, blocks, out_ref):
    n_idx, pair = blocks[0].shape
    seed_count = pair // 2
    core_rows = lax.axis_index("feat") * (2 * pcap)
    rep_pos = lax.axis_index("rep")
    row = lax.broadcasted_iota(jnp.int32, (2 * pcap, pair), 0)
    slot = jnp.where(
        row < pcap, row + core_rows + rep_pos * pcap, row + core_rows - rep_pos * pcap
    ).astype(jnp.float32)
    low = lax.broadcasted_iota(jnp.int32, (n_idx, pair), 1) < seed_count
    for s in range(0, len(blocks), 2):
        first, second = blocks[s].astype(jnp.float32), blocks[s + 1].astype(jnp.float32)
        high_part = jnp.where(low, first, pltpu.roll(second, seed_count, 1))
        low_part = jnp.where(low, pltpu.roll(first, seed_count, 1), second)
        name = high_part * 128.0 + low_part
        own = jnp.where(slot == name[:1], 1.0, 0.0)
        near = jnp.zeros((2 * pcap, pair), jnp.float32)
        for k in range(1, n_idx):
            near = near + jnp.where(slot == name[k : k + 1], 1.0, 0.0)
        place = pl.ds(s * seed_count, pair)
        for core in range(2):
            rows = slice(core * pcap, (core + 1) * pcap)
            counts = jnp.concatenate([own[rows], near[rows]], axis=0)
            lanes = slice(2 * core * pcap, 2 * (core + 1) * pcap)
            out_ref[place, lanes] = counts.T.astype(jnp.bfloat16)


def near_times_kernel(half, fslice, pcap, n_idx, _, __, *refs):
    blocks = [read_digits(ref, fslice, n_idx, 2 * pcap) for ref in refs[:half]]
    store_times(pcap, blocks, refs[half])


def far_times_kernel(half, pcap, n_idx, idx_ref, out_ref):
    blocks = [
        idx_ref[pl.ds(s // 4 * n_idx, n_idx), s % 4 * LANES : (s % 4 + 1) * LANES]
        for s in range(half)
    ]
    store_times(pcap, blocks, out_ref)


def values_of(hidden, ws_ref, wn_ref, fanout_two):
    return jnp.concatenate(
        [
            jnp.dot(hidden, ws_ref[...], preferred_element_type=jnp.float32),
            jnp.dot(hidden, wn_ref[...], preferred_element_type=jnp.float32) / fanout_two,
        ],
        axis=0,
    ).astype(jnp.bfloat16)


def own_share_kernel(
    fanout_two, near_ref, far_ref, hidden_ref, ws_ref, wn_ref, part_ref, result_ref, sem
):
    copy = pltpu.make_async_copy(hidden_ref, result_ref, sem)
    copy.start()
    values = values_of(hidden_ref[...], ws_ref, wn_ref, fanout_two)
    lanes = values.shape[0]
    for i, ref in enumerate((far_ref, near_ref)):
        part_ref[i] = jnp.dot(ref[:, :lanes], values, preferred_element_type=jnp.float32)
    copy.wait()


def near_kernel(half, *refs):
    pre_ref, w_ref, out_ref = refs[half:]
    out_ref[...] = add_means(pre_ref[...], refs[:half], w_ref)


def hidden_kernel(live_ref, pre_ref, cross_ref, hidden_ref):
    pcap, width = hidden_ref.shape
    pre = pre_ref[...] + cross_ref[:pcap, :].astype(jnp.float32)
    live = lax.broadcasted_iota(jnp.int32, (pcap, width), 0) < live_rows(live_ref)
    hidden_ref[...] = jnp.where(live, jnp.maximum(pre, 0.0), 0.0).astype(jnp.bfloat16)


def share_kernel(half, fanout_two, near_ref, far_ref, part_ref, hidden_ref, ws_ref, wn_ref, *refs):
    values = values_of(hidden_ref[...], ws_ref, wn_ref, fanout_two)
    lanes = values.shape[0]
    for i, ref in enumerate((far_ref, near_ref)):
        part = part_ref[i] + jnp.dot(ref[:, lanes:], values, preferred_element_type=jnp.float32)
        rows = part.shape[0] // half
        for s, out_ref in enumerate(refs[i * half : (i + 1) * half]):
            out_ref[...] = part[s * rows : (s + 1) * rows].astype(jnp.bfloat16)


def side_sum_kernel(*refs):
    total = refs[0][...].astype(jnp.float32)
    for ref in refs[1:-1]:
        total = total + ref[...].astype(jnp.float32)
    refs[-1][...] = total.astype(jnp.bfloat16)


def last_kernel(bias_ref, *refs):
    total = bias_ref[...]
    for ref in refs[:-1]:
        total = total + ref[...].astype(jnp.float32)
    refs[-1][...] = jnp.maximum(total, 0.0).astype(jnp.bfloat16)


def swap(value, axis, step):
    size = lax.axis_size(axis)
    return lax.ppermute(value, axis, [(i, i ^ step) for i in range(size)])


def body(
    src_feats,
    nbr_one,
    counts,
    seed_rows,
    nbr_two,
    w1_self,
    w1_nbr,
    bias_one,
    w2_self,
    w2_nbr,
    bias_two,
):
    n_feat = lax.axis_size("feat")
    half = n_feat // 2
    steps = range(half - 1, -1, -1)
    fslice, nodes = src_feats.shape
    fanout_one, pcap = nbr_one.shape[2:]
    width = w1_self.shape[1]
    seed_count, fanout_two = nbr_two.shape
    n_idx = fanout_two + 1
    bf16 = jnp.bfloat16
    vmem = pl.BlockSpec(memory_space=pltpu.VMEM)
    smem = pl.BlockSpec(memory_space=pltpu.SMEM)
    hbm = pl.BlockSpec(memory_space=pltpu.HBM)
    anywhere = pl.BlockSpec(memory_space=pl.ANY)
    table_bytes = nodes * LANES * 4

    def call(kernel, name, shapes, ins, args, after=(), scratch=(), limit=16 * MIB, cost_us=1, outs=None):
        def wrapped(*refs):
            kernel(*refs[: len(args)], *refs[len(args) + len(after) :])

        return pl.pallas_call(
            wrapped,
            out_shape=tuple(jax.ShapeDtypeStruct(shape, dtype) for shape, dtype in shapes),
            in_specs=[*ins, *([anywhere] * len(after))],
            out_specs=outs or (vmem,) * len(shapes),
            scratch_shapes=scratch,
            compiler_params=pltpu.CompilerParams(vmem_limit_bytes=limit),
            cost_estimate=pl.CostEstimate(
                flops=int(cost_us * 1_100_000_000), bytes_accessed=0, transcendentals=0
            ),
            name=name,
        )(*args, *after)

    def pinned(value):
        return pltpu.with_memory_space_constraint(value, pltpu.HBM)

    def send(chunks):
        return [swap(chunk, "feat", s) if s else chunk for s, chunk in zip(steps, chunks)]

    picks = jnp.transpose(nbr_one, (0, 2, 1, 3))
    packed = 2 if fanout_one % 2 == 0 and nodes <= 1 << 16 else 1
    words = (n_feat, 1, fanout_one // packed * (-(-pcap // LANES) * LANES))
    *parcels, picks, feats = call(
        functools.partial(pack_kernel, n_feat, pcap),
        "pack",
        [((parcel_rows(fslice, n_idx), width), bf16)] * half
        + [(words, jnp.int32), ((fslice, nodes), bf16)],
        [hbm] * 6,
        [pinned(x) for x in (src_feats, seed_rows[None], nbr_two.T, w1_self, w1_nbr, picks)],
        scratch=[
            pltpu.VMEM((1, seed_count), jnp.int32),
            pltpu.VMEM((fanout_two, seed_count), jnp.int32),
            pltpu.VMEM((fslice, width), bf16),
            pltpu.VMEM((fslice, width), bf16),
            pltpu.VMEM((n_feat, fanout_one, 1, pcap), jnp.int32),
            pltpu.SemaphoreType.DMA((7,)),
        ],
        limit=32 * MIB,
    )
    arrived = send(parcels)
    (table,) = call(
        turn_kernel,
        "turn",
        [((nodes, LANES), jnp.float32)],
        [vmem],
        (feats,),
        limit=table_bytes + 12 * MIB,
        cost_us=3,
    )
    table = table.reshape(nodes, 1, LANES)
    chunk_shape = (pcap // 4 * 3, LANES) if folds(fslice, pcap) else (pcap, fslice)

    def means(chosen, tagged=(), after=(), before=None, ins=(), outs=()):
        count = len(chosen)
        return call(
            functools.partial(
                mean_kernel,
                tuple(chosen),
                packed,
                fanout_one,
                pcap,
                fslice,
                before,
                (len(ins), len(outs)),
            ),
            "mean",
            [(chunk_shape, bf16)] * count + list(outs),
            [vmem] * len(ins) + [anywhere] + [vmem] * (1 + len(tagged)),
            (*ins, picks, table, *tagged),
            after=after,
            scratch=[
                pltpu.VMEM((count, *chunk_shape), bf16),
                pltpu.VMEM((pcap, LANES), jnp.float32),
                pltpu.SMEM((count * words[2],), jnp.int32),
                pltpu.SMEM((count,), jnp.int32),
                pltpu.SemaphoreType.DMA((count,)),
            ],
            limit=table_bytes + 8 * MIB,
            cost_us=2 * count if count > 1 else 0,
        )

    far_means = means([s + half for s in steps if s])
    tagged_shape = (chunk_shape[0] + TAG_ROWS, chunk_shape[1])
    halves, *tagged, live = call(
        functools.partial(halves_kernel, half),
        "halves",
        [
            ((half, fslice, width), bf16),
            *([(tagged_shape, bf16)] * (half - 1)),
            ((TAG_ROWS, chunk_shape[1]), bf16),
        ],
        [smem] + [vmem] * (2 * half - 1),
        (counts, *arrived, *far_means),
    )
    far_arrived = send(tagged)
    other_halves = swap(halves, "rep", 1)
    idx_rows = -(-half // 4) * n_idx
    far_own, w_nbr, pre, far_pre, idx_tags = means(
        [half],
        before=functools.partial(own_kernel, half, n_idx),
        ins=(*arrived, other_halves, bias_one[None]),
        outs=[
            ((half, fslice, width), bf16),
            ((pcap, width), jnp.float32),
            ((pcap, width), jnp.float32),
            ((idx_rows, width), bf16),
        ],
    )
    (cross,) = call(
        functools.partial(far_kernel, half),
        "far",
        [((pcap, width), bf16)],
        [vmem] * (half + 2),
        (*far_arrived, far_own, far_pre, w_nbr),
    )
    cross_arrived = swap(cross, "feat", half)
    *near_means, idx_tags = means(
        [s for s in steps if s],
        far_arrived,
        (cross,),
        before=copy_kernel,
        ins=(idx_tags,),
        outs=[((idx_rows, width), bf16)],
    )
    near_arrived = send(near_means)
    idx_arrived = swap(idx_tags, "feat", half)
    near_own, near_times = means(
        [0],
        [live],
        after=(cross,),
        before=functools.partial(near_times_kernel, half, fslice, pcap, n_idx),
        ins=(w2_self, w2_nbr, *arrived),
        outs=[((half * seed_count, 4 * pcap), bf16)],
    )
    (far_times,) = call(
        functools.partial(far_times_kernel, half, pcap, n_idx),
        "far_times",
        [((half * seed_count, 4 * pcap), bf16)],
        [vmem],
        (idx_arrived,),
        after=(near_own,),
        cost_us=0,
    )
    (near_pre,) = call(
        functools.partial(near_kernel, half),
        "near",
        [((pcap, width), jnp.float32)],
        [vmem] * (half + 2),
        (*near_arrived, near_own, pre, w_nbr),
        after=(far_times,),
        cost_us=0,
    )
    (hidden,) = call(
        hidden_kernel,
        "hidden",
        [((pcap, width), bf16)],
        [vmem] * 3,
        (live, near_pre, cross_arrived),
    )
    other_hidden = swap(hidden, "rep", 1)
    own_part, result = call(
        functools.partial(own_share_kernel, fanout_two),
        "own_share",
        [((2, half * seed_count, width), jnp.float32), ((pcap, width), bf16)],
        [vmem] * 5,
        (near_times, far_times, hidden, w2_self, w2_nbr),
        scratch=[pltpu.SemaphoreType.DMA],
        outs=(vmem, anywhere),
    )
    shares = call(
        functools.partial(share_kernel, half, fanout_two),
        "share",
        [((seed_count, width), bf16)] * (2 * half),
        [vmem] * 6,
        (near_times, far_times, own_part, other_hidden, w2_self, w2_nbr),
        limit=32 * MIB,
    )
    far_shares = send(shares[:half])
    near_shares = send(shares[half:])
    (far_sum,) = call(
        side_sum_kernel, "side_sum", [((seed_count, width), bf16)], [vmem] * half, far_shares
    )
    (seed_out,) = call(
        last_kernel,
        "seeds",
        [((seed_count, width), bf16)],
        [vmem] * (half + 2),
        (bias_two[None], *near_shares, swap(far_sum, "feat", half)),
    )
    return (result[None, None], seed_out)


def solution(mesh):
    placed = (
        P("feat", "groups"),
        P("groups", "rep", None, None),
        P(("groups", "feat"), "rep"),
        P(("groups", "feat", "rep")),
        P(("groups", "feat", "rep"), None),
        P("feat", None),
        P("feat", None),
        P(),
        P(),
        P(),
        P(),
    )
    return jax.shard_map(
        body,
        mesh=mesh,
        in_specs=placed,
        out_specs=(P(("groups", "feat"), "rep", None, None), P(("groups", "feat", "rep"), None)),
        check_vma=False,
    )
```

```python
import functools

import jax
import jax.numpy as jnp
from jax import lax
from jax.experimental import pallas as pl
from jax.experimental.pallas import tpu as pltpu
from jax.sharding import PartitionSpec as P

LANES = 128
MIB = 1024 * 1024


def folds(fslice, pcap):
    return 4 * fslice == 3 * LANES and pcap % 64 == 0


def is_dense(fslice, n_idx):
    return fslice % 32 == 0 and n_idx == 16


def parcel_rows(fslice, n_idx):
    return 2 * fslice - fslice // 4 + 8 if is_dense(fslice, n_idx) else 2 * fslice


def write_parcel(ref, weight, feats, digits):
    fslice, lanes = feats.shape
    ref[:fslice, :] = weight
    if is_dense(fslice, digits.shape[0]):
        cut = fslice // 4 * 3
        tail = jnp.concatenate([feats[cut:, i : i + LANES] for i in range(0, lanes, LANES)], axis=0)
        tags = jnp.concatenate([digits[:8], digits[8:]] * 2, axis=1)
        body = jnp.concatenate([feats[:cut], tail], axis=1)
        ref[fslice:, :] = jnp.concatenate([body, tags], axis=0).astype(jnp.bfloat16)
    else:
        ref[fslice:, :lanes] = feats.astype(jnp.bfloat16)
        ref[fslice : fslice + digits.shape[0], lanes:] = digits.astype(jnp.bfloat16)


def read_feats(ref, fslice, n_idx, lanes):
    if not is_dense(fslice, n_idx):
        return ref[fslice:, :lanes].astype(jnp.float32)
    cut, part = fslice // 4 * 3, fslice // 4
    tail = ref[fslice : fslice + cut, lanes:].astype(jnp.float32)
    tail = jnp.concatenate([tail[i : i + part] for i in range(0, cut, part)], axis=1)
    return jnp.concatenate([ref[fslice : fslice + cut, :lanes].astype(jnp.float32), tail], axis=0)


def read_digits(ref, fslice, n_idx, lanes):
    if not is_dense(fslice, n_idx):
        return ref[fslice : fslice + n_idx, lanes:].astype(jnp.float32)
    tags = ref[-8:, : 2 * LANES].astype(jnp.float32)
    return jnp.concatenate([tags[:, :LANES], tags[:, LANES:]], axis=0)


TAG_ROWS = 16


def live_rows(ref):
    return jnp.max(ref[-TAG_ROWS:, :].astype(jnp.float32)).astype(jnp.int32)


def pack_kernel(
    n_feat,
    pcap,
    src_hbm,
    seed_hbm,
    nbr_hbm,
    w_self_hbm,
    w_nbr_hbm,
    pick_hbm,
    *refs,
):
    half = n_feat // 2
    parcel_refs, pick_ref, src_ref = refs[:half], refs[half], refs[half + 1]
    seed_ref, nbr_ref, w_self_ref, w_nbr_ref, fetched_ref, sems = refs[half + 2 :]
    owned = n_feat * 2 * pcap
    first, rest = pl.ds(0, owned), pl.ds(owned, src_ref.shape[1] - owned)
    copies = [
        pltpu.make_async_copy(a, b, sems.at[i])
        for i, (a, b) in enumerate(
            (
                (src_hbm.at[:, first], src_ref.at[:, first]),
                (w_self_hbm, w_self_ref),
                (w_nbr_hbm, w_nbr_ref),
                (seed_hbm, seed_ref),
                (nbr_hbm, nbr_ref),
                (pick_hbm, fetched_ref),
                (src_hbm.at[:, rest], src_ref.at[:, rest]),
            )
        )
    ]
    for copy in copies:
        copy.start()
    for copy in copies[1:-1]:
        copy.wait()
    stride = -(-pcap // LANES) * LANES
    words = pick_ref.shape[2] // stride
    for k in range(words):
        word = fetched_ref[:, k]
        if words < fetched_ref.shape[1]:
            word = word | (fetched_ref[:, words + k] << 16)
        pick_ref[:, :, k * stride : k * stride + pcap] = word
    feat_pos = lax.axis_index("feat")
    first_core = lax.axis_index("rep") == 0
    idx = jnp.concatenate([seed_ref[...], nbr_ref[...]], axis=0)
    high = lax.shift_right_logical(idx, 7)
    digits = jnp.concatenate([high, idx - high * 128], axis=1).astype(jnp.float32)
    weight = jnp.where(first_core, w_self_ref[...], w_nbr_ref[...])
    copies[0].wait()
    for s, parcel_ref in enumerate(reversed(parcel_refs)):
        sides = []
        for step in (s, s ^ half):
            at = pl.multiple_of(jnp.bitwise_xor(feat_pos, step) * (2 * pcap), LANES)
            block = src_ref[:, pl.ds(at, 2 * pcap)].astype(jnp.float32)
            sides.append(jnp.where(first_core, block[:, :pcap], block[:, pcap:]))
        write_parcel(parcel_ref, weight, jnp.concatenate(sides, axis=1), digits)
    copies[-1].wait()


def turn_kernel(src_ref, table_ref):
    fslice, nodes = src_ref.shape
    width = 2048 if nodes % 2048 == 0 else 512

    def turn(step, carry):
        at = pl.multiple_of(step * width, width)
        table_ref[pl.ds(at, width), :fslice] = src_ref[:, pl.ds(at, width)].T.astype(jnp.float32)
        return carry

    lax.fori_loop(0, nodes // width, turn, 0)


def mean_kernel(chosen, packed, fanout, pcap, fslice, before, n_before, *refs):
    count = len(chosen)
    before_in, refs = refs[: n_before[0]], refs[n_before[0] :]
    nbr_any, table_ref, *refs = refs
    out_ref, total, nbr_ref, live_ref, sems = refs[-5:]
    refs = refs[:-5]
    before_out = refs[len(refs) - n_before[1] :]
    refs = refs[: len(refs) - n_before[1]]
    chunk_refs, tagged_refs = refs[len(refs) - count :], refs[: len(refs) - count]
    feat_pos = lax.axis_index("feat")
    words = fanout // packed
    stride = -(-pcap // LANES) * LANES
    length = words * stride
    copies = [
        pltpu.make_async_copy(
            nbr_any.at[feat_pos ^ step, 0], nbr_ref.at[pl.ds(i * length, length)], sems.at[i]
        )
        for i, step in enumerate(chosen)
    ]
    for copy in copies:
        copy.start()
    for i in range(count):
        live_ref[i] = pcap
    for i, ref in enumerate(tagged_refs):
        live_ref[i] = live_rows(ref)
    if before is not None:
        before(*before_in, *before_out)
    for copy in copies:
        copy.wait()

    def partition(i, carry):
        first = i * length

        def group(g, inner):
            at = pl.multiple_of(g * 16, 16)
            start = first + at
            sums = []
            for u in range(16):
                names = [nbr_ref[start + (k * stride + u)] for k in range(words)]
                if packed == 2:
                    names = [
                        part
                        for name in names
                        for part in (name & 0xFFFF, lax.shift_right_logical(name, 16))
                    ]
                rows = [table_ref[name] for name in names]
                while len(rows) > 1:
                    rows = [a + b for a, b in zip(rows[::2], rows[1::2])] + (
                        [rows[-1]] if len(rows) % 2 else []
                    )
                sums.append(rows[0])
            for u, row in enumerate(sums):
                total[pl.ds(at + u, 1), :] = row
            return inner

        lax.fori_loop(0, lax.div(live_ref[i] + 15, 16), group, 0)
        mean = total[...] / fanout
        if folds(fslice, pcap):
            part = pcap // 4
            lane = lax.broadcasted_iota(jnp.int32, (part, LANES), 1)
            tail = mean[3 * part :]
            for b in range(3):
                shift = (fslice - 32 * b) % LANES
                moved = pltpu.roll(tail, shift, 1) if shift else tail
                out_ref[i, pl.ds(b * part, part), :] = jnp.where(
                    lane < fslice, mean[b * part : (b + 1) * part], moved
                ).astype(jnp.bfloat16)
        else:
            out_ref[i] = mean[:, :fslice].astype(jnp.bfloat16)
        return carry

    lax.fori_loop(0, count, partition, 0)
    for i, ref in enumerate(chunk_refs):
        ref[...] = out_ref[i]


def unfold(ref, fslice, pcap):
    if not folds(fslice, pcap):
        return ref[:pcap, :]
    part = pcap // 4
    wide = ref[: 3 * part, :].astype(jnp.float32)
    lane = lax.broadcasted_iota(jnp.int32, (part, LANES), 1)
    tail = pltpu.roll(wide[:part], LANES - fslice, 1)
    for b in (1, 2):
        shift = (32 * b - fslice) % LANES
        moved = wide[b * part : (b + 1) * part]
        moved = pltpu.roll(moved, shift, 1) if shift else moved
        tail = jnp.where(lane // 32 == b, moved, tail)
    return jnp.concatenate([wide, tail], axis=0)[:, :fslice].astype(jnp.bfloat16)


def halves_kernel(half, count_ref, *refs):
    parcel_refs, chunk_refs = refs[:half], refs[half : 2 * half - 1]
    out_ref, *tagged_refs, live_ref = refs[2 * half - 1 :]
    for s, ref in enumerate(parcel_refs):
        out_ref[s] = ref[: out_ref.shape[1], :]
    live = jnp.full(live_ref.shape, count_ref[0, 0].astype(jnp.float32)).astype(jnp.bfloat16)
    live_ref[...] = live
    for chunk_ref, ref in zip(chunk_refs, tagged_refs):
        ref[:-TAG_ROWS, :] = chunk_ref[...]
        ref[-TAG_ROWS:, :] = live


def own_kernel(half, n_idx, *refs):
    parcel_refs = refs[:half]
    other_ref, bias_ref, w_ref, pre_ref, far_ref, idx_ref = refs[half:]
    fslice = w_ref.shape[1]
    pcap, width = pre_ref.shape
    first_core = lax.axis_index("rep") == 0
    feats, weights = [], []
    for s in range(half):
        mine, other = parcel_refs[s][:fslice, :], other_ref[s]
        w_ref[s] = jnp.where(first_core, other, mine)
        weights.append(jnp.where(first_core, mine, other))
        feats.append(read_feats(parcel_refs[s], fslice, n_idx, 2 * pcap))
        rows = pl.ds(s // 4 * n_idx, n_idx)
        digits = read_digits(parcel_refs[s], fslice, n_idx, 2 * pcap)
        idx_ref[rows, s % 4 * LANES : (s % 4 + 1) * LANES] = digits.astype(jnp.bfloat16)
    both = jnp.dot(
        jnp.concatenate(feats, axis=0).T.astype(jnp.bfloat16),
        jnp.concatenate(weights, axis=0),
        preferred_element_type=jnp.float32,
    )
    pre_ref[...] = both[:pcap] + bias_ref[...]
    far_ref[...] = both[pcap:]


def add_means(half, pre, mean_refs, w_ref, turn=0):
    for s, ref in enumerate(mean_refs):
        pre = pre + jnp.dot(
            unfold(ref, w_ref.shape[1], pre.shape[0]),
            w_ref[(s + turn) % (half - 1) if s < half - 1 else s],
            preferred_element_type=jnp.float32,
        )
    return pre


def far_kernel(half, *refs):
    far_ref, w_ref, idx_ref, cross_ref = refs[half:]
    pcap = far_ref.shape[0]
    cross_ref[:pcap, :] = add_means(half, far_ref[...], refs[:half], w_ref).astype(jnp.bfloat16)
    cross_ref[pcap:, :] = idx_ref[...]


def store_times(pcap, blocks, out_ref):
    n_idx, pair = blocks[0].shape
    seed_count = pair // 2
    core_rows = lax.axis_index("feat") * (2 * pcap)
    rep_pos = lax.axis_index("rep")
    row = lax.broadcasted_iota(jnp.int32, (2 * pcap, pair), 0)
    slot = jnp.where(
        row < pcap, row + core_rows + rep_pos * pcap, row + core_rows - rep_pos * pcap
    ).astype(jnp.float32)
    low = lax.broadcasted_iota(jnp.int32, (n_idx, pair), 1) < seed_count
    for s in range(0, len(blocks), 2):
        first, second = blocks[s].astype(jnp.float32), blocks[s + 1].astype(jnp.float32)
        high_part = jnp.where(low, first, pltpu.roll(second, seed_count, 1))
        low_part = jnp.where(low, pltpu.roll(first, seed_count, 1), second)
        name = high_part * 128.0 + low_part
        own = jnp.where(slot == name[:1], 1.0, 0.0)
        near = jnp.zeros((2 * pcap, pair), jnp.float32)
        for k in range(1, n_idx):
            near = near + jnp.where(slot == name[k : k + 1], 1.0, 0.0)
        place = pl.ds(s * seed_count, pair)
        out_ref[place, : 2 * pcap] = own.T.astype(jnp.bfloat16)
        out_ref[place, 2 * pcap :] = near.T.astype(jnp.bfloat16)


def near_times_kernel(half, fslice, pcap, n_idx, _, __, *refs):
    blocks = [read_digits(ref, fslice, n_idx, 2 * pcap) for ref in refs[:half]]
    store_times(pcap, blocks, refs[half])


def far_times_kernel(
    half,
    n_idx,
    fanout_two,
    cross_ref,
    hidden_ref,
    ws_ref,
    wn_ref,
    out_ref,
    value_ref,
    result_ref,
    sem,
):
    copy = pltpu.make_async_copy(hidden_ref, result_ref, sem)
    copy.start()
    pcap = hidden_ref.shape[0]
    blocks = [
        cross_ref[
            pl.ds(pcap + s // 4 * n_idx, n_idx), s % 4 * LANES : (s % 4 + 1) * LANES
        ]
        for s in range(half)
    ]
    store_times(pcap, blocks, out_ref)
    store_values(hidden_ref[...], ws_ref, wn_ref, fanout_two, value_ref)
    copy.wait()


def store_values(hidden, ws_ref, wn_ref, fanout_two, value_ref):
    value_ref[0] = jnp.dot(hidden, ws_ref[...], preferred_element_type=jnp.float32).astype(
        jnp.bfloat16
    )
    value_ref[1] = (
        jnp.dot(hidden, wn_ref[...], preferred_element_type=jnp.float32) / fanout_two
    ).astype(jnp.bfloat16)


def near_kernel(half, *refs):
    pre_ref, w_ref, out_ref = refs[half:]
    out_ref[...] = add_means(half, pre_ref[...], refs[:half], w_ref, 1)


def hidden_kernel(live_ref, pre_ref, cross_ref, hidden_ref):
    pcap, width = hidden_ref.shape
    pre = pre_ref[...] + cross_ref[:pcap, :].astype(jnp.float32)
    live = lax.broadcasted_iota(jnp.int32, (pcap, width), 0) < live_rows(live_ref)
    hidden_ref[...] = jnp.where(live, jnp.maximum(pre, 0.0), 0.0).astype(jnp.bfloat16)


def far_share_kernel(
    half, fanout_two, far_ref, value_ref, hidden_ref, ws_ref, wn_ref, *refs
):
    *out_refs, values_ref = refs
    pcap = hidden_ref.shape[0]
    for i in range(2):
        values_ref[2 * i * pcap : (2 * i + 1) * pcap, :] = value_ref[i]
    hidden = hidden_ref[...]
    values_ref[pcap : 2 * pcap, :] = jnp.dot(
        hidden, ws_ref[...], preferred_element_type=jnp.float32
    ).astype(jnp.bfloat16)
    values_ref[3 * pcap :, :] = (
        jnp.dot(hidden, wn_ref[...], preferred_element_type=jnp.float32) / fanout_two
    ).astype(jnp.bfloat16)
    store_shares(far_ref, values_ref, out_refs)


def store_shares(times_ref, values_ref, out_refs):
    rows = times_ref.shape[0] // len(out_refs)
    part = jnp.dot(times_ref[...], values_ref[...], preferred_element_type=jnp.float32)
    for s, ref in enumerate(out_refs):
        ref[...] = part[s * rows : (s + 1) * rows].astype(jnp.bfloat16)


def near_share_kernel(near_ref, values_ref, *out_refs):
    store_shares(near_ref, values_ref, out_refs)


def side_sum_kernel(*refs):
    total = refs[0][...].astype(jnp.float32)
    for ref in refs[1:-1]:
        total = total + ref[...].astype(jnp.float32)
    refs[-1][...] = total.astype(jnp.bfloat16)


def last_kernel(bias_ref, *refs):
    total = bias_ref[...]
    for ref in refs[:-1]:
        total = total + ref[...].astype(jnp.float32)
    refs[-1][...] = jnp.maximum(total, 0.0).astype(jnp.bfloat16)


def swap(value, axis, step):
    size = lax.axis_size(axis)
    return lax.ppermute(value, axis, [(i, i ^ step) for i in range(size)])


def body(
    src_feats,
    nbr_one,
    counts,
    seed_rows,
    nbr_two,
    w1_self,
    w1_nbr,
    bias_one,
    w2_self,
    w2_nbr,
    bias_two,
):
    n_feat = lax.axis_size("feat")
    half = n_feat // 2
    steps = range(half - 1, -1, -1)
    fslice, nodes = src_feats.shape
    fanout_one, pcap = nbr_one.shape[2:]
    width = w1_self.shape[1]
    seed_count, fanout_two = nbr_two.shape
    n_idx = fanout_two + 1
    bf16 = jnp.bfloat16
    vmem = pl.BlockSpec(memory_space=pltpu.VMEM)
    smem = pl.BlockSpec(memory_space=pltpu.SMEM)
    hbm = pl.BlockSpec(memory_space=pltpu.HBM)
    anywhere = pl.BlockSpec(memory_space=pl.ANY)
    table_bytes = nodes * LANES * 4

    def call(kernel, name, shapes, ins, args, after=(), scratch=(), limit=16 * MIB, cost_us=1, outs=None):
        def wrapped(*refs):
            kernel(*refs[: len(args)], *refs[len(args) + len(after) :])

        return pl.pallas_call(
            wrapped,
            out_shape=tuple(jax.ShapeDtypeStruct(shape, dtype) for shape, dtype in shapes),
            in_specs=[*ins, *([anywhere] * len(after))],
            out_specs=outs or (vmem,) * len(shapes),
            scratch_shapes=scratch,
            compiler_params=pltpu.CompilerParams(vmem_limit_bytes=limit),
            cost_estimate=pl.CostEstimate(
                flops=int(cost_us * 1_100_000_000), bytes_accessed=0, transcendentals=0
            ),
            name=name,
        )(*args, *after)

    def pinned(value):
        return pltpu.with_memory_space_constraint(value, pltpu.HBM)

    def send(chunks, steps=steps):
        return [swap(chunk, "feat", s) if s else chunk for s, chunk in zip(steps, chunks)]

    picks = jnp.transpose(nbr_one, (0, 2, 1, 3))
    packed = 2 if fanout_one % 2 == 0 and nodes <= 1 << 16 else 1
    words = (n_feat, 1, fanout_one // packed * (-(-pcap // LANES) * LANES))
    *parcels, picks, feats = call(
        functools.partial(pack_kernel, n_feat, pcap),
        "pack",
        [((parcel_rows(fslice, n_idx), width), bf16)] * half
        + [(words, jnp.int32), ((fslice, nodes), bf16)],
        [hbm] * 6,
        [pinned(x) for x in (src_feats, seed_rows[None], nbr_two.T, w1_self, w1_nbr, picks)],
        scratch=[
            pltpu.VMEM((1, seed_count), jnp.int32),
            pltpu.VMEM((fanout_two, seed_count), jnp.int32),
            pltpu.VMEM((fslice, width), bf16),
            pltpu.VMEM((fslice, width), bf16),
            pltpu.VMEM((n_feat, fanout_one, 1, pcap), jnp.int32),
            pltpu.SemaphoreType.DMA((7,)),
        ],
        limit=32 * MIB,
    )
    arrived = send(parcels)
    (table,) = call(
        turn_kernel,
        "turn",
        [((nodes, LANES), jnp.float32)],
        [vmem],
        (feats,),
        limit=table_bytes + 12 * MIB,
        cost_us=3,
    )
    table = table.reshape(nodes, 1, LANES)
    chunk_shape = (pcap // 4 * 3, LANES) if folds(fslice, pcap) else (pcap, fslice)

    def means(chosen, tagged=(), after=(), before=None, ins=(), outs=()):
        count = len(chosen)
        return call(
            functools.partial(
                mean_kernel,
                tuple(chosen),
                packed,
                fanout_one,
                pcap,
                fslice,
                before,
                (len(ins), len(outs)),
            ),
            "mean",
            [(chunk_shape, bf16)] * count + list(outs),
            [vmem] * len(ins) + [anywhere] + [vmem] * (1 + len(tagged)),
            (*ins, picks, table, *tagged),
            after=after,
            scratch=[
                pltpu.VMEM((count, *chunk_shape), bf16),
                pltpu.VMEM((pcap, LANES), jnp.float32),
                pltpu.SMEM((count * words[2],), jnp.int32),
                pltpu.SMEM((count,), jnp.int32),
                pltpu.SemaphoreType.DMA((count,)),
            ],
            limit=table_bytes + 8 * MIB,
            cost_us=2 * count if count > 1 else 0,
        )

    far_means = means([s + half for s in steps if s])
    tagged_shape = (chunk_shape[0] + TAG_ROWS, chunk_shape[1])
    halves, *tagged, live = call(
        functools.partial(halves_kernel, half),
        "halves",
        [
            ((half, fslice, width), bf16),
            *([(tagged_shape, bf16)] * (half - 1)),
            ((TAG_ROWS, chunk_shape[1]), bf16),
        ],
        [smem] + [vmem] * (2 * half - 1),
        (counts, *arrived, *far_means),
    )
    far_arrived = send(tagged)
    other_halves = swap(halves, "rep", 1)
    idx_rows = -(-half // 4) * n_idx
    far_own, w_nbr, pre, far_pre, idx_tags = means(
        [half],
        before=functools.partial(own_kernel, half, n_idx),
        ins=(*arrived, other_halves, bias_one[None]),
        outs=[
            ((half, fslice, width), bf16),
            ((pcap, width), jnp.float32),
            ((pcap, width), jnp.float32),
            ((idx_rows, width), bf16),
        ],
    )
    (cross,) = call(
        functools.partial(far_kernel, half),
        "far",
        [((pcap + idx_rows, width), bf16)],
        [vmem] * (half + 3),
        (*far_arrived, far_own, far_pre, w_nbr, idx_tags),
    )
    cross_arrived = swap(cross, "feat", half)
    turned = [*steps[1:-1], steps[0]]
    near_means = means(turned, [*far_arrived[1:], far_arrived[0]], (cross,))
    near_arrived = send(near_means, turned)
    near_own, near_times = means(
        [0],
        [live],
        after=(cross,),
        before=functools.partial(near_times_kernel, half, fslice, pcap, n_idx),
        ins=(w2_self, w2_nbr, *arrived),
        outs=[((half * seed_count, 4 * pcap), bf16)],
    )
    (near_pre,) = call(
        functools.partial(near_kernel, half),
        "near",
        [((pcap, width), jnp.float32)],
        [vmem] * (half + 2),
        (*near_arrived, near_own, pre, w_nbr),
        cost_us=0,
    )
    (hidden,) = call(
        hidden_kernel,
        "hidden",
        [((pcap, width), bf16)],
        [vmem] * 3,
        (live, near_pre, cross_arrived),
    )
    other_hidden = swap(hidden, "rep", 1)
    far_times, value, result = call(
        functools.partial(far_times_kernel, half, n_idx, fanout_two),
        "far_times",
        [
            ((half * seed_count, 4 * pcap), bf16),
            ((2, pcap, width), bf16),
            ((pcap, width), bf16),
        ],
        [vmem] * 4,
        (cross_arrived, hidden, w2_self, w2_nbr),
        scratch=[pltpu.SemaphoreType.DMA],
        outs=(vmem, vmem, anywhere),
    )
    *far_shares, values = call(
        functools.partial(far_share_kernel, half, fanout_two),
        "far_share",
        [((seed_count, width), bf16)] * half + [((4 * pcap, width), bf16)],
        [vmem] * 5,
        (far_times, value, other_hidden, w2_self, w2_nbr),
        limit=32 * MIB,
    )
    far_shares = send(far_shares)
    near_shares = call(
        near_share_kernel,
        "near_share",
        [((seed_count, width), bf16)] * half,
        [vmem] * 2,
        (near_times, values),
        limit=32 * MIB,
    )
    near_shares = send(near_shares)
    (far_sum,) = call(
        side_sum_kernel, "side_sum", [((seed_count, width), bf16)], [vmem] * half, far_shares
    )
    (seed_out,) = call(
        last_kernel,
        "seeds",
        [((seed_count, width), bf16)],
        [vmem] * (half + 2),
        (bias_two[None], *near_shares, swap(far_sum, "feat", half)),
    )
    return (result[None, None], seed_out)


def solution(mesh):
    placed = (
        P("feat", "groups"),
        P("groups", "rep", None, None),
        P(("groups", "feat"), "rep"),
        P(("groups", "feat", "rep")),
        P(("groups", "feat", "rep"), None),
        P("feat", None),
        P("feat", None),
        P(),
        P(),
        P(),
        P(),
    )
    return jax.shard_map(
        body,
        mesh=mesh,
        in_specs=placed,
        out_specs=(P(("groups", "feat"), "rep", None, None), P(("groups", "feat", "rep"), None)),
        check_vma=False,
    )
```

```python
import functools

import jax
import jax.numpy as jnp
from jax import lax
from jax.experimental import pallas as pl
from jax.experimental.pallas import tpu as pltpu
from jax.sharding import PartitionSpec as P

LANES = 128
MIB = 1024 * 1024


def folds(fslice, pcap):
    return 4 * fslice == 3 * LANES and pcap % 64 == 0


def is_dense(fslice, n_idx):
    return fslice % 32 == 0 and n_idx == 16


def parcel_rows(fslice, n_idx):
    return 2 * fslice - fslice // 4 + 8 if is_dense(fslice, n_idx) else 2 * fslice


def write_parcel(ref, weight, feats, digits):
    fslice, lanes = feats.shape
    ref[:fslice, :] = weight
    if is_dense(fslice, digits.shape[0]):
        cut = fslice // 4 * 3
        tail = jnp.concatenate([feats[cut:, i : i + LANES] for i in range(0, lanes, LANES)], axis=0)
        tags = jnp.concatenate([digits[:8], digits[8:]] * 2, axis=1)
        body = jnp.concatenate([feats[:cut], tail], axis=1)
        ref[fslice:, :] = jnp.concatenate([body, tags], axis=0).astype(jnp.bfloat16)
    else:
        ref[fslice:, :lanes] = feats.astype(jnp.bfloat16)
        ref[fslice : fslice + digits.shape[0], lanes:] = digits.astype(jnp.bfloat16)


def read_feats(ref, fslice, n_idx, lanes):
    if not is_dense(fslice, n_idx):
        return ref[fslice:, :lanes].astype(jnp.float32)
    cut, part = fslice // 4 * 3, fslice // 4
    tail = ref[fslice : fslice + cut, lanes:].astype(jnp.float32)
    tail = jnp.concatenate([tail[i : i + part] for i in range(0, cut, part)], axis=1)
    return jnp.concatenate([ref[fslice : fslice + cut, :lanes].astype(jnp.float32), tail], axis=0)


def read_digits(ref, fslice, n_idx, lanes):
    if not is_dense(fslice, n_idx):
        return ref[fslice : fslice + n_idx, lanes:].astype(jnp.float32)
    tags = ref[-8:, : 2 * LANES].astype(jnp.float32)
    return jnp.concatenate([tags[:, :LANES], tags[:, LANES:]], axis=0)


TAG_ROWS = 16


def live_rows(ref):
    return jnp.max(ref[-TAG_ROWS:, :].astype(jnp.float32)).astype(jnp.int32)


def pack_kernel(
    n_feat,
    pcap,
    src_hbm,
    seed_hbm,
    nbr_hbm,
    w_self_hbm,
    w_nbr_hbm,
    pick_hbm,
    *refs,
):
    half = n_feat // 2
    parcel_refs, pick_ref, src_ref = refs[:half], refs[half], refs[half + 1]
    seed_ref, nbr_ref, w_self_ref, w_nbr_ref, fetched_ref, sems = refs[half + 2 :]
    owned = n_feat * 2 * pcap
    first, rest = pl.ds(0, owned), pl.ds(owned, src_ref.shape[1] - owned)
    copies = [
        pltpu.make_async_copy(a, b, sems.at[i])
        for i, (a, b) in enumerate(
            (
                (src_hbm.at[:, first], src_ref.at[:, first]),
                (w_self_hbm, w_self_ref),
                (w_nbr_hbm, w_nbr_ref),
                (seed_hbm, seed_ref),
                (nbr_hbm, nbr_ref),
                (pick_hbm, fetched_ref),
                (src_hbm.at[:, rest], src_ref.at[:, rest]),
            )
        )
    ]
    for copy in copies:
        copy.start()
    for copy in copies[1:-1]:
        copy.wait()
    stride = -(-pcap // LANES) * LANES
    words = pick_ref.shape[2] // stride
    for k in range(words):
        word = fetched_ref[:, k]
        if words < fetched_ref.shape[1]:
            word = word | (fetched_ref[:, words + k] << 16)
        pick_ref[:, :, k * stride : k * stride + pcap] = word
    feat_pos = lax.axis_index("feat")
    first_core = lax.axis_index("rep") == 0
    idx = jnp.concatenate([seed_ref[...], nbr_ref[...]], axis=0)
    high = lax.shift_right_logical(idx, 7)
    digits = jnp.concatenate([high, idx - high * 128], axis=1).astype(jnp.float32)
    weight = jnp.where(first_core, w_self_ref[...], w_nbr_ref[...])
    copies[0].wait()
    for s, parcel_ref in enumerate(reversed(parcel_refs)):
        sides = []
        for step in (s, s ^ half):
            at = pl.multiple_of(jnp.bitwise_xor(feat_pos, step) * (2 * pcap), LANES)
            block = src_ref[:, pl.ds(at, 2 * pcap)].astype(jnp.float32)
            sides.append(jnp.where(first_core, block[:, :pcap], block[:, pcap:]))
        write_parcel(parcel_ref, weight, jnp.concatenate(sides, axis=1), digits)
    copies[-1].wait()


def turn_kernel(src_ref, table_ref):
    fslice, nodes = src_ref.shape
    width = 2048 if nodes % 2048 == 0 else 512

    def turn(step, carry):
        at = pl.multiple_of(step * width, width)
        table_ref[pl.ds(at, width), :fslice] = src_ref[:, pl.ds(at, width)].T.astype(jnp.float32)
        return carry

    lax.fori_loop(0, nodes // width, turn, 0)


def mean_kernel(chosen, packed, fanout, pcap, fslice, before, n_before, *refs):
    count = len(chosen)
    before_in, refs = refs[: n_before[0]], refs[n_before[0] :]
    nbr_any, table_ref, *refs = refs
    out_ref, total, nbr_ref, live_ref, sems = refs[-5:]
    refs = refs[:-5]
    before_out = refs[len(refs) - n_before[1] :]
    refs = refs[: len(refs) - n_before[1]]
    chunk_refs, tagged_refs = refs[len(refs) - count :], refs[: len(refs) - count]
    feat_pos = lax.axis_index("feat")
    words = fanout // packed
    size = 16 if len(tagged_refs) or pcap % 64 else 64
    stride = -(-pcap // LANES) * LANES
    length = words * stride
    copies = [
        pltpu.make_async_copy(
            nbr_any.at[feat_pos ^ step, 0], nbr_ref.at[pl.ds(i * length, length)], sems.at[i]
        )
        for i, step in enumerate(chosen)
    ]
    for copy in copies:
        copy.start()
    for i in range(count):
        live_ref[i] = pcap
    for i, ref in enumerate(tagged_refs):
        live_ref[i] = live_rows(ref)
    if before is not None:
        before(*before_in, *before_out)
    for copy in copies:
        copy.wait()

    def partition(i, carry):
        first = i * length

        def group(g, inner):
            at = pl.multiple_of(g * size, 16)
            start = first + at
            sums = []
            for u in range(size):
                names = [nbr_ref[start + (k * stride + u)] for k in range(words)]
                if packed == 2:
                    names = [
                        part
                        for name in names
                        for part in (name & 0xFFFF, lax.shift_right_logical(name, 16))
                    ]
                rows = [table_ref[name] for name in names]
                while len(rows) > 1:
                    rows = [a + b for a, b in zip(rows[::2], rows[1::2])] + (
                        [rows[-1]] if len(rows) % 2 else []
                    )
                sums.append(rows[0])
                if len(sums) == 16:
                    for v, row in enumerate(sums):
                        total[pl.ds(at + (u - 15 + v), 1), :] = row
                    sums = []
            return inner

        lax.fori_loop(0, lax.div(live_ref[i] + size - 1, size), group, 0)
        mean = total[...] / fanout
        if folds(fslice, pcap):
            part = pcap // 4
            lane = lax.broadcasted_iota(jnp.int32, (part, LANES), 1)
            tail = mean[3 * part :]
            for b in range(3):
                shift = (fslice - 32 * b) % LANES
                moved = pltpu.roll(tail, shift, 1) if shift else tail
                out_ref[i, pl.ds(b * part, part), :] = jnp.where(
                    lane < fslice, mean[b * part : (b + 1) * part], moved
                ).astype(jnp.bfloat16)
        else:
            out_ref[i] = mean[:, :fslice].astype(jnp.bfloat16)
        return carry

    lax.fori_loop(0, count, partition, 0)
    for i, ref in enumerate(chunk_refs):
        ref[...] = out_ref[i]


def unfold(ref, fslice, pcap):
    if not folds(fslice, pcap):
        return ref[:pcap, :]
    part = pcap // 4
    wide = ref[: 3 * part, :].astype(jnp.float32)
    lane = lax.broadcasted_iota(jnp.int32, (part, LANES), 1)
    tail = pltpu.roll(wide[:part], LANES - fslice, 1)
    for b in (1, 2):
        shift = (32 * b - fslice) % LANES
        moved = wide[b * part : (b + 1) * part]
        moved = pltpu.roll(moved, shift, 1) if shift else moved
        tail = jnp.where(lane // 32 == b, moved, tail)
    return jnp.concatenate([wide, tail], axis=0)[:, :fslice].astype(jnp.bfloat16)


def halves_kernel(half, count_ref, *refs):
    parcel_refs, chunk_refs = refs[:half], refs[half : 2 * half - 1]
    out_ref, *tagged_refs, live_ref = refs[2 * half - 1 :]
    for s, ref in enumerate(parcel_refs):
        out_ref[s] = ref[: out_ref.shape[1], :]
    live = jnp.full(live_ref.shape, count_ref[0, 0].astype(jnp.float32)).astype(jnp.bfloat16)
    live_ref[...] = live
    for chunk_ref, ref in zip(chunk_refs, tagged_refs):
        ref[:-TAG_ROWS, :] = chunk_ref[...]
        ref[-TAG_ROWS:, :] = live


def own_kernel(half, n_idx, *refs):
    parcel_refs = refs[:half]
    other_ref, bias_ref, w_ref, pre_ref, far_ref, idx_ref = refs[half:]
    fslice = w_ref.shape[1]
    pcap, width = pre_ref.shape
    first_core = lax.axis_index("rep") == 0
    feats, weights = [], []
    for s in range(half):
        mine, other = parcel_refs[s][:fslice, :], other_ref[s]
        w_ref[s] = jnp.where(first_core, other, mine)
        weights.append(jnp.where(first_core, mine, other))
        feats.append(read_feats(parcel_refs[s], fslice, n_idx, 2 * pcap))
        rows = pl.ds(s // 4 * n_idx, n_idx)
        digits = read_digits(parcel_refs[s], fslice, n_idx, 2 * pcap)
        idx_ref[rows, s % 4 * LANES : (s % 4 + 1) * LANES] = digits.astype(jnp.bfloat16)
    both = jnp.dot(
        jnp.concatenate(feats, axis=0).T.astype(jnp.bfloat16),
        jnp.concatenate(weights, axis=0),
        preferred_element_type=jnp.float32,
    )
    pre_ref[...] = both[:pcap] + bias_ref[...]
    far_ref[...] = both[pcap:]


def add_means(half, pre, mean_refs, w_ref, turn=0):
    for s, ref in enumerate(mean_refs):
        pre = pre + jnp.dot(
            unfold(ref, w_ref.shape[1], pre.shape[0]),
            w_ref[(s + turn) % (half - 1) if s < half - 1 else s],
            preferred_element_type=jnp.float32,
        )
    return pre


def far_kernel(half, *refs):
    far_ref, w_ref, idx_ref, cross_ref = refs[half:]
    pcap = far_ref.shape[0]
    cross_ref[:pcap, :] = add_means(half, far_ref[...], refs[:half], w_ref).astype(jnp.bfloat16)
    cross_ref[pcap:, :] = idx_ref[...]


def store_times(pcap, blocks, out_ref):
    n_idx, pair = blocks[0].shape
    seed_count = pair // 2
    core_rows = lax.axis_index("feat") * (2 * pcap)
    rep_pos = lax.axis_index("rep")
    row = lax.broadcasted_iota(jnp.int32, (2 * pcap, pair), 0)
    slot = jnp.where(
        row < pcap, row + core_rows + rep_pos * pcap, row + core_rows - rep_pos * pcap
    ).astype(jnp.float32)
    low = lax.broadcasted_iota(jnp.int32, (n_idx, pair), 1) < seed_count
    for s in range(0, len(blocks), 2):
        first, second = blocks[s].astype(jnp.float32), blocks[s + 1].astype(jnp.float32)
        high_part = jnp.where(low, first, pltpu.roll(second, seed_count, 1))
        low_part = jnp.where(low, pltpu.roll(first, seed_count, 1), second)
        name = high_part * 128.0 + low_part
        own = jnp.where(slot == name[:1], 1.0, 0.0)
        near = jnp.zeros((2 * pcap, pair), jnp.float32)
        for k in range(1, n_idx):
            near = near + jnp.where(slot == name[k : k + 1], 1.0, 0.0)
        place = pl.ds(s * seed_count, pair)
        out_ref[place, : 2 * pcap] = own.T.astype(jnp.bfloat16)
        out_ref[place, 2 * pcap :] = near.T.astype(jnp.bfloat16)


def near_times_kernel(half, fslice, pcap, n_idx, _, __, *refs):
    blocks = [read_digits(ref, fslice, n_idx, 2 * pcap) for ref in refs[:half]]
    store_times(pcap, blocks, refs[half])


def far_times_kernel(
    half,
    n_idx,
    fanout_two,
    cross_ref,
    hidden_ref,
    ws_ref,
    wn_ref,
    out_ref,
    value_ref,
    result_ref,
    sem,
):
    copy = pltpu.make_async_copy(hidden_ref, result_ref, sem)
    copy.start()
    pcap = hidden_ref.shape[0]
    blocks = [
        cross_ref[
            pl.ds(pcap + s // 4 * n_idx, n_idx), s % 4 * LANES : (s % 4 + 1) * LANES
        ]
        for s in range(half)
    ]
    store_times(pcap, blocks, out_ref)
    store_values(hidden_ref[...], ws_ref, wn_ref, fanout_two, value_ref)
    copy.wait()


def store_values(hidden, ws_ref, wn_ref, fanout_two, value_ref):
    value_ref[0] = jnp.dot(hidden, ws_ref[...], preferred_element_type=jnp.float32).astype(
        jnp.bfloat16
    )
    value_ref[1] = (
        jnp.dot(hidden, wn_ref[...], preferred_element_type=jnp.float32) / fanout_two
    ).astype(jnp.bfloat16)


def near_kernel(half, *refs):
    pre_ref, w_ref, out_ref = refs[half:]
    out_ref[...] = add_means(half, pre_ref[...], refs[:half], w_ref, 1)


def hidden_kernel(live_ref, pre_ref, cross_ref, hidden_ref):
    pcap, width = hidden_ref.shape
    pre = pre_ref[...] + cross_ref[:pcap, :].astype(jnp.float32)
    live = lax.broadcasted_iota(jnp.int32, (pcap, width), 0) < live_rows(live_ref)
    hidden_ref[...] = jnp.where(live, jnp.maximum(pre, 0.0), 0.0).astype(jnp.bfloat16)


def far_share_kernel(
    half, fanout_two, far_ref, value_ref, hidden_ref, ws_ref, wn_ref, *refs
):
    *out_refs, values_ref = refs
    pcap = hidden_ref.shape[0]
    for i in range(2):
        values_ref[2 * i * pcap : (2 * i + 1) * pcap, :] = value_ref[i]
    hidden = hidden_ref[...]
    values_ref[pcap : 2 * pcap, :] = jnp.dot(
        hidden, ws_ref[...], preferred_element_type=jnp.float32
    ).astype(jnp.bfloat16)
    values_ref[3 * pcap :, :] = (
        jnp.dot(hidden, wn_ref[...], preferred_element_type=jnp.float32) / fanout_two
    ).astype(jnp.bfloat16)
    store_shares(far_ref, values_ref, out_refs)


def store_shares(times_ref, values_ref, out_refs):
    rows = times_ref.shape[0] // len(out_refs)
    part = jnp.dot(times_ref[...], values_ref[...], preferred_element_type=jnp.float32)
    for s, ref in enumerate(out_refs):
        ref[...] = part[s * rows : (s + 1) * rows].astype(jnp.bfloat16)


def near_share_kernel(near_ref, values_ref, *out_refs):
    rows = near_ref.shape[0]
    pairs = len(out_refs)
    count = 2 * (pairs - 1)
    each = rows // count
    part = jnp.dot(near_ref[...], values_ref[...], preferred_element_type=jnp.float32)
    part = part.astype(jnp.bfloat16)
    for i in range(pairs - 1):
        out_refs[0][i * each : (i + 1) * each, :] = part[2 * i * each : (2 * i + 1) * each]
        out_refs[i + 1][...] = part[(2 * i + 1) * each : (2 * i + 2) * each]


def relay_kernel(relay_ref, *refs):
    count = len(refs) // 2
    for i in range(count):
        rows = refs[i].shape[0]
        refs[count + i][...] = (
            refs[i][...].astype(jnp.float32)
            + relay_ref[i * rows : (i + 1) * rows, :].astype(jnp.float32)
        ).astype(jnp.bfloat16)


def side_sum_kernel(*refs):
    total = refs[0][...].astype(jnp.float32)
    for ref in refs[1:-1]:
        total = total + ref[...].astype(jnp.float32)
    refs[-1][...] = total.astype(jnp.bfloat16)


def last_kernel(bias_ref, *refs):
    total = bias_ref[...]
    for ref in refs[:-1]:
        total = total + ref[...].astype(jnp.float32)
    refs[-1][...] = jnp.maximum(total, 0.0).astype(jnp.bfloat16)


def swap(value, axis, step):
    size = lax.axis_size(axis)
    return lax.ppermute(value, axis, [(i, i ^ step) for i in range(size)])


def body(
    src_feats,
    nbr_one,
    counts,
    seed_rows,
    nbr_two,
    w1_self,
    w1_nbr,
    bias_one,
    w2_self,
    w2_nbr,
    bias_two,
):
    n_feat = lax.axis_size("feat")
    half = n_feat // 2
    steps = range(half - 1, -1, -1)
    fslice, nodes = src_feats.shape
    fanout_one, pcap = nbr_one.shape[2:]
    width = w1_self.shape[1]
    seed_count, fanout_two = nbr_two.shape
    n_idx = fanout_two + 1
    bf16 = jnp.bfloat16
    vmem = pl.BlockSpec(memory_space=pltpu.VMEM)
    smem = pl.BlockSpec(memory_space=pltpu.SMEM)
    hbm = pl.BlockSpec(memory_space=pltpu.HBM)
    anywhere = pl.BlockSpec(memory_space=pl.ANY)
    table_bytes = nodes * LANES * 4

    def call(kernel, name, shapes, ins, args, after=(), scratch=(), limit=16 * MIB, cost_us=1, outs=None):
        def wrapped(*refs):
            kernel(*refs[: len(args)], *refs[len(args) + len(after) :])

        return pl.pallas_call(
            wrapped,
            out_shape=tuple(jax.ShapeDtypeStruct(shape, dtype) for shape, dtype in shapes),
            in_specs=[*ins, *([anywhere] * len(after))],
            out_specs=outs or (vmem,) * len(shapes),
            scratch_shapes=scratch,
            compiler_params=pltpu.CompilerParams(vmem_limit_bytes=limit),
            cost_estimate=pl.CostEstimate(
                flops=int(cost_us * 1_100_000_000), bytes_accessed=0, transcendentals=0
            ),
            name=name,
        )(*args, *after)

    def pinned(value):
        return pltpu.with_memory_space_constraint(value, pltpu.HBM)

    def send(chunks, steps=steps):
        return [swap(chunk, "feat", s) if s else chunk for s, chunk in zip(steps, chunks)]

    picks = jnp.transpose(nbr_one, (0, 2, 1, 3))
    packed = 2 if fanout_one % 2 == 0 and nodes <= 1 << 16 else 1
    words = (n_feat, 1, fanout_one // packed * (-(-pcap // LANES) * LANES))
    *parcels, picks, feats = call(
        functools.partial(pack_kernel, n_feat, pcap),
        "pack",
        [((parcel_rows(fslice, n_idx), width), bf16)] * half
        + [(words, jnp.int32), ((fslice, nodes), bf16)],
        [hbm] * 6,
        [pinned(x) for x in (src_feats, seed_rows[None], nbr_two.T, w1_self, w1_nbr, picks)],
        scratch=[
            pltpu.VMEM((1, seed_count), jnp.int32),
            pltpu.VMEM((fanout_two, seed_count), jnp.int32),
            pltpu.VMEM((fslice, width), bf16),
            pltpu.VMEM((fslice, width), bf16),
            pltpu.VMEM((n_feat, fanout_one, 1, pcap), jnp.int32),
            pltpu.SemaphoreType.DMA((7,)),
        ],
        limit=32 * MIB,
    )
    arrived = send(parcels)
    (table,) = call(
        turn_kernel,
        "turn",
        [((nodes, LANES), jnp.float32)],
        [vmem],
        (feats,),
        limit=table_bytes + 12 * MIB,
        cost_us=3,
    )
    table = table.reshape(nodes, 1, LANES)
    chunk_shape = (pcap // 4 * 3, LANES) if folds(fslice, pcap) else (pcap, fslice)

    def means(chosen, tagged=(), after=(), before=None, ins=(), outs=()):
        count = len(chosen)
        return call(
            functools.partial(
                mean_kernel,
                tuple(chosen),
                packed,
                fanout_one,
                pcap,
                fslice,
                before,
                (len(ins), len(outs)),
            ),
            "mean",
            [(chunk_shape, bf16)] * count + list(outs),
            [vmem] * len(ins) + [anywhere] + [vmem] * (1 + len(tagged)),
            (*ins, picks, table, *tagged),
            after=after,
            scratch=[
                pltpu.VMEM((count, *chunk_shape), bf16),
                pltpu.VMEM((pcap, LANES), jnp.float32),
                pltpu.SMEM((count * words[2],), jnp.int32),
                pltpu.SMEM((count,), jnp.int32),
                pltpu.SemaphoreType.DMA((count,)),
            ],
            limit=table_bytes + 8 * MIB,
            cost_us=2 * count if count > 1 else 0,
        )

    far_means = means([s + half for s in steps if s])
    tagged_shape = (chunk_shape[0] + TAG_ROWS, chunk_shape[1])
    halves, *tagged, live = call(
        functools.partial(halves_kernel, half),
        "halves",
        [
            ((half, fslice, width), bf16),
            *([(tagged_shape, bf16)] * (half - 1)),
            ((TAG_ROWS, chunk_shape[1]), bf16),
        ],
        [smem] + [vmem] * (2 * half - 1),
        (counts, *arrived, *far_means),
    )
    far_arrived = send(tagged)
    other_halves = swap(halves, "rep", 1)
    idx_rows = -(-half // 4) * n_idx
    far_own, w_nbr, pre, far_pre, idx_tags = means(
        [half],
        before=functools.partial(own_kernel, half, n_idx),
        ins=(*arrived, other_halves, bias_one[None]),
        outs=[
            ((half, fslice, width), bf16),
            ((pcap, width), jnp.float32),
            ((pcap, width), jnp.float32),
            ((idx_rows, width), bf16),
        ],
    )
    (cross,) = call(
        functools.partial(far_kernel, half),
        "far",
        [((pcap + idx_rows, width), bf16)],
        [vmem] * (half + 3),
        (*far_arrived, far_own, far_pre, w_nbr, idx_tags),
    )
    cross_arrived = swap(cross, "feat", half)
    turned = [*steps[1:-1], steps[0]]
    near_means = means(turned, [*far_arrived[1:], far_arrived[0]], (cross,))
    near_arrived = send(near_means, turned)
    near_own, near_times = means(
        [0],
        [live],
        after=(cross,),
        before=functools.partial(near_times_kernel, half, fslice, pcap, n_idx),
        ins=(w2_self, w2_nbr, *arrived),
        outs=[((half * seed_count, 4 * pcap), bf16)],
    )
    (near_pre,) = call(
        functools.partial(near_kernel, half),
        "near",
        [((pcap, width), jnp.float32)],
        [vmem] * (half + 2),
        (*near_arrived, near_own, pre, w_nbr),
        cost_us=0,
    )
    (hidden,) = call(
        hidden_kernel,
        "hidden",
        [((pcap, width), bf16)],
        [vmem] * 3,
        (live, near_pre, cross_arrived),
    )
    other_hidden = swap(hidden, "rep", 1)
    far_times, value, result = call(
        functools.partial(far_times_kernel, half, n_idx, fanout_two),
        "far_times",
        [
            ((half * seed_count, 4 * pcap), bf16),
            ((2, pcap, width), bf16),
            ((pcap, width), bf16),
        ],
        [vmem] * 4,
        (cross_arrived, hidden, w2_self, w2_nbr),
        scratch=[pltpu.SemaphoreType.DMA],
        outs=(vmem, vmem, anywhere),
    )
    *far_shares, values = call(
        functools.partial(far_share_kernel, half, fanout_two),
        "far_share",
        [((seed_count, width), bf16)] * half + [((4 * pcap, width), bf16)],
        [vmem] * 5,
        (far_times, value, other_hidden, w2_self, w2_nbr),
        limit=32 * MIB,
    )
    far_shares = send(far_shares)
    column, *near_shares = call(
        near_share_kernel,
        "near_share",
        [((half // 2 * seed_count, width), bf16)] + [((seed_count, width), bf16)] * (half // 2),
        [vmem] * 2,
        (near_times, values),
        limit=32 * MIB,
    )
    column = swap(column, "feat", 1)
    (far_sum,) = call(
        side_sum_kernel, "side_sum", [((seed_count, width), bf16)], [vmem] * half, far_shares
    )
    far_sum = swap(far_sum, "feat", half)
    near_shares = call(
        relay_kernel,
        "relay",
        [((seed_count, width), bf16)] * (half // 2),
        [vmem] * (half // 2 + 1),
        (column, *near_shares),
        after=far_shares[:1],
    )
    near_shares = [
        swap(share, "feat", s) if s else share for share, s in zip(near_shares, steps[1::2])
    ]
    (seed_out,) = call(
        last_kernel,
        "seeds",
        [((seed_count, width), bf16)],
        [vmem] * (half // 2 + 2),
        (bias_two[None], *near_shares, far_sum),
    )
    return (result[None, None], seed_out)


def solution(mesh):
    placed = (
        P("feat", "groups"),
        P("groups", "rep", None, None),
        P(("groups", "feat"), "rep"),
        P(("groups", "feat", "rep")),
        P(("groups", "feat", "rep"), None),
        P("feat", None),
        P("feat", None),
        P(),
        P(),
        P(),
        P(),
    )
    return jax.shard_map(
        body,
        mesh=mesh,
        in_specs=placed,
        out_specs=(P(("groups", "feat"), "rep", None, None), P(("groups", "feat", "rep"), None)),
        check_vma=False,
    )
```

```python
import functools

import jax
import jax.numpy as jnp
from jax import lax
from jax.experimental import pallas as pl
from jax.experimental.pallas import tpu as pltpu
from jax.sharding import PartitionSpec as P

LANES = 128
MIB = 1024 * 1024


def folds(fslice, pcap):
    return 4 * fslice == 3 * LANES and pcap % 64 == 0


def is_dense(fslice, n_idx):
    return fslice % 32 == 0 and n_idx == 16


def parcel_rows(fslice, n_idx):
    return 2 * fslice - fslice // 4 + 8 if is_dense(fslice, n_idx) else 2 * fslice


def write_parcel(ref, weight, feats, digits):
    fslice, lanes = feats.shape
    ref[:fslice, :] = weight
    if is_dense(fslice, digits.shape[0]):
        cut = fslice // 4 * 3
        tail = jnp.concatenate([feats[cut:, i : i + LANES] for i in range(0, lanes, LANES)], axis=0)
        tags = jnp.concatenate([digits[:8], digits[8:]] * 2, axis=1)
        body = jnp.concatenate([feats[:cut], tail], axis=1)
        ref[fslice:, :] = jnp.concatenate([body, tags], axis=0).astype(jnp.bfloat16)
    else:
        ref[fslice:, :lanes] = feats.astype(jnp.bfloat16)
        ref[fslice : fslice + digits.shape[0], lanes:] = digits.astype(jnp.bfloat16)


def read_feats(ref, fslice, n_idx, lanes):
    if not is_dense(fslice, n_idx):
        return ref[fslice:, :lanes].astype(jnp.float32)
    cut, part = fslice // 4 * 3, fslice // 4
    tail = ref[fslice : fslice + cut, lanes:].astype(jnp.float32)
    tail = jnp.concatenate([tail[i : i + part] for i in range(0, cut, part)], axis=1)
    return jnp.concatenate([ref[fslice : fslice + cut, :lanes].astype(jnp.float32), tail], axis=0)


def read_digits(ref, fslice, n_idx, lanes):
    if not is_dense(fslice, n_idx):
        return ref[fslice : fslice + n_idx, lanes:].astype(jnp.float32)
    tags = ref[-8:, : 2 * LANES].astype(jnp.float32)
    return jnp.concatenate([tags[:, :LANES], tags[:, LANES:]], axis=0)


TAG_ROWS = 16


def live_rows(ref):
    return jnp.max(ref[-TAG_ROWS:, :].astype(jnp.float32)).astype(jnp.int32)


def pack_kernel(
    steps,
    n_feat,
    pcap,
    src_hbm,
    seed_hbm,
    nbr_hbm,
    w_self_hbm,
    w_nbr_hbm,
    pick_hbm,
    *refs,
):
    half = n_feat // 2
    parcel_refs, pick_ref, src_ref = refs[:half], refs[half], refs[half + 1]
    seed_ref, nbr_ref, w_self_ref, w_nbr_ref, fetched_ref, sems = refs[half + 2 :]
    owned = n_feat * 2 * pcap
    first, rest = pl.ds(0, owned), pl.ds(owned, src_ref.shape[1] - owned)
    copies = [
        pltpu.make_async_copy(a, b, sems.at[i])
        for i, (a, b) in enumerate(
            (
                (src_hbm.at[:, first], src_ref.at[:, first]),
                (w_self_hbm, w_self_ref),
                (w_nbr_hbm, w_nbr_ref),
                (seed_hbm, seed_ref),
                (nbr_hbm, nbr_ref),
                (pick_hbm, fetched_ref),
                (src_hbm.at[:, rest], src_ref.at[:, rest]),
            )
        )
    ]
    for copy in copies:
        copy.start()
    for copy in copies[1:-1]:
        copy.wait()
    stride = -(-pcap // LANES) * LANES
    words = pick_ref.shape[2] // stride
    for k in range(words):
        word = fetched_ref[:, k]
        if words < fetched_ref.shape[1]:
            word = word | (fetched_ref[:, words + k] << 16)
        pick_ref[:, :, k * stride : k * stride + pcap] = word
    feat_pos = lax.axis_index("feat")
    first_core = lax.axis_index("rep") == 0
    idx = jnp.concatenate([seed_ref[...], nbr_ref[...]], axis=0)
    high = lax.shift_right_logical(idx, 7)
    digits = jnp.concatenate([high, idx - high * 128], axis=1).astype(jnp.float32)
    weight = jnp.where(first_core, w_self_ref[...], w_nbr_ref[...])
    copies[0].wait()
    for s, parcel_ref in zip(steps, parcel_refs):
        sides = []
        for step in (s, s ^ half):
            at = pl.multiple_of(jnp.bitwise_xor(feat_pos, step) * (2 * pcap), LANES)
            block = src_ref[:, pl.ds(at, 2 * pcap)].astype(jnp.float32)
            sides.append(jnp.where(first_core, block[:, :pcap], block[:, pcap:]))
        write_parcel(parcel_ref, weight, jnp.concatenate(sides, axis=1), digits)
    copies[-1].wait()


def turn_kernel(src_ref, table_ref):
    fslice, nodes = src_ref.shape
    width = 2048 if nodes % 2048 == 0 else 512

    def turn(step, carry):
        at = pl.multiple_of(step * width, width)
        table_ref[pl.ds(at, width), :fslice] = src_ref[:, pl.ds(at, width)].T.astype(jnp.float32)
        return carry

    lax.fori_loop(0, nodes // width, turn, 0)


def mean_kernel(chosen, packed, fanout, pcap, fslice, turns, before, n_before, *refs):
    count = len(chosen)
    before_in, refs = refs[: n_before[0]], refs[n_before[0] :]
    nbr_any, *refs = refs
    if not turns:
        table_ref, *refs = refs
    out_ref, total, nbr_ref, live_ref, sems = refs[-5:]
    refs = refs[:-5]
    before_out = refs[len(refs) - n_before[1] :]
    refs = refs[: len(refs) - n_before[1]]
    chunk_refs, tagged_refs = refs[len(refs) - count :], refs[: len(refs) - count]
    feat_pos = lax.axis_index("feat")
    words = fanout // packed
    size = 16 if len(tagged_refs) or pcap % 64 else 64
    stride = -(-pcap // LANES) * LANES
    length = words * stride
    copies = [
        pltpu.make_async_copy(
            nbr_any.at[feat_pos ^ step, 0], nbr_ref.at[pl.ds(i * length, length)], sems.at[i]
        )
        for i, step in enumerate(chosen)
    ]
    for copy in copies:
        copy.start()
    for i in range(count):
        live_ref[i] = pcap
    for i, ref in enumerate(tagged_refs):
        live_ref[i] = live_rows(ref)
    if before is not None:
        before(*before_in, *before_out)
    if turns:
        table_ref = before_out[0].reshape(before_out[0].shape[0], 1, LANES)
    for copy in copies:
        copy.wait()

    def partition(i, carry):
        first = i * length

        def group(g, inner):
            at = pl.multiple_of(g * size, 16)
            start = first + at
            sums = []
            for u in range(size):
                names = [nbr_ref[start + (k * stride + u)] for k in range(words)]
                if packed == 2:
                    names = [
                        part
                        for name in names
                        for part in (name & 0xFFFF, lax.shift_right_logical(name, 16))
                    ]
                rows = [table_ref[name] for name in names]
                while len(rows) > 1:
                    rows = [a + b for a, b in zip(rows[::2], rows[1::2])] + (
                        [rows[-1]] if len(rows) % 2 else []
                    )
                sums.append(rows[0])
                if len(sums) == 16:
                    for v, row in enumerate(sums):
                        total[pl.ds(at + (u - 15 + v), 1), :] = row
                    sums = []
            return inner

        lax.fori_loop(0, lax.div(live_ref[i] + size - 1, size), group, 0)
        mean = total[...] / fanout
        if folds(fslice, pcap):
            part = pcap // 4
            lane = lax.broadcasted_iota(jnp.int32, (part, LANES), 1)
            tail = mean[3 * part :]
            for b in range(3):
                shift = (fslice - 32 * b) % LANES
                moved = pltpu.roll(tail, shift, 1) if shift else tail
                out_ref[i, pl.ds(b * part, part), :] = jnp.where(
                    lane < fslice, mean[b * part : (b + 1) * part], moved
                ).astype(jnp.bfloat16)
        else:
            out_ref[i] = mean[:, :fslice].astype(jnp.bfloat16)
        return carry

    lax.fori_loop(0, count, partition, 0)
    for i, ref in enumerate(chunk_refs):
        ref[...] = out_ref[i]


def unfold(ref, fslice, pcap):
    if not folds(fslice, pcap):
        return ref[:pcap, :]
    part = pcap // 4
    wide = ref[: 3 * part, :].astype(jnp.float32)
    lane = lax.broadcasted_iota(jnp.int32, (part, LANES), 1)
    tail = pltpu.roll(wide[:part], LANES - fslice, 1)
    for b in (1, 2):
        shift = (32 * b - fslice) % LANES
        moved = wide[b * part : (b + 1) * part]
        moved = pltpu.roll(moved, shift, 1) if shift else moved
        tail = jnp.where(lane // 32 == b, moved, tail)
    return jnp.concatenate([wide, tail], axis=0)[:, :fslice].astype(jnp.bfloat16)


def halves_kernel(half, count_ref, *refs):
    parcel_refs, chunk_refs = refs[:half], refs[half : 2 * half - 1]
    out_ref, *tagged_refs, live_ref = refs[2 * half - 1 :]
    for s, ref in enumerate(parcel_refs):
        out_ref[s] = ref[: out_ref.shape[1], :]
    live = jnp.full(live_ref.shape, count_ref[0, 0].astype(jnp.float32)).astype(jnp.bfloat16)
    live_ref[...] = live
    for chunk_ref, ref in zip(chunk_refs, tagged_refs):
        ref[:-TAG_ROWS, :] = chunk_ref[...]
        ref[-TAG_ROWS:, :] = live


def own_kernel(half, n_idx, *refs):
    parcel_refs = refs[:half]
    other_ref, bias_ref, w_ref, pre_ref, far_ref, idx_ref = refs[half:]
    fslice = w_ref.shape[1]
    pcap, width = pre_ref.shape
    first_core = lax.axis_index("rep") == 0
    feats, weights = [], []
    for s in range(half):
        mine, other = parcel_refs[s][:fslice, :], other_ref[s]
        w_ref[s] = jnp.where(first_core, other, mine)
        weights.append(jnp.where(first_core, mine, other))
        feats.append(read_feats(parcel_refs[s], fslice, n_idx, 2 * pcap))
        rows = pl.ds(s // 4 * n_idx, n_idx)
        digits = read_digits(parcel_refs[s], fslice, n_idx, 2 * pcap)
        idx_ref[rows, s % 4 * LANES : (s % 4 + 1) * LANES] = digits.astype(jnp.bfloat16)
    both = jnp.dot(
        jnp.concatenate(feats, axis=0).T.astype(jnp.bfloat16),
        jnp.concatenate(weights, axis=0),
        preferred_element_type=jnp.float32,
    )
    pre_ref[...] = both[:pcap] + bias_ref[...]
    far_ref[...] = both[pcap:]


def add_means(half, pre, mean_refs, w_ref, turn=0):
    for s, ref in enumerate(mean_refs):
        pre = pre + jnp.dot(
            unfold(ref, w_ref.shape[1], pre.shape[0]),
            w_ref[(s + turn) % (half - 1) if s < half - 1 else s],
            preferred_element_type=jnp.float32,
        )
    return pre


def far_kernel(half, *refs):
    far_ref, w_ref, idx_ref, cross_ref = refs[half:]
    pcap = far_ref.shape[0]
    cross_ref[:pcap, :] = add_means(half, far_ref[...], refs[:half], w_ref).astype(jnp.bfloat16)
    cross_ref[pcap:, :] = idx_ref[...]


def store_times(pcap, blocks, out_ref):
    n_idx, pair = blocks[0].shape
    seed_count = pair // 2
    core_rows = lax.axis_index("feat") * (2 * pcap)
    rep_pos = lax.axis_index("rep")
    row = lax.broadcasted_iota(jnp.int32, (2 * pcap, pair), 0)
    slot = jnp.where(
        row < pcap, row + core_rows + rep_pos * pcap, row + core_rows - rep_pos * pcap
    ).astype(jnp.float32)
    low = lax.broadcasted_iota(jnp.int32, (n_idx, pair), 1) < seed_count
    for s in range(0, len(blocks), 2):
        first, second = blocks[s].astype(jnp.float32), blocks[s + 1].astype(jnp.float32)
        high_part = jnp.where(low, first, pltpu.roll(second, seed_count, 1))
        low_part = jnp.where(low, pltpu.roll(first, seed_count, 1), second)
        name = high_part * 128.0 + low_part
        own = jnp.where(slot == name[:1], 1.0, 0.0)
        near = jnp.zeros((2 * pcap, pair), jnp.float32)
        for k in range(1, n_idx):
            near = near + jnp.where(slot == name[k : k + 1], 1.0, 0.0)
        place = pl.ds(s * seed_count, pair)
        out_ref[place, : 2 * pcap] = own.T.astype(jnp.bfloat16)
        out_ref[place, 2 * pcap :] = near.T.astype(jnp.bfloat16)


def near_times_kernel(half, fslice, pcap, n_idx, _, __, *refs):
    blocks = [read_digits(ref, fslice, n_idx, 2 * pcap) for ref in refs[:half]]
    store_times(pcap, blocks, refs[half])


def far_times_kernel(
    half,
    n_idx,
    fanout_two,
    cross_ref,
    hidden_ref,
    ws_ref,
    wn_ref,
    out_ref,
    value_ref,
    result_ref,
    sem,
):
    copy = pltpu.make_async_copy(hidden_ref, result_ref, sem)
    copy.start()
    pcap = hidden_ref.shape[0]
    blocks = [
        cross_ref[
            pl.ds(pcap + s // 4 * n_idx, n_idx), s % 4 * LANES : (s % 4 + 1) * LANES
        ]
        for s in range(half)
    ]
    store_times(pcap, blocks, out_ref)
    store_values(hidden_ref[...], ws_ref, wn_ref, fanout_two, value_ref)
    copy.wait()


def store_values(hidden, ws_ref, wn_ref, fanout_two, value_ref):
    value_ref[0] = jnp.dot(hidden, ws_ref[...], preferred_element_type=jnp.float32).astype(
        jnp.bfloat16
    )
    value_ref[1] = (
        jnp.dot(hidden, wn_ref[...], preferred_element_type=jnp.float32) / fanout_two
    ).astype(jnp.bfloat16)


def near_kernel(half, *refs):
    pre_ref, w_ref, out_ref = refs[half:]
    out_ref[...] = add_means(half, pre_ref[...], refs[:half], w_ref, 1)


def hidden_kernel(live_ref, pre_ref, cross_ref, hidden_ref):
    pcap, width = hidden_ref.shape
    pre = pre_ref[...] + cross_ref[:pcap, :].astype(jnp.float32)
    live = lax.broadcasted_iota(jnp.int32, (pcap, width), 0) < live_rows(live_ref)
    hidden_ref[...] = jnp.where(live, jnp.maximum(pre, 0.0), 0.0).astype(jnp.bfloat16)


def far_share_kernel(
    half, fanout_two, far_ref, value_ref, hidden_ref, ws_ref, wn_ref, *refs
):
    *out_refs, values_ref = refs
    pcap = hidden_ref.shape[0]
    for i in range(2):
        values_ref[2 * i * pcap : (2 * i + 1) * pcap, :] = value_ref[i]
    hidden = hidden_ref[...]
    values_ref[pcap : 2 * pcap, :] = jnp.dot(
        hidden, ws_ref[...], preferred_element_type=jnp.float32
    ).astype(jnp.bfloat16)
    values_ref[3 * pcap :, :] = (
        jnp.dot(hidden, wn_ref[...], preferred_element_type=jnp.float32) / fanout_two
    ).astype(jnp.bfloat16)
    store_shares(far_ref, values_ref, out_refs)


def store_shares(times_ref, values_ref, out_refs):
    rows = times_ref.shape[0] // len(out_refs)
    part = jnp.dot(times_ref[...], values_ref[...], preferred_element_type=jnp.float32)
    for s, ref in enumerate(out_refs):
        ref[...] = part[s * rows : (s + 1) * rows].astype(jnp.bfloat16)


def near_share_kernel(near_ref, values_ref, *out_refs):
    store_shares(near_ref, values_ref, out_refs)


def side_sum_kernel(*refs):
    total = refs[0][...].astype(jnp.float32)
    for ref in refs[1:-1]:
        total = total + ref[...].astype(jnp.float32)
    refs[-1][...] = total.astype(jnp.bfloat16)


def last_kernel(bias_ref, *refs):
    total = bias_ref[...]
    for ref in refs[:-1]:
        total = total + ref[...].astype(jnp.float32)
    refs[-1][...] = jnp.maximum(total, 0.0).astype(jnp.bfloat16)


def swap(value, axis, step):
    size = lax.axis_size(axis)
    return lax.ppermute(value, axis, [(i, i ^ step) for i in range(size)])


def body(
    src_feats,
    nbr_one,
    counts,
    seed_rows,
    nbr_two,
    w1_self,
    w1_nbr,
    bias_one,
    w2_self,
    w2_nbr,
    bias_two,
):
    n_feat = lax.axis_size("feat")
    half = n_feat // 2
    first = half // 2
    steps = [first, *(s for s in range(half - 1, -1, -1) if s != first)]
    fslice, nodes = src_feats.shape
    fanout_one, pcap = nbr_one.shape[2:]
    width = w1_self.shape[1]
    seed_count, fanout_two = nbr_two.shape
    n_idx = fanout_two + 1
    bf16 = jnp.bfloat16
    vmem = pl.BlockSpec(memory_space=pltpu.VMEM)
    smem = pl.BlockSpec(memory_space=pltpu.SMEM)
    hbm = pl.BlockSpec(memory_space=pltpu.HBM)
    anywhere = pl.BlockSpec(memory_space=pl.ANY)
    table_bytes = nodes * LANES * 4

    def call(kernel, name, shapes, ins, args, after=(), scratch=(), limit=16 * MIB, cost_us=1, outs=None):
        def wrapped(*refs):
            kernel(*refs[: len(args)], *refs[len(args) + len(after) :])

        return pl.pallas_call(
            wrapped,
            out_shape=tuple(jax.ShapeDtypeStruct(shape, dtype) for shape, dtype in shapes),
            in_specs=[*ins, *([anywhere] * len(after))],
            out_specs=outs or (vmem,) * len(shapes),
            scratch_shapes=scratch,
            compiler_params=pltpu.CompilerParams(vmem_limit_bytes=limit),
            cost_estimate=pl.CostEstimate(
                flops=int(cost_us * 1_100_000_000), bytes_accessed=0, transcendentals=0
            ),
            name=name,
        )(*args, *after)

    def pinned(value):
        return pltpu.with_memory_space_constraint(value, pltpu.HBM)

    def send(chunks, steps=steps):
        return [swap(chunk, "feat", s) if s else chunk for s, chunk in zip(steps, chunks)]

    picks = jnp.transpose(nbr_one, (0, 2, 1, 3))
    packed = 2 if fanout_one % 2 == 0 and nodes <= 1 << 16 else 1
    words = (n_feat, 1, fanout_one // packed * (-(-pcap // LANES) * LANES))
    *parcels, picks, feats = call(
        functools.partial(pack_kernel, steps, n_feat, pcap),
        "pack",
        [((parcel_rows(fslice, n_idx), width), bf16)] * half
        + [(words, jnp.int32), ((fslice, nodes), bf16)],
        [hbm] * 6,
        [pinned(x) for x in (src_feats, seed_rows[None], nbr_two.T, w1_self, w1_nbr, picks)],
        scratch=[
            pltpu.VMEM((1, seed_count), jnp.int32),
            pltpu.VMEM((fanout_two, seed_count), jnp.int32),
            pltpu.VMEM((fslice, width), bf16),
            pltpu.VMEM((fslice, width), bf16),
            pltpu.VMEM((n_feat, fanout_one, 1, pcap), jnp.int32),
            pltpu.SemaphoreType.DMA((7,)),
        ],
        limit=32 * MIB,
    )
    arrived = send(parcels)
    chunk_shape = (pcap // 4 * 3, LANES) if folds(fslice, pcap) else (pcap, fslice)

    def means(chosen, tagged=(), after=(), before=None, ins=(), outs=(), table=None):
        count = len(chosen)
        tables = () if table is None else (table,)
        return call(
            functools.partial(
                mean_kernel,
                tuple(chosen),
                packed,
                fanout_one,
                pcap,
                fslice,
                table is None,
                before,
                (len(ins), len(outs)),
            ),
            "mean",
            [(chunk_shape, bf16)] * count + list(outs),
            [vmem] * len(ins) + [anywhere] + [vmem] * (len(tables) + len(tagged)),
            (*ins, picks, *tables, *tagged),
            after=after,
            scratch=[
                pltpu.VMEM((count, *chunk_shape), bf16),
                pltpu.VMEM((pcap, LANES), jnp.float32),
                pltpu.SMEM((count * words[2],), jnp.int32),
                pltpu.SMEM((count,), jnp.int32),
                pltpu.SemaphoreType.DMA((count,)),
            ],
            limit=table_bytes + 8 * MIB,
            cost_us=2 * count if count > 1 else 0,
        )

    *far_means, table = means(
        [s + half for s in steps if s],
        before=turn_kernel,
        ins=(feats,),
        outs=[((nodes, LANES), jnp.float32)],
    )
    table = table.reshape(nodes, 1, LANES)
    tagged_shape = (chunk_shape[0] + TAG_ROWS, chunk_shape[1])
    halves, *tagged, live = call(
        functools.partial(halves_kernel, half),
        "halves",
        [
            ((half, fslice, width), bf16),
            *([(tagged_shape, bf16)] * (half - 1)),
            ((TAG_ROWS, chunk_shape[1]), bf16),
        ],
        [smem] + [vmem] * (2 * half - 1),
        (counts, *arrived, *far_means),
    )
    far_arrived = send(tagged)
    other_halves = swap(halves, "rep", 1)
    idx_rows = -(-half // 4) * n_idx
    far_own, w_nbr, pre, far_pre, idx_tags = means(
        [half],
        table=table,
        before=functools.partial(own_kernel, half, n_idx),
        ins=(*arrived, other_halves, bias_one[None]),
        outs=[
            ((half, fslice, width), bf16),
            ((pcap, width), jnp.float32),
            ((pcap, width), jnp.float32),
            ((idx_rows, width), bf16),
        ],
    )
    (cross,) = call(
        functools.partial(far_kernel, half),
        "far",
        [((pcap + idx_rows, width), bf16)],
        [vmem] * (half + 3),
        (*far_arrived, far_own, far_pre, w_nbr, idx_tags),
    )
    cross_arrived = swap(cross, "feat", half)
    turned = [*steps[1:-1], steps[0]]
    near_means = means(turned, [*far_arrived[1:], far_arrived[0]], (cross,), table=table)
    near_arrived = send(near_means, turned)
    near_own, near_times = means(
        [0],
        [live],
        table=table,
        after=(cross,),
        before=functools.partial(near_times_kernel, half, fslice, pcap, n_idx),
        ins=(w2_self, w2_nbr, *arrived),
        outs=[((half * seed_count, 4 * pcap), bf16)],
    )
    (near_pre,) = call(
        functools.partial(near_kernel, half),
        "near",
        [((pcap, width), jnp.float32)],
        [vmem] * (half + 2),
        (*near_arrived, near_own, pre, w_nbr),
        cost_us=0,
    )
    (hidden,) = call(
        hidden_kernel,
        "hidden",
        [((pcap, width), bf16)],
        [vmem] * 3,
        (live, near_pre, cross_arrived),
    )
    other_hidden = swap(hidden, "rep", 1)
    far_times, value, result = call(
        functools.partial(far_times_kernel, half, n_idx, fanout_two),
        "far_times",
        [
            ((half * seed_count, 4 * pcap), bf16),
            ((2, pcap, width), bf16),
            ((pcap, width), bf16),
        ],
        [vmem] * 4,
        (cross_arrived, hidden, w2_self, w2_nbr),
        scratch=[pltpu.SemaphoreType.DMA],
        outs=(vmem, vmem, anywhere),
    )
    *far_shares, values = call(
        functools.partial(far_share_kernel, half, fanout_two),
        "far_share",
        [((seed_count, width), bf16)] * half + [((4 * pcap, width), bf16)],
        [vmem] * 5,
        (far_times, value, other_hidden, w2_self, w2_nbr),
        limit=32 * MIB,
    )
    far_shares = send(far_shares)
    near_shares = call(
        near_share_kernel,
        "near_share",
        [((seed_count, width), bf16)] * half,
        [vmem] * 2,
        (near_times, values),
        limit=32 * MIB,
    )
    near_shares = send(near_shares)
    (far_sum,) = call(
        side_sum_kernel, "side_sum", [((seed_count, width), bf16)], [vmem] * half, far_shares
    )
    (seed_out,) = call(
        last_kernel,
        "seeds",
        [((seed_count, width), bf16)],
        [vmem] * (half + 2),
        (bias_two[None], *near_shares, swap(far_sum, "feat", half)),
    )
    return (result[None, None], seed_out)


def solution(mesh):
    placed = (
        P("feat", "groups"),
        P("groups", "rep", None, None),
        P(("groups", "feat"), "rep"),
        P(("groups", "feat", "rep")),
        P(("groups", "feat", "rep"), None),
        P("feat", None),
        P("feat", None),
        P(),
        P(),
        P(),
        P(),
    )
    return jax.shard_map(
        body,
        mesh=mesh,
        in_specs=placed,
        out_specs=(P(("groups", "feat"), "rep", None, None), P(("groups", "feat", "rep"), None)),
        check_vma=False,
    )
```

```python
import functools

import jax
import jax.numpy as jnp
from jax import lax
from jax.experimental import pallas as pl
from jax.experimental.pallas import tpu as pltpu
from jax.sharding import PartitionSpec as P

LANES = 128
MIB = 1024 * 1024


def folds(fslice, pcap):
    return 4 * fslice == 3 * LANES and pcap % 64 == 0


def is_dense(fslice, n_idx):
    return fslice % 32 == 0 and n_idx == 16


def parcel_rows(fslice, n_idx):
    return 2 * fslice - fslice // 4 + 8 if is_dense(fslice, n_idx) else 2 * fslice


def write_parcel(ref, weight, feats, digits):
    fslice, lanes = feats.shape
    ref[:fslice, :] = weight
    if is_dense(fslice, digits.shape[0]):
        cut = fslice // 4 * 3
        tail = jnp.concatenate([feats[cut:, i : i + LANES] for i in range(0, lanes, LANES)], axis=0)
        tags = jnp.concatenate([digits[:8], digits[8:]] * 2, axis=1)
        body = jnp.concatenate([feats[:cut], tail], axis=1)
        ref[fslice:, :] = jnp.concatenate([body, tags], axis=0).astype(jnp.bfloat16)
    else:
        ref[fslice:, :lanes] = feats.astype(jnp.bfloat16)
        ref[fslice : fslice + digits.shape[0], lanes:] = digits.astype(jnp.bfloat16)


def read_feats(ref, fslice, n_idx, lanes):
    if not is_dense(fslice, n_idx):
        return ref[fslice:, :lanes].astype(jnp.float32)
    cut, part = fslice // 4 * 3, fslice // 4
    tail = ref[fslice : fslice + cut, lanes:].astype(jnp.float32)
    tail = jnp.concatenate([tail[i : i + part] for i in range(0, cut, part)], axis=1)
    return jnp.concatenate([ref[fslice : fslice + cut, :lanes].astype(jnp.float32), tail], axis=0)


def read_digits(ref, fslice, n_idx, lanes):
    if not is_dense(fslice, n_idx):
        return ref[fslice : fslice + n_idx, lanes:].astype(jnp.float32)
    tags = ref[-8:, : 2 * LANES].astype(jnp.float32)
    return jnp.concatenate([tags[:, :LANES], tags[:, LANES:]], axis=0)


TAG_ROWS = 16


def live_rows(ref):
    return jnp.max(ref[-TAG_ROWS:, :].astype(jnp.float32)).astype(jnp.int32)


def pack_kernel(
    steps,
    n_feat,
    pcap,
    src_hbm,
    seed_hbm,
    nbr_hbm,
    w_self_hbm,
    w_nbr_hbm,
    pick_hbm,
    *refs,
):
    half = n_feat // 2
    parcel_refs, pick_ref, src_ref = refs[:half], refs[half], refs[half + 1]
    seed_ref, nbr_ref, w_self_ref, w_nbr_ref, fetched_ref, sems = refs[half + 2 :]
    first = pl.ds(0, src_ref.shape[1])
    copies = [
        pltpu.make_async_copy(a, b, sems.at[i])
        for i, (a, b) in enumerate(
            (
                (src_hbm.at[:, first], src_ref),
                (w_self_hbm, w_self_ref),
                (w_nbr_hbm, w_nbr_ref),
                (seed_hbm, seed_ref),
                (nbr_hbm, nbr_ref),
                (pick_hbm, fetched_ref),
            )
        )
    ]
    for copy in copies:
        copy.start()
    for copy in copies[1:]:
        copy.wait()
    stride = -(-pcap // LANES) * LANES
    words = pick_ref.shape[2] // stride
    for k in range(words):
        word = fetched_ref[:, k]
        if words < fetched_ref.shape[1]:
            word = word | (fetched_ref[:, words + k] << 16)
        pick_ref[:, :, k * stride : k * stride + pcap] = word
    feat_pos = lax.axis_index("feat")
    first_core = lax.axis_index("rep") == 0
    idx = jnp.concatenate([seed_ref[...], nbr_ref[...]], axis=0)
    high = lax.shift_right_logical(idx, 7)
    digits = jnp.concatenate([high, idx - high * 128], axis=1).astype(jnp.float32)
    weight = jnp.where(first_core, w_self_ref[...], w_nbr_ref[...])
    copies[0].wait()
    for s, parcel_ref in zip(steps, parcel_refs):
        sides = []
        for step in (s, s ^ half):
            at = pl.multiple_of(jnp.bitwise_xor(feat_pos, step) * (2 * pcap), LANES)
            block = src_ref[:, pl.ds(at, 2 * pcap)].astype(jnp.float32)
            sides.append(jnp.where(first_core, block[:, :pcap], block[:, pcap:]))
        write_parcel(parcel_ref, weight, jnp.concatenate(sides, axis=1), digits)


def turn_kernel(owned_ref, src_hbm, table_ref):
    fslice, owned = owned_ref.shape
    pieces = src_hbm.shape[1] // owned - 1
    width = next(w for w in (2048, 1536, 1024, 512, LANES) if owned % w == 0)

    def turn(ref, low, place):
        def step(i, carry):
            at = pl.multiple_of(i * width, width)
            rows = pl.ds(pl.multiple_of(place + at, LANES), width)
            table_ref[rows, :fslice] = ref[:, pl.ds(low + at, width)].T.astype(jnp.float32)
            return carry

        lax.fori_loop(0, owned // width, step, 0)

    def rest(buffer, sems):
        copies = [
            pltpu.make_async_copy(
                src_hbm.at[:, pl.ds((i + 1) * owned, owned)],
                buffer.at[:, pl.ds(i * owned, owned)],
                sems.at[i],
            )
            for i in range(pieces)
        ]
        for copy in copies:
            copy.start()
        turn(owned_ref, 0, 0)
        for i, copy in enumerate(copies):
            copy.wait()
            turn(buffer, i * owned, (i + 1) * owned)

    pl.run_scoped(
        rest,
        pltpu.VMEM((fslice, pieces * owned), jnp.bfloat16),
        pltpu.SemaphoreType.DMA((pieces,)),
    )


def mean_kernel(chosen, packed, fanout, pcap, fslice, turns, before, n_before, *refs):
    count = len(chosen)
    before_in, refs = refs[: n_before[0]], refs[n_before[0] :]
    nbr_any, *refs = refs
    if not turns:
        table_ref, *refs = refs
    out_ref, total, nbr_ref, live_ref, sems = refs[-5:]
    refs = refs[:-5]
    before_out = refs[len(refs) - n_before[1] :]
    refs = refs[: len(refs) - n_before[1]]
    chunk_refs, tagged_refs = refs[len(refs) - count :], refs[: len(refs) - count]
    feat_pos = lax.axis_index("feat")
    words = fanout // packed
    size = 16 if len(tagged_refs) or pcap % 64 else 64
    stride = -(-pcap // LANES) * LANES
    length = words * stride
    copies = [
        pltpu.make_async_copy(
            nbr_any.at[feat_pos ^ step, 0], nbr_ref.at[pl.ds(i * length, length)], sems.at[i]
        )
        for i, step in enumerate(chosen)
    ]
    for copy in copies:
        copy.start()
    for i in range(count):
        live_ref[i] = pcap
    for i, ref in enumerate(tagged_refs):
        live_ref[i] = live_rows(ref)
    if before is not None:
        before(*before_in, *before_out)
    if turns:
        table_ref = before_out[0].reshape(before_out[0].shape[0], 1, LANES)
    for copy in copies:
        copy.wait()

    def partition(i, carry):
        first = i * length

        def group(g, inner):
            at = pl.multiple_of(g * size, 16)
            start = first + at
            sums = []
            for u in range(size):
                names = [nbr_ref[start + (k * stride + u)] for k in range(words)]
                if packed == 2:
                    names = [
                        part
                        for name in names
                        for part in (name & 0xFFFF, lax.shift_right_logical(name, 16))
                    ]
                rows = [table_ref[name] for name in names]
                while len(rows) > 1:
                    rows = [a + b for a, b in zip(rows[::2], rows[1::2])] + (
                        [rows[-1]] if len(rows) % 2 else []
                    )
                sums.append(rows[0])
                if len(sums) == 16:
                    for v, row in enumerate(sums):
                        total[pl.ds(at + (u - 15 + v), 1), :] = row
                    sums = []
            return inner

        lax.fori_loop(0, lax.div(live_ref[i] + size - 1, size), group, 0)
        mean = total[...] / fanout
        if folds(fslice, pcap):
            part = pcap // 4
            lane = lax.broadcasted_iota(jnp.int32, (part, LANES), 1)
            tail = mean[3 * part :]
            for b in range(3):
                shift = (fslice - 32 * b) % LANES
                moved = pltpu.roll(tail, shift, 1) if shift else tail
                out_ref[i, pl.ds(b * part, part), :] = jnp.where(
                    lane < fslice, mean[b * part : (b + 1) * part], moved
                ).astype(jnp.bfloat16)
        else:
            out_ref[i] = mean[:, :fslice].astype(jnp.bfloat16)
        return carry

    lax.fori_loop(0, count, partition, 0)
    for i, ref in enumerate(chunk_refs):
        ref[...] = out_ref[i]


def unfold(ref, fslice, pcap):
    if not folds(fslice, pcap):
        return ref[:pcap, :]
    part = pcap // 4
    wide = ref[: 3 * part, :].astype(jnp.float32)
    lane = lax.broadcasted_iota(jnp.int32, (part, LANES), 1)
    tail = pltpu.roll(wide[:part], LANES - fslice, 1)
    for b in (1, 2):
        shift = (32 * b - fslice) % LANES
        moved = wide[b * part : (b + 1) * part]
        moved = pltpu.roll(moved, shift, 1) if shift else moved
        tail = jnp.where(lane // 32 == b, moved, tail)
    return jnp.concatenate([wide, tail], axis=0)[:, :fslice].astype(jnp.bfloat16)


def halves_kernel(half, count_ref, *refs):
    parcel_refs, chunk_refs = refs[:half], refs[half : 2 * half - 1]
    out_ref, *tagged_refs, live_ref = refs[2 * half - 1 :]
    for s, ref in enumerate(parcel_refs):
        out_ref[s] = ref[: out_ref.shape[1], :]
    live = jnp.full(live_ref.shape, count_ref[0, 0].astype(jnp.float32)).astype(jnp.bfloat16)
    live_ref[...] = live
    for chunk_ref, ref in zip(chunk_refs, tagged_refs):
        ref[:-TAG_ROWS, :] = chunk_ref[...]
        ref[-TAG_ROWS:, :] = live


def own_kernel(half, n_idx, *refs):
    parcel_refs = refs[:half]
    other_ref, bias_ref, w_ref, pre_ref, far_ref, idx_ref = refs[half:]
    fslice = w_ref.shape[1]
    pcap, width = pre_ref.shape
    first_core = lax.axis_index("rep") == 0
    feats, weights = [], []
    for s in range(half):
        mine, other = parcel_refs[s][:fslice, :], other_ref[s]
        w_ref[s] = jnp.where(first_core, other, mine)
        weights.append(jnp.where(first_core, mine, other))
        feats.append(read_feats(parcel_refs[s], fslice, n_idx, 2 * pcap))
        rows = pl.ds(s // 4 * n_idx, n_idx)
        digits = read_digits(parcel_refs[s], fslice, n_idx, 2 * pcap)
        idx_ref[rows, s % 4 * LANES : (s % 4 + 1) * LANES] = digits.astype(jnp.bfloat16)
    both = jnp.dot(
        jnp.concatenate(feats, axis=0).T.astype(jnp.bfloat16),
        jnp.concatenate(weights, axis=0),
        preferred_element_type=jnp.float32,
    )
    pre_ref[...] = both[:pcap] + bias_ref[...]
    far_ref[...] = both[pcap:]


def add_means(half, pre, mean_refs, w_ref, turn=0):
    for s, ref in enumerate(mean_refs):
        pre = pre + jnp.dot(
            unfold(ref, w_ref.shape[1], pre.shape[0]),
            w_ref[(s + turn) % (half - 1) if s < half - 1 else s],
            preferred_element_type=jnp.float32,
        )
    return pre


def far_kernel(half, *refs):
    far_ref, w_ref, idx_ref, cross_ref = refs[half:]
    pcap = far_ref.shape[0]
    cross_ref[:pcap, :] = add_means(half, far_ref[...], refs[:half], w_ref).astype(jnp.bfloat16)
    cross_ref[pcap:, :] = idx_ref[...]


def store_times(pcap, blocks, out_ref):
    n_idx, pair = blocks[0].shape
    seed_count = pair // 2
    core_rows = lax.axis_index("feat") * (2 * pcap)
    rep_pos = lax.axis_index("rep")
    row = lax.broadcasted_iota(jnp.int32, (2 * pcap, pair), 0)
    slot = jnp.where(
        row < pcap, row + core_rows + rep_pos * pcap, row + core_rows - rep_pos * pcap
    ).astype(jnp.float32)
    low = lax.broadcasted_iota(jnp.int32, (n_idx, pair), 1) < seed_count
    for s in range(0, len(blocks), 2):
        first, second = blocks[s].astype(jnp.float32), blocks[s + 1].astype(jnp.float32)
        high_part = jnp.where(low, first, pltpu.roll(second, seed_count, 1))
        low_part = jnp.where(low, pltpu.roll(first, seed_count, 1), second)
        name = high_part * 128.0 + low_part
        own = jnp.where(slot == name[:1], 1.0, 0.0)
        near = jnp.zeros((2 * pcap, pair), jnp.float32)
        for k in range(1, n_idx):
            near = near + jnp.where(slot == name[k : k + 1], 1.0, 0.0)
        place = pl.ds(s * seed_count, pair)
        out_ref[place, : 2 * pcap] = own.T.astype(jnp.bfloat16)
        out_ref[place, 2 * pcap :] = near.T.astype(jnp.bfloat16)


def near_times_kernel(half, fslice, pcap, n_idx, _, __, *refs):
    blocks = [read_digits(ref, fslice, n_idx, 2 * pcap) for ref in refs[:half]]
    store_times(pcap, blocks, refs[half])


def far_times_kernel(
    half,
    n_idx,
    fanout_two,
    cross_ref,
    hidden_ref,
    ws_ref,
    wn_ref,
    out_ref,
    value_ref,
    result_ref,
    sem,
):
    copy = pltpu.make_async_copy(hidden_ref, result_ref, sem)
    copy.start()
    pcap = hidden_ref.shape[0]
    blocks = [
        cross_ref[
            pl.ds(pcap + s // 4 * n_idx, n_idx), s % 4 * LANES : (s % 4 + 1) * LANES
        ]
        for s in range(half)
    ]
    store_times(pcap, blocks, out_ref)
    store_values(hidden_ref[...], ws_ref, wn_ref, fanout_two, value_ref)
    copy.wait()


def store_values(hidden, ws_ref, wn_ref, fanout_two, value_ref):
    value_ref[0] = jnp.dot(hidden, ws_ref[...], preferred_element_type=jnp.float32).astype(
        jnp.bfloat16
    )
    value_ref[1] = (
        jnp.dot(hidden, wn_ref[...], preferred_element_type=jnp.float32) / fanout_two
    ).astype(jnp.bfloat16)


def near_kernel(half, *refs):
    pre_ref, w_ref, out_ref = refs[half:]
    out_ref[...] = add_means(half, pre_ref[...], refs[:half], w_ref)


def hidden_kernel(live_ref, pre_ref, cross_ref, hidden_ref):
    pcap, width = hidden_ref.shape
    pre = pre_ref[...] + cross_ref[:pcap, :].astype(jnp.float32)
    live = lax.broadcasted_iota(jnp.int32, (pcap, width), 0) < live_rows(live_ref)
    hidden_ref[...] = jnp.where(live, jnp.maximum(pre, 0.0), 0.0).astype(jnp.bfloat16)


def far_share_kernel(
    half, fanout_two, far_ref, value_ref, hidden_ref, ws_ref, wn_ref, *refs
):
    *out_refs, values_ref = refs
    pcap = hidden_ref.shape[0]
    for i in range(2):
        values_ref[2 * i * pcap : (2 * i + 1) * pcap, :] = value_ref[i]
    hidden = hidden_ref[...]
    values_ref[pcap : 2 * pcap, :] = jnp.dot(
        hidden, ws_ref[...], preferred_element_type=jnp.float32
    ).astype(jnp.bfloat16)
    values_ref[3 * pcap :, :] = (
        jnp.dot(hidden, wn_ref[...], preferred_element_type=jnp.float32) / fanout_two
    ).astype(jnp.bfloat16)
    store_shares(far_ref, values_ref, out_refs)


def store_shares(times_ref, values_ref, out_refs):
    rows = times_ref.shape[0] // len(out_refs)
    part = jnp.dot(times_ref[...], values_ref[...], preferred_element_type=jnp.float32)
    for s, ref in enumerate(out_refs):
        ref[...] = part[s * rows : (s + 1) * rows].astype(jnp.bfloat16)


def near_share_kernel(near_ref, values_ref, *out_refs):
    store_shares(near_ref, values_ref, out_refs)


def side_sum_kernel(*refs):
    total = refs[0][...].astype(jnp.float32)
    for ref in refs[1:-1]:
        total = total + ref[...].astype(jnp.float32)
    refs[-1][...] = total.astype(jnp.bfloat16)


def last_kernel(bias_ref, *refs):
    total = bias_ref[...]
    for ref in refs[:-1]:
        total = total + ref[...].astype(jnp.float32)
    refs[-1][...] = jnp.maximum(total, 0.0).astype(jnp.bfloat16)


def swap(value, axis, step):
    size = lax.axis_size(axis)
    return lax.ppermute(value, axis, [(i, i ^ step) for i in range(size)])


def body(
    src_feats,
    nbr_one,
    counts,
    seed_rows,
    nbr_two,
    w1_self,
    w1_nbr,
    bias_one,
    w2_self,
    w2_nbr,
    bias_two,
):
    n_feat = lax.axis_size("feat")
    half = n_feat // 2
    steps = list(range(half - 1, -1, -1))
    fslice, nodes = src_feats.shape
    fanout_one, pcap = nbr_one.shape[2:]
    width = w1_self.shape[1]
    seed_count, fanout_two = nbr_two.shape
    n_idx = fanout_two + 1
    bf16 = jnp.bfloat16
    vmem = pl.BlockSpec(memory_space=pltpu.VMEM)
    smem = pl.BlockSpec(memory_space=pltpu.SMEM)
    hbm = pl.BlockSpec(memory_space=pltpu.HBM)
    anywhere = pl.BlockSpec(memory_space=pl.ANY)
    table_bytes = nodes * LANES * 4

    def call(kernel, name, shapes, ins, args, after=(), scratch=(), limit=16 * MIB, cost_us=1, outs=None):
        def wrapped(*refs):
            kernel(*refs[: len(args)], *refs[len(args) + len(after) :])

        return pl.pallas_call(
            wrapped,
            out_shape=tuple(jax.ShapeDtypeStruct(shape, dtype) for shape, dtype in shapes),
            in_specs=[*ins, *([anywhere] * len(after))],
            out_specs=outs or (vmem,) * len(shapes),
            scratch_shapes=scratch,
            compiler_params=pltpu.CompilerParams(vmem_limit_bytes=limit),
            cost_estimate=pl.CostEstimate(
                flops=int(cost_us * 1_100_000_000), bytes_accessed=0, transcendentals=0
            ),
            name=name,
        )(*args, *after)

    def pinned(value):
        return pltpu.with_memory_space_constraint(value, pltpu.HBM)

    def send(chunks, steps=steps):
        return [swap(chunk, "feat", s) if s else chunk for s, chunk in zip(steps, chunks)]

    owned = n_feat * 2 * pcap
    picks = jnp.transpose(nbr_one, (0, 2, 1, 3))
    packed = 2 if fanout_one % 2 == 0 and nodes <= 1 << 16 else 1
    words = (n_feat, 1, fanout_one // packed * (-(-pcap // LANES) * LANES))
    *parcels, picks, feats = call(
        functools.partial(pack_kernel, steps, n_feat, pcap),
        "pack",
        [((parcel_rows(fslice, n_idx), width), bf16)] * half
        + [(words, jnp.int32), ((fslice, owned), bf16)],
        [hbm] * 6,
        [pinned(x) for x in (src_feats, seed_rows[None], nbr_two.T, w1_self, w1_nbr, picks)],
        scratch=[
            pltpu.VMEM((1, seed_count), jnp.int32),
            pltpu.VMEM((fanout_two, seed_count), jnp.int32),
            pltpu.VMEM((fslice, width), bf16),
            pltpu.VMEM((fslice, width), bf16),
            pltpu.VMEM((n_feat, fanout_one, 1, pcap), jnp.int32),
            pltpu.SemaphoreType.DMA((6,)),
        ],
        limit=32 * MIB,
    )
    arrived = send(parcels)
    chunk_shape = (pcap // 4 * 3, LANES) if folds(fslice, pcap) else (pcap, fslice)

    def means(chosen, tagged=(), after=(), before=None, ins=(), outs=(), table=None):
        count = len(chosen)
        tables = () if table is None else (table,)
        return call(
            functools.partial(
                mean_kernel,
                tuple(chosen),
                packed,
                fanout_one,
                pcap,
                fslice,
                table is None,
                before,
                (len(ins), len(outs)),
            ),
            "mean",
            [(chunk_shape, bf16)] * count + list(outs),
            ([vmem, hbm] if table is None else [vmem] * len(ins))
            + [anywhere]
            + [vmem] * (len(tables) + len(tagged)),
            (*ins, picks, *tables, *tagged),
            after=after,
            scratch=[
                pltpu.VMEM((count, *chunk_shape), bf16),
                pltpu.VMEM((pcap, LANES), jnp.float32),
                pltpu.SMEM((count * words[2],), jnp.int32),
                pltpu.SMEM((count,), jnp.int32),
                pltpu.SemaphoreType.DMA((count,)),
            ],
            limit=table_bytes + 8 * MIB,
            cost_us=2 * count if count > 1 else 0,
        )

    *far_means, table = means(
        [s + half for s in steps if s],
        before=turn_kernel,
        ins=(feats, pinned(src_feats)),
        outs=[((nodes, LANES), jnp.float32)],
    )
    table = table.reshape(nodes, 1, LANES)
    tagged_shape = (chunk_shape[0] + TAG_ROWS, chunk_shape[1])
    halves, *tagged, live = call(
        functools.partial(halves_kernel, half),
        "halves",
        [
            ((half, fslice, width), bf16),
            *([(tagged_shape, bf16)] * (half - 1)),
            ((TAG_ROWS, chunk_shape[1]), bf16),
        ],
        [smem] + [vmem] * (2 * half - 1),
        (counts, *arrived, *far_means),
    )
    far_arrived = send(tagged)
    other_halves = swap(halves, "rep", 1)
    idx_rows = -(-half // 4) * n_idx
    far_own, w_nbr, pre, far_pre, idx_tags = means(
        [half],
        table=table,
        before=functools.partial(own_kernel, half, n_idx),
        ins=(*arrived, other_halves, bias_one[None]),
        outs=[
            ((half, fslice, width), bf16),
            ((pcap, width), jnp.float32),
            ((pcap, width), jnp.float32),
            ((idx_rows, width), bf16),
        ],
    )
    (cross,) = call(
        functools.partial(far_kernel, half),
        "far",
        [((pcap + idx_rows, width), bf16)],
        [vmem] * (half + 3),
        (*far_arrived, far_own, far_pre, w_nbr, idx_tags),
    )
    cross_arrived = swap(cross, "feat", half)
    turned = steps[:-1]
    near_means = means(turned, far_arrived, (cross,), table=table)
    near_arrived = send(near_means, turned)
    near_own, near_times = means(
        [0],
        [live],
        table=table,
        after=(cross,),
        before=functools.partial(near_times_kernel, half, fslice, pcap, n_idx),
        ins=(w2_self, w2_nbr, *arrived),
        outs=[((half * seed_count, 4 * pcap), bf16)],
    )
    (near_pre,) = call(
        functools.partial(near_kernel, half),
        "near",
        [((pcap, width), jnp.float32)],
        [vmem] * (half + 2),
        (*near_arrived, near_own, pre, w_nbr),
        cost_us=0,
    )
    (hidden,) = call(
        hidden_kernel,
        "hidden",
        [((pcap, width), bf16)],
        [vmem] * 3,
        (live, near_pre, cross_arrived),
    )
    other_hidden = swap(hidden, "rep", 1)
    far_times, value, result = call(
        functools.partial(far_times_kernel, half, n_idx, fanout_two),
        "far_times",
        [
            ((half * seed_count, 4 * pcap), bf16),
            ((2, pcap, width), bf16),
            ((pcap, width), bf16),
        ],
        [vmem] * 4,
        (cross_arrived, hidden, w2_self, w2_nbr),
        scratch=[pltpu.SemaphoreType.DMA],
        outs=(vmem, vmem, anywhere),
    )
    *far_shares, values = call(
        functools.partial(far_share_kernel, half, fanout_two),
        "far_share",
        [((seed_count, width), bf16)] * half + [((4 * pcap, width), bf16)],
        [vmem] * 5,
        (far_times, value, other_hidden, w2_self, w2_nbr),
        limit=32 * MIB,
    )
    far_shares = send(far_shares)
    near_shares = call(
        near_share_kernel,
        "near_share",
        [((seed_count, width), bf16)] * half,
        [vmem] * 2,
        (near_times, values),
        limit=32 * MIB,
    )
    near_shares = send(near_shares)
    (far_sum,) = call(
        side_sum_kernel, "side_sum", [((seed_count, width), bf16)], [vmem] * half, far_shares
    )
    (seed_out,) = call(
        last_kernel,
        "seeds",
        [((seed_count, width), bf16)],
        [vmem] * (half + 2),
        (bias_two[None], *near_shares, swap(far_sum, "feat", half)),
    )
    return (result[None, None], seed_out)


def solution(mesh):
    placed = (
        P("feat", "groups"),
        P("groups", "rep", None, None),
        P(("groups", "feat"), "rep"),
        P(("groups", "feat", "rep")),
        P(("groups", "feat", "rep"), None),
        P("feat", None),
        P("feat", None),
        P(),
        P(),
        P(),
        P(),
    )
    return jax.shard_map(
        body,
        mesh=mesh,
        in_specs=placed,
        out_specs=(P(("groups", "feat"), "rep", None, None), P(("groups", "feat", "rep"), None)),
        check_vma=False,
    )
```

```python
import functools

import jax
import jax.numpy as jnp
from jax import lax
from jax.experimental import pallas as pl
from jax.experimental.pallas import tpu as pltpu
from jax.sharding import PartitionSpec as P

LANES = 128
MIB = 1024 * 1024


def folds(fslice, pcap):
    return 4 * fslice == 3 * LANES and pcap % 64 == 0


def is_dense(fslice, n_idx):
    return fslice % 32 == 0 and n_idx == 16


def parcel_rows(fslice, n_idx):
    return 2 * fslice - fslice // 4 + 8 if is_dense(fslice, n_idx) else 2 * fslice


def write_parcel(ref, weight, feats, digits):
    fslice, lanes = feats.shape
    ref[:fslice, :] = weight
    if is_dense(fslice, digits.shape[0]):
        cut = fslice // 4 * 3
        tail = jnp.concatenate([feats[cut:, i : i + LANES] for i in range(0, lanes, LANES)], axis=0)
        tags = jnp.concatenate([digits[:8], digits[8:]] * 2, axis=1)
        body = jnp.concatenate([feats[:cut], tail], axis=1)
        ref[fslice:, :] = jnp.concatenate([body, tags], axis=0).astype(jnp.bfloat16)
    else:
        ref[fslice:, :lanes] = feats.astype(jnp.bfloat16)
        ref[fslice : fslice + digits.shape[0], lanes:] = digits.astype(jnp.bfloat16)


def read_feats(ref, fslice, n_idx, lanes):
    if not is_dense(fslice, n_idx):
        return ref[fslice:, :lanes].astype(jnp.float32)
    cut, part = fslice // 4 * 3, fslice // 4
    tail = ref[fslice : fslice + cut, lanes:].astype(jnp.float32)
    tail = jnp.concatenate([tail[i : i + part] for i in range(0, cut, part)], axis=1)
    return jnp.concatenate([ref[fslice : fslice + cut, :lanes].astype(jnp.float32), tail], axis=0)


def read_digits(ref, fslice, n_idx, lanes):
    if not is_dense(fslice, n_idx):
        return ref[fslice : fslice + n_idx, lanes:].astype(jnp.float32)
    tags = ref[-8:, : 2 * LANES].astype(jnp.float32)
    return jnp.concatenate([tags[:, :LANES], tags[:, LANES:]], axis=0)


TAG_ROWS = 16


def live_rows(ref):
    return jnp.max(ref[-TAG_ROWS:, :].astype(jnp.float32)).astype(jnp.int32)


def pack_kernel(
    steps,
    n_feat,
    pcap,
    src_hbm,
    seed_hbm,
    nbr_hbm,
    w_self_hbm,
    w_nbr_hbm,
    pick_hbm,
    *refs,
):
    half = n_feat // 2
    parcel_refs, pick_ref, src_ref = refs[:half], refs[half], refs[half + 1]
    seed_ref, nbr_ref, w_self_ref, w_nbr_ref, fetched_ref, sems = refs[half + 2 :]
    first = pl.ds(0, src_ref.shape[1])
    copies = [
        pltpu.make_async_copy(a, b, sems.at[i])
        for i, (a, b) in enumerate(
            (
                (src_hbm.at[:, first], src_ref),
                (w_self_hbm, w_self_ref),
                (w_nbr_hbm, w_nbr_ref),
                (seed_hbm, seed_ref),
                (nbr_hbm, nbr_ref),
                (pick_hbm, fetched_ref),
            )
        )
    ]
    for copy in copies:
        copy.start()
    for copy in copies[1:]:
        copy.wait()
    stride = -(-pcap // LANES) * LANES
    words = pick_ref.shape[2] // stride
    for k in range(words):
        word = fetched_ref[:, k]
        if words < fetched_ref.shape[1]:
            word = word | (fetched_ref[:, words + k] << 16)
        pick_ref[:, :, k * stride : k * stride + pcap] = word
    feat_pos = lax.axis_index("feat")
    first_core = lax.axis_index("rep") == 0
    idx = jnp.concatenate([seed_ref[...], nbr_ref[...]], axis=0)
    high = lax.shift_right_logical(idx, 7)
    digits = jnp.concatenate([high, idx - high * 128], axis=1).astype(jnp.float32)
    weight = jnp.where(first_core, w_self_ref[...], w_nbr_ref[...])
    copies[0].wait()
    for s, parcel_ref in zip(steps, parcel_refs):
        sides = []
        for step in (s, s ^ half):
            at = pl.multiple_of(jnp.bitwise_xor(feat_pos, step) * (2 * pcap), LANES)
            block = src_ref[:, pl.ds(at, 2 * pcap)].astype(jnp.float32)
            sides.append(jnp.where(first_core, block[:, :pcap], block[:, pcap:]))
        write_parcel(parcel_ref, weight, jnp.concatenate(sides, axis=1), digits)


def turn_kernel(owned_ref, src_hbm, table_ref):
    fslice, owned = owned_ref.shape
    pieces = src_hbm.shape[1] // owned - 1
    width = next(w for w in (2048, 1536, 1024, 512, LANES) if owned % w == 0)

    def turn(ref, low, place):
        def step(i, carry):
            at = pl.multiple_of(i * width, width)
            rows = pl.ds(pl.multiple_of(place + at, LANES), width)
            table_ref[rows, :fslice] = ref[:, pl.ds(low + at, width)].T.astype(jnp.float32)
            return carry

        lax.fori_loop(0, owned // width, step, 0)

    def rest(buffer, sems):
        copies = [
            pltpu.make_async_copy(
                src_hbm.at[:, pl.ds((i + 1) * owned, owned)],
                buffer.at[:, pl.ds(i * owned, owned)],
                sems.at[i],
            )
            for i in range(pieces)
        ]
        for copy in copies:
            copy.start()
        turn(owned_ref, 0, 0)
        for i, copy in enumerate(copies):
            copy.wait()
            turn(buffer, i * owned, (i + 1) * owned)

    pl.run_scoped(
        rest,
        pltpu.VMEM((fslice, pieces * owned), jnp.bfloat16),
        pltpu.SemaphoreType.DMA((pieces,)),
    )


def mean_kernel(chosen, packed, fanout, pcap, fslice, turns, before, n_before, *refs):
    count = len(chosen)
    before_in, refs = refs[: n_before[0]], refs[n_before[0] :]
    nbr_any, *refs = refs
    if not turns:
        table_ref, *refs = refs
    out_ref, total, nbr_ref, live_ref, sems = refs[-5:]
    refs = refs[:-5]
    before_out = refs[len(refs) - n_before[1] :]
    refs = refs[: len(refs) - n_before[1]]
    chunk_refs, tagged_refs = refs[len(refs) - count :], refs[: len(refs) - count]
    feat_pos = lax.axis_index("feat")
    words = fanout // packed
    size = 16 if len(tagged_refs) or pcap % 64 else 64
    stride = -(-pcap // LANES) * LANES
    length = words * stride
    copies = [
        pltpu.make_async_copy(
            nbr_any.at[feat_pos ^ step, 0], nbr_ref.at[pl.ds(i * length, length)], sems.at[i]
        )
        for i, step in enumerate(chosen)
    ]
    for copy in copies:
        copy.start()
    for i in range(count):
        live_ref[i] = pcap
    for i, ref in enumerate(tagged_refs):
        live_ref[i] = live_rows(ref)
    if before is not None:
        before(*before_in, *before_out)
    if turns:
        table_ref = before_out[0].reshape(before_out[0].shape[0], 1, LANES)
    for copy in copies:
        copy.wait()

    def partition(i, carry):
        first = i * length

        def group(g, inner):
            at = pl.multiple_of(g * size, 16)
            start = first + at
            sums = []
            for u in range(size):
                names = [nbr_ref[start + (k * stride + u)] for k in range(words)]
                if packed == 2:
                    names = [
                        part
                        for name in names
                        for part in (name & 0xFFFF, lax.shift_right_logical(name, 16))
                    ]
                rows = [table_ref[name] for name in names]
                while len(rows) > 1:
                    rows = [a + b for a, b in zip(rows[::2], rows[1::2])] + (
                        [rows[-1]] if len(rows) % 2 else []
                    )
                sums.append(rows[0])
                if len(sums) == 16:
                    for v, row in enumerate(sums):
                        total[pl.ds(at + (u - 15 + v), 1), :] = row
                    sums = []
            return inner

        lax.fori_loop(0, lax.div(live_ref[i] + size - 1, size), group, 0)
        mean = total[...] / fanout
        if folds(fslice, pcap):
            part = pcap // 4
            lane = lax.broadcasted_iota(jnp.int32, (part, LANES), 1)
            tail = mean[3 * part :]
            for b in range(3):
                shift = (fslice - 32 * b) % LANES
                moved = pltpu.roll(tail, shift, 1) if shift else tail
                out_ref[i, pl.ds(b * part, part), :] = jnp.where(
                    lane < fslice, mean[b * part : (b + 1) * part], moved
                ).astype(jnp.bfloat16)
        else:
            out_ref[i] = mean[:, :fslice].astype(jnp.bfloat16)
        return carry

    lax.fori_loop(0, count, partition, 0)
    for i, ref in enumerate(chunk_refs):
        ref[...] = out_ref[i]


def unfold(ref, fslice, pcap):
    if not folds(fslice, pcap):
        return ref[:pcap, :]
    part = pcap // 4
    wide = ref[: 3 * part, :].astype(jnp.float32)
    lane = lax.broadcasted_iota(jnp.int32, (part, LANES), 1)
    tail = pltpu.roll(wide[:part], LANES - fslice, 1)
    for b in (1, 2):
        shift = (32 * b - fslice) % LANES
        moved = wide[b * part : (b + 1) * part]
        moved = pltpu.roll(moved, shift, 1) if shift else moved
        tail = jnp.where(lane // 32 == b, moved, tail)
    return jnp.concatenate([wide, tail], axis=0)[:, :fslice].astype(jnp.bfloat16)


def halves_kernel(half, count_ref, *refs):
    parcel_refs, chunk_refs = refs[:half], refs[half : 2 * half - 1]
    out_ref, *tagged_refs, live_ref = refs[2 * half - 1 :]
    for s, ref in enumerate(parcel_refs):
        out_ref[s] = ref[: out_ref.shape[1], :]
    live = jnp.full(live_ref.shape, count_ref[0, 0].astype(jnp.float32)).astype(jnp.bfloat16)
    live_ref[...] = live
    for chunk_ref, ref in zip(chunk_refs, tagged_refs):
        ref[:-TAG_ROWS, :] = chunk_ref[...]
        ref[-TAG_ROWS:, :] = live


def own_kernel(half, n_idx, *refs):
    parcel_refs = refs[:half]
    other_ref, bias_ref, w_ref, pre_ref, far_ref, idx_ref = refs[half:]
    fslice = w_ref.shape[1]
    pcap, width = pre_ref.shape
    first_core = lax.axis_index("rep") == 0
    feats, weights = [], []
    for s in range(half):
        mine, other = parcel_refs[s][:fslice, :], other_ref[s]
        w_ref[s] = jnp.where(first_core, other, mine)
        weights.append(jnp.where(first_core, mine, other))
        feats.append(read_feats(parcel_refs[s], fslice, n_idx, 2 * pcap))
        rows = pl.ds(s // 4 * n_idx, n_idx)
        digits = read_digits(parcel_refs[s], fslice, n_idx, 2 * pcap)
        idx_ref[rows, s % 4 * LANES : (s % 4 + 1) * LANES] = digits.astype(jnp.bfloat16)
    both = jnp.dot(
        jnp.concatenate(feats, axis=0).T.astype(jnp.bfloat16),
        jnp.concatenate(weights, axis=0),
        preferred_element_type=jnp.float32,
    )
    pre_ref[...] = both[:pcap] + bias_ref[...]
    far_ref[...] = both[pcap:]


def add_means(half, pre, mean_refs, w_ref, turn=0):
    for s, ref in enumerate(mean_refs):
        pre = pre + jnp.dot(
            unfold(ref, w_ref.shape[1], pre.shape[0]),
            w_ref[(s + turn) % (half - 1) if s < half - 1 else s],
            preferred_element_type=jnp.float32,
        )
    return pre


def far_kernel(half, *refs):
    far_ref, w_ref, idx_ref, cross_ref = refs[half:]
    pcap = far_ref.shape[0]
    cross_ref[:pcap, :] = add_means(half, far_ref[...], refs[:half], w_ref).astype(jnp.bfloat16)
    cross_ref[pcap:, :] = idx_ref[...]


def store_times(pcap, blocks, out_ref):
    n_idx, pair = blocks[0].shape
    seed_count = pair // 2
    core_rows = lax.axis_index("feat") * (2 * pcap)
    rep_pos = lax.axis_index("rep")
    row = lax.broadcasted_iota(jnp.int32, (2 * pcap, pair), 0)
    slot = jnp.where(
        row < pcap, row + core_rows + rep_pos * pcap, row + core_rows - rep_pos * pcap
    ).astype(jnp.float32)
    low = lax.broadcasted_iota(jnp.int32, (n_idx, pair), 1) < seed_count
    for s in range(0, len(blocks), 2):
        first, second = blocks[s].astype(jnp.float32), blocks[s + 1].astype(jnp.float32)
        high_part = jnp.where(low, first, pltpu.roll(second, seed_count, 1))
        low_part = jnp.where(low, pltpu.roll(first, seed_count, 1), second)
        name = high_part * 128.0 + low_part
        own = jnp.where(slot == name[:1], 1.0, 0.0)
        near = jnp.zeros((2 * pcap, pair), jnp.float32)
        for k in range(1, n_idx):
            near = near + jnp.where(slot == name[k : k + 1], 1.0, 0.0)
        place = pl.ds(s * seed_count, pair)
        out_ref[place, : 2 * pcap] = own.T.astype(jnp.bfloat16)
        out_ref[place, 2 * pcap :] = near.T.astype(jnp.bfloat16)


def near_times_kernel(half, fslice, pcap, n_idx, _, __, *refs):
    blocks = [read_digits(ref, fslice, n_idx, 2 * pcap) for ref in refs[:half]]
    store_times(pcap, blocks, refs[half])


def far_times_kernel(
    half,
    n_idx,
    fanout_two,
    cross_ref,
    hidden_ref,
    ws_ref,
    wn_ref,
    out_ref,
    value_ref,
    result_ref,
    sem,
):
    copy = pltpu.make_async_copy(hidden_ref, result_ref, sem)
    copy.start()
    pcap = hidden_ref.shape[0]
    blocks = [
        cross_ref[
            pl.ds(pcap + s // 4 * n_idx, n_idx), s % 4 * LANES : (s % 4 + 1) * LANES
        ]
        for s in range(half)
    ]
    store_times(pcap, blocks, out_ref)
    store_values(hidden_ref[...], ws_ref, wn_ref, fanout_two, value_ref)
    copy.wait()


def store_values(hidden, ws_ref, wn_ref, fanout_two, value_ref):
    value_ref[0] = jnp.dot(hidden, ws_ref[...], preferred_element_type=jnp.float32).astype(
        jnp.bfloat16
    )
    value_ref[1] = (
        jnp.dot(hidden, wn_ref[...], preferred_element_type=jnp.float32) / fanout_two
    ).astype(jnp.bfloat16)


def near_kernel(half, *refs):
    pre_ref, w_ref, out_ref = refs[half:]
    out_ref[...] = add_means(half, pre_ref[...], refs[:half], w_ref)


def hidden_kernel(live_ref, pre_ref, cross_ref, hidden_ref):
    pcap, width = hidden_ref.shape
    pre = pre_ref[...] + cross_ref[:pcap, :].astype(jnp.float32)
    live = lax.broadcasted_iota(jnp.int32, (pcap, width), 0) < live_rows(live_ref)
    hidden_ref[...] = jnp.where(live, jnp.maximum(pre, 0.0), 0.0).astype(jnp.bfloat16)


def far_share_kernel(
    half, fanout_two, far_ref, value_ref, hidden_ref, ws_ref, wn_ref, *refs
):
    *out_refs, values_ref = refs
    pcap = hidden_ref.shape[0]
    for i in range(2):
        values_ref[2 * i * pcap : (2 * i + 1) * pcap, :] = value_ref[i]
    hidden = hidden_ref[...]
    values_ref[pcap : 2 * pcap, :] = jnp.dot(
        hidden, ws_ref[...], preferred_element_type=jnp.float32
    ).astype(jnp.bfloat16)
    values_ref[3 * pcap :, :] = (
        jnp.dot(hidden, wn_ref[...], preferred_element_type=jnp.float32) / fanout_two
    ).astype(jnp.bfloat16)
    store_shares(far_ref, values_ref, out_refs)


def store_shares(times_ref, values_ref, out_refs):
    rows = times_ref.shape[0] // len(out_refs)
    part = jnp.dot(times_ref[...], values_ref[...], preferred_element_type=jnp.float32)
    for s, ref in enumerate(out_refs):
        ref[...] = part[s * rows : (s + 1) * rows].astype(jnp.bfloat16)


def near_share_kernel(places, near_ref, values_ref, *out_refs):
    for place, ref in zip(places, out_refs):
        rows = ref.shape[0]
        times = near_ref[place * rows : (place + 1) * rows, :]
        ref[...] = jnp.dot(times, values_ref[...], preferred_element_type=jnp.float32).astype(
            jnp.bfloat16
        )


def side_sum_kernel(*refs):
    total = refs[0][...].astype(jnp.float32)
    for ref in refs[1:-1]:
        total = total + ref[...].astype(jnp.float32)
    refs[-1][: total.shape[0], :] = total.astype(jnp.bfloat16)


def last_kernel(bias_ref, *refs):
    total = bias_ref[...]
    for ref in refs[:-1]:
        total = total + ref[: refs[-1].shape[0], :].astype(jnp.float32)
    refs[-1][...] = jnp.maximum(total, 0.0).astype(jnp.bfloat16)


def swap(value, axis, step):
    size = lax.axis_size(axis)
    return lax.ppermute(value, axis, [(i, i ^ step) for i in range(size)])


def body(
    src_feats,
    nbr_one,
    counts,
    seed_rows,
    nbr_two,
    w1_self,
    w1_nbr,
    bias_one,
    w2_self,
    w2_nbr,
    bias_two,
):
    n_feat = lax.axis_size("feat")
    half = n_feat // 2
    steps = list(range(half - 1, -1, -1))
    fslice, nodes = src_feats.shape
    fanout_one, pcap = nbr_one.shape[2:]
    width = w1_self.shape[1]
    seed_count, fanout_two = nbr_two.shape
    n_idx = fanout_two + 1
    bf16 = jnp.bfloat16
    vmem = pl.BlockSpec(memory_space=pltpu.VMEM)
    smem = pl.BlockSpec(memory_space=pltpu.SMEM)
    hbm = pl.BlockSpec(memory_space=pltpu.HBM)
    anywhere = pl.BlockSpec(memory_space=pl.ANY)
    table_bytes = nodes * LANES * 4

    def call(kernel, name, shapes, ins, args, after=(), scratch=(), limit=16 * MIB, cost_us=1, outs=None):
        def wrapped(*refs):
            kernel(*refs[: len(args)], *refs[len(args) + len(after) :])

        return pl.pallas_call(
            wrapped,
            out_shape=tuple(jax.ShapeDtypeStruct(shape, dtype) for shape, dtype in shapes),
            in_specs=[*ins, *([anywhere] * len(after))],
            out_specs=outs or (vmem,) * len(shapes),
            scratch_shapes=scratch,
            compiler_params=pltpu.CompilerParams(vmem_limit_bytes=limit),
            cost_estimate=pl.CostEstimate(
                flops=int(cost_us * 1_100_000_000), bytes_accessed=0, transcendentals=0
            ),
            name=name,
        )(*args, *after)

    def pinned(value):
        return pltpu.with_memory_space_constraint(value, pltpu.HBM)

    def send(chunks, steps=steps):
        return [swap(chunk, "feat", s) if s else chunk for s, chunk in zip(steps, chunks)]

    owned = n_feat * 2 * pcap
    picks = jnp.transpose(nbr_one, (0, 2, 1, 3))
    packed = 2 if fanout_one % 2 == 0 and nodes <= 1 << 16 else 1
    words = (n_feat, 1, fanout_one // packed * (-(-pcap // LANES) * LANES))
    *parcels, picks, feats = call(
        functools.partial(pack_kernel, steps, n_feat, pcap),
        "pack",
        [((parcel_rows(fslice, n_idx), width), bf16)] * half
        + [(words, jnp.int32), ((fslice, owned), bf16)],
        [hbm] * 6,
        [pinned(x) for x in (src_feats, seed_rows[None], nbr_two.T, w1_self, w1_nbr, picks)],
        scratch=[
            pltpu.VMEM((1, seed_count), jnp.int32),
            pltpu.VMEM((fanout_two, seed_count), jnp.int32),
            pltpu.VMEM((fslice, width), bf16),
            pltpu.VMEM((fslice, width), bf16),
            pltpu.VMEM((n_feat, fanout_one, 1, pcap), jnp.int32),
            pltpu.SemaphoreType.DMA((6,)),
        ],
        limit=32 * MIB,
    )
    arrived = send(parcels)
    chunk_shape = (pcap // 4 * 3, LANES) if folds(fslice, pcap) else (pcap, fslice)

    def means(chosen, tagged=(), after=(), before=None, ins=(), outs=(), table=None):
        count = len(chosen)
        tables = () if table is None else (table,)
        return call(
            functools.partial(
                mean_kernel,
                tuple(chosen),
                packed,
                fanout_one,
                pcap,
                fslice,
                table is None,
                before,
                (len(ins), len(outs)),
            ),
            "mean",
            [(chunk_shape, bf16)] * count + list(outs),
            ([vmem, hbm] if table is None else [vmem] * len(ins))
            + [anywhere]
            + [vmem] * (len(tables) + len(tagged)),
            (*ins, picks, *tables, *tagged),
            after=after,
            scratch=[
                pltpu.VMEM((count, *chunk_shape), bf16),
                pltpu.VMEM((pcap, LANES), jnp.float32),
                pltpu.SMEM((count * words[2],), jnp.int32),
                pltpu.SMEM((count,), jnp.int32),
                pltpu.SemaphoreType.DMA((count,)),
            ],
            limit=table_bytes + 8 * MIB,
            cost_us=2 * count if count > 1 else 0,
        )

    *far_means, table = means(
        [s + half for s in steps if s],
        before=turn_kernel,
        ins=(feats, pinned(src_feats)),
        outs=[((nodes, LANES), jnp.float32)],
    )
    table = table.reshape(nodes, 1, LANES)
    tagged_shape = (chunk_shape[0] + TAG_ROWS, chunk_shape[1])
    halves, *tagged, live = call(
        functools.partial(halves_kernel, half),
        "halves",
        [
            ((half, fslice, width), bf16),
            *([(tagged_shape, bf16)] * (half - 1)),
            ((TAG_ROWS, chunk_shape[1]), bf16),
        ],
        [smem] + [vmem] * (2 * half - 1),
        (counts, *arrived, *far_means),
    )
    far_arrived = send(tagged)
    other_halves = swap(halves, "rep", 1)
    idx_rows = -(-half // 4) * n_idx
    far_own, w_nbr, pre, far_pre, idx_tags = means(
        [half],
        table=table,
        before=functools.partial(own_kernel, half, n_idx),
        ins=(*arrived, other_halves, bias_one[None]),
        outs=[
            ((half, fslice, width), bf16),
            ((pcap, width), jnp.float32),
            ((pcap, width), jnp.float32),
            ((idx_rows, width), bf16),
        ],
    )
    (cross,) = call(
        functools.partial(far_kernel, half),
        "far",
        [((pcap + idx_rows, width), bf16)],
        [vmem] * (half + 3),
        (*far_arrived, far_own, far_pre, w_nbr, idx_tags),
    )
    cross_arrived = swap(cross, "feat", half)
    turned = steps[:-1]
    near_means = means(turned, far_arrived, (cross,), table=table)
    near_arrived = send(near_means, turned)
    near_own, near_times = means(
        [0],
        [live],
        table=table,
        after=(cross,),
        before=functools.partial(near_times_kernel, half, fslice, pcap, n_idx),
        ins=(w2_self, w2_nbr, *arrived),
        outs=[((half * seed_count, 4 * pcap), bf16)],
    )
    (near_pre,) = call(
        functools.partial(near_kernel, half),
        "near",
        [((pcap, width), jnp.float32)],
        [vmem] * (half + 2),
        (*near_arrived, near_own, pre, w_nbr),
        cost_us=0,
    )
    (hidden,) = call(
        hidden_kernel,
        "hidden",
        [((pcap, width), bf16)],
        [vmem] * 3,
        (live, near_pre, cross_arrived),
    )
    other_hidden = swap(hidden, "rep", 1)
    far_times, value, result = call(
        functools.partial(far_times_kernel, half, n_idx, fanout_two),
        "far_times",
        [
            ((half * seed_count, 4 * pcap), bf16),
            ((2, pcap, width), bf16),
            ((pcap, width), bf16),
        ],
        [vmem] * 4,
        (cross_arrived, hidden, w2_self, w2_nbr),
        scratch=[pltpu.SemaphoreType.DMA],
        outs=(vmem, vmem, anywhere),
    )
    *far_shares, values = call(
        functools.partial(far_share_kernel, half, fanout_two),
        "far_share",
        [((seed_count, width), bf16)] * half + [((4 * pcap, width), bf16)],
        [vmem] * 5,
        (far_times, value, other_hidden, w2_self, w2_nbr),
        limit=32 * MIB,
    )
    far_shares = send(far_shares)
    def near_share(places, after=()):
        return call(
            functools.partial(near_share_kernel, places),
            "near_share",
            [((seed_count, width), bf16)] * len(places),
            [vmem] * 2,
            (near_times, values),
            after=after,
            limit=32 * MIB,
        )

    *near_shares, near_last = near_share([*range(half - 2), half - 1])
    near_shares = [swap(share, "feat", s) for share, s in zip(near_shares, steps)]
    (far_sum,) = call(
        side_sum_kernel, "side_sum", [((seed_count + 8, width), bf16)], [vmem] * half, far_shares
    )
    (near_late,) = near_share([half - 2], (far_sum,))
    (seed_out,) = call(
        last_kernel,
        "seeds",
        [((seed_count, width), bf16)],
        [vmem] * (half + 2),
        (
            bias_two[None],
            *near_shares,
            swap(near_late, "feat", 1),
            near_last,
            swap(far_sum, "feat", half),
        ),
    )
    return (result[None, None], seed_out)


def solution(mesh):
    placed = (
        P("feat", "groups"),
        P("groups", "rep", None, None),
        P(("groups", "feat"), "rep"),
        P(("groups", "feat", "rep")),
        P(("groups", "feat", "rep"), None),
        P("feat", None),
        P("feat", None),
        P(),
        P(),
        P(),
        P(),
    )
    return jax.shard_map(
        body,
        mesh=mesh,
        in_specs=placed,
        out_specs=(P(("groups", "feat"), "rep", None, None), P(("groups", "feat", "rep"), None)),
        check_vma=False,
    )
```

```python
import functools

import jax
import jax.numpy as jnp
from jax import lax
from jax.experimental import pallas as pl
from jax.experimental.pallas import tpu as pltpu
from jax.sharding import PartitionSpec as P

LANES = 128
MIB = 1024 * 1024


def folds(fslice, pcap):
    return 4 * fslice == 3 * LANES and pcap % 64 == 0


def is_dense(fslice, n_idx):
    return fslice % 32 == 0 and n_idx == 16


def parcel_rows(fslice, n_idx):
    return 2 * fslice - fslice // 4 + 8 if is_dense(fslice, n_idx) else 2 * fslice


def write_parcel(ref, weight, feats, digits):
    fslice, lanes = feats.shape
    ref[:fslice, :] = weight
    if is_dense(fslice, digits.shape[0]):
        cut = fslice // 4 * 3
        tail = jnp.concatenate([feats[cut:, i : i + LANES] for i in range(0, lanes, LANES)], axis=0)
        tags = jnp.concatenate([digits[:8], digits[8:]] * 2, axis=1)
        body = jnp.concatenate([feats[:cut], tail], axis=1)
        ref[fslice:, :] = jnp.concatenate([body, tags], axis=0).astype(jnp.bfloat16)
    else:
        ref[fslice:, :lanes] = feats.astype(jnp.bfloat16)
        ref[fslice : fslice + digits.shape[0], lanes:] = digits.astype(jnp.bfloat16)


def read_feats(ref, fslice, n_idx, lanes):
    if not is_dense(fslice, n_idx):
        return ref[fslice:, :lanes].astype(jnp.float32)
    cut, part = fslice // 4 * 3, fslice // 4
    tail = ref[fslice : fslice + cut, lanes:].astype(jnp.float32)
    tail = jnp.concatenate([tail[i : i + part] for i in range(0, cut, part)], axis=1)
    return jnp.concatenate([ref[fslice : fslice + cut, :lanes].astype(jnp.float32), tail], axis=0)


def read_digits(ref, fslice, n_idx, lanes):
    if not is_dense(fslice, n_idx):
        return ref[fslice : fslice + n_idx, lanes:].astype(jnp.float32)
    tags = ref[-8:, : 2 * LANES].astype(jnp.float32)
    return jnp.concatenate([tags[:, :LANES], tags[:, LANES:]], axis=0)


TAG_ROWS = 16


def live_rows(ref):
    return jnp.max(ref[-TAG_ROWS:, :].astype(jnp.float32)).astype(jnp.int32)


def pack_kernel(
    steps,
    n_feat,
    pcap,
    src_hbm,
    seed_hbm,
    nbr_hbm,
    w_self_hbm,
    w_nbr_hbm,
    pick_hbm,
    *refs,
):
    half = n_feat // 2
    parcel_refs, pick_ref, src_ref = refs[:half], refs[half], refs[half + 1]
    seed_ref, nbr_ref, w_self_ref, w_nbr_ref, fetched_ref, sems = refs[half + 2 :]
    first = pl.ds(0, src_ref.shape[1])
    copies = [
        pltpu.make_async_copy(a, b, sems.at[i])
        for i, (a, b) in enumerate(
            (
                (src_hbm.at[:, first], src_ref),
                (w_self_hbm, w_self_ref),
                (w_nbr_hbm, w_nbr_ref),
                (seed_hbm, seed_ref),
                (nbr_hbm, nbr_ref),
                (pick_hbm, fetched_ref),
            )
        )
    ]
    for copy in copies:
        copy.start()
    for copy in copies[1:]:
        copy.wait()
    stride = -(-pcap // LANES) * LANES
    words = pick_ref.shape[2] // stride
    for k in range(words):
        word = fetched_ref[:, k]
        if words < fetched_ref.shape[1]:
            word = word | (fetched_ref[:, words + k] << 16)
        pick_ref[:, :, k * stride : k * stride + pcap] = word
    feat_pos = lax.axis_index("feat")
    first_core = lax.axis_index("rep") == 0
    idx = jnp.concatenate([seed_ref[...], nbr_ref[...]], axis=0)
    high = lax.shift_right_logical(idx, 7)
    digits = jnp.concatenate([high, idx - high * 128], axis=1).astype(jnp.float32)
    weight = jnp.where(first_core, w_self_ref[...], w_nbr_ref[...])
    copies[0].wait()
    for s, parcel_ref in zip(steps, parcel_refs):
        sides = []
        for step in (s, s ^ half):
            at = pl.multiple_of(jnp.bitwise_xor(feat_pos, step) * (2 * pcap), LANES)
            block = src_ref[:, pl.ds(at, 2 * pcap)].astype(jnp.float32)
            sides.append(jnp.where(first_core, block[:, :pcap], block[:, pcap:]))
        write_parcel(parcel_ref, weight, jnp.concatenate(sides, axis=1), digits)


def turn_kernel(owned_ref, src_hbm, table_ref):
    fslice, owned = owned_ref.shape
    pieces = src_hbm.shape[1] // owned - 1
    width = next(w for w in (2048, 1536, 1024, 512, LANES) if owned % w == 0)

    def turn(ref, low, place):
        def step(i, carry):
            at = pl.multiple_of(i * width, width)
            rows = pl.ds(pl.multiple_of(place + at, LANES), width)
            table_ref[rows, :fslice] = ref[:, pl.ds(low + at, width)].T.astype(jnp.float32)
            return carry

        lax.fori_loop(0, owned // width, step, 0)

    def rest(buffer, sems):
        copies = [
            pltpu.make_async_copy(
                src_hbm.at[:, pl.ds((i + 1) * owned, owned)],
                buffer.at[:, pl.ds(i * owned, owned)],
                sems.at[i],
            )
            for i in range(pieces)
        ]
        for copy in copies:
            copy.start()
        turn(owned_ref, 0, 0)
        for i, copy in enumerate(copies):
            copy.wait()
            turn(buffer, i * owned, (i + 1) * owned)

    pl.run_scoped(
        rest,
        pltpu.VMEM((fslice, pieces * owned), jnp.bfloat16),
        pltpu.SemaphoreType.DMA((pieces,)),
    )


def mean_kernel(chosen, packed, fanout, pcap, fslice, turns, before, n_before, *refs):
    count = len(chosen)
    before_in, refs = refs[: n_before[0]], refs[n_before[0] :]
    nbr_any, *refs = refs
    if not turns:
        table_ref, *refs = refs
    out_ref, total, nbr_ref, live_ref, sems = refs[-5:]
    refs = refs[:-5]
    before_out = refs[len(refs) - n_before[1] :]
    refs = refs[: len(refs) - n_before[1]]
    chunk_refs, tagged_refs = refs[len(refs) - count :], refs[: len(refs) - count]
    feat_pos = lax.axis_index("feat")
    words = fanout // packed
    size = 16 if len(tagged_refs) or pcap % 64 else 64
    stride = -(-pcap // LANES) * LANES
    length = words * stride
    copies = [
        pltpu.make_async_copy(
            nbr_any.at[feat_pos ^ step, 0], nbr_ref.at[pl.ds(i * length, length)], sems.at[i]
        )
        for i, step in enumerate(chosen)
    ]
    for copy in copies:
        copy.start()
    for i in range(count):
        live_ref[i] = pcap
    for i, ref in enumerate(tagged_refs):
        live_ref[i] = live_rows(ref)
    if before is not None:
        before(*before_in, *before_out)
    if turns:
        table_ref = before_out[0].reshape(before_out[0].shape[0], 1, LANES)
    for copy in copies:
        copy.wait()

    def partition(i, carry):
        first = i * length

        def group(g, inner):
            at = pl.multiple_of(g * size, 16)
            start = first + at
            sums = []
            for u in range(size):
                names = [nbr_ref[start + (k * stride + u)] for k in range(words)]
                if packed == 2:
                    names = [
                        part
                        for name in names
                        for part in (name & 0xFFFF, lax.shift_right_logical(name, 16))
                    ]
                rows = [table_ref[name] for name in names]
                while len(rows) > 1:
                    rows = [a + b for a, b in zip(rows[::2], rows[1::2])] + (
                        [rows[-1]] if len(rows) % 2 else []
                    )
                sums.append(rows[0])
                if len(sums) == 16:
                    for v, row in enumerate(sums):
                        total[pl.ds(at + (u - 15 + v), 1), :] = row
                    sums = []
            return inner

        lax.fori_loop(0, lax.div(live_ref[i] + size - 1, size), group, 0)
        mean = total[...] / fanout
        if folds(fslice, pcap):
            part = pcap // 4
            lane = lax.broadcasted_iota(jnp.int32, (part, LANES), 1)
            tail = mean[3 * part :]
            for b in range(3):
                shift = (fslice - 32 * b) % LANES
                moved = pltpu.roll(tail, shift, 1) if shift else tail
                out_ref[i, pl.ds(b * part, part), :] = jnp.where(
                    lane < fslice, mean[b * part : (b + 1) * part], moved
                ).astype(jnp.bfloat16)
        else:
            out_ref[i] = mean[:, :fslice].astype(jnp.bfloat16)
        return carry

    lax.fori_loop(0, count, partition, 0)
    for i, ref in enumerate(chunk_refs):
        ref[...] = out_ref[i]


def unfold(ref, fslice, pcap):
    if not folds(fslice, pcap):
        return ref[:pcap, :]
    part = pcap // 4
    wide = ref[: 3 * part, :].astype(jnp.float32)
    lane = lax.broadcasted_iota(jnp.int32, (part, LANES), 1)
    tail = pltpu.roll(wide[:part], LANES - fslice, 1)
    for b in (1, 2):
        shift = (32 * b - fslice) % LANES
        moved = wide[b * part : (b + 1) * part]
        moved = pltpu.roll(moved, shift, 1) if shift else moved
        tail = jnp.where(lane // 32 == b, moved, tail)
    return jnp.concatenate([wide, tail], axis=0)[:, :fslice].astype(jnp.bfloat16)


def halves_kernel(half, count_ref, *refs):
    parcel_refs, chunk_refs = refs[:half], refs[half : 2 * half - 1]
    out_ref, *tagged_refs, live_ref = refs[2 * half - 1 :]
    for s, ref in enumerate(parcel_refs):
        out_ref[s] = ref[: out_ref.shape[1], :]
    live = jnp.full(live_ref.shape, count_ref[0, 0].astype(jnp.float32)).astype(jnp.bfloat16)
    live_ref[...] = live
    for chunk_ref, ref in zip(chunk_refs, tagged_refs):
        ref[:-TAG_ROWS, :] = chunk_ref[...]
        ref[-TAG_ROWS:, :] = live


def own_kernel(half, n_idx, *refs):
    parcel_refs = refs[:half]
    other_ref, bias_ref, w_ref, pre_ref, far_ref, idx_ref = refs[half:]
    fslice = w_ref.shape[1]
    pcap, width = pre_ref.shape
    first_core = lax.axis_index("rep") == 0
    feats, weights = [], []
    for s in range(half):
        mine, other = parcel_refs[s][:fslice, :], other_ref[s]
        w_ref[s] = jnp.where(first_core, other, mine)
        weights.append(jnp.where(first_core, mine, other))
        feats.append(read_feats(parcel_refs[s], fslice, n_idx, 2 * pcap))
        rows = pl.ds(s // 4 * n_idx, n_idx)
        digits = read_digits(parcel_refs[s], fslice, n_idx, 2 * pcap)
        idx_ref[rows, s % 4 * LANES : (s % 4 + 1) * LANES] = digits.astype(jnp.bfloat16)
    both = jnp.dot(
        jnp.concatenate(feats, axis=0).T.astype(jnp.bfloat16),
        jnp.concatenate(weights, axis=0),
        preferred_element_type=jnp.float32,
    )
    pre_ref[...] = both[:pcap] + bias_ref[...]
    far_ref[...] = both[pcap:]


def add_means(half, pre, mean_refs, w_ref, turn=0):
    for s, ref in enumerate(mean_refs):
        pre = pre + jnp.dot(
            unfold(ref, w_ref.shape[1], pre.shape[0]),
            w_ref[(s + turn) % (half - 1) if s < half - 1 else s],
            preferred_element_type=jnp.float32,
        )
    return pre


def far_kernel(half, *refs):
    far_ref, w_ref, idx_ref, cross_ref = refs[half:]
    pcap = far_ref.shape[0]
    cross_ref[:pcap, :] = add_means(half, far_ref[...], refs[:half], w_ref).astype(jnp.bfloat16)
    cross_ref[pcap:, :] = idx_ref[...]


def store_times(pcap, blocks, out_ref):
    n_idx, pair = blocks[0].shape
    seed_count = pair // 2
    core_rows = lax.axis_index("feat") * (2 * pcap)
    rep_pos = lax.axis_index("rep")
    row = lax.broadcasted_iota(jnp.int32, (2 * pcap, pair), 0)
    slot = jnp.where(
        row < pcap, row + core_rows + rep_pos * pcap, row + core_rows - rep_pos * pcap
    ).astype(jnp.float32)
    low = lax.broadcasted_iota(jnp.int32, (n_idx, pair), 1) < seed_count
    for s in range(0, len(blocks), 2):
        first, second = blocks[s].astype(jnp.float32), blocks[s + 1].astype(jnp.float32)
        high_part = jnp.where(low, first, pltpu.roll(second, seed_count, 1))
        low_part = jnp.where(low, pltpu.roll(first, seed_count, 1), second)
        name = high_part * 128.0 + low_part
        own = jnp.where(slot == name[:1], 1.0, 0.0)
        near = jnp.zeros((2 * pcap, pair), jnp.float32)
        for k in range(1, n_idx):
            near = near + jnp.where(slot == name[k : k + 1], 1.0, 0.0)
        place = pl.ds(s * seed_count, pair)
        out_ref[place, : 2 * pcap] = own.T.astype(jnp.bfloat16)
        out_ref[place, 2 * pcap :] = near.T.astype(jnp.bfloat16)


def near_times_kernel(half, fslice, pcap, n_idx, _, __, *refs):
    blocks = [read_digits(ref, fslice, n_idx, 2 * pcap) for ref in refs[:half]]
    store_times(pcap, blocks, refs[half])


def far_times_kernel(
    half,
    n_idx,
    fanout_two,
    cross_ref,
    hidden_ref,
    ws_ref,
    wn_ref,
    out_ref,
    value_ref,
    result_ref,
    sem,
):
    copy = pltpu.make_async_copy(hidden_ref, result_ref, sem)
    copy.start()
    pcap = hidden_ref.shape[0]
    blocks = [
        cross_ref[
            pl.ds(pcap + s // 4 * n_idx, n_idx), s % 4 * LANES : (s % 4 + 1) * LANES
        ]
        for s in range(half)
    ]
    store_times(pcap, blocks, out_ref)
    store_values(hidden_ref[...], ws_ref, wn_ref, fanout_two, value_ref)
    copy.wait()


def store_values(hidden, ws_ref, wn_ref, fanout_two, value_ref):
    value_ref[0] = jnp.dot(hidden, ws_ref[...], preferred_element_type=jnp.float32).astype(
        jnp.bfloat16
    )
    value_ref[1] = (
        jnp.dot(hidden, wn_ref[...], preferred_element_type=jnp.float32) / fanout_two
    ).astype(jnp.bfloat16)


def near_kernel(half, *refs):
    pre_ref, w_ref, out_ref = refs[half:]
    out_ref[...] = add_means(half, pre_ref[...], refs[:half], w_ref)


def hidden_kernel(live_ref, pre_ref, cross_ref, hidden_ref):
    pcap, width = hidden_ref.shape
    pre = pre_ref[...] + cross_ref[:pcap, :].astype(jnp.float32)
    live = lax.broadcasted_iota(jnp.int32, (pcap, width), 0) < live_rows(live_ref)
    hidden_ref[...] = jnp.where(live, jnp.maximum(pre, 0.0), 0.0).astype(jnp.bfloat16)


def far_share_kernel(
    half, fanout_two, far_ref, value_ref, hidden_ref, ws_ref, wn_ref, *refs
):
    *out_refs, values_ref = refs
    pcap = hidden_ref.shape[0]
    for i in range(2):
        values_ref[2 * i * pcap : (2 * i + 1) * pcap, :] = value_ref[i]
    hidden = hidden_ref[...]
    values_ref[pcap : 2 * pcap, :] = jnp.dot(
        hidden, ws_ref[...], preferred_element_type=jnp.float32
    ).astype(jnp.bfloat16)
    values_ref[3 * pcap :, :] = (
        jnp.dot(hidden, wn_ref[...], preferred_element_type=jnp.float32) / fanout_two
    ).astype(jnp.bfloat16)
    store_shares(far_ref, values_ref, out_refs)


def store_shares(times_ref, values_ref, out_refs):
    rows = times_ref.shape[0] // len(out_refs)
    part = jnp.dot(times_ref[...], values_ref[...], preferred_element_type=jnp.float32)
    for s, ref in enumerate(out_refs):
        ref[...] = part[s * rows : (s + 1) * rows].astype(jnp.bfloat16)


def near_share_kernel(near_ref, values_ref, *out_refs):
    store_shares(near_ref, values_ref, out_refs)


def copy_kernel(in_ref, out_ref):
    out_ref[...] = in_ref[...]


def side_sum_kernel(*refs):
    total = refs[0][...].astype(jnp.float32)
    for ref in refs[1:-1]:
        total = total + ref[...].astype(jnp.float32)
    refs[-1][: total.shape[0], :] = total.astype(jnp.bfloat16)


def last_kernel(bias_ref, *refs):
    total = bias_ref[...]
    for ref in refs[:-1]:
        total = total + ref[: refs[-1].shape[0], :].astype(jnp.float32)
    refs[-1][...] = jnp.maximum(total, 0.0).astype(jnp.bfloat16)


def swap(value, axis, step):
    size = lax.axis_size(axis)
    return lax.ppermute(value, axis, [(i, i ^ step) for i in range(size)])


def body(
    src_feats,
    nbr_one,
    counts,
    seed_rows,
    nbr_two,
    w1_self,
    w1_nbr,
    bias_one,
    w2_self,
    w2_nbr,
    bias_two,
):
    n_feat = lax.axis_size("feat")
    half = n_feat // 2
    steps = list(range(half - 1, -1, -1))
    fslice, nodes = src_feats.shape
    fanout_one, pcap = nbr_one.shape[2:]
    width = w1_self.shape[1]
    seed_count, fanout_two = nbr_two.shape
    n_idx = fanout_two + 1
    bf16 = jnp.bfloat16
    vmem = pl.BlockSpec(memory_space=pltpu.VMEM)
    smem = pl.BlockSpec(memory_space=pltpu.SMEM)
    hbm = pl.BlockSpec(memory_space=pltpu.HBM)
    anywhere = pl.BlockSpec(memory_space=pl.ANY)
    table_bytes = nodes * LANES * 4

    def call(kernel, name, shapes, ins, args, after=(), scratch=(), limit=16 * MIB, cost_us=1, outs=None):
        def wrapped(*refs):
            kernel(*refs[: len(args)], *refs[len(args) + len(after) :])

        return pl.pallas_call(
            wrapped,
            out_shape=tuple(jax.ShapeDtypeStruct(shape, dtype) for shape, dtype in shapes),
            in_specs=[*ins, *([anywhere] * len(after))],
            out_specs=outs or (vmem,) * len(shapes),
            scratch_shapes=scratch,
            compiler_params=pltpu.CompilerParams(vmem_limit_bytes=limit),
            cost_estimate=pl.CostEstimate(
                flops=int(cost_us * 1_100_000_000), bytes_accessed=0, transcendentals=0
            ),
            name=name,
        )(*args, *after)

    def pinned(value):
        return pltpu.with_memory_space_constraint(value, pltpu.HBM)

    def send(chunks, steps=steps):
        return [swap(chunk, "feat", s) if s else chunk for s, chunk in zip(steps, chunks)]

    owned = n_feat * 2 * pcap
    picks = jnp.transpose(nbr_one, (0, 2, 1, 3))
    packed = 2 if fanout_one % 2 == 0 and nodes <= 1 << 16 else 1
    words = (n_feat, 1, fanout_one // packed * (-(-pcap // LANES) * LANES))
    *parcels, picks, feats = call(
        functools.partial(pack_kernel, steps, n_feat, pcap),
        "pack",
        [((parcel_rows(fslice, n_idx), width), bf16)] * half
        + [(words, jnp.int32), ((fslice, owned), bf16)],
        [hbm] * 6,
        [pinned(x) for x in (src_feats, seed_rows[None], nbr_two.T, w1_self, w1_nbr, picks)],
        scratch=[
            pltpu.VMEM((1, seed_count), jnp.int32),
            pltpu.VMEM((fanout_two, seed_count), jnp.int32),
            pltpu.VMEM((fslice, width), bf16),
            pltpu.VMEM((fslice, width), bf16),
            pltpu.VMEM((n_feat, fanout_one, 1, pcap), jnp.int32),
            pltpu.SemaphoreType.DMA((6,)),
        ],
        limit=32 * MIB,
    )
    arrived = send(parcels)
    chunk_shape = (pcap // 4 * 3, LANES) if folds(fslice, pcap) else (pcap, fslice)

    def means(chosen, tagged=(), after=(), before=None, ins=(), outs=(), table=None):
        count = len(chosen)
        tables = () if table is None else (table,)
        return call(
            functools.partial(
                mean_kernel,
                tuple(chosen),
                packed,
                fanout_one,
                pcap,
                fslice,
                table is None,
                before,
                (len(ins), len(outs)),
            ),
            "mean",
            [(chunk_shape, bf16)] * count + list(outs),
            ([vmem, hbm] if table is None else [vmem] * len(ins))
            + [anywhere]
            + [vmem] * (len(tables) + len(tagged)),
            (*ins, picks, *tables, *tagged),
            after=after,
            scratch=[
                pltpu.VMEM((count, *chunk_shape), bf16),
                pltpu.VMEM((pcap, LANES), jnp.float32),
                pltpu.SMEM((count * words[2],), jnp.int32),
                pltpu.SMEM((count,), jnp.int32),
                pltpu.SemaphoreType.DMA((count,)),
            ],
            limit=table_bytes + 8 * MIB,
            cost_us=2 * count if count > 1 else 0,
        )

    *far_means, table = means(
        [s + half for s in steps if s],
        before=turn_kernel,
        ins=(feats, pinned(src_feats)),
        outs=[((nodes, LANES), jnp.float32)],
    )
    table = table.reshape(nodes, 1, LANES)
    tagged_shape = (chunk_shape[0] + TAG_ROWS, chunk_shape[1])
    halves, *tagged, live = call(
        functools.partial(halves_kernel, half),
        "halves",
        [
            ((half, fslice, width), bf16),
            *([(tagged_shape, bf16)] * (half - 1)),
            ((TAG_ROWS, chunk_shape[1]), bf16),
        ],
        [smem] + [vmem] * (2 * half - 1),
        (counts, *arrived, *far_means),
    )
    far_arrived = send(tagged)
    other_halves = swap(halves, "rep", 1)
    idx_rows = -(-half // 4) * n_idx
    far_own, w_nbr, pre, far_pre, idx_tags = means(
        [half],
        table=table,
        before=functools.partial(own_kernel, half, n_idx),
        ins=(*arrived, other_halves, bias_one[None]),
        outs=[
            ((half, fslice, width), bf16),
            ((pcap, width), jnp.float32),
            ((pcap, width), jnp.float32),
            ((idx_rows, width), bf16),
        ],
    )
    (cross,) = call(
        functools.partial(far_kernel, half),
        "far",
        [((pcap + idx_rows, width), bf16)],
        [vmem] * (half + 3),
        (*far_arrived, far_own, far_pre, w_nbr, idx_tags),
    )
    cross_arrived = swap(cross, "feat", half)
    turned = steps[:-1]
    near_means = means(turned, far_arrived, (cross,), table=table)
    near_arrived = send(near_means, turned)
    near_own, near_times = means(
        [0],
        [live],
        table=table,
        after=(cross,),
        before=functools.partial(near_times_kernel, half, fslice, pcap, n_idx),
        ins=(w2_self, w2_nbr, *arrived),
        outs=[((half * seed_count, 4 * pcap), bf16)],
    )
    (near_pre,) = call(
        functools.partial(near_kernel, half),
        "near",
        [((pcap, width), jnp.float32)],
        [vmem] * (half + 2),
        (*near_arrived, near_own, pre, w_nbr),
        cost_us=0,
    )
    (hidden,) = call(
        hidden_kernel,
        "hidden",
        [((pcap, width), bf16)],
        [vmem] * 3,
        (live, near_pre, cross_arrived),
    )
    other_hidden = swap(hidden, "rep", 1)
    far_times, value, result = call(
        functools.partial(far_times_kernel, half, n_idx, fanout_two),
        "far_times",
        [
            ((half * seed_count, 4 * pcap), bf16),
            ((2, pcap, width), bf16),
            ((pcap, width), bf16),
        ],
        [vmem] * 4,
        (cross_arrived, hidden, w2_self, w2_nbr),
        scratch=[pltpu.SemaphoreType.DMA],
        outs=(vmem, vmem, anywhere),
    )
    *far_shares, values = call(
        functools.partial(far_share_kernel, half, fanout_two),
        "far_share",
        [((seed_count, width), bf16)] * half + [((4 * pcap, width), bf16)],
        [vmem] * 5,
        (far_times, value, other_hidden, w2_self, w2_nbr),
        limit=32 * MIB,
    )
    far_shares = send(far_shares)
    *near_shares, near_late, near_last = call(
        near_share_kernel,
        "near_share",
        [((seed_count, width), bf16)] * half,
        [vmem] * 2,
        (near_times, values),
        limit=32 * MIB,
    )
    near_shares = [swap(share, "feat", s) for share, s in zip(near_shares, steps)]
    (far_sum,) = call(
        side_sum_kernel, "side_sum", [((seed_count + 8, width), bf16)], [vmem] * half, far_shares
    )
    (near_late,) = call(
        copy_kernel, "late", [((seed_count, width), bf16)], [vmem], (near_late,), after=(far_sum,)
    )
    (seed_out,) = call(
        last_kernel,
        "seeds",
        [((seed_count, width), bf16)],
        [vmem] * (half + 2),
        (
            bias_two[None],
            *near_shares,
            swap(near_late, "feat", 1),
            near_last,
            swap(far_sum, "feat", half),
        ),
    )
    return (result[None, None], seed_out)


def solution(mesh):
    placed = (
        P("feat", "groups"),
        P("groups", "rep", None, None),
        P(("groups", "feat"), "rep"),
        P(("groups", "feat", "rep")),
        P(("groups", "feat", "rep"), None),
        P("feat", None),
        P("feat", None),
        P(),
        P(),
        P(),
        P(),
    )
    return jax.shard_map(
        body,
        mesh=mesh,
        in_specs=placed,
        out_specs=(P(("groups", "feat"), "rep", None, None), P(("groups", "feat", "rep"), None)),
        check_vma=False,
    )
```

```python
import functools

import jax
import jax.numpy as jnp
from jax import lax
from jax.experimental import pallas as pl
from jax.experimental.pallas import tpu as pltpu
from jax.sharding import PartitionSpec as P

LANES = 128
MIB = 1024 * 1024


def folds(fslice, pcap):
    return 4 * fslice == 3 * LANES and pcap % 64 == 0


def is_dense(fslice, n_idx):
    return fslice % 32 == 0 and n_idx == 16


def parcel_rows(fslice, n_idx):
    return 2 * fslice - fslice // 4 + 8 if is_dense(fslice, n_idx) else 2 * fslice


def write_parcel(ref, weight, feats, digits):
    fslice, lanes = feats.shape
    ref[:fslice, :] = weight
    if is_dense(fslice, digits.shape[0]):
        cut = fslice // 4 * 3
        tail = jnp.concatenate([feats[cut:, i : i + LANES] for i in range(0, lanes, LANES)], axis=0)
        tags = jnp.concatenate([digits[:8], digits[8:]] * 2, axis=1)
        body = jnp.concatenate([feats[:cut], tail], axis=1)
        ref[fslice:, :] = jnp.concatenate([body, tags], axis=0).astype(jnp.bfloat16)
    else:
        ref[fslice:, :lanes] = feats.astype(jnp.bfloat16)
        ref[fslice : fslice + digits.shape[0], lanes:] = digits.astype(jnp.bfloat16)


def read_feats(ref, fslice, n_idx, lanes):
    if not is_dense(fslice, n_idx):
        return ref[fslice:, :lanes].astype(jnp.float32)
    cut, part = fslice // 4 * 3, fslice // 4
    tail = ref[fslice : fslice + cut, lanes:].astype(jnp.float32)
    tail = jnp.concatenate([tail[i : i + part] for i in range(0, cut, part)], axis=1)
    return jnp.concatenate([ref[fslice : fslice + cut, :lanes].astype(jnp.float32), tail], axis=0)


def read_digits(ref, fslice, n_idx, lanes):
    if not is_dense(fslice, n_idx):
        return ref[fslice : fslice + n_idx, lanes:].astype(jnp.float32)
    tags = ref[-8:, : 2 * LANES].astype(jnp.float32)
    return jnp.concatenate([tags[:, :LANES], tags[:, LANES:]], axis=0)


TAG_ROWS = 16


def live_rows(ref):
    return jnp.max(ref[-TAG_ROWS:, :].astype(jnp.float32)).astype(jnp.int32)


def row_code(row):
    high = lax.shift_right_logical(row, 7)
    code = (128 + (row & 127)).astype(jnp.float32)
    for bit in range(7):
        code = code * jnp.where((high >> bit) & 1 == 1, float(2 ** (2**bit)), 1.0)
    return code


def pair_codes(ref_low, ref_high, seed_count, fslice, n_idx, lanes):
    low = lax.broadcasted_iota(jnp.int32, (n_idx, 2 * seed_count), 1) < seed_count
    return jnp.where(
        low,
        read_digits(ref_low, fslice, n_idx, lanes),
        read_digits(ref_high, fslice, n_idx, lanes),
    )


def pack_kernel(
    steps,
    n_feat,
    pcap,
    src_hbm,
    seed_hbm,
    nbr_hbm,
    w_self_hbm,
    w_nbr_hbm,
    pick_hbm,
    *refs,
):
    half = n_feat // 2
    parcel_refs, pick_ref, src_ref = refs[:half], refs[half], refs[half + 1]
    seed_ref, nbr_ref, w_self_ref, w_nbr_ref, fetched_ref, sems = refs[half + 2 :]
    first = pl.ds(0, src_ref.shape[1])
    copies = [
        pltpu.make_async_copy(a, b, sems.at[i])
        for i, (a, b) in enumerate(
            (
                (src_hbm.at[:, first], src_ref),
                (w_self_hbm, w_self_ref),
                (w_nbr_hbm, w_nbr_ref),
                (seed_hbm, seed_ref),
                (nbr_hbm, nbr_ref),
                (pick_hbm, fetched_ref),
            )
        )
    ]
    for copy in copies:
        copy.start()
    for copy in copies[1:]:
        copy.wait()
    stride = -(-pcap // LANES) * LANES
    words = pick_ref.shape[2] // stride
    for k in range(words):
        word = fetched_ref[:, k]
        if words < fetched_ref.shape[1]:
            word = word | (fetched_ref[:, words + k] << 16)
        pick_ref[:, :, k * stride : k * stride + pcap] = word
    feat_pos = lax.axis_index("feat")
    first_core = lax.axis_index("rep") == 0
    idx = jnp.concatenate([seed_ref[...], nbr_ref[...]], axis=0)
    code = row_code(idx)
    digits = jnp.concatenate([code, code], axis=1)
    weight = jnp.where(first_core, w_self_ref[...], w_nbr_ref[...])
    copies[0].wait()
    for s, parcel_ref in zip(steps, parcel_refs):
        sides = []
        for step in (s, s ^ half):
            at = pl.multiple_of(jnp.bitwise_xor(feat_pos, step) * (2 * pcap), LANES)
            block = src_ref[:, pl.ds(at, 2 * pcap)].astype(jnp.float32)
            sides.append(jnp.where(first_core, block[:, :pcap], block[:, pcap:]))
        write_parcel(parcel_ref, weight, jnp.concatenate(sides, axis=1), digits)


def turn_kernel(owned_ref, src_hbm, table_ref):
    fslice, owned = owned_ref.shape
    pieces = src_hbm.shape[1] // owned - 1
    width = next(w for w in (2048, 1536, 1024, 512, LANES) if owned % w == 0)

    def turn(ref, low, place):
        def step(i, carry):
            at = pl.multiple_of(i * width, width)
            rows = pl.ds(pl.multiple_of(place + at, LANES), width)
            table_ref[rows, :fslice] = ref[:, pl.ds(low + at, width)].T.astype(jnp.float32)
            return carry

        lax.fori_loop(0, owned // width, step, 0)

    def rest(buffer, sems):
        copies = [
            pltpu.make_async_copy(
                src_hbm.at[:, pl.ds((i + 1) * owned, owned)],
                buffer.at[:, pl.ds(i * owned, owned)],
                sems.at[i],
            )
            for i in range(pieces)
        ]
        for copy in copies:
            copy.start()
        turn(owned_ref, 0, 0)
        for i, copy in enumerate(copies):
            copy.wait()
            turn(buffer, i * owned, (i + 1) * owned)

    pl.run_scoped(
        rest,
        pltpu.VMEM((fslice, pieces * owned), jnp.bfloat16),
        pltpu.SemaphoreType.DMA((pieces,)),
    )


def mean_kernel(chosen, packed, fanout, pcap, fslice, turns, before, n_before, *refs):
    count = len(chosen)
    before_in, refs = refs[: n_before[0]], refs[n_before[0] :]
    nbr_any, *refs = refs
    if not turns:
        table_ref, *refs = refs
    out_ref, total, nbr_ref, live_ref, sems = refs[-5:]
    refs = refs[:-5]
    before_out = refs[len(refs) - n_before[1] :]
    refs = refs[: len(refs) - n_before[1]]
    chunk_refs, tagged_refs = refs[len(refs) - count :], refs[: len(refs) - count]
    feat_pos = lax.axis_index("feat")
    words = fanout // packed
    size = 16 if len(tagged_refs) or pcap % 64 else 64
    stride = -(-pcap // LANES) * LANES
    length = words * stride
    copies = [
        pltpu.make_async_copy(
            nbr_any.at[feat_pos ^ step, 0], nbr_ref.at[pl.ds(i * length, length)], sems.at[i]
        )
        for i, step in enumerate(chosen)
    ]
    for copy in copies:
        copy.start()
    for i in range(count):
        live_ref[i] = pcap
    for i, ref in enumerate(tagged_refs):
        live_ref[i] = live_rows(ref)
    if before is not None:
        before(*before_in, *before_out)
    if turns:
        table_ref = before_out[0].reshape(before_out[0].shape[0], 1, LANES)
    for copy in copies:
        copy.wait()

    def partition(i, carry):
        first = i * length

        def group(g, inner):
            at = pl.multiple_of(g * size, 16)
            start = first + at
            sums = []
            for u in range(size):
                names = [nbr_ref[start + (k * stride + u)] for k in range(words)]
                if packed == 2:
                    names = [
                        part
                        for name in names
                        for part in (name & 0xFFFF, lax.shift_right_logical(name, 16))
                    ]
                rows = [table_ref[name] for name in names]
                while len(rows) > 1:
                    rows = [a + b for a, b in zip(rows[::2], rows[1::2])] + (
                        [rows[-1]] if len(rows) % 2 else []
                    )
                sums.append(rows[0])
                if len(sums) == 16:
                    for v, row in enumerate(sums):
                        total[pl.ds(at + (u - 15 + v), 1), :] = row
                    sums = []
            return inner

        lax.fori_loop(0, lax.div(live_ref[i] + size - 1, size), group, 0)
        mean = total[...] / fanout
        if folds(fslice, pcap):
            part = pcap // 4
            lane = lax.broadcasted_iota(jnp.int32, (part, LANES), 1)
            tail = mean[3 * part :]
            for b in range(3):
                shift = (fslice - 32 * b) % LANES
                moved = pltpu.roll(tail, shift, 1) if shift else tail
                out_ref[i, pl.ds(b * part, part), :] = jnp.where(
                    lane < fslice, mean[b * part : (b + 1) * part], moved
                ).astype(jnp.bfloat16)
        else:
            out_ref[i] = mean[:, :fslice].astype(jnp.bfloat16)
        return carry

    lax.fori_loop(0, count, partition, 0)
    for i, ref in enumerate(chunk_refs):
        ref[...] = out_ref[i]


def unfold(ref, fslice, pcap):
    if not folds(fslice, pcap):
        return ref[:pcap, :]
    part = pcap // 4
    wide = ref[: 3 * part, :].astype(jnp.float32)
    lane = lax.broadcasted_iota(jnp.int32, (part, LANES), 1)
    tail = pltpu.roll(wide[:part], LANES - fslice, 1)
    for b in (1, 2):
        shift = (32 * b - fslice) % LANES
        moved = wide[b * part : (b + 1) * part]
        moved = pltpu.roll(moved, shift, 1) if shift else moved
        tail = jnp.where(lane // 32 == b, moved, tail)
    return jnp.concatenate([wide, tail], axis=0)[:, :fslice].astype(jnp.bfloat16)


def halves_kernel(half, count_ref, *refs):
    parcel_refs, chunk_refs = refs[:half], refs[half : 2 * half - 1]
    out_ref, *tagged_refs, live_ref = refs[2 * half - 1 :]
    for s, ref in enumerate(parcel_refs):
        out_ref[s] = ref[: out_ref.shape[1], :]
    live = jnp.full(live_ref.shape, count_ref[0, 0].astype(jnp.float32)).astype(jnp.bfloat16)
    live_ref[...] = live
    for chunk_ref, ref in zip(chunk_refs, tagged_refs):
        ref[:-TAG_ROWS, :] = chunk_ref[...]
        ref[-TAG_ROWS:, :] = live


def own_kernel(half, n_idx, *refs):
    parcel_refs = refs[:half]
    other_ref, bias_ref, w_ref, pre_ref, far_ref, idx_ref = refs[half:]
    fslice = w_ref.shape[1]
    pcap, width = pre_ref.shape
    first_core = lax.axis_index("rep") == 0
    feats, weights = [], []
    for s in range(half):
        mine, other = parcel_refs[s][:fslice, :], other_ref[s]
        w_ref[s] = jnp.where(first_core, other, mine)
        weights.append(jnp.where(first_core, mine, other))
        feats.append(read_feats(parcel_refs[s], fslice, n_idx, 2 * pcap))
    both = jnp.dot(
        jnp.concatenate(feats, axis=0).T.astype(jnp.bfloat16),
        jnp.concatenate(weights, axis=0),
        preferred_element_type=jnp.float32,
    )
    part = n_idx // 2
    blocks = []
    for s in range(0, half, 2):
        codes = pair_codes(
            parcel_refs[s], parcel_refs[s + 1], LANES // 2, fslice, n_idx, 2 * pcap
        )
        blocks += [codes[:part], codes[part:]]
    for i in range(0, len(blocks), 4):
        rows = slice(i // 4 * part, (i // 4 + 1) * part)
        idx_ref[rows, :] = jnp.concatenate(blocks[i : i + 4], axis=1).astype(jnp.bfloat16)
    pre_ref[...] = both[:pcap] + bias_ref[...]
    far_ref[...] = both[pcap:]


def add_means(half, pre, mean_refs, w_ref, turn=0):
    for s, ref in enumerate(mean_refs):
        pre = pre + jnp.dot(
            unfold(ref, w_ref.shape[1], pre.shape[0]),
            w_ref[(s + turn) % (half - 1) if s < half - 1 else s],
            preferred_element_type=jnp.float32,
        )
    return pre


def far_kernel(half, *refs):
    far_ref, w_ref, idx_ref, cross_ref = refs[half:]
    pcap = far_ref.shape[0]
    cross_ref[:pcap, :] = add_means(half, far_ref[...], refs[:half], w_ref).astype(jnp.bfloat16)
    cross_ref[pcap:, :] = idx_ref[...]


def store_times(pcap, names, out_ref):
    n_idx, pair = names[0].shape
    seed_count = pair // 2
    core_rows = lax.axis_index("feat") * (2 * pcap)
    rep_pos = lax.axis_index("rep")
    row = lax.broadcasted_iota(jnp.int32, (2 * pcap, pair), 0)
    slot = row_code(
        jnp.where(row < pcap, row + core_rows + rep_pos * pcap, row + core_rows - rep_pos * pcap)
    )
    for s, name in zip(range(0, 2 * len(names), 2), names):
        own = jnp.where(slot == name[:1], 1.0, 0.0)
        near = jnp.zeros((2 * pcap, pair), jnp.float32)
        for k in range(1, n_idx):
            near = near + jnp.where(slot == name[k : k + 1], 1.0, 0.0)
        place = pl.ds(s * seed_count, pair)
        out_ref[place, : 2 * pcap] = own.T.astype(jnp.bfloat16)
        out_ref[place, 2 * pcap :] = near.T.astype(jnp.bfloat16)


def near_times_kernel(half, fslice, pcap, n_idx, _, __, *refs):
    names = [
        pair_codes(refs[s], refs[s + 1], LANES // 2, fslice, n_idx, 2 * pcap)
        for s in range(0, half, 2)
    ]
    store_times(pcap, names, refs[half])


def far_times_kernel(
    half,
    n_idx,
    fanout_two,
    cross_ref,
    hidden_ref,
    ws_ref,
    wn_ref,
    out_ref,
    value_ref,
    result_ref,
    sem,
):
    copy = pltpu.make_async_copy(hidden_ref, result_ref, sem)
    copy.start()
    pcap = hidden_ref.shape[0]
    part = n_idx // 2
    blocks = [
        cross_ref[
            pcap + i // 4 * part : pcap + (i // 4 + 1) * part, i % 4 * LANES : (i % 4 + 1) * LANES
        ].astype(jnp.float32)
        for i in range(half)
    ]
    names = [jnp.concatenate(blocks[i : i + 2], axis=0) for i in range(0, half, 2)]
    store_times(pcap, names, out_ref)
    store_values(hidden_ref[...], ws_ref, wn_ref, fanout_two, value_ref)
    copy.wait()


def store_values(hidden, ws_ref, wn_ref, fanout_two, value_ref):
    value_ref[0] = jnp.dot(hidden, ws_ref[...], preferred_element_type=jnp.float32).astype(
        jnp.bfloat16
    )
    value_ref[1] = (
        jnp.dot(hidden, wn_ref[...], preferred_element_type=jnp.float32) / fanout_two
    ).astype(jnp.bfloat16)


def near_kernel(half, *refs):
    pre_ref, w_ref, out_ref = refs[half:]
    out_ref[...] = add_means(half, pre_ref[...], refs[:half], w_ref)


def hidden_kernel(live_ref, pre_ref, cross_ref, hidden_ref):
    pcap, width = hidden_ref.shape
    pre = pre_ref[...] + cross_ref[:pcap, :].astype(jnp.float32)
    live = lax.broadcasted_iota(jnp.int32, (pcap, width), 0) < live_rows(live_ref)
    hidden_ref[...] = jnp.where(live, jnp.maximum(pre, 0.0), 0.0).astype(jnp.bfloat16)


def far_share_kernel(
    half, fanout_two, far_ref, value_ref, hidden_ref, ws_ref, wn_ref, *refs
):
    *out_refs, values_ref = refs
    pcap = hidden_ref.shape[0]
    for i in range(2):
        values_ref[2 * i * pcap : (2 * i + 1) * pcap, :] = value_ref[i]
    hidden = hidden_ref[...]
    values_ref[pcap : 2 * pcap, :] = jnp.dot(
        hidden, ws_ref[...], preferred_element_type=jnp.float32
    ).astype(jnp.bfloat16)
    values_ref[3 * pcap :, :] = (
        jnp.dot(hidden, wn_ref[...], preferred_element_type=jnp.float32) / fanout_two
    ).astype(jnp.bfloat16)
    store_shares(far_ref, values_ref, out_refs)


def store_shares(times_ref, values_ref, out_refs):
    rows = times_ref.shape[0] // len(out_refs)
    part = jnp.dot(times_ref[...], values_ref[...], preferred_element_type=jnp.float32)
    for s, ref in enumerate(out_refs):
        ref[...] = part[s * rows : (s + 1) * rows].astype(jnp.bfloat16)


def near_share_kernel(places, near_ref, values_ref, *out_refs):
    for place, ref in zip(places, out_refs):
        rows = ref.shape[0]
        times = near_ref[place * rows : (place + 1) * rows, :]
        ref[...] = jnp.dot(times, values_ref[...], preferred_element_type=jnp.float32).astype(
            jnp.bfloat16
        )


def side_sum_kernel(*refs):
    total = refs[0][...].astype(jnp.float32)
    for ref in refs[1:-1]:
        total = total + ref[...].astype(jnp.float32)
    refs[-1][: total.shape[0], :] = total.astype(jnp.bfloat16)


def last_kernel(bias_ref, *refs):
    total = bias_ref[...]
    for ref in refs[:-1]:
        total = total + ref[: refs[-1].shape[0], :].astype(jnp.float32)
    refs[-1][...] = jnp.maximum(total, 0.0).astype(jnp.bfloat16)


def swap(value, axis, step):
    size = lax.axis_size(axis)
    return lax.ppermute(value, axis, [(i, i ^ step) for i in range(size)])


def body(
    src_feats,
    nbr_one,
    counts,
    seed_rows,
    nbr_two,
    w1_self,
    w1_nbr,
    bias_one,
    w2_self,
    w2_nbr,
    bias_two,
):
    n_feat = lax.axis_size("feat")
    half = n_feat // 2
    steps = list(range(half - 1, -1, -1))
    fslice, nodes = src_feats.shape
    fanout_one, pcap = nbr_one.shape[2:]
    width = w1_self.shape[1]
    seed_count, fanout_two = nbr_two.shape
    n_idx = fanout_two + 1
    bf16 = jnp.bfloat16
    vmem = pl.BlockSpec(memory_space=pltpu.VMEM)
    smem = pl.BlockSpec(memory_space=pltpu.SMEM)
    hbm = pl.BlockSpec(memory_space=pltpu.HBM)
    anywhere = pl.BlockSpec(memory_space=pl.ANY)
    table_bytes = nodes * LANES * 4

    def call(kernel, name, shapes, ins, args, after=(), scratch=(), limit=16 * MIB, cost_us=1, outs=None):
        def wrapped(*refs):
            kernel(*refs[: len(args)], *refs[len(args) + len(after) :])

        return pl.pallas_call(
            wrapped,
            out_shape=tuple(jax.ShapeDtypeStruct(shape, dtype) for shape, dtype in shapes),
            in_specs=[*ins, *([anywhere] * len(after))],
            out_specs=outs or (vmem,) * len(shapes),
            scratch_shapes=scratch,
            compiler_params=pltpu.CompilerParams(vmem_limit_bytes=limit),
            cost_estimate=pl.CostEstimate(
                flops=int(cost_us * 1_100_000_000), bytes_accessed=0, transcendentals=0
            ),
            name=name,
        )(*args, *after)

    def pinned(value):
        return pltpu.with_memory_space_constraint(value, pltpu.HBM)

    def send(chunks, steps=steps):
        return [swap(chunk, "feat", s) if s else chunk for s, chunk in zip(steps, chunks)]

    owned = n_feat * 2 * pcap
    picks = jnp.transpose(nbr_one, (0, 2, 1, 3))
    packed = 2 if fanout_one % 2 == 0 and nodes <= 1 << 16 else 1
    words = (n_feat, 1, fanout_one // packed * (-(-pcap // LANES) * LANES))
    *parcels, picks, feats = call(
        functools.partial(pack_kernel, steps, n_feat, pcap),
        "pack",
        [((parcel_rows(fslice, n_idx), width), bf16)] * half
        + [(words, jnp.int32), ((fslice, owned), bf16)],
        [hbm] * 6,
        [pinned(x) for x in (src_feats, seed_rows[None], nbr_two.T, w1_self, w1_nbr, picks)],
        scratch=[
            pltpu.VMEM((1, seed_count), jnp.int32),
            pltpu.VMEM((fanout_two, seed_count), jnp.int32),
            pltpu.VMEM((fslice, width), bf16),
            pltpu.VMEM((fslice, width), bf16),
            pltpu.VMEM((n_feat, fanout_one, 1, pcap), jnp.int32),
            pltpu.SemaphoreType.DMA((6,)),
        ],
        limit=32 * MIB,
    )
    arrived = send(parcels)
    chunk_shape = (pcap // 4 * 3, LANES) if folds(fslice, pcap) else (pcap, fslice)

    def means(chosen, tagged=(), after=(), before=None, ins=(), outs=(), table=None):
        count = len(chosen)
        tables = () if table is None else (table,)
        return call(
            functools.partial(
                mean_kernel,
                tuple(chosen),
                packed,
                fanout_one,
                pcap,
                fslice,
                table is None,
                before,
                (len(ins), len(outs)),
            ),
            "mean",
            [(chunk_shape, bf16)] * count + list(outs),
            ([vmem, hbm] if table is None else [vmem] * len(ins))
            + [anywhere]
            + [vmem] * (len(tables) + len(tagged)),
            (*ins, picks, *tables, *tagged),
            after=after,
            scratch=[
                pltpu.VMEM((count, *chunk_shape), bf16),
                pltpu.VMEM((pcap, LANES), jnp.float32),
                pltpu.SMEM((count * words[2],), jnp.int32),
                pltpu.SMEM((count,), jnp.int32),
                pltpu.SemaphoreType.DMA((count,)),
            ],
            limit=table_bytes + 8 * MIB,
            cost_us=2 * count if count > 1 else 0,
        )

    *far_means, table = means(
        [s + half for s in steps if s],
        before=turn_kernel,
        ins=(feats, pinned(src_feats)),
        outs=[((nodes, LANES), jnp.float32)],
    )
    table = table.reshape(nodes, 1, LANES)
    tagged_shape = (chunk_shape[0] + TAG_ROWS, chunk_shape[1])
    halves, *tagged, live = call(
        functools.partial(halves_kernel, half),
        "halves",
        [
            ((half, fslice, width), bf16),
            *([(tagged_shape, bf16)] * (half - 1)),
            ((TAG_ROWS, chunk_shape[1]), bf16),
        ],
        [smem] + [vmem] * (2 * half - 1),
        (counts, *arrived, *far_means),
    )
    far_arrived = send(tagged)
    other_halves = swap(halves, "rep", 1)
    idx_rows = half // 4 * (n_idx // 2)
    far_own, w_nbr, pre, far_pre, idx_tags = means(
        [half],
        table=table,
        before=functools.partial(own_kernel, half, n_idx),
        ins=(*arrived, other_halves, bias_one[None]),
        outs=[
            ((half, fslice, width), bf16),
            ((pcap, width), jnp.float32),
            ((pcap, width), jnp.float32),
            ((idx_rows, width), bf16),
        ],
    )
    (cross,) = call(
        functools.partial(far_kernel, half),
        "far",
        [((pcap + idx_rows, width), bf16)],
        [vmem] * (half + 3),
        (*far_arrived, far_own, far_pre, w_nbr, idx_tags),
    )
    cross_arrived = swap(cross, "feat", half)
    turned = steps[:-1]
    near_means = means(turned, far_arrived, (cross,), table=table)
    near_arrived = send(near_means, turned)
    near_own, near_times = means(
        [0],
        [live],
        table=table,
        after=(cross,),
        before=functools.partial(near_times_kernel, half, fslice, pcap, n_idx),
        ins=(w2_self, w2_nbr, *arrived),
        outs=[((half * seed_count, 4 * pcap), bf16)],
    )
    (near_pre,) = call(
        functools.partial(near_kernel, half),
        "near",
        [((pcap, width), jnp.float32)],
        [vmem] * (half + 2),
        (*near_arrived, near_own, pre, w_nbr),
        cost_us=0,
    )
    (hidden,) = call(
        hidden_kernel,
        "hidden",
        [((pcap, width), bf16)],
        [vmem] * 3,
        (live, near_pre, cross_arrived),
    )
    other_hidden = swap(hidden, "rep", 1)
    far_times, value, result = call(
        functools.partial(far_times_kernel, half, n_idx, fanout_two),
        "far_times",
        [
            ((half * seed_count, 4 * pcap), bf16),
            ((2, pcap, width), bf16),
            ((pcap, width), bf16),
        ],
        [vmem] * 4,
        (cross_arrived, hidden, w2_self, w2_nbr),
        scratch=[pltpu.SemaphoreType.DMA],
        outs=(vmem, vmem, anywhere),
    )
    *far_shares, values = call(
        functools.partial(far_share_kernel, half, fanout_two),
        "far_share",
        [((seed_count, width), bf16)] * half + [((4 * pcap, width), bf16)],
        [vmem] * 5,
        (far_times, value, other_hidden, w2_self, w2_nbr),
        limit=32 * MIB,
    )
    far_shares = send(far_shares)
    def near_share(places, after=()):
        return call(
            functools.partial(near_share_kernel, places),
            "near_share",
            [((seed_count, width), bf16)] * len(places),
            [vmem] * 2,
            (near_times, values),
            after=after,
            limit=32 * MIB,
        )

    *near_shares, near_last = near_share([*range(half - 2), half - 1])
    near_shares = [swap(share, "feat", s) for share, s in zip(near_shares, steps)]
    (far_sum,) = call(
        side_sum_kernel, "side_sum", [((seed_count + 8, width), bf16)], [vmem] * half, far_shares
    )
    (near_late,) = near_share([half - 2], (far_sum,))
    (seed_out,) = call(
        last_kernel,
        "seeds",
        [((seed_count, width), bf16)],
        [vmem] * (half + 2),
        (
            bias_two[None],
            *near_shares,
            swap(near_late, "feat", 1),
            near_last,
            swap(far_sum, "feat", half),
        ),
    )
    return (result[None, None], seed_out)


def solution(mesh):
    placed = (
        P("feat", "groups"),
        P("groups", "rep", None, None),
        P(("groups", "feat"), "rep"),
        P(("groups", "feat", "rep")),
        P(("groups", "feat", "rep"), None),
        P("feat", None),
        P("feat", None),
        P(),
        P(),
        P(),
        P(),
    )
    return jax.shard_map(
        body,
        mesh=mesh,
        in_specs=placed,
        out_specs=(P(("groups", "feat"), "rep", None, None), P(("groups", "feat", "rep"), None)),
        check_vma=False,
    )
```

```python
import functools

import jax
import jax.numpy as jnp
from jax import lax
from jax.experimental import pallas as pl
from jax.experimental.pallas import tpu as pltpu
from jax.sharding import PartitionSpec as P

LANES = 128
MIB = 1024 * 1024


def folds(fslice, pcap):
    return 4 * fslice == 3 * LANES and pcap % 64 == 0


def is_dense(fslice, n_idx):
    return fslice % 32 == 0 and n_idx == 16


def parcel_rows(fslice, n_idx):
    return 2 * fslice - fslice // 4 + 8 if is_dense(fslice, n_idx) else 2 * fslice


def write_parcel(ref, weight, feats, digits):
    fslice, lanes = feats.shape
    ref[:fslice, :] = weight
    if is_dense(fslice, digits.shape[0]):
        cut = fslice // 4 * 3
        tail = jnp.concatenate([feats[cut:, i : i + LANES] for i in range(0, lanes, LANES)], axis=0)
        tags = jnp.concatenate([digits[:8], digits[8:]] * 2, axis=1)
        body = jnp.concatenate([feats[:cut], tail], axis=1)
        ref[fslice:, :] = jnp.concatenate([body, tags], axis=0).astype(jnp.bfloat16)
    else:
        ref[fslice:, :lanes] = feats.astype(jnp.bfloat16)
        ref[fslice : fslice + digits.shape[0], lanes:] = digits.astype(jnp.bfloat16)


def read_feats(ref, fslice, n_idx, lanes):
    if not is_dense(fslice, n_idx):
        return ref[fslice:, :lanes].astype(jnp.float32)
    cut, part = fslice // 4 * 3, fslice // 4
    tail = ref[fslice : fslice + cut, lanes:].astype(jnp.float32)
    tail = jnp.concatenate([tail[i : i + part] for i in range(0, cut, part)], axis=1)
    return jnp.concatenate([ref[fslice : fslice + cut, :lanes].astype(jnp.float32), tail], axis=0)


def read_digits(ref, fslice, n_idx, lanes):
    if not is_dense(fslice, n_idx):
        return ref[fslice : fslice + n_idx, lanes:].astype(jnp.float32)
    tags = ref[-8:, : 2 * LANES].astype(jnp.float32)
    return jnp.concatenate([tags[:, :LANES], tags[:, LANES:]], axis=0)


TAG_ROWS = 16


def live_rows(ref):
    return jnp.max(ref[-TAG_ROWS:, :].astype(jnp.float32)).astype(jnp.int32)


def row_code(row):
    high = lax.shift_right_logical(row, 7)
    code = (128 + (row & 127)).astype(jnp.float32)
    for bit in range(7):
        code = code * jnp.where((high >> bit) & 1 == 1, float(2 ** (2**bit)), 1.0)
    return code


def pair_codes(ref_low, ref_high, seed_count, fslice, n_idx, lanes):
    low = lax.broadcasted_iota(jnp.int32, (n_idx, 2 * seed_count), 1) < seed_count
    return jnp.where(
        low,
        read_digits(ref_low, fslice, n_idx, lanes),
        read_digits(ref_high, fslice, n_idx, lanes),
    )


def pack_kernel(
    steps,
    n_feat,
    pcap,
    src_hbm,
    seed_hbm,
    nbr_hbm,
    w_self_hbm,
    w_nbr_hbm,
    pick_hbm,
    *refs,
):
    half = n_feat // 2
    parcel_refs, pick_ref, src_ref = refs[:half], refs[half], refs[half + 1]
    seed_ref, nbr_ref, w_self_ref, w_nbr_ref, fetched_ref, sems = refs[half + 2 :]
    first = pl.ds(0, src_ref.shape[1])
    copies = [
        pltpu.make_async_copy(a, b, sems.at[i])
        for i, (a, b) in enumerate(
            (
                (src_hbm.at[:, first], src_ref),
                (w_self_hbm, w_self_ref),
                (w_nbr_hbm, w_nbr_ref),
                (seed_hbm, seed_ref),
                (nbr_hbm, nbr_ref),
                (pick_hbm, fetched_ref),
            )
        )
    ]
    for copy in copies:
        copy.start()
    for copy in copies[1:]:
        copy.wait()
    stride = -(-pcap // LANES) * LANES
    words = pick_ref.shape[2] // stride
    for k in range(words):
        word = fetched_ref[:, k]
        if words < fetched_ref.shape[1]:
            word = word | (fetched_ref[:, words + k] << 16)
        pick_ref[:, :, k * stride : k * stride + pcap] = word
    feat_pos = lax.axis_index("feat")
    first_core = lax.axis_index("rep") == 0
    idx = jnp.concatenate([seed_ref[...], nbr_ref[...]], axis=0)
    code = row_code(idx)
    digits = jnp.concatenate([code, code], axis=1)
    weight = jnp.where(first_core, w_self_ref[...], w_nbr_ref[...])
    copies[0].wait()
    for s, parcel_ref in zip(steps, parcel_refs):
        sides = []
        for step in (s, s ^ half):
            at = pl.multiple_of(jnp.bitwise_xor(feat_pos, step) * (2 * pcap), LANES)
            block = src_ref[:, pl.ds(at, 2 * pcap)].astype(jnp.float32)
            sides.append(jnp.where(first_core, block[:, :pcap], block[:, pcap:]))
        write_parcel(parcel_ref, weight, jnp.concatenate(sides, axis=1), digits)


def turn_kernel(owned_ref, src_hbm, table_ref):
    fslice, owned = owned_ref.shape
    pieces = src_hbm.shape[1] // owned - 1
    width = next(w for w in (2048, 1536, 1024, 512, LANES) if owned % w == 0)

    def turn(ref, low, place):
        def step(i, carry):
            at = pl.multiple_of(i * width, width)
            rows = pl.ds(pl.multiple_of(place + at, LANES), width)
            table_ref[rows, :fslice] = ref[:, pl.ds(low + at, width)].T.astype(jnp.float32)
            return carry

        lax.fori_loop(0, owned // width, step, 0)

    def rest(buffer, sems):
        copies = [
            pltpu.make_async_copy(
                src_hbm.at[:, pl.ds((i + 1) * owned, owned)],
                buffer.at[:, pl.ds(i * owned, owned)],
                sems.at[i],
            )
            for i in range(pieces)
        ]
        for copy in copies:
            copy.start()
        turn(owned_ref, 0, 0)
        for i, copy in enumerate(copies):
            copy.wait()
            turn(buffer, i * owned, (i + 1) * owned)

    pl.run_scoped(
        rest,
        pltpu.VMEM((fslice, pieces * owned), jnp.bfloat16),
        pltpu.SemaphoreType.DMA((pieces,)),
    )


def mean_kernel(chosen, packed, fanout, pcap, fslice, turns, before, n_before, *refs):
    count = len(chosen)
    before_in, refs = refs[: n_before[0]], refs[n_before[0] :]
    nbr_any, *refs = refs
    if not turns:
        table_ref, *refs = refs
    out_ref, total, nbr_ref, live_ref, sems = refs[-5:]
    refs = refs[:-5]
    before_out = refs[len(refs) - n_before[1] :]
    refs = refs[: len(refs) - n_before[1]]
    chunk_refs, tagged_refs = refs[len(refs) - count :], refs[: len(refs) - count]
    feat_pos = lax.axis_index("feat")
    words = fanout // packed
    size = 16 if len(tagged_refs) or pcap % 64 else 64
    stride = -(-pcap // LANES) * LANES
    length = words * stride
    copies = [
        pltpu.make_async_copy(
            nbr_any.at[feat_pos ^ step, 0], nbr_ref.at[pl.ds(i * length, length)], sems.at[i]
        )
        for i, step in enumerate(chosen)
    ]
    for copy in copies:
        copy.start()
    for i in range(count):
        live_ref[i] = pcap
    for i, ref in enumerate(tagged_refs):
        live_ref[i] = live_rows(ref)
    if before is not None:
        before(*before_in, *before_out)
    if turns:
        table_ref = before_out[0].reshape(before_out[0].shape[0], 1, LANES)
    for copy in copies:
        copy.wait()

    def partition(i, carry):
        first = i * length

        def group(g, inner):
            at = pl.multiple_of(g * size, 16)
            start = first + at
            sums = []
            for u in range(size):
                names = [nbr_ref[start + (k * stride + u)] for k in range(words)]
                if packed == 2:
                    names = [
                        part
                        for name in names
                        for part in (name & 0xFFFF, lax.shift_right_logical(name, 16))
                    ]
                rows = [table_ref[name] for name in names]
                while len(rows) > 1:
                    rows = [a + b for a, b in zip(rows[::2], rows[1::2])] + (
                        [rows[-1]] if len(rows) % 2 else []
                    )
                sums.append(rows[0])
                if len(sums) == 16:
                    for v, row in enumerate(sums):
                        total[pl.ds(at + (u - 15 + v), 1), :] = row
                    sums = []
            return inner

        lax.fori_loop(0, lax.div(live_ref[i] + size - 1, size), group, 0)
        mean = total[...] / fanout
        if folds(fslice, pcap):
            part = pcap // 4
            lane = lax.broadcasted_iota(jnp.int32, (part, LANES), 1)
            tail = mean[3 * part :]
            for b in range(3):
                shift = (fslice - 32 * b) % LANES
                moved = pltpu.roll(tail, shift, 1) if shift else tail
                out_ref[i, pl.ds(b * part, part), :] = jnp.where(
                    lane < fslice, mean[b * part : (b + 1) * part], moved
                ).astype(jnp.bfloat16)
        else:
            out_ref[i] = mean[:, :fslice].astype(jnp.bfloat16)
        return carry

    lax.fori_loop(0, count, partition, 0)
    for i, ref in enumerate(chunk_refs):
        ref[...] = out_ref[i]


def unfold(ref, fslice, pcap):
    if not folds(fslice, pcap):
        return ref[:pcap, :]
    part = pcap // 4
    wide = ref[: 3 * part, :].astype(jnp.float32)
    lane = lax.broadcasted_iota(jnp.int32, (part, LANES), 1)
    tail = pltpu.roll(wide[:part], LANES - fslice, 1)
    for b in (1, 2):
        shift = (32 * b - fslice) % LANES
        moved = wide[b * part : (b + 1) * part]
        moved = pltpu.roll(moved, shift, 1) if shift else moved
        tail = jnp.where(lane // 32 == b, moved, tail)
    return jnp.concatenate([wide, tail], axis=0)[:, :fslice].astype(jnp.bfloat16)


def halves_kernel(half, count_ref, *refs):
    parcel_refs, chunk_refs = refs[:half], refs[half : 2 * half - 1]
    out_ref, *tagged_refs, live_ref = refs[2 * half - 1 :]
    for s, ref in enumerate(parcel_refs):
        out_ref[s] = ref[: out_ref.shape[1], :]
    live = jnp.full(live_ref.shape, count_ref[0, 0].astype(jnp.float32)).astype(jnp.bfloat16)
    live_ref[...] = live
    for chunk_ref, ref in zip(chunk_refs, tagged_refs):
        ref[:-TAG_ROWS, :] = chunk_ref[...]
        ref[-TAG_ROWS:, :] = live


def own_product(parcel_refs, other_ref, n_idx, pcap, lanes):
    first_core = lax.axis_index("rep") == 0
    fslice = other_ref.shape[1]
    feats, weights = [], []
    for s, ref in enumerate(parcel_refs):
        weights.append(jnp.where(first_core, ref[:fslice, :], other_ref[s]))
        feats.append(read_feats(ref, fslice, n_idx, 2 * pcap)[:, lanes])
    return jnp.dot(
        jnp.concatenate(feats, axis=0).T.astype(jnp.bfloat16),
        jnp.concatenate(weights, axis=0),
        preferred_element_type=jnp.float32,
    )


def own_kernel(half, n_idx, *refs):
    parcel_refs = refs[:half]
    other_ref, w_ref, far_ref, idx_ref = refs[half:]
    fslice = w_ref.shape[1]
    pcap = far_ref.shape[0]
    first_core = lax.axis_index("rep") == 0
    for s in range(half):
        w_ref[s] = jnp.where(first_core, other_ref[s], parcel_refs[s][:fslice, :])
    part = n_idx // 2
    blocks = []
    for s in range(0, half, 2):
        codes = pair_codes(
            parcel_refs[s], parcel_refs[s + 1], LANES // 2, fslice, n_idx, 2 * pcap
        )
        blocks += [codes[:part], codes[part:]]
    for i in range(0, len(blocks), 4):
        rows = slice(i // 4 * part, (i // 4 + 1) * part)
        idx_ref[rows, :] = jnp.concatenate(blocks[i : i + 4], axis=1).astype(jnp.bfloat16)
    far_ref[...] = own_product(parcel_refs, other_ref, n_idx, pcap, slice(pcap, 2 * pcap))


def add_means(half, pre, mean_refs, w_ref, turn=0):
    for s, ref in enumerate(mean_refs):
        pre = pre + jnp.dot(
            unfold(ref, w_ref.shape[1], pre.shape[0]),
            w_ref[(s + turn) % (half - 1) if s < half - 1 else s],
            preferred_element_type=jnp.float32,
        )
    return pre


def far_kernel(half, *refs):
    far_ref, w_ref, idx_ref, cross_ref = refs[half:]
    pcap = far_ref.shape[0]
    cross_ref[:pcap, :] = add_means(half, far_ref[...], refs[:half], w_ref).astype(jnp.bfloat16)
    cross_ref[pcap:, :] = idx_ref[...]


def store_times(pcap, names, out_ref):
    n_idx, pair = names[0].shape
    seed_count = pair // 2
    core_rows = lax.axis_index("feat") * (2 * pcap)
    rep_pos = lax.axis_index("rep")
    row = lax.broadcasted_iota(jnp.int32, (2 * pcap, pair), 0)
    slot = row_code(
        jnp.where(row < pcap, row + core_rows + rep_pos * pcap, row + core_rows - rep_pos * pcap)
    )
    for s, name in zip(range(0, 2 * len(names), 2), names):
        own = jnp.where(slot == name[:1], 1.0, 0.0)
        near = jnp.zeros((2 * pcap, pair), jnp.float32)
        for k in range(1, n_idx):
            near = near + jnp.where(slot == name[k : k + 1], 1.0, 0.0)
        place = pl.ds(s * seed_count, pair)
        out_ref[place, : 2 * pcap] = own.T.astype(jnp.bfloat16)
        out_ref[place, 2 * pcap :] = near.T.astype(jnp.bfloat16)


def near_times_kernel(half, fslice, pcap, n_idx, _, __, other_ref, bias_ref, *refs):
    names = [
        pair_codes(refs[s], refs[s + 1], LANES // 2, fslice, n_idx, 2 * pcap)
        for s in range(0, half, 2)
    ]
    store_times(pcap, names, refs[half])
    own = own_product(refs[:half], other_ref, n_idx, pcap, slice(0, pcap))
    refs[half + 1][...] = own + bias_ref[...]


def far_times_kernel(
    half,
    n_idx,
    fanout_two,
    cross_ref,
    hidden_ref,
    ws_ref,
    wn_ref,
    out_ref,
    value_ref,
    result_ref,
    sem,
):
    copy = pltpu.make_async_copy(hidden_ref, result_ref, sem)
    copy.start()
    pcap = hidden_ref.shape[0]
    part = n_idx // 2
    blocks = [
        cross_ref[
            pcap + i // 4 * part : pcap + (i // 4 + 1) * part, i % 4 * LANES : (i % 4 + 1) * LANES
        ].astype(jnp.float32)
        for i in range(half)
    ]
    names = [jnp.concatenate(blocks[i : i + 2], axis=0) for i in range(0, half, 2)]
    store_times(pcap, names, out_ref)
    store_values(hidden_ref[...], ws_ref, wn_ref, fanout_two, value_ref)
    copy.wait()


def store_values(hidden, ws_ref, wn_ref, fanout_two, value_ref):
    value_ref[0] = jnp.dot(hidden, ws_ref[...], preferred_element_type=jnp.float32).astype(
        jnp.bfloat16
    )
    value_ref[1] = (
        jnp.dot(hidden, wn_ref[...], preferred_element_type=jnp.float32) / fanout_two
    ).astype(jnp.bfloat16)


def near_kernel(half, *refs):
    pre_ref, w_ref, out_ref = refs[half:]
    out_ref[...] = add_means(half, pre_ref[...], refs[:half], w_ref)


def hidden_kernel(live_ref, pre_ref, cross_ref, hidden_ref):
    pcap, width = hidden_ref.shape
    pre = pre_ref[...] + cross_ref[:pcap, :].astype(jnp.float32)
    live = lax.broadcasted_iota(jnp.int32, (pcap, width), 0) < live_rows(live_ref)
    hidden_ref[...] = jnp.where(live, jnp.maximum(pre, 0.0), 0.0).astype(jnp.bfloat16)


def far_share_kernel(
    half, fanout_two, far_ref, value_ref, hidden_ref, ws_ref, wn_ref, *refs
):
    *out_refs, values_ref = refs
    pcap = hidden_ref.shape[0]
    for i in range(2):
        values_ref[2 * i * pcap : (2 * i + 1) * pcap, :] = value_ref[i]
    hidden = hidden_ref[...]
    values_ref[pcap : 2 * pcap, :] = jnp.dot(
        hidden, ws_ref[...], preferred_element_type=jnp.float32
    ).astype(jnp.bfloat16)
    values_ref[3 * pcap :, :] = (
        jnp.dot(hidden, wn_ref[...], preferred_element_type=jnp.float32) / fanout_two
    ).astype(jnp.bfloat16)
    store_shares(far_ref, values_ref, out_refs)


def store_shares(times_ref, values_ref, out_refs):
    rows = times_ref.shape[0] // len(out_refs)
    part = jnp.dot(times_ref[...], values_ref[...], preferred_element_type=jnp.float32)
    for s, ref in enumerate(out_refs):
        ref[...] = part[s * rows : (s + 1) * rows].astype(jnp.bfloat16)


def near_share_kernel(places, near_ref, values_ref, *out_refs):
    for place, ref in zip(places, out_refs):
        rows = ref.shape[0]
        times = near_ref[place * rows : (place + 1) * rows, :]
        ref[...] = jnp.dot(times, values_ref[...], preferred_element_type=jnp.float32).astype(
            jnp.bfloat16
        )


def side_sum_kernel(*refs):
    total = refs[0][...].astype(jnp.float32)
    for ref in refs[1:-1]:
        total = total + ref[...].astype(jnp.float32)
    refs[-1][: total.shape[0], :] = total.astype(jnp.bfloat16)


def last_kernel(bias_ref, *refs):
    total = bias_ref[...]
    for ref in refs[:-1]:
        total = total + ref[: refs[-1].shape[0], :].astype(jnp.float32)
    refs[-1][...] = jnp.maximum(total, 0.0).astype(jnp.bfloat16)


def swap(value, axis, step):
    size = lax.axis_size(axis)
    return lax.ppermute(value, axis, [(i, i ^ step) for i in range(size)])


def body(
    src_feats,
    nbr_one,
    counts,
    seed_rows,
    nbr_two,
    w1_self,
    w1_nbr,
    bias_one,
    w2_self,
    w2_nbr,
    bias_two,
):
    n_feat = lax.axis_size("feat")
    half = n_feat // 2
    steps = list(range(half - 1, -1, -1))
    fslice, nodes = src_feats.shape
    fanout_one, pcap = nbr_one.shape[2:]
    width = w1_self.shape[1]
    seed_count, fanout_two = nbr_two.shape
    n_idx = fanout_two + 1
    bf16 = jnp.bfloat16
    vmem = pl.BlockSpec(memory_space=pltpu.VMEM)
    smem = pl.BlockSpec(memory_space=pltpu.SMEM)
    hbm = pl.BlockSpec(memory_space=pltpu.HBM)
    anywhere = pl.BlockSpec(memory_space=pl.ANY)
    table_bytes = nodes * LANES * 4

    def call(kernel, name, shapes, ins, args, after=(), scratch=(), limit=16 * MIB, cost_us=1, outs=None):
        def wrapped(*refs):
            kernel(*refs[: len(args)], *refs[len(args) + len(after) :])

        return pl.pallas_call(
            wrapped,
            out_shape=tuple(jax.ShapeDtypeStruct(shape, dtype) for shape, dtype in shapes),
            in_specs=[*ins, *([anywhere] * len(after))],
            out_specs=outs or (vmem,) * len(shapes),
            scratch_shapes=scratch,
            compiler_params=pltpu.CompilerParams(vmem_limit_bytes=limit),
            cost_estimate=pl.CostEstimate(
                flops=int(cost_us * 1_100_000_000), bytes_accessed=0, transcendentals=0
            ),
            name=name,
        )(*args, *after)

    def pinned(value):
        return pltpu.with_memory_space_constraint(value, pltpu.HBM)

    def send(chunks, steps=steps):
        return [swap(chunk, "feat", s) if s else chunk for s, chunk in zip(steps, chunks)]

    owned = n_feat * 2 * pcap
    picks = jnp.transpose(nbr_one, (0, 2, 1, 3))
    packed = 2 if fanout_one % 2 == 0 and nodes <= 1 << 16 else 1
    words = (n_feat, 1, fanout_one // packed * (-(-pcap // LANES) * LANES))
    *parcels, picks, feats = call(
        functools.partial(pack_kernel, steps, n_feat, pcap),
        "pack",
        [((parcel_rows(fslice, n_idx), width), bf16)] * half
        + [(words, jnp.int32), ((fslice, owned), bf16)],
        [hbm] * 6,
        [pinned(x) for x in (src_feats, seed_rows[None], nbr_two.T, w1_self, w1_nbr, picks)],
        scratch=[
            pltpu.VMEM((1, seed_count), jnp.int32),
            pltpu.VMEM((fanout_two, seed_count), jnp.int32),
            pltpu.VMEM((fslice, width), bf16),
            pltpu.VMEM((fslice, width), bf16),
            pltpu.VMEM((n_feat, fanout_one, 1, pcap), jnp.int32),
            pltpu.SemaphoreType.DMA((6,)),
        ],
        limit=32 * MIB,
    )
    arrived = send(parcels)
    chunk_shape = (pcap // 4 * 3, LANES) if folds(fslice, pcap) else (pcap, fslice)

    def means(chosen, tagged=(), after=(), before=None, ins=(), outs=(), table=None):
        count = len(chosen)
        tables = () if table is None else (table,)
        return call(
            functools.partial(
                mean_kernel,
                tuple(chosen),
                packed,
                fanout_one,
                pcap,
                fslice,
                table is None,
                before,
                (len(ins), len(outs)),
            ),
            "mean",
            [(chunk_shape, bf16)] * count + list(outs),
            ([vmem, hbm] if table is None else [vmem] * len(ins))
            + [anywhere]
            + [vmem] * (len(tables) + len(tagged)),
            (*ins, picks, *tables, *tagged),
            after=after,
            scratch=[
                pltpu.VMEM((count, *chunk_shape), bf16),
                pltpu.VMEM((pcap, LANES), jnp.float32),
                pltpu.SMEM((count * words[2],), jnp.int32),
                pltpu.SMEM((count,), jnp.int32),
                pltpu.SemaphoreType.DMA((count,)),
            ],
            limit=table_bytes + 8 * MIB,
            cost_us=2 * count if count > 1 else 0,
        )

    *far_means, table = means(
        [s + half for s in steps if s],
        before=turn_kernel,
        ins=(feats, pinned(src_feats)),
        outs=[((nodes, LANES), jnp.float32)],
    )
    table = table.reshape(nodes, 1, LANES)
    tagged_shape = (chunk_shape[0] + TAG_ROWS, chunk_shape[1])
    halves, *tagged, live = call(
        functools.partial(halves_kernel, half),
        "halves",
        [
            ((half, fslice, width), bf16),
            *([(tagged_shape, bf16)] * (half - 1)),
            ((TAG_ROWS, chunk_shape[1]), bf16),
        ],
        [smem] + [vmem] * (2 * half - 1),
        (counts, *arrived, *far_means),
    )
    far_arrived = send(tagged)
    other_halves = swap(halves, "rep", 1)
    idx_rows = half // 4 * (n_idx // 2)
    far_own, w_nbr, far_pre, idx_tags = means(
        [half],
        table=table,
        before=functools.partial(own_kernel, half, n_idx),
        ins=(*arrived, other_halves),
        outs=[
            ((half, fslice, width), bf16),
            ((pcap, width), jnp.float32),
            ((idx_rows, width), bf16),
        ],
    )
    (cross,) = call(
        functools.partial(far_kernel, half),
        "far",
        [((pcap + idx_rows, width), bf16)],
        [vmem] * (half + 3),
        (*far_arrived, far_own, far_pre, w_nbr, idx_tags),
    )
    cross_arrived = swap(cross, "feat", half)
    turned = steps[:-1]
    near_means = means(turned, far_arrived, (cross,), table=table)
    near_arrived = send(near_means, turned)
    near_own, near_times, pre = means(
        [0],
        [live],
        table=table,
        after=(cross,),
        before=functools.partial(near_times_kernel, half, fslice, pcap, n_idx),
        ins=(w2_self, w2_nbr, other_halves, bias_one[None], *arrived),
        outs=[((half * seed_count, 4 * pcap), bf16), ((pcap, width), jnp.float32)],
    )
    (near_pre,) = call(
        functools.partial(near_kernel, half),
        "near",
        [((pcap, width), jnp.float32)],
        [vmem] * (half + 2),
        (*near_arrived, near_own, pre, w_nbr),
        cost_us=0,
    )
    (hidden,) = call(
        hidden_kernel,
        "hidden",
        [((pcap, width), bf16)],
        [vmem] * 3,
        (live, near_pre, cross_arrived),
    )
    other_hidden = swap(hidden, "rep", 1)
    far_times, value, result = call(
        functools.partial(far_times_kernel, half, n_idx, fanout_two),
        "far_times",
        [
            ((half * seed_count, 4 * pcap), bf16),
            ((2, pcap, width), bf16),
            ((pcap, width), bf16),
        ],
        [vmem] * 4,
        (cross_arrived, hidden, w2_self, w2_nbr),
        scratch=[pltpu.SemaphoreType.DMA],
        outs=(vmem, vmem, anywhere),
    )
    *far_shares, values = call(
        functools.partial(far_share_kernel, half, fanout_two),
        "far_share",
        [((seed_count, width), bf16)] * half + [((4 * pcap, width), bf16)],
        [vmem] * 5,
        (far_times, value, other_hidden, w2_self, w2_nbr),
        limit=32 * MIB,
    )
    far_shares = send(far_shares)
    def near_share(places, after=()):
        return call(
            functools.partial(near_share_kernel, places),
            "near_share",
            [((seed_count, width), bf16)] * len(places),
            [vmem] * 2,
            (near_times, values),
            after=after,
            limit=32 * MIB,
        )

    *near_shares, near_last = near_share([*range(half - 2), half - 1])
    near_shares = [swap(share, "feat", s) for share, s in zip(near_shares, steps)]
    (far_sum,) = call(
        side_sum_kernel, "side_sum", [((seed_count + 8, width), bf16)], [vmem] * half, far_shares
    )
    (near_late,) = near_share([half - 2], (far_sum,))
    (seed_out,) = call(
        last_kernel,
        "seeds",
        [((seed_count, width), bf16)],
        [vmem] * (half + 2),
        (
            bias_two[None],
            *near_shares,
            swap(near_late, "feat", 1),
            near_last,
            swap(far_sum, "feat", half),
        ),
    )
    return (result[None, None], seed_out)


def solution(mesh):
    placed = (
        P("feat", "groups"),
        P("groups", "rep", None, None),
        P(("groups", "feat"), "rep"),
        P(("groups", "feat", "rep")),
        P(("groups", "feat", "rep"), None),
        P("feat", None),
        P("feat", None),
        P(),
        P(),
        P(),
        P(),
    )
    return jax.shard_map(
        body,
        mesh=mesh,
        in_specs=placed,
        out_specs=(P(("groups", "feat"), "rep", None, None), P(("groups", "feat", "rep"), None)),
        check_vma=False,
    )
```
